32 devices in a mesh: rep: 2 (over x), fsdp: 16 (over z, y, core).
Axes of the slice: x: 2, y: 2, z: 4, core: 2. Of those that a mesh axis runs over, the one named last changes fastest.
Arguments:
- tokens: bfloat16 [12288, 1536], P(('rep', 'fsdp')), may hold values from -6 to 6
- cotangent: bfloat16 [12288, 1536], P(('rep', 'fsdp')), may hold values from -6 to 6
- routes: int32 [12288, 8], P(('rep', 'fsdp')), may hold values from 0 to 15, all different within a row; in each aligned block of 384 rows (0 to 383, 384 to 767, ...) at most 240 rows name the same one
- gates: float32 [12288, 8], P(('rep', 'fsdp')), may hold values from 0.0625 to 0.25
- starts: int32 [32], P(('rep', 'fsdp')), may hold values from 0 to 128
- norm1_gain: float32 [1536], P('fsdp'), may hold values from 0.1 to 1.9
- w_query: float32 [1536, 1536], P('fsdp'), may hold values from -0.21875 to 0.21875
- w_key: float32 [1536, 512], P('fsdp'), may hold values from -0.21875 to 0.21875
- w_value: float32 [1536, 512], P('fsdp'), may hold values from -0.15625 to 0.15625
- w_out: float32 [1536, 1536], P('fsdp'), may hold values from -0.625 to 0.625
- norm2_gain: float32 [1536], P('fsdp'), may hold values from 0.1 to 1.9
- w_gate: float32 [1536, 16, 512], P('fsdp'), may hold values from -0.15625 to 0.15625
- w_up: float32 [1536, 16, 512], P('fsdp'), may hold values from -0.15625 to 0.15625
- w_down: float32 [512, 16, 1536], P('fsdp'), may hold values from -1 to 1
Outputs:
- output: float32 [12288, 1536], P(('rep', 'fsdp'))
- input_grad: float32 [12288, 1536], P(('rep', 'fsdp'))
- norm1_gain_grad: float32 [1536], P('fsdp')
- w_query_grad: float32 [1536, 1536], P('fsdp')
- w_key_grad: float32 [1536, 512], P('fsdp')
- w_value_grad: float32 [1536, 512], P('fsdp')
- w_out_grad: float32 [1536, 1536], P('fsdp')
- norm2_gain_grad: float32 [1536], P('fsdp')
- w_gate_grad: float32 [1536, 16, 512], P('fsdp')
- w_up_grad: float32 [1536, 16, 512], P('fsdp')
- w_down_grad: float32 [512, 16, 1536], P('fsdp')
The draws below stay inside these ranges and needn't reach their ends.
Inputs may be any that keep to these rules, and one draw needn't show every extreme that they name: `routes`: each row names 8 different experts; in the rows of one device no expert is named by more than 240 rows, and in some device one expert is named by exactly 240.
All inputs are finite; a program needn't handle non-finite values.
Results may differ from the reference program's by a relative error of at most 0.023.
Values may be sent and summed in bfloat16 or wider, within the bound.
A program may use at most 448 MiB of HBM per device.

```python
import math
import jax
import jax.numpy as jnp
import numpy as np
from jax import lax

HEADS = 24
KV_HEADS = 8
HEAD = 64
HID = 512
EXP = 16
TOP = 8
PIECE = 256
TOK_DEV = 384
D = 1536
KVD = 512
CAP = 240
SEQS = 32
TOKENS = 12288


def with_ends(drawn, rng, low, largest):
    shape = drawn.shape
    place = [jax.random.randint(jax.random.fold_in(rng, axis), (), 0, shape[axis]) for axis in range(len(shape))]
    drawn = drawn.at[tuple(place)].set(low)
    longest = shape.index(max(shape))
    place[longest] = (place[longest] + 1) % shape[longest]
    return drawn.at[tuple(place)].set(largest)


def block_levels(key, dims, split, low, largest):
    def one(position, shards_of):
        heights = jax.random.uniform(jax.random.fold_in(jax.random.fold_in(key, 6), position), (shards_of,), jnp.float32, low / len(split), largest / len(split))
        return jnp.repeat(jnp.exp(heights), dims[position] // shards_of).reshape((-1,) + (1,) * (len(dims) - position - 1))

    level = one(*split[0])
    for cut in split[1:]:
        level = level * one(*cut)
    return level


def routed_block(stream_key, own, number, rows, amount, top, limit, slope):
    order = jax.random.permutation(stream_key, amount)
    heavy_load, ordinary = load_shares(amount, rows * top, limit, slope, True), load_shares(amount, rows * top, limit, slope, False)
    places = jnp.arange(amount)

    def named(lengths, rotation):
        used = int((lengths > 0).sum())
        fixed = max(1, used // 4)
        shifted = fixed + (places - fixed + rotation * (used - fixed)) % max(1, amount - fixed)
        return jnp.zeros((amount,), jnp.int32).at[order[jnp.where(places < fixed, places, shifted)]].set(jnp.asarray(lengths, jnp.int32))

    lengths = jnp.where(number % 4 == 0, named(heavy_load, number // 4), named(ordinary, number - number // 4 - 1))
    mixed = jax.random.permutation(jax.random.fold_in(own, 3), amount)
    giver, receiver = mixed[0:amount // 2 * 2:2], mixed[1:amount // 2 * 2:2]
    slack = jnp.minimum(lengths[giver] - 1, limit - lengths[receiver]) // 2
    slack = jnp.where((giver == order[0]) | (receiver == order[0]) | (lengths[receiver] == 0), 0, jnp.maximum(slack, 0))
    shifted = jax.random.randint(jax.random.fold_in(own, 4), (amount // 2,), 0, 1 << 20) % (slack + 1)
    lengths = lengths.at[giver].add(-shifted).at[receiver].add(shifted)
    members = jnp.searchsorted(jnp.cumsum(lengths), jnp.arange(rows * top), side="right").astype(jnp.int32)
    listing = members.reshape(top, rows).T
    listing = listing[jax.random.permutation(jax.random.fold_in(own, 1), rows)]
    rotation = jax.random.randint(jax.random.fold_in(own, 2), (rows, 1), 0, top)
    return jnp.take_along_axis(listing, (jnp.arange(top)[None, :] + rotation) % top, axis=1)


def load_shares(number_of, total, limit, slope, full):
    loads = [(1 << 20) // math.isqrt(rank ** slope) + 1 for rank in range(1, number_of + 1)]
    largest = limit if full else min(limit, max(-(-total // number_of), total * loads[0] // sum(loads)))
    least = 1 if total - largest >= number_of - 1 else 0
    counts, rest = [largest] + [least] * (number_of - 1), total - largest - least * (number_of - 1)
    while rest > 0:
        candidates = [i for i in range(1, number_of) if counts[i] < largest] or [i for i in range(1, number_of) if counts[i] < limit]
        whole, budget = sum([loads[i] for i in candidates]), rest
        for i in candidates:
            extra = min(limit - counts[i], max(1, budget * loads[i] // whole), rest)
            counts[i] = counts[i] + extra
            rest = rest - extra
    return np.array(counts)


def bell_draw(key, shape, scale, limit, split=(), kind=jnp.bfloat16):
    result = jax.random.normal(key, shape, jnp.float32) * scale
    if len(split) > 0:
        result = block_levels(key, shape, split, -0.22, 0.18) * result
    return jnp.clip(result, min=-limit, max=limit).astype(kind)


def setup_inputs(seed: int = 0) -> dict:
    arg_keys = jax.random.split(jax.random.key(seed), 15)
    tokens = bell_draw(arg_keys[0], (TOKENS, D), 1.0, 6.0, ((0, 32),))
    cotangent = bell_draw(arg_keys[1], (TOKENS, D), 1.0, 6.0, ((0, 32),))
    routes_keys = jax.random.split(jax.random.fold_in(arg_keys[2], 1), TOKENS // TOK_DEV)
    routes_turns = jax.random.permutation(jax.random.fold_in(arg_keys[2], 3), TOKENS // TOK_DEV)
    routes = jax.vmap(lambda own, number: routed_block(jax.random.fold_in(arg_keys[2], 2), own, number, TOK_DEV, EXP, TOP, CAP, 1))(routes_keys, routes_turns).reshape((TOKENS, TOP))
    gates = jnp.clip(jnp.exp(math.log(0.25) - 1.3862944 * jax.random.uniform(arg_keys[3], (TOKENS, TOP), jnp.float32) ** block_levels(arg_keys[3], (TOKENS, TOP), ((0, 32),), -0.2, 0.2)), 0.0625, 0.25)
    starts = with_ends(jax.random.randint(arg_keys[4], (SEQS,), 0, TOK_DEV - PIECE + 1), jax.random.fold_in(arg_keys[4], 1), 0, TOK_DEV - PIECE).astype(jnp.int32)
    norm1_gain = jnp.clip(1.0 + 0.18 * jax.random.normal(arg_keys[5], (D,), jnp.float32), 0.1, 1.9)
    w_query = bell_draw(arg_keys[6], (D, D), (D // 2) ** -0.5, 0.21875, ((0, 16),), jnp.float32)
    w_key = bell_draw(arg_keys[7], (D, KVD), (D // 2) ** -0.5, 0.21875, ((0, 16),), jnp.float32)
    w_value = bell_draw(arg_keys[8], (D, KVD), D ** -0.5, 0.15625, ((0, 16),), jnp.float32)
    w_out = bell_draw(arg_keys[9], (D, D), (D // 16) ** -0.5, 0.625, ((0, 16),), jnp.float32)
    norm2_gain = jnp.clip(1.0 + 0.18 * jax.random.normal(arg_keys[10], (D,), jnp.float32), 0.1, 1.9)
    w_gate = bell_draw(arg_keys[11], (D, EXP, HID), D ** -0.5, 0.15625, ((0, 16),), jnp.float32)
    w_up = bell_draw(arg_keys[12], (D, EXP, HID), D ** -0.5, 0.15625, ((0, 16),), jnp.float32)
    w_down = bell_draw(arg_keys[13], (HID, EXP, D), (HID // 16) ** -0.5, 1.0, ((0, 16),), jnp.float32)
    return dict(tokens=tokens, cotangent=cotangent, routes=routes, gates=gates, starts=starts, norm1_gain=norm1_gain, w_query=w_query, w_key=w_key, w_value=w_value, w_out=w_out, norm2_gain=norm2_gain, w_gate=w_gate, w_up=w_up, w_down=w_down)


@jax.custom_vjp
def low(v):
    return lax.optimization_barrier(v.astype(jnp.bfloat16)).astype(jnp.float32)

@jax.custom_vjp
def low_back(v):
    return v

def low_keep(v):
    return (low(v), None)

def low_pass(kept, grad):
    return (grad,)

def back_keep(v):
    return (v, None)

def back_low(kept, grad):
    return (low(grad),)
low.defvjp(low_keep, low_pass)
low_back.defvjp(back_keep, back_low)
EPSILON = 1e-05
NEG_FILL = -1e+30
HIGH = lax.Precision.HIGHEST

def rope_tables(length, head_dim):
    half_dim = head_dim // 2
    positions = jnp.arange(length, dtype=jnp.float32)[:, None]
    inverse_rates = jnp.exp(jnp.arange(half_dim, dtype=jnp.float32) * (-2.0 * math.log(10000.0) / head_dim))
    angles = positions * inverse_rates[None, :]
    return (jnp.cos(angles)[:, None, :], jnp.sin(angles)[:, None, :])

def rotate(values, cosine_table, sine_table):
    half_dim = values.shape[-1] // 2
    leading_half_dims = values[..., :half_dim]
    second_half = values[..., half_dim:]
    return jnp.concatenate([leading_half_dims * cosine_table - second_half * sine_table, second_half * cosine_table + leading_half_dims * sine_table], axis=-1)

def forward(inputs, norm1_gain, w_query, w_key, w_value, w_out, norm2_gain, w_gate, w_up, w_down, starts, routes, gates):
    seq_count, length, width = inputs.shape
    group_size = HEADS // KV_HEADS
    score_scale = 1.0 / math.sqrt(HEAD)
    gain_one = low(norm1_gain)
    query_w = low(w_query)
    key_w = low(w_key)
    value_w = low(w_value)
    out_w = low(w_out)
    gain_two = low(norm2_gain)
    gate_w = low(w_gate)
    up_w = low(w_up)
    down_w = low(w_down)
    inv_one = lax.rsqrt(lax.optimization_barrier(jnp.mean(inputs * inputs, axis=2, keepdims=True)) + EPSILON)
    normed = low(inputs * inv_one * gain_one)
    query_raw = low_back(jnp.einsum('bld,de->ble', normed, query_w, precision=HIGH)).reshape(seq_count, length, HEADS, HEAD)
    key_unrotated = low_back(jnp.einsum('bld,de->ble', normed, key_w, precision=HIGH)).reshape(seq_count, length, KV_HEADS, HEAD)
    value_reduced_precision = low(low_back(jnp.einsum('bld,de->ble', normed, value_w, precision=HIGH))).reshape(seq_count, length, KV_HEADS, HEAD)
    cosine_table, sine_table = rope_tables(length, HEAD)
    query_rotated = low(rotate(query_raw, cosine_table, sine_table)).reshape(seq_count, length, KV_HEADS, group_size, HEAD)
    key_rotated = low(rotate(key_unrotated, cosine_table, sine_table))
    places = jnp.arange(length, dtype=jnp.int32)
    inside = (places[None, :] >= starts[:, None]) & (places[None, :] < starts[:, None] + PIECE)
    allowed = (places[:, None] >= places[None, :])[None] | inside[:, :, None] & inside[:, None, :]
    scores = jnp.einsum('btgrc,bsgc->bgrts', query_rotated, key_rotated, precision=HIGH) * score_scale
    scores = low_back(jnp.where(allowed[:, None, None], scores, NEG_FILL))
    row_peak = lax.optimization_barrier(jnp.max(scores, axis=4, keepdims=True))
    exponent = jnp.exp(scores - row_peak)
    attn_probs = low(exponent / lax.optimization_barrier(jnp.sum(exponent, axis=4, keepdims=True)))
    attended = low(low_back(jnp.einsum('bgrts,bsgc->btgrc', attn_probs, value_reduced_precision, precision=HIGH))).reshape(seq_count, length, width)
    residual = inputs + low_back(jnp.einsum('bld,de->ble', attended, out_w, precision=HIGH))
    inv_two = lax.rsqrt(lax.optimization_barrier(jnp.mean(residual * residual, axis=2, keepdims=True)) + EPSILON)
    normed_two = low(residual * inv_two * gain_two).reshape(seq_count * length, width)
    matches = (routes[:, :, None] == jnp.arange(EXP, dtype=jnp.int32)[None, None, :]).astype(jnp.float32)
    shares = lax.optimization_barrier(jnp.sum(gates[:, :, None] * matches, axis=1))

    def one_expert(moe_sum, pack):
        expert_gate, expert_up, expert_down, expert_share = pack
        gate_pre = low_back(jnp.dot(normed_two, expert_gate, precision=HIGH))
        up_pre = low_back(jnp.dot(normed_two, expert_up, precision=HIGH))
        inner_act = low(gate_pre * jax.nn.sigmoid(gate_pre) * up_pre)
        expert_out = low_back(jnp.dot(inner_act, expert_down, precision=HIGH))
        return (moe_sum + expert_share[:, None] * expert_out, None)
    moe_start = jnp.zeros((seq_count * length, width), jnp.float32)
    moe_sum, leftover = lax.scan(jax.checkpoint(one_expert), moe_start, (jnp.moveaxis(gate_w, 1, 0), jnp.moveaxis(up_w, 1, 0), jnp.moveaxis(down_w, 1, 0), shares.T))
    return residual + moe_sum.reshape(seq_count, length, width)

def reference(tokens, cotangent, routes, gates, starts, norm1_gain, w_query, w_key, w_value, w_out, norm2_gain, w_gate, w_up, w_down):
    blocks = SEQS // 8
    inputs = tokens.astype(jnp.float32).reshape(blocks, 8, TOK_DEV, D)
    grad_out = cotangent.astype(jnp.float32).reshape(blocks, 8, TOK_DEV, D)
    route_blocks = routes.reshape(blocks, 8 * TOK_DEV, TOP)
    gate_blocks = gates.reshape(blocks, 8 * TOK_DEV, TOP)
    start_blocks = starts.reshape(blocks, 8)
    weights = (norm1_gain, w_query, w_key, w_value, w_out, norm2_gain, w_gate, w_up, w_down)

    def accumulate(totals, pack):
        block_in, block_grad, block_routes, block_gates, block_starts = pack

        def applied(block_x, *params):
            return forward(block_x, *params, block_starts, block_routes, block_gates)
        block_out, pullback = jax.vjp(applied, block_in, *weights)
        gradients = pullback(block_grad)
        summed = jax.tree.map(jnp.add, totals, tuple(gradients[1:]))
        return (summed, (block_out, gradients[0]))
    initial = jax.tree.map(jnp.zeros_like, weights)
    totals, outs = lax.scan(accumulate, initial, (inputs, grad_out, route_blocks, gate_blocks, start_blocks))
    output = outs[0].reshape(TOKENS, D)
    input_grad = outs[1].reshape(TOKENS, D)
    return (output, input_grad, totals[0], totals[1], totals[2], totals[3], totals[4], totals[5], totals[6], totals[7], totals[8])
```

```python
import math

import jax
import jax.numpy as jnp
from jax import lax
from jax.experimental import pallas as pl
from jax.experimental.pallas import tpu as pltpu
from jax.sharding import PartitionSpec as P

HEADS = 24
KV_HEADS = 8
HEAD = 64
EXP = 16
PIECE = 256
AXES = ("rep", "fsdp")
EPSILON = 1e-05
NEG_FILL = -1e30
BF = jnp.bfloat16
F32 = jnp.float32
PLANE = 8
EPD = EXP // PLANE


def rope_tables(length, head_dim):
    half_dim = head_dim // 2
    positions = jnp.arange(length, dtype=F32)[:, None]
    inverse_rates = jnp.exp(
        jnp.arange(half_dim, dtype=F32) * (-2.0 * math.log(10000.0) / head_dim)
    )
    angles = positions * inverse_rates[None, :]
    return (jnp.cos(angles)[:, None, :], jnp.sin(angles)[:, None, :])


def rotate(values, cosine_table, sine_table):
    half_dim = values.shape[-1] // 2
    first = values[..., :half_dim]
    second = values[..., half_dim:]
    return jnp.concatenate(
        [
            first * cosine_table - second * sine_table,
            second * cosine_table + first * sine_table,
        ],
        axis=-1,
    )


def rotate_back(gradients, cosine_table, sine_table):
    return rotate(gradients, cosine_table, -sine_table)


def piece_mask(length, piece_start):
    places = jnp.arange(length, dtype=jnp.int32)
    inside = (places >= piece_start) & (places < piece_start + PIECE)
    return (places[:, None] >= places[None, :]) | inside[:, None] & inside[None, :]


def dot(a, b):
    return jnp.dot(a, b, preferred_element_type=F32)


def dot_nt(a, b):
    return lax.dot_general(a, b, (((1,), (1,)), ((), ())), preferred_element_type=F32)


def dot_tn(a, b):
    return lax.dot_general(a, b, (((0,), (0,)), ((), ())), preferred_element_type=F32)


def place(pieces, moves, out_shape):
    scalars = []

    def number(value):
        scalars.append(jnp.asarray(value, jnp.int32))
        return len(scalars) - 1

    plan = []
    for i, src, (lead, row, rows, col, cols) in moves:
        plan.append(
            (i, src, None if lead is None else number(lead), number(row), rows, number(col), cols)
        )

    def kernel(offs, *refs):
        ins, out, sems = refs[: len(pieces)], refs[len(pieces)], refs[len(pieces) + 1]
        copies = []
        for n, (i, src, lead, row, rows, col, cols) in enumerate(plan):
            to = (
                pl.ds(pl.multiple_of(offs[row], 16), rows),
                pl.ds(pl.multiple_of(offs[col], 128), cols),
            )
            if lead is not None:
                to = (offs[lead],) + to
            copies.append(
                pltpu.make_async_copy(ins[i].at[src], out.at[to], sems.at[n])
            )
        for copy in copies:
            copy.start()
        for copy in copies:
            copy.wait()

    return pl.pallas_call(
        kernel,
        out_shape=out_shape,
        in_specs=[pl.BlockSpec(memory_space=pltpu.SMEM)]
        + [pl.BlockSpec(memory_space=pl.ANY)] * len(pieces),
        out_specs=pl.BlockSpec(memory_space=pltpu.VMEM),
        scratch_shapes=[pltpu.SemaphoreType.DMA((len(plan),))],
        compiler_params=pltpu.CompilerParams(vmem_limit_bytes=40 * 2**20),
    )(jnp.stack(scalars), *pieces)


def shards(
    reps,
    group,
    tokens,
    cotangent,
    routes,
    gates,
    starts,
    norm1_gain,
    w_query,
    w_key,
    w_value,
    w_out,
    norm2_gain,
    w_gate,
    w_up,
    w_down,
):
    planes = group // 4
    r, f = lax.axis_index("rep"), lax.axis_index("fsdp")
    xb, yb, c, z = r % 2, (f // 2) % 2, f % 2, f // 4
    mine = xb * 4 + yb * 2 + c

    def perm(to):
        return [
            (a * group + b, to(a, b)[0] * group + to(a, b)[1])
            for a in range(reps)
            for b in range(group)
        ]

    def pp(value, to):
        return lax.ppermute(value, AXES, perm(to))

    def go(value, dx, dy, dc):
        return pp(value, lambda a, b: (a ^ dx, b ^ (dy * 2 + dc)))

    def along(value, k):
        return pp(value, lambda a, b: (a, (b + 4 * k) % group))

    def all_reps(value):
        step = 2
        while step < reps:
            value = value + pp(value, lambda a, b, s=step: (a ^ s, b))
            step *= 2
        return value

    length, width = tokens.shape
    ds = w_query.shape[0]
    hs = w_down.shape[0]
    hid = w_gate.shape[2]
    kvd = w_key.shape[1]
    group_size = HEADS // KV_HEADS
    score_scale = 1.0 / math.sqrt(HEAD)
    half_rows = length // 2

    def split_axes(columns):
        half = columns // 2
        part = (half // 128 + 1) // 2 * 128
        return half, part

    def gather_rows(own):
        columns = own.shape[1]
        half, part = split_axes(columns)
        send = lax.dynamic_slice(own, (0, xb * half), (ds, half))
        stack = jnp.concatenate([send] + [along(send, k) for k in range(1, planes)], axis=0)
        a, b = stack[:, :part], stack[:, part:]
        ax, by = go(a, 1, 0, 0), go(b, 0, 1, 0)
        a_all = {(0, 0): a, (1, 0): ax, (0, 1): go(a, 0, 1, 0), (1, 1): go(ax, 0, 1, 0)}
        b_all = {(0, 0): b, (0, 1): by, (1, 0): go(b, 1, 0, 0), (1, 1): go(by, 1, 0, 0)}
        pieces, moves = [], []
        for held, col, cols in ((a_all, 0, part), (b_all, part, half - part)):
            for (dx, dy), piece in held.items():
                for dc in range(2):
                    pieces.append(piece if dc == 0 else go(piece, 0, 0, 1))
                    for k in range(planes):
                        owner = ((z - k) % planes) * 4 + (yb ^ dy) * 2 + (c ^ dc)
                        moves.append(
                            (
                                len(pieces) - 1,
                                (pl.ds(k * ds, ds),),
                                (None, owner * ds, ds, (xb ^ dx) * half + col, cols),
                            )
                        )
        return place(pieces, moves, jax.ShapeDtypeStruct((width, columns), BF))

    def scatter_rows(grad):
        columns = grad.shape[1]
        half, part = split_axes(columns)
        by_core = grad.reshape(planes, 2, 2, ds, columns)

        def pick(value, index, axis):
            return lax.dynamic_index_in_dim(value, index, axis, keepdims=False)

        kept = pick(by_core, c, 2) + go(pick(by_core, 1 - c, 2), 0, 0, 1)
        kept = kept.reshape(planes, 2, ds, 2, half)
        a, b = kept[..., :part], kept[..., part:]
        a = pick(a, yb, 1) + go(pick(a, 1 - yb, 1), 0, 1, 0)
        b = pick(b, xb, 3) + go(pick(b, 1 - xb, 3), 1, 0, 0)
        a = pick(a, xb, 2) + go(pick(a, 1 - xb, 2), 1, 0, 0)
        b = pick(b, yb, 1) + go(pick(b, 1 - yb, 1), 0, 1, 0)
        both = jnp.concatenate([a, b], axis=2)
        total = pick(both, z, 0).astype(F32)
        for k in range(1, planes):
            total = total + along(pick(both, (z + k) % planes, 0), k).astype(F32)
        total = all_reps(total.astype(BF))
        other = go(total, 1, 0, 0)
        return jnp.where(
            xb == 0,
            jnp.concatenate([total, other], axis=1),
            jnp.concatenate([other, total], axis=1),
        ).astype(F32)

    def gather_tokens(own):
        a, b = own[:half_rows], own[half_rows:]
        ax, by = go(a, 1, 0, 0), go(b, 0, 1, 0)
        a_all = {(0, 0): a, (1, 0): ax, (0, 1): go(a, 0, 1, 0), (1, 1): go(ax, 0, 1, 0)}
        b_all = {(0, 0): b, (0, 1): by, (1, 0): go(b, 1, 0, 0), (1, 1): go(by, 1, 0, 0)}
        parts = []
        for dx in range(2):
            for dy in range(2):
                for dc in range(2):
                    for held in (a_all, b_all):
                        piece = held[(dx, dy)]
                        parts.append(piece if dc == 0 else go(piece, 0, 0, 1))
        return jnp.concatenate(parts, axis=0)

    def scatter_tokens(partial):
        slots = partial.reshape(2, 2, 2, length, width)
        kept = slots[:, :, 0] + go(slots[:, :, 1], 0, 0, 1)
        a, b = kept[:, :, :half_rows], kept[:, :, half_rows:]
        a = a[:, 0] + go(a[:, 1], 0, 1, 0)
        b = b[0] + go(b[1], 1, 0, 0)
        a = a[0].astype(F32) + go(a[1], 1, 0, 0).astype(F32)
        b = b[0].astype(F32) + go(b[1], 0, 1, 0).astype(F32)
        return jnp.concatenate([a, b], axis=0)

    pad = jnp.zeros((ds, 254), BF)
    front = jnp.concatenate(
        [
            w_query.astype(BF),
            w_key.astype(BF),
            w_value.astype(BF),
            norm1_gain.astype(BF)[:, None],
            norm2_gain.astype(BF)[:, None],
            pad,
        ],
        axis=1,
    )
    front = gather_rows(front)
    out_w = gather_rows(w_out.astype(BF))

    gate_up = jnp.concatenate([w_gate.astype(BF), w_up.astype(BF)], axis=2).transpose(1, 0, 2)
    down = w_down.astype(BF).transpose(1, 0, 2)

    def expert_weights(source, e, rows):
        columns = source.shape[2]
        pieces, moves = [], []
        for dy in range(2):
            for dc in range(2):
                target = (mine ^ (dy * 2 + dc)) * EPD + e
                block = lax.dynamic_index_in_dim(source, target, 0, keepdims=False)
                pieces.append(block if dy + dc == 0 else go(block, 0, dy, dc))
                moves.append(
                    (
                        len(pieces) - 1,
                        (),
                        (None, ((yb ^ dy) * 2 + (c ^ dc)) * rows, rows, 0, columns),
                    )
                )
        piece = place(pieces, moves, jax.ShapeDtypeStruct((4 * rows, columns), BF))
        ring, moves = [piece], [(0, (), (None, z * 4 * rows, 4 * rows, 0, columns))]
        for k in range(1, planes):
            ring.append(along(ring[-1], 1))
            moves.append(
                (k, (), (None, ((z - k) % planes) * 4 * rows, 4 * rows, 0, columns))
            )
        return place(ring, moves, jax.ShapeDtypeStruct((planes * 4 * rows, columns), BF))

    expert_in = [expert_weights(gate_up, e, ds) for e in range(EPD)]
    expert_down = [expert_weights(down, e, hs) for e in range(EPD)]

    experts = jnp.arange(EXP, dtype=jnp.int32)[:, None, None]
    share = jnp.sum(jnp.where(routes[None] == experts, gates[None], 0.0), axis=2)
    shares = []
    for j in range(PLANE):
        block = lax.dynamic_slice(share, ((mine ^ j) * EPD, 0), (EPD, length))
        shares.append(block if j == 0 else go(block, j // 4, (j // 2) % 2, j % 2))
    shares = jnp.concatenate(shares, axis=1)

    grads_all = gather_tokens(cotangent)

    inputs = tokens.astype(F32)
    gain_one = front[:, 2560].astype(F32)[None, :]
    gain_two = front[:, 2561].astype(F32)[None, :]
    inv_one = lax.rsqrt(jnp.mean(inputs * inputs, axis=1, keepdims=True) + EPSILON)
    normed = (inputs * inv_one * gain_one).astype(BF)
    mixed = dot(normed, front[:, : width + 2 * kvd])
    query_raw = mixed[:, :width].reshape(length, HEADS, HEAD)
    key_raw = mixed[:, width : width + kvd].reshape(length, KV_HEADS, HEAD)
    value = mixed[:, width + kvd :].astype(BF).reshape(length, KV_HEADS, HEAD)
    cosine_table, sine_table = rope_tables(length, HEAD)
    query_rotated = (
        rotate(query_raw, cosine_table, sine_table)
        .astype(BF)
        .reshape(length, KV_HEADS, group_size, HEAD)
    )
    key_rotated = rotate(key_raw, cosine_table, sine_table).astype(BF)
    allowed = piece_mask(length, starts[0])
    scores = (
        jnp.einsum("voua,zoa->ouvz", query_rotated, key_rotated, preferred_element_type=F32)
        * score_scale
    )
    scores = jnp.where(allowed, scores, NEG_FILL)
    row_peak = jnp.max(scores, axis=3, keepdims=True)
    exponent = jnp.exp(scores - row_peak)
    row_total = jnp.sum(exponent, axis=3, keepdims=True)
    attn_probs = exponent / row_total
    attended = (
        jnp.einsum("xkfq,qxb->fxkb", attn_probs.astype(BF), value, preferred_element_type=F32)
        .astype(BF)
        .reshape(length, width)
    )
    residual = inputs + dot(attended, out_w)
    inv_two = lax.rsqrt(jnp.mean(residual * residual, axis=1, keepdims=True) + EPSILON)
    normed_two = (residual * inv_two * gain_two).astype(BF)

    rows_all = gather_tokens(normed_two)
    out_sum, row_sum = None, None
    in_grads, down_grads = [], []
    for e in range(EPD):
        weight_in, weight_down = expert_in[e], expert_down[e]
        part = shares[e][:, None]
        pre = dot(rows_all, weight_in)
        gate_pre, up_pre = pre[:, :hid], pre[:, hid:]
        sig = jax.nn.sigmoid(gate_pre)
        swish = gate_pre * sig
        act = (part * (swish * up_pre)).astype(BF)
        grad_inner = dot_nt(grads_all, weight_down) * part
        grad_gate = (grad_inner * up_pre * sig * (1.0 + gate_pre * (1.0 - sig))).astype(BF)
        grad_up = (grad_inner * swish).astype(BF)
        grad_pre = jnp.concatenate([grad_gate, grad_up], axis=1)
        out_part = dot(act, weight_down)
        row_part = dot_nt(grad_pre, weight_in)
        out_sum = out_part if e == 0 else out_sum + out_part
        row_sum = row_part if e == 0 else row_sum + row_part
        down_grads.append(dot_tn(act, grads_all).astype(BF))
        in_grads.append(dot_tn(rows_all, grad_pre).astype(BF))
    grad_normed_two = scatter_tokens(row_sum.astype(BF))
    output = residual + scatter_tokens(out_sum.astype(BF))

    def expert_grads(grad, rows):
        columns = grad.shape[1]
        block = 4 * rows

        def own(k):
            return lax.dynamic_slice(grad, (((z - k) % planes) * block, 0), (block, columns))

        total = own(1)
        for k in range(2, planes + 1):
            total = along(total, 1) + own(k % planes)
        total = all_reps(total)
        held = []
        for dy in range(2):
            for dc in range(2):
                shard = lax.dynamic_slice(
                    total, (((yb ^ dy) * 2 + (c ^ dc)) * rows, 0), (rows, columns)
                )
                held.append(shard if dy + dc == 0 else go(shard, 0, dy, dc))
        return held + [go(shard, 1, 0, 0) for shard in held]

    def expert_shards(grads, rows):
        columns = grads[0].shape[1]
        pieces, moves = [], []
        for e in range(EPD):
            for j, shard in enumerate(expert_grads(grads[e], rows)):
                pieces.append(shard)
                moves.append(
                    (len(pieces) - 1, (), ((mine ^ j) * EPD + e, 0, rows, 0, columns))
                )
        whole = place(pieces, moves, jax.ShapeDtypeStruct((EXP, rows, columns), BF))
        return whole.transpose(1, 0, 2).astype(F32)

    in_shards = expert_shards(in_grads, ds)
    down_shards = expert_shards(down_grads, hs)

    grad_out = cotangent.astype(F32)
    scaled_two = grad_normed_two * gain_two
    grad_resid = (
        grad_out
        + inv_two * scaled_two
        - residual * inv_two**3 * jnp.mean(scaled_two * residual, axis=1, keepdims=True)
    )
    grad_gain_two = jnp.sum(grad_normed_two * residual * inv_two, axis=0)
    grad_mixed = grad_resid.astype(BF)
    grad_out_w = dot_tn(attended, grad_mixed)
    context_grad = dot_nt(grad_mixed, out_w).astype(BF).reshape(length, KV_HEADS, group_size, HEAD)
    grad_probs = jnp.einsum("voua,zoa->ouvz", context_grad, value, preferred_element_type=F32)
    grad_value = (
        jnp.einsum("fxyq,yfxk->qfk", attn_probs.astype(BF), context_grad, preferred_element_type=F32)
        .astype(BF)
        .reshape(length, kvd)
    )
    inner_sum = jnp.sum(attn_probs * grad_probs, axis=3, keepdims=True)
    logit_grad = (attn_probs * (grad_probs - inner_sum)).astype(BF)
    grad_query_rot = (
        jnp.einsum("xkfq,qxb->fxkb", logit_grad, key_rotated, preferred_element_type=F32).reshape(
            length, HEADS, HEAD
        )
        * score_scale
    )
    grad_key_rot = (
        jnp.einsum("fxyq,yfxk->qfk", logit_grad, query_rotated, preferred_element_type=F32)
        * score_scale
    )
    grad_query = rotate_back(grad_query_rot, cosine_table, sine_table).astype(BF)
    grad_key = rotate_back(grad_key_rot, cosine_table, sine_table).astype(BF)
    grad_mix = jnp.concatenate(
        [grad_query.reshape(length, width), grad_key.reshape(length, kvd), grad_value], axis=1
    )
    grad_mix_w = dot_tn(normed, grad_mix)
    grad_normed = dot_nt(grad_mix, front[:, : width + 2 * kvd])
    scaled_one = grad_normed * gain_one
    input_grad = (
        grad_resid
        + inv_one * scaled_one
        - inputs * inv_one**3 * jnp.mean(scaled_one * inputs, axis=1, keepdims=True)
    )
    grad_gain_one = jnp.sum(grad_normed * inputs * inv_one, axis=0)
    out_shard = scatter_rows(grad_out_w.astype(BF))
    front_grad = jnp.concatenate(
        [
            grad_mix_w.astype(BF),
            grad_gain_one.astype(BF)[:, None],
            grad_gain_two.astype(BF)[:, None],
            jnp.zeros((width, 254), BF),
        ],
        axis=1,
    )
    front_shard = scatter_rows(front_grad)
    return (
        output,
        input_grad,
        front_shard[:, width + 2 * kvd],
        front_shard[:, :width],
        front_shard[:, width : width + kvd],
        front_shard[:, width + kvd : width + 2 * kvd],
        out_shard,
        front_shard[:, width + 2 * kvd + 1],
        in_shards[..., :hid],
        in_shards[..., hid:],
        down_shards,
    )


def solution(mesh):
    reps, group = mesh.shape["rep"], mesh.shape["fsdp"]
    both, one = P(AXES, None), P("fsdp")
    flat, deep = P("fsdp", None), P("fsdp", None, None)

    def whole(*args):
        return shards(reps, group, *args)

    return jax.shard_map(
        whole,
        mesh=mesh,
        in_specs=(both, both, both, both, P(AXES), one, flat, flat, flat, flat, one, deep, deep, deep),
        out_specs=(both, both, one, flat, flat, flat, flat, one, deep, deep, deep),
        check_vma=False,
    )
```

```python
import math

import jax
import jax.numpy as jnp
from jax import lax
from jax.experimental import pallas as pl
from jax.experimental.pallas import tpu as pltpu
from jax.sharding import PartitionSpec as P

HEADS = 24
KV_HEADS = 8
HEAD = 64
EXP = 16
PIECE = 256
AXES = ("rep", "fsdp")
EPSILON = 1e-05
NEG_FILL = -1e30
BF = jnp.bfloat16
F32 = jnp.float32
PLANE = 8
EPD = EXP // PLANE


def rope_tables(length, head_dim):
    half_dim = head_dim // 2
    positions = jnp.arange(length, dtype=F32)[:, None]
    inverse_rates = jnp.exp(
        jnp.arange(half_dim, dtype=F32) * (-2.0 * math.log(10000.0) / head_dim)
    )
    angles = positions * inverse_rates[None, :]
    return (jnp.cos(angles)[:, None, :], jnp.sin(angles)[:, None, :])


def rotate(values, cosine_table, sine_table):
    half_dim = values.shape[-1] // 2
    first = values[..., :half_dim]
    second = values[..., half_dim:]
    return jnp.concatenate(
        [
            first * cosine_table - second * sine_table,
            second * cosine_table + first * sine_table,
        ],
        axis=-1,
    )


def rotate_back(gradients, cosine_table, sine_table):
    return rotate(gradients, cosine_table, -sine_table)


def piece_mask(length, piece_start):
    places = jnp.arange(length, dtype=jnp.int32)
    inside = (places >= piece_start) & (places < piece_start + PIECE)
    return (places[:, None] >= places[None, :]) | inside[:, None] & inside[None, :]


def dot(a, b):
    return jnp.dot(a, b, preferred_element_type=F32)


def dot_nt(a, b):
    return lax.dot_general(a, b, (((1,), (1,)), ((), ())), preferred_element_type=F32)


def dot_tn(a, b):
    return lax.dot_general(a, b, (((0,), (0,)), ((), ())), preferred_element_type=F32)


def place(pieces, moves, out_shape):
    scalars = []

    def number(value):
        scalars.append(jnp.asarray(value, jnp.int32))
        return len(scalars) - 1

    plan = []
    for i, src, (lead, row, rows, col, cols) in moves:
        plan.append(
            (i, src, None if lead is None else number(lead), number(row), rows, number(col), cols)
        )

    def kernel(offs, *refs):
        ins, out, sems = refs[: len(pieces)], refs[len(pieces)], refs[len(pieces) + 1]
        copies = []
        for n, (i, src, lead, row, rows, col, cols) in enumerate(plan):
            to = (
                pl.ds(pl.multiple_of(offs[row], 16), rows),
                pl.ds(pl.multiple_of(offs[col], 128), cols),
            )
            if lead is not None:
                to = (offs[lead],) + to
            copies.append(
                pltpu.make_async_copy(ins[i].at[src], out.at[to], sems.at[n])
            )
        for copy in copies:
            copy.start()
        for copy in copies:
            copy.wait()

    return pl.pallas_call(
        kernel,
        out_shape=out_shape,
        in_specs=[pl.BlockSpec(memory_space=pltpu.SMEM)]
        + [pl.BlockSpec(memory_space=pl.ANY)] * len(pieces),
        out_specs=pl.BlockSpec(memory_space=pltpu.VMEM),
        scratch_shapes=[pltpu.SemaphoreType.DMA((len(plan),))],
        compiler_params=pltpu.CompilerParams(vmem_limit_bytes=40 * 2**20),
    )(jnp.stack(scalars), *pieces)


def add_rows(store, terms, rows, step=32):
    step = min(step, rows)

    @pl.loop(0, rows // step)
    def _(n):
        chunk = pl.ds(pl.multiple_of(n * step, 16), step)
        total = terms[0](chunk).astype(F32)
        for term in terms[1:]:
            total = total + term(chunk).astype(F32)
        store(chunk, total)


class Links:
    def __init__(self, planes, group, send_sems, recv_sems):
        r, f = lax.axis_index("rep"), lax.axis_index("fsdp")
        self.xb, self.yb, self.c, self.z = r % 2, (f // 2) % 2, f % 2, f // 4
        self.x = (r + 1 - 2 * self.xb, f)
        self.y = (r, f + 2 - 4 * self.yb)
        self.core = (r, f + 1 - 2 * self.c)
        self.along = [None] + [(r, (f + 4 * k) % group) for k in range(1, planes)]
        self.planes, self.send_sems, self.recv_sems, self.copies = planes, send_sems, recv_sems, []

    def barrier(self, devices):
        semaphore = pltpu.get_barrier_semaphore()
        for device in devices:
            pl.semaphore_signal(
                semaphore, inc=1, device_id=device, device_id_type=pl.DeviceIdType.MESH
            )
        pl.semaphore_wait(semaphore, len(devices))

    def send(self, src, dst, device):
        n = len(self.copies)
        copy = pltpu.make_async_remote_copy(
            src_ref=src,
            dst_ref=dst,
            send_sem=self.send_sems.at[n],
            recv_sem=self.recv_sems.at[n],
            device_id=device,
            device_id_type=pl.DeviceIdType.MESH,
        )
        copy.start()
        self.copies.append(copy)
        return copy

    def finish(self):
        for copy in self.copies:
            copy.wait_send()


def comm_params(number):
    return pltpu.CompilerParams(
        collective_id=number, has_side_effects=True, vmem_limit_bytes=56 * 2**20
    )


def dma_pairs(count):
    return [pltpu.SemaphoreType.DMA((count,)), pltpu.SemaphoreType.DMA((count,))]


def whole_vmem():
    return pl.BlockSpec(memory_space=pltpu.VMEM)


def anywhere():
    return pl.BlockSpec(memory_space=pl.ANY)


def split_half(half):
    return (half // 128 + 1) // 2 * 128


def gather_front(own, planes, group):
    ds, half = own.shape
    part = split_half(half)
    first, second, every = (0, part), (part, half - part), (0, half)

    def kernel(own_ref, out_ref, send_sems, recv_sems, local_sem):
        at = Links(planes, group, send_sems, recv_sems)

        def region(k, dx, dy, span):
            row = (((at.z + planes - k) % planes) * 4 + (at.yb + dy) % 2 * 2 + at.c) * ds
            col = (at.xb + dx) % 2 * half + span[0]
            return out_ref.at[
                pl.ds(pl.multiple_of(row, 16), ds), pl.ds(pl.multiple_of(col, 128), span[1])
            ]

        def pass_on(k, dx, dy, span, device):
            here = region(k, dx, dy, span)
            return at.send(here, here, device)

        at.barrier([at.x, at.y, at.core] + at.along[1:])
        local = pltpu.make_async_copy(own_ref, region(0, 0, 0, every), local_sem)
        local.start()
        arrive = [None] + [
            at.send(own_ref, region(0, 0, 0, every), at.along[k]) for k in range(1, planes)
        ]
        to_core = [at.send(own_ref, region(0, 0, 0, every), at.core)]
        x_first, x_second, y_first, y_second, diagonal = [], [], [], [], []

        def spread(k):
            for device, span, copies in (
                (at.x, first, x_first),
                (at.y, second, y_second),
                (at.x, second, x_second),
                (at.y, first, y_first),
            ):
                here = region(k, 0, 0, span)
                src = own_ref.at[:, pl.ds(span[0], span[1])] if k == 0 else here
                copies.append(at.send(src, here, device))
            if k > 0:
                to_core.append(pass_on(k, 0, 0, every, at.core))

        def forward(k):
            x_first[k].wait_recv()
            diagonal.append((k, first, pass_on(k, 1, 0, first, at.y)))
            y_second[k].wait_recv()
            diagonal.append((k, second, pass_on(k, 0, 1, second, at.x)))
            x_second[k].wait_recv()
            to_core.append(pass_on(k, 1, 0, every, at.core))
            y_first[k].wait_recv()
            to_core.append(pass_on(k, 0, 1, every, at.core))

        for k in range(planes):
            if k > 0:
                arrive[k].wait_recv()
            spread(k)
            if k > 0:
                forward(k - 1)
        forward(planes - 1)
        for k, span, copy in diagonal:
            copy.wait_recv()
            to_core.append(pass_on(k, 1, 1, span, at.core))
        for copy in to_core:
            copy.wait_recv()
        local.wait()
        at.finish()

    count = planes - 1 + planes * 4 + planes * 2 + planes * 5
    return pl.pallas_call(
        kernel,
        out_shape=jax.ShapeDtypeStruct((planes * 4 * ds, 2 * half), BF),
        in_specs=[whole_vmem()],
        out_specs=anywhere(),
        scratch_shapes=dma_pairs(count) + [pltpu.SemaphoreType.DMA],
        compiler_params=comm_params(0),
        cost_estimate=pl.CostEstimate(
            flops=50_000_000_000, bytes_accessed=20_000_000, transcendentals=0
        ),
    )(own)


def gather_plane(own, planes, group):
    length, width = own.shape
    half = length // 2
    first, second = pl.ds(0, half), pl.ds(half, half)

    def kernel(own_ref, out_ref, send_sems, recv_sems, local_sem):
        at = Links(planes, group, send_sems, recv_sems)
        at.barrier([at.x, at.y, at.core])

        def slot(j, rows=pl.ds(0, length)):
            return out_ref.at[j, rows]

        x_first = at.send(own_ref.at[first], slot(4, first), at.x)
        y_second = at.send(own_ref.at[second], slot(2, second), at.y)
        x_second = at.send(own_ref.at[second], slot(4, second), at.x)
        y_first = at.send(own_ref.at[first], slot(2, first), at.y)
        cores = [at.send(own_ref, slot(1), at.core)]
        local = pltpu.make_async_copy(own_ref, slot(0), local_sem)
        local.start()
        x_first.wait_recv()
        far_first = at.send(slot(4, first), slot(6, first), at.y)
        cores.append(at.send(slot(4, first), slot(5, first), at.core))
        y_second.wait_recv()
        far_second = at.send(slot(2, second), slot(6, second), at.x)
        cores.append(at.send(slot(2, second), slot(3, second), at.core))
        x_second.wait_recv()
        cores.append(at.send(slot(4, second), slot(5, second), at.core))
        y_first.wait_recv()
        cores.append(at.send(slot(2, first), slot(3, first), at.core))
        far_first.wait_recv()
        cores.append(at.send(slot(6, first), slot(7, first), at.core))
        far_second.wait_recv()
        cores.append(at.send(slot(6, second), slot(7, second), at.core))
        for copy in cores:
            copy.wait_recv()
        local.wait()
        at.finish()

    return pl.pallas_call(
        kernel,
        out_shape=jax.ShapeDtypeStruct((PLANE, length, width), BF),
        in_specs=[whole_vmem()],
        out_specs=anywhere(),
        scratch_shapes=dma_pairs(13) + [pltpu.SemaphoreType.DMA],
        compiler_params=comm_params(1),
        cost_estimate=pl.CostEstimate(
            flops=45_000_000_000, bytes_accessed=20_000_000, transcendentals=0
        ),
    )(own)


def scatter_plane(partial, planes, group):
    slots, length, width = partial.shape
    half = length // 2
    first, second = pl.ds(0, half), pl.ds(half, half)

    def kernel(p_ref, out_ref, from_core, kept, far, near, send_sems, recv_sems):
        at = Links(planes, group, send_sems, recv_sems)
        at.barrier([at.x, at.y, at.core])
        order = (3, 2, 1, 0)
        arrive = {
            j: at.send(p_ref.at[2 * j + 1], from_core.at[j], at.core) for j in order
        }

        def add_core(j):
            arrive[j].wait_recv()

            def store(chunk, total):
                kept[j, chunk] = total.astype(BF)

            add_rows(store, [lambda q: p_ref[2 * j, q], lambda q: from_core[j, q]], length)

        def add_far(j, n, base):
            def store(chunk, total):
                kept[j, pl.ds(pl.multiple_of(chunk.start + base, 16), chunk.size)] = total.astype(BF)

            add_rows(
                store,
                [
                    lambda q: kept[j, pl.ds(pl.multiple_of(q.start + base, 16), q.size)],
                    lambda q: far[n, q],
                ],
                half,
            )

        add_core(3)
        far_y = at.send(kept.at[3, first], far.at[0], at.y)
        far_x = at.send(kept.at[3, second], far.at[1], at.x)
        add_core(2)
        x_second = at.send(kept.at[2, second], near.at[0, second], at.x)
        add_core(1)
        y_first = at.send(kept.at[1, first], near.at[1, first], at.y)
        far_y.wait_recv()
        add_far(2, 0, 0)
        x_first = at.send(kept.at[2, first], near.at[0, first], at.x)
        far_x.wait_recv()
        add_far(1, 1, half)
        y_second = at.send(kept.at[1, second], near.at[1, second], at.y)
        arrive[0].wait_recv()
        for copy in (x_second, y_first, x_first, y_second):
            copy.wait_recv()

        def store(chunk, total):
            out_ref[chunk] = total

        add_rows(
            store,
            [
                lambda q: p_ref[0, q],
                lambda q: from_core[0, q],
                lambda q: near[0, q],
                lambda q: near[1, q],
            ],
            length,
        )
        at.finish()

    return pl.pallas_call(
        kernel,
        out_shape=jax.ShapeDtypeStruct((length, width), F32),
        in_specs=[whole_vmem()],
        out_specs=whole_vmem(),
        scratch_shapes=[
            pltpu.VMEM((4, length, width), BF),
            pltpu.VMEM((4, length, width), BF),
            pltpu.VMEM((2, half, width), BF),
            pltpu.VMEM((2, length, width), BF),
        ]
        + dma_pairs(10),
        compiler_params=comm_params(2),
        cost_estimate=pl.CostEstimate(
            flops=45_000_000_000, bytes_accessed=20_000_000, transcendentals=0
        ),
    )(partial)


def scatter_front(grad, planes, group):
    rows, columns = grad.shape
    ds, half = rows // (4 * planes), columns // 2
    part = split_half(half)
    first, second = pl.ds(0, part), pl.ds(part, half - part)

    def kernel(
        g_ref, out_ref, from_core, kept, far_a, far_b, near_x, near_y, total_ref, from_z, send_sems, recv_sems
    ):
        at = Links(planes, group, send_sems, recv_sems)
        at.barrier([at.x, at.y, at.core] + at.along[1:])

        def row(k, dy, core):
            owner = ((at.z + k) % planes) * 4 + (at.yb + dy) % 2 * 2 + core
            return pl.multiple_of(owner * ds, 16)

        def column(dx):
            return pl.ds(pl.multiple_of((at.xb + dx) % 2 * half, 128), half)

        order = list(range(1, planes)) + [0]
        arrive = {}
        for k in order:
            for dy in (1, 0):
                arrive[k, dy] = at.send(
                    g_ref.at[pl.ds(row(k, dy, 1 - at.c), ds)], from_core.at[k, dy], at.core
                )
        step = 16
        x_second, y_first, x_first, y_second, to_x, to_y = {}, {}, {}, {}, {}, {}
        for k in order:
            for dy in (1, 0):
                arrive[k, dy].wait_recv()
                for dx in (1, 0):

                    def store(chunk, total, k=k, dx=dx, dy=dy):
                        kept[k, dx, dy, chunk] = total.astype(BF)

                    add_rows(
                        store,
                        [
                            lambda q, k=k, dx=dx, dy=dy: g_ref[
                                pl.ds(pl.multiple_of(row(k, dy, at.c) + q.start, 16), q.size),
                                column(dx),
                            ],
                            lambda q, k=k, dx=dx, dy=dy: from_core[k, dy, q, column(dx)],
                        ],
                        ds,
                        step,
                    )
                    if (dx, dy) == (1, 1):
                        to_y[k] = at.send(kept.at[k, 1, 1, :, first], far_a.at[k], at.y)
                        to_x[k] = at.send(kept.at[k, 1, 1, :, second], far_b.at[k], at.x)
                    elif (dx, dy) == (0, 1):
                        y_first[k] = at.send(
                            kept.at[k, 0, 1, :, first], near_y.at[k, :, first], at.y
                        )
                    elif (dx, dy) == (1, 0):
                        x_second[k] = at.send(
                            kept.at[k, 1, 0, :, second], near_x.at[k, :, second], at.x
                        )
        for k in order:
            to_y[k].wait_recv()

            def store(chunk, total, k=k):
                kept[k, 1, 0, chunk, first] = total.astype(BF)

            add_rows(
                store,
                [lambda q, k=k: kept[k, 1, 0, q, first], lambda q, k=k: far_a[k, q]],
                ds,
                step,
            )
            x_first[k] = at.send(kept.at[k, 1, 0, :, first], near_x.at[k, :, first], at.x)
            to_x[k].wait_recv()

            def store(chunk, total, k=k):
                kept[k, 0, 1, chunk, second] = total.astype(BF)

            add_rows(
                store,
                [lambda q, k=k: kept[k, 0, 1, q, second], lambda q, k=k: far_b[k, q]],
                ds,
                step,
            )
            y_second[k] = at.send(kept.at[k, 0, 1, :, second], near_y.at[k, :, second], at.y)
        arrive_z = {}
        for k in order:
            for copies in (x_second, y_first, x_first, y_second):
                copies[k].wait_recv()

            def store(chunk, total, k=k):
                total_ref[k, chunk] = total.astype(BF)

            add_rows(
                store,
                [
                    lambda q, k=k: kept[k, 0, 0, q],
                    lambda q, k=k: near_x[k, q],
                    lambda q, k=k: near_y[k, q],
                ],
                ds,
                step,
            )
            if k > 0:
                arrive_z[k] = at.send(total_ref.at[k], from_z.at[k], at.along[k])
        for k in range(1, planes):
            arrive_z[k].wait_recv()

        def store(chunk, total):
            out_ref[chunk] = total.astype(BF)

        add_rows(
            store,
            [lambda q: total_ref[0, q]]
            + [lambda q, k=k: from_z[k, q] for k in range(1, planes)],
            ds,
            step,
        )
        at.finish()

    return pl.pallas_call(
        kernel,
        out_shape=jax.ShapeDtypeStruct((ds, half), BF),
        in_specs=[whole_vmem()],
        out_specs=whole_vmem(),
        scratch_shapes=[
            pltpu.VMEM((planes, 2, ds, columns), BF),
            pltpu.VMEM((planes, 2, 2, ds, half), BF),
            pltpu.VMEM((planes, ds, part), BF),
            pltpu.VMEM((planes, ds, half - part), BF),
            pltpu.VMEM((planes, ds, half), BF),
            pltpu.VMEM((planes, ds, half), BF),
            pltpu.VMEM((planes, ds, half), BF),
            pltpu.VMEM((planes, ds, half), BF),
        ]
        + dma_pairs(planes * 8 + planes - 1),
        compiler_params=comm_params(3),
        cost_estimate=pl.CostEstimate(
            flops=50_000_000_000, bytes_accessed=20_000_000, transcendentals=0
        ),
    )(grad)


def shards(
    reps,
    group,
    tokens,
    cotangent,
    routes,
    gates,
    starts,
    norm1_gain,
    w_query,
    w_key,
    w_value,
    w_out,
    norm2_gain,
    w_gate,
    w_up,
    w_down,
):
    planes = group // 4
    r, f = lax.axis_index("rep"), lax.axis_index("fsdp")
    xb, yb, c, z = r % 2, (f // 2) % 2, f % 2, f // 4
    mine = xb * 4 + yb * 2 + c

    def perm(to):
        return [
            (a * group + b, to(a, b)[0] * group + to(a, b)[1])
            for a in range(reps)
            for b in range(group)
        ]

    def pp(value, to):
        return lax.ppermute(value, AXES, perm(to))

    def go(value, dx, dy, dc):
        return pp(value, lambda a, b: (a ^ dx, b ^ (dy * 2 + dc)))

    def along(value, k):
        return pp(value, lambda a, b: (a, (b + 4 * k) % group))

    def all_reps(value):
        step = 2
        while step < reps:
            value = value + pp(value, lambda a, b, s=step: (a ^ s, b))
            step *= 2
        return value

    length, width = tokens.shape
    ds = w_query.shape[0]
    hs = w_down.shape[0]
    hid = w_gate.shape[2]
    kvd = w_key.shape[1]
    group_size = HEADS // KV_HEADS
    score_scale = 1.0 / math.sqrt(HEAD)
    half_rows = length // 2

    def gather_tokens(own):
        a, b = slice(0, half_rows), slice(half_rows, length)
        x, y = go(own, 1, 0, 0), go(own, 0, 1, 0)
        far_a, far_b = go(x[a], 0, 1, 0), go(y[b], 1, 0, 0)
        slots = [own, go(own, 0, 0, 1), y, go(y, 0, 0, 1), x, go(x, 0, 0, 1)]
        slots += [far_a, far_b, go(far_a, 0, 0, 1), go(far_b, 0, 0, 1)]
        return jnp.concatenate(slots, axis=0)

    def scatter_tokens(partial):
        slots = partial.reshape(2, 2, 2, length, width)
        kept = slots[:, :, 0] + go(slots[:, :, 1], 0, 0, 1)
        a, b = kept[:, :, :half_rows], kept[:, :, half_rows:]
        a = a[:, 0] + go(a[:, 1], 0, 1, 0)
        b = b[0] + go(b[1], 1, 0, 0)
        a = a[0].astype(F32) + go(a[1], 1, 0, 0).astype(F32)
        b = b[0].astype(F32) + go(b[1], 0, 1, 0).astype(F32)
        return jnp.concatenate([a, b], axis=0)

    mix = width + 2 * kvd
    columns = mix + width + 256
    half = columns // 2
    gains = jnp.stack([norm1_gain.astype(BF), norm2_gain.astype(BF)], axis=1)
    front_own = jnp.concatenate(
        [
            w_query.astype(BF),
            w_key.astype(BF),
            w_value.astype(BF),
            w_out.astype(BF),
            gains,
            jnp.zeros((ds, 254), BF),
        ],
        axis=1,
    )
    front = gather_front(lax.dynamic_slice(front_own, (0, xb * half), (ds, half)), planes, group)
    out_w = front[:, mix : mix + width]

    blocks = width // hid
    packed = jnp.concatenate(
        [
            w_gate.astype(BF).transpose(1, 0, 2),
            w_up.astype(BF).transpose(1, 0, 2),
            w_down.astype(BF)
            .reshape(hs, EXP, blocks, hid)
            .transpose(1, 2, 0, 3)
            .reshape(EXP, ds, hid),
        ],
        axis=2,
    )
    packs = []
    for dy in range(2):
        for dc in range(2):
            block = lax.dynamic_slice(
                packed, ((mine ^ (dy * 2 + dc)) * EPD, 0, 0), (EPD, ds, 3 * hid)
            )
            packs.append(block if dy + dc == 0 else go(block, 0, dy, dc))

    def expert_weights(e):
        moves = []
        for i in range(4):
            moves.append(
                (i, (e,), (None, ((yb ^ (i // 2)) * 2 + (c ^ (i % 2))) * ds, ds, 0, 3 * hid))
            )
        ring = [place(packs, moves, jax.ShapeDtypeStruct((4 * ds, 3 * hid), BF))]
        for k in range(1, planes):
            ring.append(along(ring[-1], 1))
        moves, down_moves = [], []
        for k in range(planes):
            moves.append(
                (
                    k,
                    (slice(None), pl.ds(0, 2 * hid)),
                    (None, ((z - k) % planes) * 4 * ds, 4 * ds, 0, 2 * hid),
                )
            )
            for i in range(4):
                for n in range(blocks):
                    down_moves.append(
                        (
                            k,
                            (pl.ds(i * ds + n * hs, hs), pl.ds(2 * hid, hid)),
                            (None, (((z - k) % planes) * 4 + i) * hs, hs, n * hid, hid),
                        )
                    )
        return (
            place(ring, moves, jax.ShapeDtypeStruct((width, 2 * hid), BF)),
            place(ring, down_moves, jax.ShapeDtypeStruct((hid, width), BF)),
        )

    weights = [expert_weights(e) for e in range(EPD)]

    experts = jnp.arange(EXP, dtype=jnp.int32)[:, None, None]
    share = jnp.sum(jnp.where(routes[None] == experts, gates[None], 0.0), axis=2)
    shares = []
    for j in range(PLANE):
        block = lax.dynamic_slice(share, ((mine ^ j) * EPD, 0), (EPD, length))
        shares.append(block if j == 0 else go(block, j // 4, (j // 2) % 2, j % 2))
    shares = jnp.concatenate(shares, axis=1)

    grads_all = gather_tokens(cotangent)

    inputs = tokens.astype(F32)
    gain_one = front[:, mix + width].astype(F32)[None, :]
    gain_two = front[:, mix + width + 1].astype(F32)[None, :]
    inv_one = lax.rsqrt(jnp.mean(inputs * inputs, axis=1, keepdims=True) + EPSILON)
    normed = (inputs * inv_one * gain_one).astype(BF)
    mixed = dot(normed, front[:, :mix])
    query_raw = mixed[:, :width].reshape(length, HEADS, HEAD)
    key_raw = mixed[:, width : width + kvd].reshape(length, KV_HEADS, HEAD)
    value = mixed[:, width + kvd :].astype(BF).reshape(length, KV_HEADS, HEAD)
    cosine_table, sine_table = rope_tables(length, HEAD)
    query_rotated = (
        rotate(query_raw, cosine_table, sine_table)
        .astype(BF)
        .reshape(length, KV_HEADS, group_size, HEAD)
    )
    key_rotated = rotate(key_raw, cosine_table, sine_table).astype(BF)
    allowed = piece_mask(length, starts[0])
    scores = (
        jnp.einsum("voua,zoa->ouvz", query_rotated, key_rotated, preferred_element_type=F32)
        * score_scale
    )
    scores = jnp.where(allowed, scores, NEG_FILL)
    row_peak = jnp.max(scores, axis=3, keepdims=True)
    exponent = jnp.exp(scores - row_peak)
    row_total = jnp.sum(exponent, axis=3, keepdims=True)
    attn_probs = exponent / row_total
    attended = (
        jnp.einsum("xkfq,qxb->fxkb", attn_probs.astype(BF), value, preferred_element_type=F32)
        .astype(BF)
        .reshape(length, width)
    )
    residual = inputs + dot(attended, out_w)
    inv_two = lax.rsqrt(jnp.mean(residual * residual, axis=1, keepdims=True) + EPSILON)
    normed_two = (residual * inv_two * gain_two).astype(BF)

    rows_all = gather_plane(normed_two, planes, group).reshape(PLANE * length, width)
    out_sum, row_sum = None, None
    pack_grads = []
    for e in range(EPD):
        weight_in, weight_down = weights[e]
        part = shares[e][:, None]
        pre = dot(rows_all, weight_in)
        gate_pre, up_pre = pre[:, :hid], pre[:, hid:]
        sig = jax.nn.sigmoid(gate_pre)
        swish = gate_pre * sig
        act = (part * (swish * up_pre)).astype(BF)
        grad_inner = dot_nt(grads_all, weight_down) * part
        grad_gate = (grad_inner * up_pre * sig * (1.0 + gate_pre * (1.0 - sig))).astype(BF)
        grad_up = (grad_inner * swish).astype(BF)
        grad_pre = jnp.concatenate([grad_gate, grad_up], axis=1)
        out_part = dot(act, weight_down)
        row_part = dot_nt(grad_pre, weight_in)
        out_sum = out_part if e == 0 else out_sum + out_part
        row_sum = row_part if e == 0 else row_sum + row_part
        down_grad = dot_tn(act, grads_all).astype(BF)
        in_grad = dot_tn(rows_all, grad_pre).astype(BF)
        down_grad = (
            down_grad.reshape(group, hs, blocks, hid).transpose(0, 2, 1, 3).reshape(width, hid)
        )
        pack_grads.append(jnp.concatenate([in_grad, down_grad], axis=1))
    grad_normed_two = scatter_plane(
        row_sum.astype(BF).reshape(PLANE, length, width), planes, group
    )
    output = residual + scatter_tokens(out_sum.astype(BF))

    def expert_grads(grad):
        block = 4 * ds

        def own(k):
            return lax.dynamic_slice(grad, (((z - k) % planes) * block, 0), (block, 3 * hid))

        total = own(1)
        for k in range(2, planes + 1):
            total = along(total, 1) + own(k % planes)
        total = all_reps(total)
        held = []
        for dy in range(2):
            for dc in range(2):
                shard = lax.dynamic_slice(
                    total, (((yb ^ dy) * 2 + (c ^ dc)) * ds, 0), (ds, 3 * hid)
                )
                held.append(shard if dy + dc == 0 else go(shard, 0, dy, dc))
        other = go(jnp.stack(held), 1, 0, 0)
        return held, other

    pieces, moves = [], []
    for e in range(EPD):
        held, other = expert_grads(pack_grads[e])
        pieces += held + [other]
        for j in range(PLANE):
            moves.append(
                (
                    e * 5 + min(j, 4),
                    () if j < 4 else (j - 4,),
                    ((mine ^ j) * EPD + e, 0, ds, 0, 3 * hid),
                )
            )
    shard_pack = place(pieces, moves, jax.ShapeDtypeStruct((EXP, ds, 3 * hid), BF))
    gate_shard = shard_pack[..., :hid].transpose(1, 0, 2).astype(F32)
    up_shard = shard_pack[..., hid : 2 * hid].transpose(1, 0, 2).astype(F32)
    down_shard = (
        shard_pack[..., 2 * hid :]
        .reshape(EXP, blocks, hs, hid)
        .transpose(2, 0, 1, 3)
        .reshape(hs, EXP, width)
        .astype(F32)
    )

    grad_out = cotangent.astype(F32)
    scaled_two = grad_normed_two * gain_two
    grad_resid = (
        grad_out
        + inv_two * scaled_two
        - residual * inv_two**3 * jnp.mean(scaled_two * residual, axis=1, keepdims=True)
    )
    grad_gain_two = jnp.sum(grad_normed_two * residual * inv_two, axis=0)
    grad_mixed = grad_resid.astype(BF)
    grad_out_w = dot_tn(attended, grad_mixed)
    context_grad = dot_nt(grad_mixed, out_w).astype(BF).reshape(length, KV_HEADS, group_size, HEAD)
    grad_probs = jnp.einsum("voua,zoa->ouvz", context_grad, value, preferred_element_type=F32)
    grad_value = (
        jnp.einsum("fxyq,yfxk->qfk", attn_probs.astype(BF), context_grad, preferred_element_type=F32)
        .astype(BF)
        .reshape(length, kvd)
    )
    inner_sum = jnp.sum(attn_probs * grad_probs, axis=3, keepdims=True)
    logit_grad = (attn_probs * (grad_probs - inner_sum)).astype(BF)
    grad_query_rot = (
        jnp.einsum("xkfq,qxb->fxkb", logit_grad, key_rotated, preferred_element_type=F32).reshape(
            length, HEADS, HEAD
        )
        * score_scale
    )
    grad_key_rot = (
        jnp.einsum("fxyq,yfxk->qfk", logit_grad, query_rotated, preferred_element_type=F32)
        * score_scale
    )
    grad_query = rotate_back(grad_query_rot, cosine_table, sine_table).astype(BF)
    grad_key = rotate_back(grad_key_rot, cosine_table, sine_table).astype(BF)
    grad_mix = jnp.concatenate(
        [grad_query.reshape(length, width), grad_key.reshape(length, kvd), grad_value], axis=1
    )
    grad_mix_w = dot_tn(normed, grad_mix)
    grad_normed = dot_nt(grad_mix, front[:, :mix])
    scaled_one = grad_normed * gain_one
    input_grad = (
        grad_resid
        + inv_one * scaled_one
        - inputs * inv_one**3 * jnp.mean(scaled_one * inputs, axis=1, keepdims=True)
    )
    grad_gain_one = jnp.sum(grad_normed * inputs * inv_one, axis=0)
    front_grad = jnp.concatenate(
        [
            grad_mix_w.astype(BF),
            grad_out_w.astype(BF),
            grad_gain_one.astype(BF)[:, None],
            grad_gain_two.astype(BF)[:, None],
            jnp.zeros((width, 254), BF),
        ],
        axis=1,
    )
    total = all_reps(scatter_front(front_grad, planes, group))
    other = go(total, 1, 0, 0)
    front_shard = jnp.where(
        xb == 0,
        jnp.concatenate([total, other], axis=1),
        jnp.concatenate([other, total], axis=1),
    ).astype(F32)
    return (
        output,
        input_grad,
        front_shard[:, mix + width],
        front_shard[:, :width],
        front_shard[:, width : width + kvd],
        front_shard[:, width + kvd : mix],
        front_shard[:, mix : mix + width],
        front_shard[:, mix + width + 1],
        gate_shard,
        up_shard,
        down_shard,
    )


def solution(mesh):
    reps, group = mesh.shape["rep"], mesh.shape["fsdp"]
    both, one = P(AXES, None), P("fsdp")
    flat, deep = P("fsdp", None), P("fsdp", None, None)

    def whole(*args):
        return shards(reps, group, *args)

    return jax.shard_map(
        whole,
        mesh=mesh,
        in_specs=(both, both, both, both, P(AXES), one, flat, flat, flat, flat, one, deep, deep, deep),
        out_specs=(both, both, one, flat, flat, flat, flat, one, deep, deep, deep),
        check_vma=False,
    )
```

```python
import math

import jax
import jax.numpy as jnp
from jax import lax
from jax.experimental import pallas as pl
from jax.experimental.pallas import tpu as pltpu
from jax.sharding import PartitionSpec as P

HEADS = 24
KV_HEADS = 8
HEAD = 64
EXP = 16
PIECE = 256
AXES = ("rep", "fsdp")
EPSILON = 1e-05
NEG_FILL = -1e30
BF = jnp.bfloat16
F32 = jnp.float32
PLANE = 8
EPD = EXP // PLANE


def turn_tables(length):
    positions = jnp.arange(length, dtype=F32)[:, None]
    lanes = jnp.arange(2 * HEAD)
    rates = jnp.exp((lanes % (HEAD // 2)).astype(F32) * (-2.0 * math.log(10000.0) / HEAD))
    angles = positions * rates[None, :]
    low = (lanes % HEAD < HEAD // 2)[None, :]
    sines = jnp.sin(angles)
    return jnp.stack([jnp.cos(angles), jnp.where(low, -sines, 0.0), jnp.where(low, 0.0, sines)])


def turned(values, tables, sign):
    ahead = pltpu.roll(values, 2 * HEAD - HEAD // 2, 1)
    back = pltpu.roll(values, HEAD // 2, 1)
    return values * tables[0] + sign * (ahead * tables[1] + back * tables[2])


def row_loop(rows, step, body):
    @pl.loop(0, rows // step)
    def _(n):
        body(pl.ds(pl.multiple_of(n * step, step), step))


def dot(a, b):
    return jnp.dot(a, b, preferred_element_type=F32)


def dot_nt(a, b):
    return lax.dot_general(a, b, (((1,), (1,)), ((), ())), preferred_element_type=F32)


def dot_tn(a, b):
    return lax.dot_general(a, b, (((0,), (0,)), ((), ())), preferred_element_type=F32)


def add_rows(store, terms, rows, step=32):
    step = min(step, rows)

    @pl.loop(0, rows // step)
    def _(n):
        chunk = pl.ds(pl.multiple_of(n * step, 16), step)
        total = terms[0](chunk).astype(F32)
        for term in terms[1:]:
            total = total + term(chunk).astype(F32)
        store(chunk, total)


class Links:
    def __init__(self, planes, group, send_sems, recv_sems):
        r, f = lax.axis_index("rep"), lax.axis_index("fsdp")
        self.xb, self.yb, self.c, self.z = r % 2, (f // 2) % 2, f % 2, f // 4
        self.x = (r + 1 - 2 * self.xb, f)
        self.y = (r, f + 2 - 4 * self.yb)
        self.core = (r, f + 1 - 2 * self.c)
        self.diagonal = (r, f + 3 - 4 * self.yb - 2 * self.c)
        self.along = [None] + [(r, (f + 4 * k) % group) for k in range(1, planes)]
        self.planes, self.send_sems, self.recv_sems, self.copies = planes, send_sems, recv_sems, []

    def barrier(self, devices):
        semaphore = pltpu.get_barrier_semaphore()
        for device in devices:
            pl.semaphore_signal(
                semaphore, inc=1, device_id=device, device_id_type=pl.DeviceIdType.MESH
            )
        pl.semaphore_wait(semaphore, len(devices))

    def send(self, src, dst, device):
        n = len(self.copies)
        copy = pltpu.make_async_remote_copy(
            src_ref=src,
            dst_ref=dst,
            send_sem=self.send_sems.at[n],
            recv_sem=self.recv_sems.at[n],
            device_id=device,
            device_id_type=pl.DeviceIdType.MESH,
        )
        copy.start()
        self.copies.append(copy)
        return copy

    def finish(self):
        for copy in self.copies:
            copy.wait_send()


def comm_params(number):
    return pltpu.CompilerParams(
        collective_id=number, has_side_effects=True, vmem_limit_bytes=56 * 2**20
    )


def dma_pairs(count):
    return [pltpu.SemaphoreType.DMA((count,)), pltpu.SemaphoreType.DMA((count,))]


def whole_vmem():
    return pl.BlockSpec(memory_space=pltpu.VMEM)


def anywhere():
    return pl.BlockSpec(memory_space=pl.ANY)


def share_of(half, share):
    return int(half * share) // 128 * 128


def both_sides(values, store, pair):
    low = lax.broadcasted_iota(jnp.int32, values.shape, 1) < HEAD
    swapped = pltpu.roll(values, HEAD, 1)
    store(0, 2 * pair, jnp.where(low, values, 0.0).astype(BF))
    store(1, 2 * pair, jnp.where(low, 0.0, swapped).astype(BF))
    store(0, 2 * pair + 1, jnp.where(low, swapped, 0.0).astype(BF))
    store(1, 2 * pair + 1, jnp.where(low, 0.0, values).astype(BF))


def fill_bias(bias, start):
    length = bias.shape[0]

    def body(chunk):
        shape = (chunk.size, length)
        i = lax.broadcasted_iota(jnp.int32, shape, 0) + chunk.start
        j = lax.broadcasted_iota(jnp.int32, shape, 1)
        in_i = (i >= start) & (i < start + PIECE)
        in_j = (j >= start) & (j < start + PIECE)
        bias[chunk] = jnp.where((j <= i) | (in_i & in_j), 0.0, NEG_FILL)

    row_loop(length, 64, body)


def softmax_rows(query, key, bias):
    scores = dot_nt(query, key) + bias
    exponent = jnp.exp(scores - jnp.max(scores, axis=1, keepdims=True))
    return exponent * (1.0 / jnp.sum(exponent, axis=1, keepdims=True))


PAIRS = HEADS // 2
GROUP = HEADS // KV_HEADS
LANES = 2 * HEAD


def forward(starts, tokens, cotangent, own, w_gate, w_up, w_down, planes, group):
    length, width = tokens.shape
    ds, half = own.shape
    hid, hs = w_gate.shape[2], w_down.shape[0]
    wide = 3 * hid
    part = share_of(half, 0.25)
    first, second, every = (0, part), (part, half - part), (0, half)
    kvd = KV_HEADS * HEAD
    mix = width + 2 * kvd
    row_half = length // 2
    low_rows, high_rows = pl.ds(0, row_half), pl.ds(row_half, row_half)
    tables = turn_tables(length)

    def kernel(
        starts_ref,
        x_ref,
        cot_ref,
        own_ref,
        gate_hbm,
        up_hbm,
        down_hbm,
        tab_ref,
        front_out,
        wall_a,
        wall_b,
        grads_out,
        rows_out,
        gain_ref,
        q_ref,
        kk_ref,
        vv_ref,
        att_ref,
        res_ref,
        n1_ref,
        front,
        bias,
        n2_ref,
        packed,
        raw_in,
        raw_down,
        send_sems,
        recv_sems,
        local_sems,
        load_sems,
    ):
        at = Links(planes, group, send_sems, recv_sems)
        at.barrier([at.x, at.y, at.core, at.diagonal] + at.along[1:])
        walls = (wall_a, wall_b)
        shard = at.yb * 2 + at.c

        order = [(s, e) for e in range(EPD) for s in range(4)]

        def load(n):
            s, e = order[n]
            index = (at.xb * 4 + s) * EPD + e
            copies = [
                pltpu.make_async_copy(src, dst, load_sems.at[n % 2, i])
                for i, (src, dst) in enumerate(
                    (
                        (gate_hbm.at[:, index], raw_in.at[n % 2, 0]),
                        (up_hbm.at[:, index], raw_in.at[n % 2, 1]),
                        (down_hbm.at[:, index], raw_down.at[n % 2]),
                    )
                )
            ]
            for copy in copies:
                copy.start()
            return copies

        loads = {n: load(n) for n in range(2)}

        def pack(e):
            for n in range(4 * e, 4 * e + 4):
                s = order[n][0]
                for copy in loads[n]:
                    copy.wait()

                def cast(chunk, n=n, s=s):
                    packed[s, e, chunk, :hid] = raw_in[n % 2, 0, chunk].astype(BF)
                    packed[s, e, chunk, hid : 2 * hid] = raw_in[n % 2, 1, chunk].astype(BF)

                row_loop(ds, 16, cast)
                for i in range(width // hid):
                    packed[s, e, i * hs : (i + 1) * hs, 2 * hid :] = raw_down[
                        n % 2, :, i * hid : (i + 1) * hid
                    ].astype(BF)
                if n + 2 < len(order):
                    loads[n + 2] = load(n + 2)
            copy = pltpu.make_async_copy(
                packed.at[shard, e], walls[e].at[at.z, shard], local_sems.at[e]
            )
            copy.start()
            locals_.append(copy)

        locals_ = []

        def exchange(e):
            copies = []
            for dy, dc, device in ((1, 0, at.y), (1, 1, at.diagonal), (0, 1, at.core)):
                target = (at.yb + dy) % 2 * 2 + (at.c + dc) % 2
                copies.append(
                    at.send(packed.at[target, e], walls[e].at[at.z, shard], device)
                )
            return copies

        ring = {}

        def ring_first(e, copies):
            sent = [
                at.send(packed.at[shard, e], walls[e].at[at.z, shard], at.along[1])
            ]
            for copy, (dy, dc) in zip(copies, ((1, 0), (1, 1), (0, 1))):
                copy.wait_recv()
                piece = walls[e].at[at.z, (at.yb + dy) % 2 * 2 + (at.c + dc) % 2]
                sent.append(at.send(piece, piece, at.along[1]))
            ring[e] = (1, sent)

        def ring_next(e):
            step, sent = ring[e]
            for copy in sent:
                copy.wait_recv()
            if step < planes - 1:
                piece = walls[e].at[(at.z + planes - step) % planes]
                ring[e] = (step + 1, [at.send(piece, piece, at.along[1])])
            else:
                ring[e] = (planes, [])

        def region(k, dx, dy, span):
            row = (((at.z + planes - k) % planes) * 4 + (at.yb + dy) % 2 * 2 + at.c) * ds
            col = (at.xb + dx) % 2 * half + span[0]
            return front.at[
                pl.ds(pl.multiple_of(row, 16), ds), pl.ds(pl.multiple_of(col, 128), span[1])
            ]

        def pass_on(k, dx, dy, span, device):
            here = region(k, dx, dy, span)
            return at.send(here, here, device)

        x_first, x_second, y_first, y_second, far = [], [], [], [], []

        def spread(k):
            for device, span, copies in (
                (at.x, first, x_first),
                (at.y, second, y_second),
                (at.x, second, x_second),
                (at.y, first, y_first),
            ):
                here = region(k, 0, 0, span)
                src = own_ref.at[:, pl.ds(span[0], span[1])] if k == 0 else here
                copies.append(at.send(src, here, device))
            if k > 0:
                to_core.append(pass_on(k, 0, 0, every, at.core))

        def onward(k):
            x_first[k].wait_recv()
            far.append((k, first, pass_on(k, 1, 0, first, at.y)))
            y_second[k].wait_recv()
            far.append((k, second, pass_on(k, 0, 1, second, at.x)))
            x_second[k].wait_recv()
            to_core.append(pass_on(k, 1, 0, every, at.core))
            y_first[k].wait_recv()
            to_core.append(pass_on(k, 0, 1, every, at.core))

        own_copy = pltpu.make_async_copy(own_ref, region(0, 0, 0, every), local_sems.at[2])
        own_copy.start()
        arrive = [None] + [
            at.send(own_ref, region(0, 0, 0, every), at.along[k]) for k in range(1, planes)
        ]
        to_core = [at.send(own_ref, region(0, 0, 0, every), at.core)]
        spread(0)
        pack(0)
        first_exchange = exchange(0)
        pack(1)
        second_exchange = exchange(1)
        fill_bias(bias, starts_ref[0])
        for k in range(1, planes):
            arrive[k].wait_recv()
            spread(k)
            onward(k - 1)
        ring_first(0, first_exchange)
        ring_first(1, second_exchange)
        onward(planes - 1)
        for k, span, copy in far:
            copy.wait_recv()
            to_core.append(pass_on(k, 1, 1, span, at.core))
        for copy in to_core:
            copy.wait_recv()
        own_copy.wait()
        front_copy = pltpu.make_async_copy(front, front_out, local_sems.at[3])
        front_copy.start()

        def gather_start(src, out):
            def slot(j, rows=pl.ds(0, length)):
                return out.at[j, rows]

            got = {
                "x_low": at.send(src.at[low_rows], slot(4, low_rows), at.x),
                "y_high": at.send(src.at[high_rows], slot(2, high_rows), at.y),
                "x_high": at.send(src.at[high_rows], slot(4, high_rows), at.x),
                "y_low": at.send(src.at[low_rows], slot(2, low_rows), at.y),
                "core": [at.send(src, slot(1), at.core)],
            }
            return slot, got

        def gather_middle(slot, got):
            got["x_low"].wait_recv()
            got["far_low"] = at.send(slot(4, low_rows), slot(6, low_rows), at.y)
            got["core"].append(at.send(slot(4, low_rows), slot(5, low_rows), at.core))
            got["y_high"].wait_recv()
            got["far_high"] = at.send(slot(2, high_rows), slot(6, high_rows), at.x)
            got["core"].append(at.send(slot(2, high_rows), slot(3, high_rows), at.core))

        def gather_last(slot, got):
            got["x_high"].wait_recv()
            got["core"].append(at.send(slot(4, high_rows), slot(5, high_rows), at.core))
            got["y_low"].wait_recv()
            got["core"].append(at.send(slot(2, low_rows), slot(3, low_rows), at.core))
            got["far_low"].wait_recv()
            got["core"].append(at.send(slot(6, low_rows), slot(7, low_rows), at.core))
            got["far_high"].wait_recv()
            got["core"].append(at.send(slot(6, high_rows), slot(7, high_rows), at.core))

        grads = gather_start(cot_ref, grads_out)
        cot_copy = pltpu.make_async_copy(cot_ref, grads_out.at[0], local_sems.at[4])
        cot_copy.start()

        gain_ref[...] = front[:, mix + width : mix + width + 128].astype(F32).T[:8]

        def norm(chunk):
            x = x_ref[chunk].astype(F32)
            inv = lax.rsqrt(jnp.mean(x * x, axis=1, keepdims=True) + EPSILON)
            n1_ref[chunk] = (x * inv * gain_ref[0:1, :]).astype(BF)

        row_loop(length, 64, norm)
        block = 4 * LANES
        for n in range(mix // block):
            raw = dot(n1_ref[...], front[:, n * block : (n + 1) * block])
            for j in range(4):
                col = n * block + j * LANES
                values = raw[:, j * LANES : (j + 1) * LANES]
                if col < width:
                    turned_low = turned(values, tab_ref, 1.0).astype(BF).astype(F32)
                    q_ref[:, col : col + LANES] = (turned_low * (1.0 / math.sqrt(HEAD))).astype(BF)
                else:
                    target, base = (kk_ref, width) if col < width + kvd else (vv_ref, width + kvd)
                    if col < width + kvd:
                        values = turned(values, tab_ref, 1.0)

                    def store(side, head, side_values, target=target):
                        target[side, head] = side_values

                    both_sides(values, store, (col - base) // LANES)
        ring_next(0)

        def attend(pairs):
            @pl.loop(*pairs)
            def _(p):
                cols = pl.ds(pl.multiple_of(p * LANES, LANES), LANES)
                for n in range(length // 128):
                    rows = slice(n * 128, (n + 1) * 128)
                    total = None
                    for side in range(2):
                        head = (2 * p + side) // GROUP
                        probs = softmax_rows(q_ref[rows, cols], kk_ref[side, head], bias[rows])
                        term = dot(probs.astype(BF), vv_ref[side, head])
                        total = term if total is None else total + term
                    att_ref[rows, cols] = total.astype(BF)

        attend((0, PAIRS // 2))
        gather_middle(*grads)
        ring_next(1)
        attend((PAIRS // 2, PAIRS))
        for n in range(width // block):
            cols = slice(n * block, (n + 1) * block)
            res_ref[:, cols] = x_ref[:, cols].astype(F32) + dot(
                att_ref[...], front[:, mix + n * block : mix + (n + 1) * block]
            )

        def norm_two(chunk):
            r = res_ref[chunk]
            inv = lax.rsqrt(jnp.mean(r * r, axis=1, keepdims=True) + EPSILON)
            n2_ref[chunk] = (r * inv * gain_ref[1:2, :]).astype(BF)

        row_loop(length, 64, norm_two)
        rows = gather_start(n2_ref, rows_out)
        rows_copy = pltpu.make_async_copy(n2_ref, rows_out.at[0], local_sems.at[5])
        rows_copy.start()
        gather_last(*grads)
        gather_middle(*rows)
        ring_next(0)
        gather_last(*rows)
        for e in (1, 0):
            while ring[e][0] < planes:
                ring_next(e)
        for copy in grads[1]["core"] + rows[1]["core"]:
            copy.wait_recv()
        for copy in locals_ + [front_copy, cot_copy, rows_copy]:
            copy.wait()
        at.finish()

    shape = jax.ShapeDtypeStruct
    count = planes - 1 + planes * 11 + 2 * 3 + 2 * (4 + planes - 2) + 2 * 13
    return pl.pallas_call(
        kernel,
        out_shape=[
            shape((width, 2 * half), BF),
            shape((planes, 4, ds, wide), BF),
            shape((planes, 4, ds, wide), BF),
            shape((PLANE, length, width), BF),
            shape((PLANE, length, width), BF),
            shape((8, width), F32),
            shape((length, width), BF),
            shape((2, KV_HEADS, length, LANES), BF),
            shape((2, KV_HEADS, length, LANES), BF),
            shape((length, width), BF),
            shape((length, width), F32),
            shape((length, width), BF),
        ],
        in_specs=[pl.BlockSpec(memory_space=pltpu.SMEM)]
        + [whole_vmem()] * 3
        + [anywhere()] * 3
        + [whole_vmem()],
        out_specs=[anywhere()] * 5 + [whole_vmem()] * 7,
        scratch_shapes=[
            pltpu.VMEM((width, 2 * half), BF),
            pltpu.VMEM((length, length), F32),
            pltpu.VMEM((length, width), BF),
            pltpu.VMEM((4, EPD, ds, wide), BF),
            pltpu.VMEM((2, 2, ds, hid), F32),
            pltpu.VMEM((2, hs, width), F32),
        ]
        + dma_pairs(count)
        + [pltpu.SemaphoreType.DMA((6,)), pltpu.SemaphoreType.DMA((2, 3))],
        compiler_params=comm_params(0),
        cost_estimate=pl.CostEstimate(
            flops=150_000_000_000, bytes_accessed=20_000_000, transcendentals=0
        ),
    )(starts, tokens, cotangent, own, w_gate, w_up, w_down, tables)


def expert(rows, grads, share, pack, before, group):
    count, width = rows.shape
    hid = width // 3
    tile = 512
    ds, hs, blocks = width // group, hid // group, width // hid

    def kernel(*refs):
        x_ref, g_ref, s_ref, w_ref = refs[:4]
        old = refs[4:6] if before else None
        o_ref, dx_ref, dw_ref, down, in_sum, down_sum, pre, act = refs[6 if before else 4 :]
        step = pl.program_id(0)

        @pl.when(step == 0)
        def _():
            for s in range(group):
                for b in range(blocks):
                    down[s * hs : (s + 1) * hs, b * hid : (b + 1) * hid] = w_ref[
                        s * ds + b * hs : s * ds + (b + 1) * hs, 2 * hid :
                    ]
            in_sum[...] = jnp.zeros_like(in_sum)
            down_sum[...] = jnp.zeros_like(down_sum)

        half = hid // 2
        for n in range(2):
            cols = slice(n * half, (n + 1) * half)
            up_cols = slice(hid + n * half, hid + (n + 1) * half)
            gate = dot(x_ref[...], w_ref[:, cols])
            up = dot(x_ref[...], w_ref[:, up_cols])
            inner = dot_nt(g_ref[...], down[cols, :]) * s_ref[...]
            sig = jax.nn.sigmoid(gate)
            swish = gate * sig
            act[:, cols] = (s_ref[...] * (swish * up)).astype(BF)
            pre[:, cols] = (inner * up * sig * (1.0 + gate * (1.0 - sig))).astype(BF)
            pre[:, up_cols] = (inner * swish).astype(BF)
        for n in range(width // hid):
            cols = slice(n * hid, (n + 1) * hid)
            out = dot(act[...], down[:, cols])
            dx = dot_nt(pre[...], w_ref[cols, : 2 * hid])
            if before:
                out = out + old[0][:, cols].astype(F32)
                dx = dx + old[1][:, cols].astype(F32)
            o_ref[:, cols] = out.astype(BF)
            dx_ref[:, cols] = dx.astype(BF)
            in_sum[cols, :] += dot_tn(x_ref[:, cols], pre[...])
            down_sum[:, cols] += dot_tn(act[...], g_ref[:, cols])

        @pl.when(step == count // tile - 1)
        def _():
            dw_ref[:, : 2 * hid] = in_sum[...].astype(BF)
            for s in range(group):
                for b in range(blocks):
                    dw_ref[s * ds + b * hs : s * ds + (b + 1) * hs, 2 * hid :] = down_sum[
                        s * hs : (s + 1) * hs, b * hid : (b + 1) * hid
                    ].astype(BF)

    tiles = pl.BlockSpec((tile, width), lambda i: (i, 0))
    whole = pl.BlockSpec((width, width), lambda i: (0, 0))
    shape = jax.ShapeDtypeStruct
    return pl.pallas_call(
        kernel,
        grid=(count // tile,),
        in_specs=[tiles, tiles, pl.BlockSpec((tile, 1), lambda i: (i, 0)), whole]
        + [tiles] * len(before),
        out_specs=[tiles, tiles, whole],
        out_shape=[shape((count, width), BF), shape((count, width), BF), shape((width, width), BF)],
        scratch_shapes=[
            pltpu.VMEM((hid, width), BF),
            pltpu.VMEM((width, 2 * hid), F32),
            pltpu.VMEM((hid, width), F32),
            pltpu.VMEM((tile, 2 * hid), BF),
            pltpu.VMEM((tile, hid), BF),
        ],
        compiler_params=pltpu.CompilerParams(vmem_limit_bytes=58 * 2**20),
        cost_estimate=pl.CostEstimate(
            flops=44_000_000_000, bytes_accessed=50_000_000, transcendentals=0
        ),
    )(rows, grads, share, pack, *before)


class PlaneSum:
    def __init__(self, at, odd, even, from_core, far, near):
        self.at, self.odd, self.even, self.core = at, odd, even, from_core
        self.far, self.near = far, near
        self.length = from_core.shape[1]
        self.half = self.length // 2
        self.low, self.high = pl.ds(0, self.half), pl.ds(self.half, self.half)

    def start(self):
        self.arrive = {
            j: self.at.send(self.odd(j), self.core.at[j], self.at.core) for j in (3, 2, 1, 0)
        }

    def add_core(self, j):
        self.arrive[j].wait_recv()
        core = self.core

        def store(chunk, total):
            core[j, chunk] = total.astype(BF)

        add_rows(store, [lambda q: self.even(j, q), lambda q: core[j, q]], self.length)

    def add_far(self, j, n, base):
        core, far = self.core, self.far

        def moved(chunk):
            return pl.ds(pl.multiple_of(chunk.start + base, 16), chunk.size)

        def store(chunk, total):
            core[j, moved(chunk)] = total.astype(BF)

        add_rows(store, [lambda q: core[j, moved(q)], lambda q: far[n, q]], self.half)

    def neighbours(self):
        at, core, far, near, low, high = self.at, self.core, self.far, self.near, self.low, self.high
        self.add_core(3)
        self.far_y = at.send(core.at[3, low], far.at[0], at.y)
        self.far_x = at.send(core.at[3, high], far.at[1], at.x)
        self.add_core(2)
        self.last = [at.send(core.at[2, high], near.at[0, high], at.x)]
        self.add_core(1)
        self.last.append(at.send(core.at[1, low], near.at[1, low], at.y))

    def onward(self):
        at, core, near, low, high = self.at, self.core, self.near, self.low, self.high
        self.far_y.wait_recv()
        self.add_far(2, 0, 0)
        self.last.append(at.send(core.at[2, low], near.at[0, low], at.x))
        self.far_x.wait_recv()
        self.add_far(1, 1, self.half)
        self.last.append(at.send(core.at[1, high], near.at[1, high], at.y))

    def end(self, store):
        self.arrive[0].wait_recv()
        for copy in self.last:
            copy.wait_recv()
        core, near = self.core, self.near
        terms = [lambda q: self.even(0, q), lambda q: core[0, q]]
        terms += [lambda q: near[0, q], lambda q: near[1, q]]
        add_rows(store, terms, self.length)

    copies = 10


class RingSum:
    def __init__(self, at, pack, own, own_sem):
        self.at, self.pack, self.own, self.own_sem = at, pack, own, own_sem

    def block(self, k):
        return self.pack.at[(self.at.z + self.at.planes - k) % self.at.planes]

    def fetch(self, k):
        self.fetched = pltpu.make_async_copy(self.block(k), self.own, self.own_sem)
        self.fetched.start()

    def add(self, source, target):
        self.fetched.wait()

        def store(chunk, total):
            target[chunk] = total.astype(BF)

        add_rows(store, [lambda q: source[q], lambda q: self.own[q]], self.own.shape[0], 16)

    def first(self, slots):
        self.slots, self.step = slots, 1
        self.copy = self.at.send(self.block(1), slots[0], self.at.along[1])
        self.fetch(2)

    def next(self):
        if self.step < len(self.slots):
            here = self.slots[self.step - 1]
            self.copy.wait_recv()
            self.add(here, here)
            self.copy = self.at.send(here, self.slots[self.step], self.at.along[1])
            self.step += 1
            if self.step < len(self.slots):
                self.fetch(self.step + 1)

    def rest(self):
        while self.step < len(self.slots):
            self.next()
        self.copy.wait_recv()

    def last(self, before, sent, landing):
        self.add(before, sent)
        self.landing = landing
        self.copy = self.at.send(sent, landing, self.at.along[1])
        self.fetch(0)

    def total(self):
        self.copy.wait_recv()
        self.add(self.landing, self.landing)
        return self.landing


class Exchange:
    def __init__(self, at, total, out, ds):
        self.at, self.total, self.out, self.ds = at, total, out, ds
        self.shard = at.yb * 2 + at.c

    def place(self, dx, dy, dc):
        at = self.at
        return (at.xb + dx) % 2 * 4 + (at.yb + dy) % 2 * 2 + (at.c + dc) % 2

    def rows(self, dy, dc):
        at = self.at
        shard = (at.yb + dy) % 2 * 2 + (at.c + dc) % 2
        return self.total.at[pl.ds(pl.multiple_of(shard * self.ds, 16), self.ds)]

    def start(self, sem):
        at = self.at
        here = self.out.at[self.place(0, 0, 0)]
        self.local = pltpu.make_async_copy(self.rows(0, 0), here, sem)
        self.local.start()
        self.got = [
            (dy, dc, at.send(self.rows(dy, dc), here, device))
            for dy, dc, device in ((1, 0, at.y), (1, 1, at.diagonal), (0, 1, at.core))
        ]
        self.across = [at.send(self.rows(0, 0), here, at.x)]

    def onward(self):
        at = self.at
        for dy, dc, copy in self.got:
            copy.wait_recv()
            piece = self.out.at[self.place(0, dy, dc)]
            self.across.append(at.send(piece, piece, at.x))

    def end(self):
        for copy in self.across:
            copy.wait_recv()
        self.local.wait()

    copies = 7


def backward(
    starts,
    grad_two,
    cotangent,
    tokens,
    residual,
    front,
    gains,
    q,
    kk,
    vv,
    att,
    n1,
    outs,
    pack_a,
    before_a,
    pack_b,
    planes,
    group,
):
    length, width = tokens.shape
    columns = front.shape[1]
    kvd = KV_HEADS * HEAD
    mix = width + 2 * kvd
    block = 4 * LANES
    tables = turn_tables(length)
    piece, wide = pack_a.shape[1:]
    ds = piece // 4
    extra = columns - mix - width

    def kernel(
        starts_ref,
        d_ref,
        cot_ref,
        tab_ref,
        gain_ref,
        q_ref,
        kk_ref,
        vv_ref,
        att_ref,
        before_ref,
        x_hbm,
        n1_hbm,
        res_hbm,
        w_hbm,
        outs_ref,
        pack_a_ref,
        pack_b_ref,
        in_ref,
        sum_ref,
        passed_b,
        grad_hbm,
        shards_ref,
        bias,
        gain_sum,
        mixed,
        context,
        grad_mix,
        key_sum,
        value_sum,
        w_ref,
        stage,
        even,
        from_core,
        far,
        near,
        own_a,
        sent_a,
        landing_a,
        own_b,
        slots_b,
        send_sems,
        recv_sems,
        local_sems,
    ):
        at = Links(planes, group, send_sems, recv_sems)
        at.barrier([at.x, at.y, at.core, at.diagonal] + at.along[1:])

        def local(src, dst, n):
            copy = pltpu.make_async_copy(src, dst, local_sems.at[n])
            copy.start()
            return copy

        load_res = local(res_hbm, in_ref, 0)
        load_out_w = local(
            w_hbm.at[:, pl.ds(mix, width)], w_ref.at[:, pl.ds(0, width)], 1
        )
        plane = PlaneSum(
            at, lambda j: outs_ref.at[2 * j + 1], lambda j, q: even[j, q], from_core, far, near
        )
        plane.start()
        ring_a = RingSum(at, pack_a_ref, own_a, local_sems.at[6])
        ring_b = RingSum(at, pack_b_ref, own_b, local_sems.at[7])
        ring_a.fetch(planes - 1)
        loads = [local(outs_ref.at[2 * j], even.at[j], 2 + j) for j in range(4)]
        ring_a.last(before_ref, sent_a, landing_a)
        ring_b.first([slots_b.at[n] for n in range(planes - 3)] + [passed_b])
        staged = [None, None]
        turn = [0]

        def put(values, column, count):
            n = turn[0] % 2
            turn[0] += 1
            if staged[n] is not None:
                staged[n].wait()
            stage[n, :, :count] = values
            staged[n] = local(
                stage.at[n, :, pl.ds(0, count)], grad_hbm.at[:, pl.ds(column, count)], 8 + n
            )

        fill_bias(bias, starts_ref[0])
        gain_sum[...] = jnp.zeros_like(gain_sum)

        load_res.wait()

        def residual_grad(chunk):
            d, r = d_ref[chunk], in_ref[chunk]
            inv = lax.rsqrt(jnp.mean(r * r, axis=1, keepdims=True) + EPSILON)
            scaled = d * gain_ref[1:2, :]
            grad = (
                cot_ref[chunk].astype(F32)
                + inv * scaled
                - r * (inv * inv * inv * jnp.mean(scaled * r, axis=1, keepdims=True))
            )
            sum_ref[chunk] = grad
            mixed[chunk] = grad.astype(BF)
            gain_sum[1:2, :] += jnp.sum(d * r * inv, axis=0, keepdims=True)

        row_loop(length, 32, residual_grad)
        load_out_w.wait()
        for n in range(width // block):
            cols = slice(n * block, (n + 1) * block)
            context[:, cols] = dot_nt(mixed[...], w_ref[cols, :width]).astype(BF)
        load_mix_w = local(w_hbm.at[:, pl.ds(0, mix)], w_ref, 1)
        for n in range(width // block):
            cols = slice(n * block, (n + 1) * block)
            put(dot_tn(att_ref[...], mixed[:, cols]).astype(BF), mix + n * block, block)
        load_n1 = local(n1_hbm, mixed, 0)
        for copy in loads:
            copy.wait()
        plane.neighbours()
        key_sum[...] = jnp.zeros_like(key_sum)
        value_sum[...] = jnp.zeros_like(value_sum)

        def attend(lower, upper):
            @pl.loop(lower, upper)
            def _(p):
                cols = pl.ds(pl.multiple_of(p * LANES, LANES), LANES)
                for n in range(length // 128):
                    rows = slice(n * 128, (n + 1) * 128)
                    total = None
                    for side in range(2):
                        head = (2 * p + side) // GROUP
                        query, grad = q_ref[rows, cols], context[rows, cols]
                        probs = softmax_rows(query, kk_ref[side, head], bias[rows])
                        grad_probs = dot_nt(grad, vv_ref[side, head])
                        value_sum[side, head] += dot_tn(probs.astype(BF), grad)
                        inner = jnp.sum(probs * grad_probs, axis=1, keepdims=True)
                        logit = (probs * (grad_probs - inner)).astype(BF)
                        term = dot(logit, kk_ref[side, head])
                        total = term if total is None else total + term
                        key_sum[side, head] += dot_tn(logit, query)
                    back = turned(total, tab_ref.at[:, rows], -1.0) * (1.0 / math.sqrt(HEAD))
                    grad_mix[rows, cols] = back.astype(BF)

        attend(0, PAIRS // 3)
        plane.onward()
        exchange = Exchange(at, ring_a.total(), shards_ref, ds)
        exchange.start(local_sems.at[10])
        attend(PAIRS // 3, 2 * PAIRS // 3)
        ring_b.next()
        exchange.onward()
        attend(2 * PAIRS // 3, PAIRS)
        load_x = local(x_hbm, context, 11)
        load_n1.wait()
        for pair in range(KV_HEADS // 2):
            for sums, base in ((key_sum, width), (value_sum, width + kvd)):

                def join(chunk, pair=pair, sums=sums, base=base):
                    low = lax.broadcasted_iota(jnp.int32, (chunk.size, LANES), 1) < HEAD
                    even = sums[0, 2 * pair, chunk] + pltpu.roll(sums[1, 2 * pair, chunk], HEAD, 1)
                    odd = sums[1, 2 * pair + 1, chunk] + pltpu.roll(
                        sums[0, 2 * pair + 1, chunk], HEAD, 1
                    )
                    values = jnp.where(low, even, odd)
                    if base == width:
                        values = turned(values, tab_ref.at[:, chunk], -1.0)
                    grad_mix[chunk, base + pair * LANES : base + (pair + 1) * LANES] = values.astype(BF)

                row_loop(length, 64, join)
        for n in range(mix // block):
            cols = slice(n * block, (n + 1) * block)
            put(dot_tn(mixed[...], grad_mix[:, cols]).astype(BF), n * block, block)
        load_mix_w.wait()
        for n in range(width // block):
            cols = slice(n * block, (n + 1) * block)
            in_ref[:, cols] = dot_nt(grad_mix[...], w_ref[cols, :mix])

        load_x.wait()

        def input_grad(chunk):
            d, x = in_ref[chunk], context[chunk].astype(F32)
            inv = lax.rsqrt(jnp.mean(x * x, axis=1, keepdims=True) + EPSILON)
            scaled = d * gain_ref[0:1, :]
            gain_sum[0:1, :] += jnp.sum(d * x * inv, axis=0, keepdims=True)
            in_ref[chunk] = (
                sum_ref[chunk]
                + inv * scaled
                - x * (inv * inv * inv * jnp.mean(scaled * x, axis=1, keepdims=True))
            )

        row_loop(length, 32, input_grad)
        gain_rows = jnp.concatenate([gain_sum[...].T, jnp.zeros((width, extra - 8), F32)], axis=1)
        put(gain_rows.astype(BF), mix + width, extra)

        def store(chunk, total):
            sum_ref[chunk] = total

        plane.end(store)
        ring_b.rest()
        exchange.end()
        for copy in staged:
            copy.wait()
        at.finish()

    shape = jax.ShapeDtypeStruct
    return pl.pallas_call(
        kernel,
        in_specs=[pl.BlockSpec(memory_space=pltpu.SMEM)]
        + [whole_vmem()] * 9
        + [anywhere()] * 7,
        out_specs=[whole_vmem()] * 3 + [anywhere()] * 2,
        out_shape=[
            shape((length, width), F32),
            shape((length, width), F32),
            shape((piece, wide), BF),
            shape((width, columns), BF),
            shape((PLANE, ds, wide), BF),
        ],
        scratch_shapes=[
            pltpu.VMEM((length, length), F32),
            pltpu.VMEM((8, width), F32),
            pltpu.VMEM((length, width), BF),
            pltpu.VMEM((length, width), BF),
            pltpu.VMEM((length, mix), BF),
            pltpu.VMEM((2, KV_HEADS, length, LANES), F32),
            pltpu.VMEM((2, KV_HEADS, length, LANES), F32),
            pltpu.VMEM((width, mix), BF),
            pltpu.VMEM((2, width, block), BF),
            pltpu.VMEM((4, length, width), BF),
            pltpu.VMEM((4, length, width), BF),
            pltpu.VMEM((2, length // 2, width), BF),
            pltpu.VMEM((2, length, width), BF),
            pltpu.VMEM((piece, wide), BF),
            pltpu.VMEM((piece, wide), BF),
            pltpu.VMEM((piece, wide), BF),
            pltpu.VMEM((piece, wide), BF),
            pltpu.VMEM((planes - 3, piece, wide), BF),
        ]
        + dma_pairs(PlaneSum.copies + 1 + Exchange.copies + planes - 2)
        + [pltpu.SemaphoreType.DMA((12,))],
        compiler_params=pltpu.CompilerParams(
            collective_id=1, has_side_effects=True, vmem_limit_bytes=62 * 2**20
        ),
        cost_estimate=pl.CostEstimate(
            flops=80_000_000_000, bytes_accessed=50_000_000, transcendentals=0
        ),
    )(
        starts,
        grad_two,
        cotangent,
        tables,
        gains,
        q,
        kk,
        vv,
        att,
        before_a,
        tokens,
        n1,
        residual,
        front,
        outs,
        pack_a,
        pack_b,
    )


def scatter_plane(partial, pack, planes, group):
    slots, length, width = partial.shape
    half = length // 2
    block, wide = pack.shape[1:]

    def kernel(
        p_ref, pack_ref, out_ref, passed, even, from_core, far, near, ring_slots, own, send_sems, recv_sems, local_sems
    ):
        at = Links(planes, group, send_sems, recv_sems)
        at.barrier([at.x, at.y, at.core] + at.along[1:])
        ring = RingSum(at, pack_ref, own, local_sems.at[4])
        loads = []
        for j in range(4):
            loads.append(pltpu.make_async_copy(p_ref.at[2 * j], even.at[j], local_sems.at[j]))
            loads[-1].start()
        plane = PlaneSum(
            at, lambda j: p_ref.at[2 * j + 1], lambda j, q: even[j, q], from_core, far, near
        )
        plane.start()
        ring.first([ring_slots.at[n] for n in range(planes - 3)] + [passed])
        for copy in loads:
            copy.wait()
        plane.neighbours()
        plane.onward()
        ring.next()

        def store(chunk, total):
            out_ref[chunk] = total

        plane.end(store)
        ring.rest()
        at.finish()

    return pl.pallas_call(
        kernel,
        out_shape=[
            jax.ShapeDtypeStruct((length, width), F32),
            jax.ShapeDtypeStruct((block, wide), BF),
        ],
        in_specs=[anywhere(), anywhere()],
        out_specs=[whole_vmem(), whole_vmem()],
        scratch_shapes=[
            pltpu.VMEM((4, length, width), BF),
            pltpu.VMEM((4, length, width), BF),
            pltpu.VMEM((2, half, width), BF),
            pltpu.VMEM((2, length, width), BF),
            pltpu.VMEM((planes - 3, block, wide), BF),
            pltpu.VMEM((block, wide), BF),
        ]
        + dma_pairs(PlaneSum.copies + planes - 2)
        + [pltpu.SemaphoreType.DMA((5,))],
        compiler_params=comm_params(2),
        cost_estimate=pl.CostEstimate(
            flops=45_000_000_000, bytes_accessed=20_000_000, transcendentals=0
        ),
    )(partial, pack)


def scatter_front(grad, pack, before, planes, group):
    rows, columns = grad.shape
    ds, half = rows // (4 * planes), columns // 2
    part = share_of(half, 0.6)
    first, second = pl.ds(0, part), pl.ds(part, half - part)
    block, wide = pack.shape[1:]

    def kernel(
        g_ref,
        pack_ref,
        before_ref,
        out_ref,
        shards_ref,
        from_core,
        kept,
        far_a,
        far_b,
        near_x,
        near_y,
        total_ref,
        from_z,
        own,
        passed,
        landing,
        send_sems,
        recv_sems,
        local_sems,
    ):
        at = Links(planes, group, send_sems, recv_sems)
        at.barrier([at.x, at.y, at.core, at.diagonal] + at.along[1:])
        ring = RingSum(at, pack_ref, own, local_sems.at[0])
        ring.fetch(planes - 1)

        def row(k, dy, core):
            owner = ((at.z + k) % planes) * 4 + (at.yb + dy) % 2 * 2 + core
            return pl.multiple_of(owner * ds, 16)

        def column(dx):
            return pl.ds(pl.multiple_of((at.xb + dx) % 2 * half, 128), half)

        order = list(range(1, planes)) + [0]
        arrive = {}
        for k in order:
            for dy in (1, 0):
                arrive[k, dy] = at.send(
                    g_ref.at[pl.ds(row(k, dy, 1 - at.c), ds)], from_core.at[k, dy], at.core
                )
        ring.last(before_ref, passed, landing)
        step = 16
        x_second, y_first, x_first, y_second, to_x, to_y = {}, {}, {}, {}, {}, {}
        for k in order:
            for dy in (1, 0):
                arrive[k, dy].wait_recv()
                for dx in (1, 0):

                    def store(chunk, total, k=k, dx=dx, dy=dy):
                        kept[k, dx, dy, chunk] = total.astype(BF)

                    add_rows(
                        store,
                        [
                            lambda q, k=k, dx=dx, dy=dy: g_ref[
                                pl.ds(pl.multiple_of(row(k, dy, at.c) + q.start, 16), q.size),
                                column(dx),
                            ],
                            lambda q, k=k, dx=dx, dy=dy: from_core[k, dy, q, column(dx)],
                        ],
                        ds,
                        step,
                    )
                    if (dx, dy) == (1, 1):
                        to_y[k] = at.send(kept.at[k, 1, 1, :, first], far_a.at[k], at.y)
                        to_x[k] = at.send(kept.at[k, 1, 1, :, second], far_b.at[k], at.x)
                    elif (dx, dy) == (0, 1):
                        y_first[k] = at.send(
                            kept.at[k, 0, 1, :, first], near_y.at[k, :, first], at.y
                        )
                    elif (dx, dy) == (1, 0):
                        x_second[k] = at.send(
                            kept.at[k, 1, 0, :, second], near_x.at[k, :, second], at.x
                        )
        for k in order:
            to_y[k].wait_recv()

            def store(chunk, total, k=k):
                kept[k, 1, 0, chunk, first] = total.astype(BF)

            add_rows(
                store,
                [lambda q, k=k: kept[k, 1, 0, q, first], lambda q, k=k: far_a[k, q]],
                ds,
                step,
            )
            x_first[k] = at.send(kept.at[k, 1, 0, :, first], near_x.at[k, :, first], at.x)
            to_x[k].wait_recv()

            def store(chunk, total, k=k):
                kept[k, 0, 1, chunk, second] = total.astype(BF)

            add_rows(
                store,
                [lambda q, k=k: kept[k, 0, 1, q, second], lambda q, k=k: far_b[k, q]],
                ds,
                step,
            )
            y_second[k] = at.send(kept.at[k, 0, 1, :, second], near_y.at[k, :, second], at.y)
        exchange = Exchange(at, ring.total(), shards_ref, ds)
        exchange.start(local_sems.at[1])
        arrive_z = {}
        for k in order:
            for copies in (x_second, y_first, x_first, y_second):
                copies[k].wait_recv()

            def store(chunk, total, k=k):
                total_ref[k, chunk] = total.astype(BF)

            add_rows(
                store,
                [
                    lambda q, k=k: kept[k, 0, 0, q],
                    lambda q, k=k: near_x[k, q],
                    lambda q, k=k: near_y[k, q],
                ],
                ds,
                step,
            )
            if k > 0:
                arrive_z[k] = at.send(total_ref.at[k], from_z.at[k], at.along[k])
        exchange.onward()
        for k in range(1, planes):
            arrive_z[k].wait_recv()

        def store(chunk, total):
            out_ref[chunk] = total.astype(BF)

        add_rows(
            store,
            [lambda q: total_ref[0, q]]
            + [lambda q, k=k: from_z[k, q] for k in range(1, planes)],
            ds,
            step,
        )
        exchange.end()
        at.finish()

    return pl.pallas_call(
        kernel,
        out_shape=[
            jax.ShapeDtypeStruct((ds, half), BF),
            jax.ShapeDtypeStruct((PLANE, ds, wide), BF),
        ],
        in_specs=[whole_vmem(), anywhere(), whole_vmem()],
        out_specs=[whole_vmem(), anywhere()],
        scratch_shapes=[
            pltpu.VMEM((planes, 2, ds, columns), BF),
            pltpu.VMEM((planes, 2, 2, ds, half), BF),
            pltpu.VMEM((planes, ds, part), BF),
            pltpu.VMEM((planes, ds, half - part), BF),
            pltpu.VMEM((planes, ds, half), BF),
            pltpu.VMEM((planes, ds, half), BF),
            pltpu.VMEM((planes, ds, half), BF),
            pltpu.VMEM((planes, ds, half), BF),
            pltpu.VMEM((block, wide), BF),
            pltpu.VMEM((block, wide), BF),
            pltpu.VMEM((block, wide), BF),
        ]
        + dma_pairs(planes * 8 + planes - 1 + 1 + Exchange.copies)
        + [pltpu.SemaphoreType.DMA((2,))],
        compiler_params=comm_params(3),
        cost_estimate=pl.CostEstimate(
            flops=50_000_000_000, bytes_accessed=20_000_000, transcendentals=0
        ),
    )(grad, pack, before)


def unpack(packs, hs):
    ds, wide = packs[0].shape[1:]
    hid = wide // 3
    blocks = ds // hs

    def kernel(*refs):
        ins, (gate_out, up_out, down_out, raw_in, raw_down, sems) = refs[:EPD], refs[EPD:]
        copies = {}
        for n, (p, e) in enumerate((p, e) for p in range(PLANE) for e in range(EPD)):
            slot = n % 4
            if n >= 4:
                for copy in copies[n - 4]:
                    copy.wait()

            def cast(chunk, p=p, e=e, slot=slot):
                raw_in[slot, 0, chunk] = ins[e][p, chunk, :hid].astype(F32)
                raw_in[slot, 1, chunk] = ins[e][p, chunk, hid : 2 * hid].astype(F32)

            row_loop(ds, 16, cast)
            for b in range(blocks):
                raw_down[slot, :, b * hid : (b + 1) * hid] = ins[e][
                    p, b * hs : (b + 1) * hs, 2 * hid :
                ].astype(F32)
            index = p * EPD + e
            copies[n] = [
                pltpu.make_async_copy(src, dst, sems.at[slot, i])
                for i, (src, dst) in enumerate(
                    (
                        (raw_in.at[slot, 0], gate_out.at[:, index]),
                        (raw_in.at[slot, 1], up_out.at[:, index]),
                        (raw_down.at[slot], down_out.at[:, index]),
                    )
                )
            ]
            for copy in copies[n]:
                copy.start()
        for n in range(EXP - 4, EXP):
            for copy in copies[n]:
                copy.wait()

    shape = jax.ShapeDtypeStruct
    return pl.pallas_call(
        kernel,
        in_specs=[whole_vmem()] * EPD,
        out_specs=[anywhere()] * 3,
        out_shape=[
            shape((ds, EXP, hid), F32),
            shape((ds, EXP, hid), F32),
            shape((hs, EXP, blocks * hid), F32),
        ],
        scratch_shapes=[
            pltpu.VMEM((4, 2, ds, hid), F32),
            pltpu.VMEM((4, hs, blocks * hid), F32),
            pltpu.SemaphoreType.DMA((4, 3)),
        ],
        compiler_params=pltpu.CompilerParams(vmem_limit_bytes=32 * 2**20),
    )(*packs)


def shards(
    reps,
    group,
    tokens,
    cotangent,
    routes,
    gates,
    starts,
    norm1_gain,
    w_query,
    w_key,
    w_value,
    w_out,
    norm2_gain,
    w_gate,
    w_up,
    w_down,
):
    planes = group // 4
    r, f = lax.axis_index("rep"), lax.axis_index("fsdp")
    xb, yb, c, z = r % 2, (f // 2) % 2, f % 2, f // 4
    mine = xb * 4 + yb * 2 + c

    def perm(to):
        return [
            (a * group + b, to(a, b)[0] * group + to(a, b)[1])
            for a in range(reps)
            for b in range(group)
        ]

    def pp(value, to):
        return lax.ppermute(value, AXES, perm(to))

    def go(value, dx, dy, dc):
        return pp(value, lambda a, b: (a ^ dx, b ^ (dy * 2 + dc)))

    def along(value, k):
        return pp(value, lambda a, b: (a, (b + 4 * k) % group))

    def all_reps(value):
        step = 2
        while step < reps:
            value = value + pp(value, lambda a, b, s=step: (a ^ s, b))
            step *= 2
        return value

    length, width = tokens.shape
    ds = w_query.shape[0]
    hs = w_down.shape[0]
    hid = w_gate.shape[2]
    kvd = w_key.shape[1]
    half_rows = length // 2

    mix = width + 2 * kvd
    columns = mix + width + 256
    half = columns // 2
    gains = jnp.stack([norm1_gain.astype(BF), norm2_gain.astype(BF)], axis=1)
    front_own = jnp.concatenate(
        [
            w_query.astype(BF),
            w_key.astype(BF),
            w_value.astype(BF),
            w_out.astype(BF),
            gains,
            jnp.zeros((ds, 254), BF),
        ],
        axis=1,
    )
    experts = jnp.arange(EXP, dtype=jnp.int32)[:, None, None]
    share = jnp.sum(jnp.where(routes[None] == experts, gates[None], 0.0), axis=2)
    shares = []
    for j in range(PLANE):
        block = lax.dynamic_slice(share, ((mine ^ j) * EPD, 0), (EPD, length))
        shares.append(block if j == 0 else go(block, j // 4, (j // 2) % 2, j % 2))
    shares = jnp.concatenate(shares, axis=1)

    front, wall_a, wall_b, grads_all, rows_all, gains_all, q, kk, vv, att, residual, n1 = forward(
        starts,
        tokens,
        cotangent,
        lax.dynamic_slice(front_own, (0, xb * half), (ds, half)),
        w_gate,
        w_up,
        w_down,
        planes,
        group,
    )
    grads_all = grads_all.reshape(PLANE * length, width)
    rows_all = rows_all.reshape(PLANE * length, width)
    before, pack_grads = (), []
    for e, wall in enumerate((wall_a, wall_b)):
        *before, pack_grad = expert(
            rows_all, grads_all, shares[e][:, None], wall.reshape(width, 3 * hid), before, group
        )
        pack_grads.append(pack_grad)
    out_sum, row_sum = before
    pack_a, pack_b = [grad.reshape(planes, 4 * ds, 3 * hid) for grad in pack_grads]
    grad_normed_two, before_a = scatter_plane(
        row_sum.reshape(PLANE, length, width), pack_a, planes, group
    )
    input_grad, out_term, before_b, front_grad, shards_a = backward(
        starts,
        grad_normed_two,
        cotangent,
        tokens,
        residual,
        front,
        gains_all,
        q,
        kk,
        vv,
        att,
        n1,
        out_sum.reshape(PLANE, length, width),
        pack_a,
        before_a,
        pack_b,
        planes,
        group,
    )
    output = residual + out_term
    front_total, shards_b = scatter_front(front_grad, pack_b, before_b, planes, group)
    total = all_reps(front_total)
    gate_shard, up_shard, down_shard = unpack([all_reps(shards_a), all_reps(shards_b)], hs)
    other = go(total, 1, 0, 0)
    front_shard = jnp.where(
        xb == 0,
        jnp.concatenate([total, other], axis=1),
        jnp.concatenate([other, total], axis=1),
    ).astype(F32)
    return (
        output,
        input_grad,
        front_shard[:, mix + width],
        front_shard[:, :width],
        front_shard[:, width : width + kvd],
        front_shard[:, width + kvd : mix],
        front_shard[:, mix : mix + width],
        front_shard[:, mix + width + 1],
        gate_shard,
        up_shard,
        down_shard,
    )


def solution(mesh):
    reps, group = mesh.shape["rep"], mesh.shape["fsdp"]
    both, one = P(AXES, None), P("fsdp")
    flat, deep = P("fsdp", None), P("fsdp", None, None)

    def whole(*args):
        return shards(reps, group, *args)

    return jax.shard_map(
        whole,
        mesh=mesh,
        in_specs=(both, both, both, both, P(AXES), one, flat, flat, flat, flat, one, deep, deep, deep),
        out_specs=(both, both, one, flat, flat, flat, flat, one, deep, deep, deep),
        check_vma=False,
    )
```

```python
import math

import jax
import jax.numpy as jnp
from jax import lax
from jax.experimental import pallas as pl
from jax.experimental.pallas import tpu as pltpu
from jax.sharding import PartitionSpec as P

HEADS = 24
KV_HEADS = 8
HEAD = 64
EXP = 16
PIECE = 256
AXES = ("rep", "fsdp")
EPSILON = 1e-05
NEG_FILL = -1e30
BF = jnp.bfloat16
F32 = jnp.float32
PLANE = 8
EPD = EXP // PLANE


def turn_tables(length):
    positions = jnp.arange(length, dtype=F32)[:, None]
    lanes = jnp.arange(2 * HEAD)
    rates = jnp.exp((lanes % (HEAD // 2)).astype(F32) * (-2.0 * math.log(10000.0) / HEAD))
    angles = positions * rates[None, :]
    low = (lanes % HEAD < HEAD // 2)[None, :]
    sines = jnp.sin(angles)
    return jnp.stack([jnp.cos(angles), jnp.where(low, -sines, 0.0), jnp.where(low, 0.0, sines)])


def turned(values, tables, sign):
    ahead = pltpu.roll(values, 2 * HEAD - HEAD // 2, 1)
    back = pltpu.roll(values, HEAD // 2, 1)
    return values * tables[0] + sign * (ahead * tables[1] + back * tables[2])


def row_loop(rows, step, body):
    @pl.loop(0, rows // step)
    def _(n):
        body(pl.ds(pl.multiple_of(n * step, step), step))


def dot(a, b):
    return jnp.dot(a, b, preferred_element_type=F32)


def dot_nt(a, b):
    return lax.dot_general(a, b, (((1,), (1,)), ((), ())), preferred_element_type=F32)


def dot_tn(a, b):
    return lax.dot_general(a, b, (((0,), (0,)), ((), ())), preferred_element_type=F32)


def add_rows(store, terms, rows, step=32):
    step = min(step, rows)

    @pl.loop(0, rows // step)
    def _(n):
        chunk = pl.ds(pl.multiple_of(n * step, 16), step)
        total = terms[0](chunk).astype(F32)
        for term in terms[1:]:
            total = total + term(chunk).astype(F32)
        store(chunk, total)


class Links:
    def __init__(self, planes, group, send_sems, recv_sems):
        r, f = lax.axis_index("rep"), lax.axis_index("fsdp")
        self.xb, self.yb, self.c, self.z = r % 2, (f // 2) % 2, f % 2, f // 4
        self.x = (r + 1 - 2 * self.xb, f)
        self.y = (r, f + 2 - 4 * self.yb)
        self.core = (r, f + 1 - 2 * self.c)
        self.diagonal = (r, f + 3 - 4 * self.yb - 2 * self.c)
        self.along = [None] + [(r, (f + 4 * k) % group) for k in range(1, planes)]
        self.planes, self.send_sems, self.recv_sems, self.copies = planes, send_sems, recv_sems, []

    def barrier(self, devices):
        semaphore = pltpu.get_barrier_semaphore()
        for device in devices:
            pl.semaphore_signal(
                semaphore, inc=1, device_id=device, device_id_type=pl.DeviceIdType.MESH
            )
        pl.semaphore_wait(semaphore, len(devices))

    def make(self, src, dst, device):
        n = len(self.copies)
        copy = pltpu.make_async_remote_copy(
            src_ref=src,
            dst_ref=dst,
            send_sem=self.send_sems.at[n],
            recv_sem=self.recv_sems.at[n],
            device_id=device,
            device_id_type=pl.DeviceIdType.MESH,
        )
        self.copies.append(copy)
        return copy

    def send(self, src, dst, device):
        copy = self.make(src, dst, device)
        copy.start()
        return copy

    def finish(self):
        for copy in self.copies:
            copy.wait_send()


def comm_params(number):
    return pltpu.CompilerParams(
        collective_id=number, has_side_effects=True, vmem_limit_bytes=56 * 2**20
    )


def dma_pairs(count):
    return [pltpu.SemaphoreType.DMA((count,)), pltpu.SemaphoreType.DMA((count,))]


def whole_vmem():
    return pl.BlockSpec(memory_space=pltpu.VMEM)


def anywhere():
    return pl.BlockSpec(memory_space=pl.ANY)


def share_of(half, share):
    return int(half * share) // 128 * 128


def both_sides(values, store, pair):
    low = lax.broadcasted_iota(jnp.int32, values.shape, 1) < HEAD
    swapped = pltpu.roll(values, HEAD, 1)
    store(0, 2 * pair, jnp.where(low, values, 0.0).astype(BF))
    store(1, 2 * pair, jnp.where(low, 0.0, swapped).astype(BF))
    store(0, 2 * pair + 1, jnp.where(low, swapped, 0.0).astype(BF))
    store(1, 2 * pair + 1, jnp.where(low, 0.0, values).astype(BF))


def fill_bias(bias, start):
    length = bias.shape[0]

    def body(chunk):
        shape = (chunk.size, length)
        i = lax.broadcasted_iota(jnp.int32, shape, 0) + chunk.start
        j = lax.broadcasted_iota(jnp.int32, shape, 1)
        in_i = (i >= start) & (i < start + PIECE)
        in_j = (j >= start) & (j < start + PIECE)
        bias[chunk] = jnp.where((j <= i) | (in_i & in_j), 0.0, NEG_FILL)

    row_loop(length, 64, body)


def softmax_rows(query, key, bias):
    scores = dot_nt(query, key) + bias
    exponent = jnp.exp(scores - jnp.max(scores, axis=1, keepdims=True))
    return exponent * (1.0 / jnp.sum(exponent, axis=1, keepdims=True))


PAIRS = HEADS // 2
GROUP = HEADS // KV_HEADS
LANES = 2 * HEAD


def forward(starts, tokens, cotangent, own, w_gate, w_up, w_down, planes, group):
    length, width = tokens.shape
    ds, half = own.shape
    hid, hs = w_gate.shape[2], w_down.shape[0]
    wide = 3 * hid
    part = share_of(half, 0.25)
    first, second, every = (0, part), (part, half - part), (0, half)
    kvd = KV_HEADS * HEAD
    mix = width + 2 * kvd
    row_half = length // 2
    low_rows, high_rows = pl.ds(0, row_half), pl.ds(row_half, row_half)
    tables = turn_tables(length)

    def kernel(
        starts_ref,
        x_ref,
        cot_ref,
        own_ref,
        gate_hbm,
        up_hbm,
        down_hbm,
        tab_ref,
        front_out,
        wall_a,
        wall_b,
        grads_out,
        gain_ref,
        q_ref,
        kk_ref,
        vv_ref,
        att_ref,
        res_ref,
        n1_ref,
        n2_ref,
        front,
        bias,
        packed,
        raw_in,
        raw_down,
        send_sems,
        recv_sems,
        local_sems,
        load_sems,
    ):
        at = Links(planes, group, send_sems, recv_sems)
        at.barrier([at.x, at.y, at.core, at.diagonal] + at.along[1:])
        walls = (wall_a, wall_b)
        shard = at.yb * 2 + at.c

        order = [(s, e) for e in range(EPD) for s in range(4)]

        def load(n):
            s, e = order[n]
            index = (at.xb * 4 + s) * EPD + e
            copies = [
                pltpu.make_async_copy(src, dst, load_sems.at[n % 2, i])
                for i, (src, dst) in enumerate(
                    (
                        (gate_hbm.at[:, index], raw_in.at[n % 2, 0]),
                        (up_hbm.at[:, index], raw_in.at[n % 2, 1]),
                        (down_hbm.at[:, index], raw_down.at[n % 2]),
                    )
                )
            ]
            for copy in copies:
                copy.start()
            return copies

        loads = {n: load(n) for n in range(2)}

        def pack(e):
            for n in range(4 * e, 4 * e + 4):
                s = order[n][0]
                for copy in loads[n]:
                    copy.wait()

                def cast(chunk, n=n, s=s):
                    packed[s, e, chunk, :hid] = raw_in[n % 2, 0, chunk].astype(BF)
                    packed[s, e, chunk, hid : 2 * hid] = raw_in[n % 2, 1, chunk].astype(BF)

                row_loop(ds, 16, cast)
                for i in range(width // hid):
                    packed[s, e, i * hs : (i + 1) * hs, 2 * hid :] = raw_down[
                        n % 2, :, i * hid : (i + 1) * hid
                    ].astype(BF)
                if n + 2 < len(order):
                    loads[n + 2] = load(n + 2)
            copy = pltpu.make_async_copy(
                packed.at[shard, e], walls[e].at[at.z, shard], local_sems.at[e]
            )
            copy.start()
            locals_.append(copy)

        locals_ = []

        def exchange(e):
            copies = []
            for dy, dc, device in ((1, 0, at.y), (1, 1, at.diagonal), (0, 1, at.core)):
                target = (at.yb + dy) % 2 * 2 + (at.c + dc) % 2
                copies.append(
                    at.send(packed.at[target, e], walls[e].at[at.z, shard], device)
                )
            return copies

        ring = {}

        def ring_first(e, copies):
            sent = [
                at.send(packed.at[shard, e], walls[e].at[at.z, shard], at.along[1])
            ]
            for copy, (dy, dc) in zip(copies, ((1, 0), (1, 1), (0, 1))):
                copy.wait_recv()
                piece = walls[e].at[at.z, (at.yb + dy) % 2 * 2 + (at.c + dc) % 2]
                sent.append(at.send(piece, piece, at.along[1]))
            ring[e] = (1, sent)

        def ring_next(e):
            step, sent = ring[e]
            for copy in sent:
                copy.wait_recv()
            if step < planes - 1:
                piece = walls[e].at[(at.z + planes - step) % planes]
                ring[e] = (step + 1, [at.send(piece, piece, at.along[1])])
            else:
                ring[e] = (planes, [])

        def region(k, dx, dy, span):
            row = (((at.z + planes - k) % planes) * 4 + (at.yb + dy) % 2 * 2 + at.c) * ds
            col = (at.xb + dx) % 2 * half + span[0]
            return front.at[
                pl.ds(pl.multiple_of(row, 16), ds), pl.ds(pl.multiple_of(col, 128), span[1])
            ]

        def pass_on(k, dx, dy, span, device):
            here = region(k, dx, dy, span)
            return at.send(here, here, device)

        x_first, x_second, y_first, y_second, far = [], [], [], [], []

        def spread(k):
            for device, span, copies in (
                (at.x, first, x_first),
                (at.y, second, y_second),
                (at.x, second, x_second),
                (at.y, first, y_first),
            ):
                here = region(k, 0, 0, span)
                src = own_ref.at[:, pl.ds(span[0], span[1])] if k == 0 else here
                copies.append(at.send(src, here, device))
            if k > 0:
                to_core.append(pass_on(k, 0, 0, every, at.core))

        def onward(k):
            x_first[k].wait_recv()
            far.append((k, first, pass_on(k, 1, 0, first, at.y)))
            y_second[k].wait_recv()
            far.append((k, second, pass_on(k, 0, 1, second, at.x)))
            x_second[k].wait_recv()
            to_core.append(pass_on(k, 1, 0, every, at.core))
            y_first[k].wait_recv()
            to_core.append(pass_on(k, 0, 1, every, at.core))

        own_copy = pltpu.make_async_copy(own_ref, region(0, 0, 0, every), local_sems.at[2])
        own_copy.start()
        arrive = [None] + [
            at.send(own_ref, region(0, 0, 0, every), at.along[k]) for k in range(1, planes)
        ]
        to_core = [at.send(own_ref, region(0, 0, 0, every), at.core)]
        spread(0)
        pack(0)
        first_exchange = exchange(0)
        pack(1)
        second_exchange = exchange(1)
        fill_bias(bias, starts_ref[0])
        for k in range(1, planes):
            arrive[k].wait_recv()
            spread(k)
            onward(k - 1)
        ring_first(0, first_exchange)
        onward(planes - 1)
        for k, span, copy in far:
            copy.wait_recv()
            to_core.append(pass_on(k, 1, 1, span, at.core))
        for copy in to_core:
            copy.wait_recv()
        own_copy.wait()
        front_copy = pltpu.make_async_copy(front, front_out, local_sems.at[3])
        front_copy.start()

        def gather_start(src, out):
            def slot(j, rows=pl.ds(0, length)):
                return out.at[j, rows]

            got = {
                "x_low": at.send(src.at[low_rows], slot(4, low_rows), at.x),
                "y_high": at.send(src.at[high_rows], slot(2, high_rows), at.y),
                "x_high": at.send(src.at[high_rows], slot(4, high_rows), at.x),
                "y_low": at.send(src.at[low_rows], slot(2, low_rows), at.y),
                "core": [at.send(src, slot(1), at.core)],
            }
            return slot, got

        def gather_middle(slot, got):
            got["x_low"].wait_recv()
            got["far_low"] = at.send(slot(4, low_rows), slot(6, low_rows), at.y)
            got["core"].append(at.send(slot(4, low_rows), slot(5, low_rows), at.core))
            got["y_high"].wait_recv()
            got["far_high"] = at.send(slot(2, high_rows), slot(6, high_rows), at.x)
            got["core"].append(at.send(slot(2, high_rows), slot(3, high_rows), at.core))

        def gather_last(slot, got):
            got["x_high"].wait_recv()
            got["core"].append(at.send(slot(4, high_rows), slot(5, high_rows), at.core))
            got["y_low"].wait_recv()
            got["core"].append(at.send(slot(2, low_rows), slot(3, low_rows), at.core))
            got["far_low"].wait_recv()
            got["core"].append(at.send(slot(6, low_rows), slot(7, low_rows), at.core))
            got["far_high"].wait_recv()
            got["core"].append(at.send(slot(6, high_rows), slot(7, high_rows), at.core))

        grads = gather_start(cot_ref, grads_out)
        cot_copy = pltpu.make_async_copy(cot_ref, grads_out.at[0], local_sems.at[4])
        cot_copy.start()

        gain_ref[...] = front[:, mix + width : mix + width + 128].astype(F32).T[:8]

        def norm(chunk):
            x = x_ref[chunk].astype(F32)
            inv = lax.rsqrt(jnp.mean(x * x, axis=1, keepdims=True) + EPSILON)
            n1_ref[chunk] = (x * inv * gain_ref[0:1, :]).astype(BF)

        row_loop(length, 64, norm)
        block = 4 * LANES
        for n in range(mix // block):
            raw = dot(n1_ref[...], front[:, n * block : (n + 1) * block])
            for j in range(4):
                col = n * block + j * LANES
                values = raw[:, j * LANES : (j + 1) * LANES]
                if col < width:
                    turned_low = turned(values, tab_ref, 1.0).astype(BF).astype(F32)
                    q_ref[:, col : col + LANES] = (turned_low * (1.0 / math.sqrt(HEAD))).astype(BF)
                else:
                    target, base = (kk_ref, width) if col < width + kvd else (vv_ref, width + kvd)
                    if col < width + kvd:
                        values = turned(values, tab_ref, 1.0)

                    def store(side, head, side_values, target=target):
                        target[side, head] = side_values

                    both_sides(values, store, (col - base) // LANES)
        ring_next(0)

        def attend(pairs):
            @pl.loop(*pairs)
            def _(p):
                cols = pl.ds(pl.multiple_of(p * LANES, LANES), LANES)
                for n in range(length // 128):
                    rows = slice(n * 128, (n + 1) * 128)
                    total = None
                    for side in range(2):
                        head = (2 * p + side) // GROUP
                        probs = softmax_rows(q_ref[rows, cols], kk_ref[side, head], bias[rows])
                        term = dot(probs.astype(BF), vv_ref[side, head])
                        total = term if total is None else total + term
                    att_ref[rows, cols] = total.astype(BF)

        attend((0, PAIRS // 2))
        gather_middle(*grads)
        ring_next(0)
        attend((PAIRS // 2, PAIRS))
        for n in range(width // block):
            cols = slice(n * block, (n + 1) * block)
            res_ref[:, cols] = x_ref[:, cols].astype(F32) + dot(
                att_ref[...], front[:, mix + n * block : mix + (n + 1) * block]
            )

        def norm_two(chunk):
            r = res_ref[chunk]
            inv = lax.rsqrt(jnp.mean(r * r, axis=1, keepdims=True) + EPSILON)
            n2_ref[chunk] = (r * inv * gain_ref[1:2, :]).astype(BF)

        row_loop(length, 64, norm_two)
        gather_last(*grads)
        while ring[0][0] < planes:
            ring_next(0)
        for copy in grads[1]["core"] + second_exchange:
            copy.wait_recv()
        for copy in locals_ + [front_copy, cot_copy]:
            copy.wait()
        at.finish()

    shape = jax.ShapeDtypeStruct
    count = planes - 1 + planes * 11 + 2 * 3 + 4 + planes - 2 + 13
    return pl.pallas_call(
        kernel,
        out_shape=[
            shape((width, 2 * half), BF),
            shape((planes, 4, ds, wide), BF),
            shape((planes, 4, ds, wide), BF),
            shape((PLANE, length, width), BF),
            shape((8, width), F32),
            shape((length, width), BF),
            shape((2, KV_HEADS, length, LANES), BF),
            shape((2, KV_HEADS, length, LANES), BF),
            shape((length, width), BF),
            shape((length, width), F32),
            shape((length, width), BF),
            shape((length, width), BF),
        ],
        in_specs=[pl.BlockSpec(memory_space=pltpu.SMEM)]
        + [whole_vmem()] * 3
        + [anywhere()] * 3
        + [whole_vmem()],
        out_specs=[anywhere()] * 4 + [whole_vmem()] * 8,
        scratch_shapes=[
            pltpu.VMEM((width, 2 * half), BF),
            pltpu.VMEM((length, length), F32),
            pltpu.VMEM((4, EPD, ds, wide), BF),
            pltpu.VMEM((2, 2, ds, hid), F32),
            pltpu.VMEM((2, hs, width), F32),
        ]
        + dma_pairs(count)
        + [pltpu.SemaphoreType.DMA((5,)), pltpu.SemaphoreType.DMA((2, 3))],
        compiler_params=comm_params(0),
        cost_estimate=pl.CostEstimate(
            flops=150_000_000_000, bytes_accessed=20_000_000, transcendentals=0
        ),
    )(starts, tokens, cotangent, own, w_gate, w_up, w_down, tables)


class PlaneSum:
    def __init__(self, at, length, odd, even, from_core, far, near):
        self.at, self.odd, self.even, self.core = at, odd, even, from_core
        self.far, self.near = far, near
        self.length = length
        self.half = self.length // 2
        self.low, self.high = pl.ds(0, self.half), pl.ds(self.half, self.half)
        self.arrive = {
            j: at.make(odd(j), self.part(j, pl.ds(0, length)), at.core) for j in (3, 2, 1, 0)
        }
        low, high = self.low, self.high
        self.far_y = at.make(self.part(3, low), far.at[0], at.y)
        self.far_x = at.make(self.part(3, high), far.at[1], at.x)
        self.x_high = at.make(self.part(2, high), near.at[0, high], at.x)
        self.y_low = at.make(self.part(1, low), near.at[1, low], at.y)
        self.x_low = at.make(self.part(2, low), near.at[0, low], at.x)
        self.y_high = at.make(self.part(1, high), near.at[1, high], at.y)

    def rows(self, j, chunk, base=0):
        return pl.ds(pl.multiple_of(chunk.start + j * self.length + base, 16), chunk.size)

    def part(self, j, rows):
        return self.core.at[pl.ds(j * self.length + rows.start, rows.size)]

    def start(self, j):
        self.arrive[j].start()

    def add_core(self, j):
        self.arrive[j].wait_recv()
        core = self.core

        def store(chunk, total):
            core[self.rows(j, chunk)] = total.astype(BF)

        add_rows(store, [lambda q: self.even(j, q), lambda q: core[self.rows(j, q)]], self.length)

    def add_far(self, j, n, base):
        core, far = self.core, self.far

        def store(chunk, total):
            core[self.rows(j, chunk, base)] = total.astype(BF)

        add_rows(store, [lambda q: core[self.rows(j, q, base)], lambda q: far[n, q]], self.half)

    def send_far(self):
        self.add_core(3)
        self.far_y.start()
        self.far_x.start()

    def send_x(self):
        self.add_core(2)
        self.x_high.start()

    def send_y(self):
        self.add_core(1)
        self.y_low.start()

    def onward_x(self):
        self.far_y.wait_recv()
        self.add_far(2, 0, 0)
        self.x_low.start()

    def onward_y(self):
        self.far_x.wait_recv()
        self.add_far(1, 1, self.half)
        self.y_high.start()

    def end(self, store):
        self.arrive[0].wait_recv()
        for copy in (self.x_high, self.y_low, self.x_low, self.y_high):
            copy.wait_recv()
        core, near = self.core, self.near
        terms = [lambda q: self.even(0, q), lambda q: core[q]]
        terms += [lambda q: near[0, q], lambda q: near[1, q]]
        add_rows(store, terms, self.length)

    copies = 10


class RingSum:
    def __init__(self, at, pack, own, own_sem):
        self.at, self.pack, self.own, self.own_sem = at, pack, own, own_sem
        self.index = [(at.z + at.planes - k) % at.planes for k in range(at.planes)]

    def block(self, k):
        return self.pack.at[self.index[k]]

    def fetch(self, k):
        self.fetched = pltpu.make_async_copy(self.block(k), self.own, self.own_sem)
        self.fetched.start()

    def add(self, source, target):
        self.fetched.wait()

        def store(chunk, total):
            target[chunk] = total.astype(BF)

        add_rows(store, [lambda q: source[q], lambda q: self.own[q]], self.own.shape[0], 16)

    def first(self, slots):
        self.slots, self.step = slots, 1
        sources = [self.block(1)] + slots[:-1]
        self.sent = [
            self.at.make(src, dst, self.at.along[1]) for src, dst in zip(sources, slots)
        ]
        self.fetches = {
            k: pltpu.make_async_copy(self.block(k), self.own, self.own_sem)
            for k in range(2, len(slots) + 1)
        }
        self.sent[0].start()
        self.begin_fetch(2)

    def begin_fetch(self, k):
        if k in self.fetches:
            self.fetched = self.fetches[k]
            self.fetched.start()

    def next(self):
        if self.step < len(self.slots):
            here = self.slots[self.step - 1]
            self.sent[self.step - 1].wait_recv()
            self.add(here, here)
            self.sent[self.step].start()
            self.step += 1
            self.begin_fetch(self.step + 1)

    def rest(self):
        while self.step < len(self.slots):
            self.next()
        self.sent[-1].wait_recv()

    def last(self, before, sent, landing):
        self.add(before, sent)
        self.landing = landing
        self.copy = self.at.send(sent, landing, self.at.along[1])
        self.fetch(0)

    def total(self):
        self.copy.wait_recv()
        self.add(self.landing, self.landing)
        return self.landing


def run_experts(tokens, grads, shares, wall_a, wall_b, planes, group):
    pairs, count, width = grads.shape
    length = count // 2
    piece, wide = wall_a.shape[1:]
    hid = wide // 3
    ds, hs, blocks = width // group, hid // group, width // hid
    half = length // 2
    low, high, full = pl.ds(0, half), pl.ds(half, half), pl.ds(0, length)

    def kernel(
        n2_hbm,
        g_hbm,
        share_ref,
        wall_a_ref,
        wall_b_ref,
        out_hbm,
        pack_a,
        pack_b,
        sum_ref,
        passed,
        xs,
        dxs,
        w_a,
        w_b,
        down_a,
        down_b,
        in_sum,
        down_sum,
        g_tile,
        o_tile,
        pre,
        act,
        far,
        near,
        ring_slots,
        own,
        free,
        send_sems,
        recv_sems,
        local_sems,
    ):
        at = Links(planes, group, send_sems, recv_sems)
        at.barrier([at.x, at.y, at.core] + at.along[1:])
        index = [(at.z + planes - k) % planes for k in range(planes)]

        def local(src, dst, n):
            copy = pltpu.make_async_copy(src, dst, local_sems.at[n])
            copy.start()
            return copy

        def slot(j, rows=full):
            return xs.at[j // 2, pl.ds(j % 2 * length + rows.start, rows.size)]

        pieces = [
            w_b.at[pl.ds(pl.multiple_of(index[k] * piece, 16), piece)] for k in range(planes)
        ]

        local(n2_hbm, slot(0), 0).wait()
        x_low = at.send(slot(0, low), slot(4, low), at.x)
        y_high = at.send(slot(0, high), slot(2, high), at.y)
        x_high = at.send(slot(0, high), slot(4, high), at.x)
        y_low = at.send(slot(0, low), slot(2, low), at.y)
        near_core = at.send(slot(0), slot(1), at.core)
        ring = [at.make(wall_b_ref.at[at.z], pieces[0], at.along[1])]
        ring += [at.make(piece_ref, piece_ref, at.along[1]) for piece_ref in pieces[1:-1]]
        ring[0].start()
        load_b = local(wall_b_ref.at[at.z], pieces[0], 1)
        loads = [
            local(wall_a_ref.at[n], w_a.at[pl.ds(n * piece, piece)], 2 + n) for n in range(planes)
        ]
        state = {"ring": 0}
        far_low = at.make(slot(4, low), slot(6, low), at.y)
        far_high = at.make(slot(2, high), slot(6, high), at.x)
        passed_on = {
            (j, rows.start): at.make(slot(j, rows), slot(j + 1, rows), at.core)
            for j in (4, 2, 6)
            for rows in (low, high)
        }

        def ring_next():
            ring[state["ring"]].wait_recv()
            state["ring"] += 1
            if state["ring"] < planes - 1:
                ring[state["ring"]].start()

        def core_arrival(j):
            passed_on[j, low.start].wait_recv()
            passed_on[j, high.start].wait_recv()

        def spread():
            x_low.wait_recv()
            far_low.start()
            passed_on[4, low.start].start()
            y_high.wait_recv()
            far_high.start()
            passed_on[2, high.start].start()
            x_high.wait_recv()
            passed_on[4, high.start].start()
            y_low.wait_recv()
            passed_on[2, low.start].start()
            core_arrival(4)

        def spread_far():
            far_low.wait_recv()
            passed_on[6, low.start].start()
            far_high.wait_recv()
            passed_on[6, high.start].start()
            core_arrival(6)

        def unpack_down(w, down):
            for s in range(group):
                for b in range(blocks):
                    down[s * hs : (s + 1) * hs, b * hid : (b + 1) * hid] = w[
                        s * ds + b * hs : s * ds + (b + 1) * hs, 2 * hid :
                    ]

        def clear():
            def body(chunk):
                in_sum[chunk] = jnp.zeros((chunk.size, 2 * hid), F32)

            row_loop(width, 64, body)

            def body_down(chunk):
                down_sum[chunk] = jnp.zeros((chunk.size, width), F32)

            row_loop(hid, 64, body_down)

        def out_copy(pair):
            return pltpu.make_async_copy(o_tile, out_hbm.at[pair], local_sems.at[0])

        def tile(e, step, pair, w, down, middle):
            g_load = pltpu.make_async_copy(g_hbm.at[pair], g_tile, local_sems.at[1])
            g_load.start()
            x = xs.at[pair]
            share = share_ref[pair].T[:, e : e + 1]
            part = hid // 2
            for n in range(2):
                cols = slice(n * part, (n + 1) * part)
                up_cols = slice(hid + n * part, hid + (n + 1) * part)
                gate = dot(x[...], w[:, cols])
                up = dot(x[...], w[:, up_cols])
                if n == 0:
                    g_load.wait()
                inner = dot_nt(g_tile[...], down[cols, :]) * share
                sig = jax.nn.sigmoid(gate)
                swish = gate * sig
                act[:, cols] = (share * (swish * up)).astype(BF)
                pre[:, cols] = (inner * up * sig * (1.0 + gate * (1.0 - sig))).astype(BF)
                pre[:, up_cols] = (inner * swish).astype(BF)
            middle()

            @pl.when(step > 0)
            def _():
                out_copy(pair).wait()

            if e > 0:
                before = pltpu.make_async_copy(out_hbm.at[pair], o_tile, local_sems.at[2])
                before.start()
                before.wait()
            for n in range(width // hid):
                cols = slice(n * hid, (n + 1) * hid)
                out = dot(act[...], down[:, cols])
                dx = dot_nt(pre[...], w[cols, : 2 * hid])
                if e > 0:
                    out = out + o_tile[:, cols].astype(F32)
                    dx = dx + dxs[pair, :, cols].astype(F32)
                o_tile[:, cols] = out.astype(BF)
                dxs[pair, :, cols] = dx.astype(BF)
                in_sum[cols, :] += dot_tn(x[:, cols], pre[...])
                down_sum[:, cols] += dot_tn(act[...], g_tile[:, cols])
            out_copy(pair).start()

        def pack(target):
            out_copy(0).wait()
            copies = [None, None]
            for n in range(planes):
                base = n % 2 * piece
                if copies[n % 2] is not None:
                    copies[n % 2].wait()

                def body(chunk, n=n, base=base):
                    rows = pl.ds(pl.multiple_of(chunk.start + base, 16), chunk.size)
                    source = pl.ds(pl.multiple_of(chunk.start + n * piece, 16), chunk.size)
                    o_tile[rows, : 2 * hid] = in_sum[source].astype(BF)

                row_loop(piece, 32, body)
                for s in range(4):
                    for b in range(blocks):
                        row = base + s * ds + b * hs
                        o_tile[row : row + hs, 2 * hid :] = down_sum[
                            (n * 4 + s) * hs : (n * 4 + s + 1) * hs, b * hid : (b + 1) * hid
                        ].astype(BF)
                copies[n % 2] = local(o_tile.at[pl.ds(base, piece)], target.at[n], 3 + n % 2)
            for copy in copies:
                copy.wait()

        clear()
        for copy in loads:
            copy.wait()
        load_b.wait()
        unpack_down(w_a, down_a)
        near_core.wait_recv()

        @pl.loop(0, pairs)
        def _(step):
            @pl.when(step == 1)
            def _():
                spread()
                ring_next()

            @pl.when(step == 2)
            def _():
                core_arrival(2)

            @pl.when(step == 3)
            def _():
                spread_far()
                ring_next()

            tile(0, step, 2 * step % 3 + step // 3 * 3, w_a, down_a, lambda: None)

        pl.semaphore_signal(free, inc=1, device_id=at.core, device_id_type=pl.DeviceIdType.MESH)
        pack(pack_a)
        sums = RingSum(at, pack_a, own, local_sems.at[5])
        sums.first([ring_slots.at[n] for n in range(planes - 3)] + [passed])
        clear()
        while state["ring"] < planes - 1:
            ring_next()
        unpack_down(w_b, down_b)
        pl.semaphore_wait(free, 1)
        plane = PlaneSum(
            at,
            length,
            lambda j: dxs.at[j, pl.ds(length, length)],
            lambda j, q: dxs[j, q],
            w_a,
            far,
            near,
        )

        @pl.loop(0, pairs)
        def _(step):
            def middle():
                @pl.when(step == 1)
                def _():
                    plane.send_far()

                @pl.when(step == 2)
                def _():
                    plane.send_x()
                    sums.next()

                @pl.when(step == 3)
                def _():
                    plane.send_y()
                    plane.onward_y()

            tile(1, step, pairs - 1 - step, w_b, down_b, middle)
            for n in range(pairs):

                @pl.when(step == n)
                def _(n=n):
                    plane.start(pairs - 1 - n)
                    if n == 2:
                        plane.onward_x()

        pack(pack_b)

        def store(chunk, total):
            sum_ref[chunk] = total

        plane.end(store)
        sums.rest()
        at.finish()

    shape = jax.ShapeDtypeStruct
    return pl.pallas_call(
        kernel,
        in_specs=[anywhere()] * 2 + [whole_vmem()] + [anywhere()] * 2,
        out_specs=[anywhere()] * 3 + [whole_vmem()] * 2,
        out_shape=[
            shape((pairs, count, width), BF),
            shape((planes, piece, wide), BF),
            shape((planes, piece, wide), BF),
            shape((length, width), F32),
            shape((piece, wide), BF),
        ],
        scratch_shapes=[
            pltpu.VMEM((pairs, count, width), BF),
            pltpu.VMEM((pairs, count, width), BF),
            pltpu.VMEM((width, wide), BF),
            pltpu.VMEM((width, wide), BF),
            pltpu.VMEM((hid, width), BF),
            pltpu.VMEM((hid, width), BF),
            pltpu.VMEM((width, 2 * hid), F32),
            pltpu.VMEM((hid, width), F32),
            pltpu.VMEM((count, width), BF),
            pltpu.VMEM((count, width), BF),
            pltpu.VMEM((count, 2 * hid), BF),
            pltpu.VMEM((count, hid), BF),
            pltpu.VMEM((2, half, width), BF),
            pltpu.VMEM((2, length, width), BF),
            pltpu.VMEM((planes - 3, piece, wide), BF),
            pltpu.VMEM((piece, wide), BF),
            pltpu.SemaphoreType.REGULAR,
        ]
        + dma_pairs(13 + planes - 1 + PlaneSum.copies + planes - 2)
        + [pltpu.SemaphoreType.DMA((2 + planes,))],
        compiler_params=pltpu.CompilerParams(
            collective_id=2, has_side_effects=True, vmem_limit_bytes=63 * 2**20
        ),
        cost_estimate=pl.CostEstimate(
            flops=100_000_000_000, bytes_accessed=50_000_000, transcendentals=0
        ),
    )(tokens, grads, shares, wall_a, wall_b)


class Exchange:
    def __init__(self, at, total, out, ds):
        self.at, self.total, self.out, self.ds = at, total, out, ds
        self.shard = at.yb * 2 + at.c

    def place(self, dx, dy, dc):
        at = self.at
        return (at.xb + dx) % 2 * 4 + (at.yb + dy) % 2 * 2 + (at.c + dc) % 2

    def rows(self, dy, dc):
        at = self.at
        shard = (at.yb + dy) % 2 * 2 + (at.c + dc) % 2
        return self.total.at[pl.ds(pl.multiple_of(shard * self.ds, 16), self.ds)]

    def start(self, sem):
        at = self.at
        here = self.out.at[self.place(0, 0, 0)]
        self.local = pltpu.make_async_copy(self.rows(0, 0), here, sem)
        self.local.start()
        self.got = [
            (dy, dc, at.send(self.rows(dy, dc), here, device))
            for dy, dc, device in ((1, 0, at.y), (1, 1, at.diagonal), (0, 1, at.core))
        ]
        self.across = [at.send(self.rows(0, 0), here, at.x)]

    def onward(self):
        at = self.at
        for dy, dc, copy in self.got:
            copy.wait_recv()
            piece = self.out.at[self.place(0, dy, dc)]
            self.across.append(at.send(piece, piece, at.x))

    def end(self):
        for copy in self.across:
            copy.wait_recv()
        self.local.wait()

    copies = 7


def backward(
    starts,
    grad_two,
    cotangent,
    tokens,
    residual,
    front,
    gains,
    q,
    kk,
    vv,
    att,
    n1,
    outs,
    pack_a,
    before_a,
    pack_b,
    planes,
    group,
):
    length, width = tokens.shape
    columns = front.shape[1]
    kvd = KV_HEADS * HEAD
    mix = width + 2 * kvd
    block = 4 * LANES
    tables = turn_tables(length)
    piece, wide = pack_a.shape[1:]
    ds = piece // 4
    extra = columns - mix - width

    def kernel(
        starts_ref,
        d_ref,
        cot_ref,
        tab_ref,
        gain_ref,
        q_ref,
        kk_ref,
        vv_ref,
        att_ref,
        before_ref,
        x_hbm,
        n1_hbm,
        res_hbm,
        w_hbm,
        outs_ref,
        pack_a_ref,
        pack_b_ref,
        in_ref,
        sum_ref,
        passed_b,
        grad_hbm,
        shards_ref,
        bias,
        gain_sum,
        mixed,
        context,
        grad_mix,
        key_sum,
        value_sum,
        w_ref,
        stage,
        even,
        from_core,
        far,
        near,
        own_a,
        sent_a,
        landing_a,
        own_b,
        slots_b,
        send_sems,
        recv_sems,
        local_sems,
    ):
        at = Links(planes, group, send_sems, recv_sems)
        at.barrier([at.x, at.y, at.core, at.diagonal] + at.along[1:])

        def local(src, dst, n):
            copy = pltpu.make_async_copy(src, dst, local_sems.at[n])
            copy.start()
            return copy

        load_res = local(res_hbm, in_ref, 0)
        load_out_w = local(
            w_hbm.at[:, pl.ds(mix, width)], w_ref.at[:, pl.ds(0, width)], 1
        )
        plane = PlaneSum(
            at,
            length,
            lambda j: outs_ref.at[2 * j + 1],
            lambda j, q: even[j, q],
            from_core,
            far,
            near,
        )
        for j in (3, 2, 1, 0):
            plane.start(j)
        ring_a = RingSum(at, pack_a_ref, own_a, local_sems.at[6])
        ring_b = RingSum(at, pack_b_ref, own_b, local_sems.at[7])
        ring_a.fetch(planes - 1)
        loads = [local(outs_ref.at[2 * j], even.at[j], 2 + j) for j in range(4)]
        ring_a.last(before_ref, sent_a, landing_a)
        ring_b.first([slots_b.at[n] for n in range(planes - 3)] + [passed_b])
        staged = [None, None]
        turn = [0]

        def put(values, column, count):
            n = turn[0] % 2
            turn[0] += 1
            if staged[n] is not None:
                staged[n].wait()
            stage[n, :, :count] = values
            staged[n] = local(
                stage.at[n, :, pl.ds(0, count)], grad_hbm.at[:, pl.ds(column, count)], 8 + n
            )

        fill_bias(bias, starts_ref[0])
        gain_sum[...] = jnp.zeros_like(gain_sum)

        load_res.wait()

        def residual_grad(chunk):
            d, r = d_ref[chunk], in_ref[chunk]
            inv = lax.rsqrt(jnp.mean(r * r, axis=1, keepdims=True) + EPSILON)
            scaled = d * gain_ref[1:2, :]
            grad = (
                cot_ref[chunk].astype(F32)
                + inv * scaled
                - r * (inv * inv * inv * jnp.mean(scaled * r, axis=1, keepdims=True))
            )
            sum_ref[chunk] = grad
            mixed[chunk] = grad.astype(BF)
            gain_sum[1:2, :] += jnp.sum(d * r * inv, axis=0, keepdims=True)

        row_loop(length, 32, residual_grad)
        load_out_w.wait()
        for n in range(width // block):
            cols = slice(n * block, (n + 1) * block)
            context[:, cols] = dot_nt(mixed[...], w_ref[cols, :width]).astype(BF)
        load_mix_w = local(w_hbm.at[:, pl.ds(0, mix)], w_ref, 1)
        for n in range(width // block):
            cols = slice(n * block, (n + 1) * block)
            put(dot_tn(att_ref[...], mixed[:, cols]).astype(BF), mix + n * block, block)
        load_n1 = local(n1_hbm, mixed, 0)
        for copy in loads:
            copy.wait()
        plane.send_far()
        plane.send_x()
        plane.send_y()
        key_sum[...] = jnp.zeros_like(key_sum)
        value_sum[...] = jnp.zeros_like(value_sum)

        def attend(lower, upper):
            @pl.loop(lower, upper)
            def _(p):
                cols = pl.ds(pl.multiple_of(p * LANES, LANES), LANES)
                for n in range(length // 128):
                    rows = slice(n * 128, (n + 1) * 128)
                    total = None
                    for side in range(2):
                        head = (2 * p + side) // GROUP
                        query, grad = q_ref[rows, cols], context[rows, cols]
                        probs = softmax_rows(query, kk_ref[side, head], bias[rows])
                        grad_probs = dot_nt(grad, vv_ref[side, head])
                        value_sum[side, head] += dot_tn(probs.astype(BF), grad)
                        inner = jnp.sum(probs * grad_probs, axis=1, keepdims=True)
                        logit = (probs * (grad_probs - inner)).astype(BF)
                        term = dot(logit, kk_ref[side, head])
                        total = term if total is None else total + term
                        key_sum[side, head] += dot_tn(logit, query)
                    back = turned(total, tab_ref.at[:, rows], -1.0) * (1.0 / math.sqrt(HEAD))
                    grad_mix[rows, cols] = back.astype(BF)

        attend(0, PAIRS // 3)
        plane.onward_x()
        plane.onward_y()
        exchange = Exchange(at, ring_a.total(), shards_ref, ds)
        exchange.start(local_sems.at[10])
        attend(PAIRS // 3, 2 * PAIRS // 3)
        ring_b.next()
        exchange.onward()
        attend(2 * PAIRS // 3, PAIRS)
        load_x = local(x_hbm, context, 11)
        load_n1.wait()
        for pair in range(KV_HEADS // 2):
            for sums, base in ((key_sum, width), (value_sum, width + kvd)):

                def join(chunk, pair=pair, sums=sums, base=base):
                    low = lax.broadcasted_iota(jnp.int32, (chunk.size, LANES), 1) < HEAD
                    even = sums[0, 2 * pair, chunk] + pltpu.roll(sums[1, 2 * pair, chunk], HEAD, 1)
                    odd = sums[1, 2 * pair + 1, chunk] + pltpu.roll(
                        sums[0, 2 * pair + 1, chunk], HEAD, 1
                    )
                    values = jnp.where(low, even, odd)
                    if base == width:
                        values = turned(values, tab_ref.at[:, chunk], -1.0)
                    grad_mix[chunk, base + pair * LANES : base + (pair + 1) * LANES] = values.astype(BF)

                row_loop(length, 64, join)
        for n in range(mix // block):
            cols = slice(n * block, (n + 1) * block)
            put(dot_tn(mixed[...], grad_mix[:, cols]).astype(BF), n * block, block)
        load_mix_w.wait()
        for n in range(width // block):
            cols = slice(n * block, (n + 1) * block)
            in_ref[:, cols] = dot_nt(grad_mix[...], w_ref[cols, :mix])

        load_x.wait()

        def input_grad(chunk):
            d, x = in_ref[chunk], context[chunk].astype(F32)
            inv = lax.rsqrt(jnp.mean(x * x, axis=1, keepdims=True) + EPSILON)
            scaled = d * gain_ref[0:1, :]
            gain_sum[0:1, :] += jnp.sum(d * x * inv, axis=0, keepdims=True)
            in_ref[chunk] = (
                sum_ref[chunk]
                + inv * scaled
                - x * (inv * inv * inv * jnp.mean(scaled * x, axis=1, keepdims=True))
            )

        row_loop(length, 32, input_grad)
        gain_rows = jnp.concatenate([gain_sum[...].T, jnp.zeros((width, extra - 8), F32)], axis=1)
        put(gain_rows.astype(BF), mix + width, extra)

        def store(chunk, total):
            sum_ref[chunk] = total

        plane.end(store)
        ring_b.rest()
        exchange.end()
        for copy in staged:
            copy.wait()
        at.finish()

    shape = jax.ShapeDtypeStruct
    return pl.pallas_call(
        kernel,
        in_specs=[pl.BlockSpec(memory_space=pltpu.SMEM)]
        + [whole_vmem()] * 9
        + [anywhere()] * 7,
        out_specs=[whole_vmem()] * 3 + [anywhere()] * 2,
        out_shape=[
            shape((length, width), F32),
            shape((length, width), F32),
            shape((piece, wide), BF),
            shape((width, columns), BF),
            shape((PLANE, ds, wide), BF),
        ],
        scratch_shapes=[
            pltpu.VMEM((length, length), F32),
            pltpu.VMEM((8, width), F32),
            pltpu.VMEM((length, width), BF),
            pltpu.VMEM((length, width), BF),
            pltpu.VMEM((length, mix), BF),
            pltpu.VMEM((2, KV_HEADS, length, LANES), F32),
            pltpu.VMEM((2, KV_HEADS, length, LANES), F32),
            pltpu.VMEM((width, mix), BF),
            pltpu.VMEM((2, width, block), BF),
            pltpu.VMEM((4, length, width), BF),
            pltpu.VMEM((4 * length, width), BF),
            pltpu.VMEM((2, length // 2, width), BF),
            pltpu.VMEM((2, length, width), BF),
            pltpu.VMEM((piece, wide), BF),
            pltpu.VMEM((piece, wide), BF),
            pltpu.VMEM((piece, wide), BF),
            pltpu.VMEM((piece, wide), BF),
            pltpu.VMEM((planes - 3, piece, wide), BF),
        ]
        + dma_pairs(PlaneSum.copies + 1 + Exchange.copies + planes - 2)
        + [pltpu.SemaphoreType.DMA((12,))],
        compiler_params=pltpu.CompilerParams(
            collective_id=1, has_side_effects=True, vmem_limit_bytes=62 * 2**20
        ),
        cost_estimate=pl.CostEstimate(
            flops=80_000_000_000, bytes_accessed=50_000_000, transcendentals=0
        ),
    )(
        starts,
        grad_two,
        cotangent,
        tables,
        gains,
        q,
        kk,
        vv,
        att,
        before_a,
        tokens,
        n1,
        residual,
        front,
        outs,
        pack_a,
        pack_b,
    )


def scatter_front(grad, pack, before, planes, group):
    rows, columns = grad.shape
    ds, half = rows // (4 * planes), columns // 2
    part = share_of(half, 0.6)
    first, second = pl.ds(0, part), pl.ds(part, half - part)
    block, wide = pack.shape[1:]

    def kernel(
        g_ref,
        pack_ref,
        before_ref,
        out_ref,
        shards_ref,
        from_core,
        kept,
        far_a,
        far_b,
        near_x,
        near_y,
        total_ref,
        from_z,
        own,
        passed,
        landing,
        send_sems,
        recv_sems,
        local_sems,
    ):
        at = Links(planes, group, send_sems, recv_sems)
        at.barrier([at.x, at.y, at.core, at.diagonal] + at.along[1:])
        ring = RingSum(at, pack_ref, own, local_sems.at[0])
        ring.fetch(planes - 1)

        def row(k, dy, core):
            owner = ((at.z + k) % planes) * 4 + (at.yb + dy) % 2 * 2 + core
            return pl.multiple_of(owner * ds, 16)

        def column(dx):
            return pl.ds(pl.multiple_of((at.xb + dx) % 2 * half, 128), half)

        order = list(range(1, planes)) + [0]
        arrive = {}
        for k in order:
            for dy in (1, 0):
                arrive[k, dy] = at.send(
                    g_ref.at[pl.ds(row(k, dy, 1 - at.c), ds)], from_core.at[k, dy], at.core
                )
        ring.last(before_ref, passed, landing)
        step = 16
        x_second, y_first, x_first, y_second, to_x, to_y = {}, {}, {}, {}, {}, {}
        for k in order:
            for dy in (1, 0):
                arrive[k, dy].wait_recv()
                for dx in (1, 0):

                    def store(chunk, total, k=k, dx=dx, dy=dy):
                        kept[k, dx, dy, chunk] = total.astype(BF)

                    add_rows(
                        store,
                        [
                            lambda q, k=k, dx=dx, dy=dy: g_ref[
                                pl.ds(pl.multiple_of(row(k, dy, at.c) + q.start, 16), q.size),
                                column(dx),
                            ],
                            lambda q, k=k, dx=dx, dy=dy: from_core[k, dy, q, column(dx)],
                        ],
                        ds,
                        step,
                    )
                    if (dx, dy) == (1, 1):
                        to_y[k] = at.send(kept.at[k, 1, 1, :, first], far_a.at[k], at.y)
                        to_x[k] = at.send(kept.at[k, 1, 1, :, second], far_b.at[k], at.x)
                    elif (dx, dy) == (0, 1):
                        y_first[k] = at.send(
                            kept.at[k, 0, 1, :, first], near_y.at[k, :, first], at.y
                        )
                    elif (dx, dy) == (1, 0):
                        x_second[k] = at.send(
                            kept.at[k, 1, 0, :, second], near_x.at[k, :, second], at.x
                        )
        for k in order:
            to_y[k].wait_recv()

            def store(chunk, total, k=k):
                kept[k, 1, 0, chunk, first] = total.astype(BF)

            add_rows(
                store,
                [lambda q, k=k: kept[k, 1, 0, q, first], lambda q, k=k: far_a[k, q]],
                ds,
                step,
            )
            x_first[k] = at.send(kept.at[k, 1, 0, :, first], near_x.at[k, :, first], at.x)
            to_x[k].wait_recv()

            def store(chunk, total, k=k):
                kept[k, 0, 1, chunk, second] = total.astype(BF)

            add_rows(
                store,
                [lambda q, k=k: kept[k, 0, 1, q, second], lambda q, k=k: far_b[k, q]],
                ds,
                step,
            )
            y_second[k] = at.send(kept.at[k, 0, 1, :, second], near_y.at[k, :, second], at.y)
        exchange = Exchange(at, ring.total(), shards_ref, ds)
        exchange.start(local_sems.at[1])
        arrive_z = {}
        for k in order:
            for copies in (x_second, y_first, x_first, y_second):
                copies[k].wait_recv()

            def store(chunk, total, k=k):
                total_ref[k, chunk] = total.astype(BF)

            add_rows(
                store,
                [
                    lambda q, k=k: kept[k, 0, 0, q],
                    lambda q, k=k: near_x[k, q],
                    lambda q, k=k: near_y[k, q],
                ],
                ds,
                step,
            )
            if k > 0:
                arrive_z[k] = at.send(total_ref.at[k], from_z.at[k], at.along[k])
        exchange.onward()
        for k in range(1, planes):
            arrive_z[k].wait_recv()

        def store(chunk, total):
            out_ref[chunk] = total.astype(BF)

        add_rows(
            store,
            [lambda q: total_ref[0, q]]
            + [lambda q, k=k: from_z[k, q] for k in range(1, planes)],
            ds,
            step,
        )
        exchange.end()
        at.finish()

    return pl.pallas_call(
        kernel,
        out_shape=[
            jax.ShapeDtypeStruct((ds, half), BF),
            jax.ShapeDtypeStruct((PLANE, ds, wide), BF),
        ],
        in_specs=[whole_vmem(), anywhere(), whole_vmem()],
        out_specs=[whole_vmem(), anywhere()],
        scratch_shapes=[
            pltpu.VMEM((planes, 2, ds, columns), BF),
            pltpu.VMEM((planes, 2, 2, ds, half), BF),
            pltpu.VMEM((planes, ds, part), BF),
            pltpu.VMEM((planes, ds, half - part), BF),
            pltpu.VMEM((planes, ds, half), BF),
            pltpu.VMEM((planes, ds, half), BF),
            pltpu.VMEM((planes, ds, half), BF),
            pltpu.VMEM((planes, ds, half), BF),
            pltpu.VMEM((block, wide), BF),
            pltpu.VMEM((block, wide), BF),
            pltpu.VMEM((block, wide), BF),
        ]
        + dma_pairs(planes * 8 + planes - 1 + 1 + Exchange.copies)
        + [pltpu.SemaphoreType.DMA((2,))],
        compiler_params=comm_params(3),
        cost_estimate=pl.CostEstimate(
            flops=50_000_000_000, bytes_accessed=20_000_000, transcendentals=0
        ),
    )(grad, pack, before)


def unpack(packs, hs):
    ds, wide = packs[0].shape[1:]
    hid = wide // 3
    blocks = ds // hs

    def kernel(*refs):
        ins, (gate_out, up_out, down_out, raw_in, raw_down, sems) = refs[:EPD], refs[EPD:]
        copies = {}
        for n, (p, e) in enumerate((p, e) for p in range(PLANE) for e in range(EPD)):
            slot = n % 4
            if n >= 4:
                for copy in copies[n - 4]:
                    copy.wait()

            def cast(chunk, p=p, e=e, slot=slot):
                raw_in[slot, 0, chunk] = ins[e][p, chunk, :hid].astype(F32)
                raw_in[slot, 1, chunk] = ins[e][p, chunk, hid : 2 * hid].astype(F32)

            row_loop(ds, 16, cast)
            for b in range(blocks):
                raw_down[slot, :, b * hid : (b + 1) * hid] = ins[e][
                    p, b * hs : (b + 1) * hs, 2 * hid :
                ].astype(F32)
            index = p * EPD + e
            copies[n] = [
                pltpu.make_async_copy(src, dst, sems.at[slot, i])
                for i, (src, dst) in enumerate(
                    (
                        (raw_in.at[slot, 0], gate_out.at[:, index]),
                        (raw_in.at[slot, 1], up_out.at[:, index]),
                        (raw_down.at[slot], down_out.at[:, index]),
                    )
                )
            ]
            for copy in copies[n]:
                copy.start()
        for n in range(EXP - 4, EXP):
            for copy in copies[n]:
                copy.wait()

    shape = jax.ShapeDtypeStruct
    return pl.pallas_call(
        kernel,
        in_specs=[whole_vmem()] * EPD,
        out_specs=[anywhere()] * 3,
        out_shape=[
            shape((ds, EXP, hid), F32),
            shape((ds, EXP, hid), F32),
            shape((hs, EXP, blocks * hid), F32),
        ],
        scratch_shapes=[
            pltpu.VMEM((4, 2, ds, hid), F32),
            pltpu.VMEM((4, hs, blocks * hid), F32),
            pltpu.SemaphoreType.DMA((4, 3)),
        ],
        compiler_params=pltpu.CompilerParams(vmem_limit_bytes=32 * 2**20),
    )(*packs)


def shards(
    reps,
    group,
    tokens,
    cotangent,
    routes,
    gates,
    starts,
    norm1_gain,
    w_query,
    w_key,
    w_value,
    w_out,
    norm2_gain,
    w_gate,
    w_up,
    w_down,
):
    planes = group // 4
    r, f = lax.axis_index("rep"), lax.axis_index("fsdp")
    xb, yb, c, z = r % 2, (f // 2) % 2, f % 2, f // 4
    mine = xb * 4 + yb * 2 + c

    def perm(to):
        return [
            (a * group + b, to(a, b)[0] * group + to(a, b)[1])
            for a in range(reps)
            for b in range(group)
        ]

    def pp(value, to):
        return lax.ppermute(value, AXES, perm(to))

    def go(value, dx, dy, dc):
        return pp(value, lambda a, b: (a ^ dx, b ^ (dy * 2 + dc)))

    def along(value, k):
        return pp(value, lambda a, b: (a, (b + 4 * k) % group))

    def all_reps(value):
        step = 2
        while step < reps:
            value = value + pp(value, lambda a, b, s=step: (a ^ s, b))
            step *= 2
        return value

    length, width = tokens.shape
    ds = w_query.shape[0]
    hs = w_down.shape[0]
    hid = w_gate.shape[2]
    kvd = w_key.shape[1]
    half_rows = length // 2

    mix = width + 2 * kvd
    columns = mix + width + 256
    half = columns // 2
    gains = jnp.stack([norm1_gain.astype(BF), norm2_gain.astype(BF)], axis=1)
    front_own = jnp.concatenate(
        [
            w_query.astype(BF),
            w_key.astype(BF),
            w_value.astype(BF),
            w_out.astype(BF),
            gains,
            jnp.zeros((ds, 254), BF),
        ],
        axis=1,
    )
    experts = jnp.arange(EXP, dtype=jnp.int32)[:, None, None]
    share = jnp.sum(jnp.where(routes[None] == experts, gates[None], 0.0), axis=2)
    shares = []
    for j in range(PLANE):
        block = lax.dynamic_slice(share, ((mine ^ j) * EPD, 0), (EPD, length))
        shares.append(block if j == 0 else go(block, j // 4, (j // 2) % 2, j % 2))
    pairs = PLANE // 2
    shares = jnp.concatenate(shares, axis=1).reshape(EPD, pairs, 2 * length).transpose(1, 0, 2)
    shares = jnp.pad(shares, ((0, 0), (0, 8 - EPD), (0, 0)))

    front, wall_a, wall_b, grads_all, gains_all, q, kk, vv, att, residual, n1, n2 = forward(
        starts,
        tokens,
        cotangent,
        lax.dynamic_slice(front_own, (0, xb * half), (ds, half)),
        w_gate,
        w_up,
        w_down,
        planes,
        group,
    )
    out_sum, pack_a, pack_b, grad_normed_two, before_a = run_experts(
        n2,
        grads_all.reshape(pairs, 2 * length, width),
        shares,
        wall_a.reshape(planes, 4 * ds, 3 * hid),
        wall_b.reshape(planes, 4 * ds, 3 * hid),
        planes,
        group,
    )
    input_grad, out_term, before_b, front_grad, shards_a = backward(
        starts,
        grad_normed_two,
        cotangent,
        tokens,
        residual,
        front,
        gains_all,
        q,
        kk,
        vv,
        att,
        n1,
        out_sum.reshape(PLANE, length, width),
        pack_a,
        before_a,
        pack_b,
        planes,
        group,
    )
    output = residual + out_term
    front_total, shards_b = scatter_front(front_grad, pack_b, before_b, planes, group)
    total = all_reps(front_total)
    gate_shard, up_shard, down_shard = unpack([all_reps(shards_a), all_reps(shards_b)], hs)
    other = go(total, 1, 0, 0)
    front_shard = jnp.where(
        xb == 0,
        jnp.concatenate([total, other], axis=1),
        jnp.concatenate([other, total], axis=1),
    ).astype(F32)
    return (
        output,
        input_grad,
        front_shard[:, mix + width],
        front_shard[:, :width],
        front_shard[:, width : width + kvd],
        front_shard[:, width + kvd : mix],
        front_shard[:, mix : mix + width],
        front_shard[:, mix + width + 1],
        gate_shard,
        up_shard,
        down_shard,
    )


def solution(mesh):
    reps, group = mesh.shape["rep"], mesh.shape["fsdp"]
    both, one = P(AXES, None), P("fsdp")
    flat, deep = P("fsdp", None), P("fsdp", None, None)

    def whole(*args):
        return shards(reps, group, *args)

    return jax.shard_map(
        whole,
        mesh=mesh,
        in_specs=(both, both, both, both, P(AXES), one, flat, flat, flat, flat, one, deep, deep, deep),
        out_specs=(both, both, one, flat, flat, flat, flat, one, deep, deep, deep),
        check_vma=False,
    )
```

```python
import math

import jax
import jax.numpy as jnp
from jax import lax
from jax.experimental import pallas as pl
from jax.experimental.pallas import tpu as pltpu
from jax.sharding import PartitionSpec as P

HEADS = 24
KV_HEADS = 8
HEAD = 64
EXP = 16
PIECE = 256
AXES = ("rep", "fsdp")
EPSILON = 1e-05
NEG_FILL = -1e30
BF = jnp.bfloat16
F32 = jnp.float32
PLANE = 8
EPD = EXP // PLANE


def turn_tables(length):
    positions = jnp.arange(length, dtype=F32)[:, None]
    lanes = jnp.arange(2 * HEAD)
    rates = jnp.exp((lanes % (HEAD // 2)).astype(F32) * (-2.0 * math.log(10000.0) / HEAD))
    angles = positions * rates[None, :]
    low = (lanes % HEAD < HEAD // 2)[None, :]
    sines = jnp.sin(angles)
    return jnp.stack([jnp.cos(angles), jnp.where(low, -sines, 0.0), jnp.where(low, 0.0, sines)])


def turned(values, tables, sign):
    ahead = pltpu.roll(values, 2 * HEAD - HEAD // 2, 1)
    back = pltpu.roll(values, HEAD // 2, 1)
    return values * tables[0] + sign * (ahead * tables[1] + back * tables[2])


def row_loop(rows, step, body):
    @pl.loop(0, rows // step)
    def _(n):
        body(pl.ds(pl.multiple_of(n * step, step), step))


def dot(a, b):
    return jnp.dot(a, b, preferred_element_type=F32)


def dot_nt(a, b):
    return lax.dot_general(a, b, (((1,), (1,)), ((), ())), preferred_element_type=F32)


def dot_tn(a, b):
    return lax.dot_general(a, b, (((0,), (0,)), ((), ())), preferred_element_type=F32)


def add_rows(store, terms, rows, step=32):
    step = min(step, rows)

    @pl.loop(0, rows // step)
    def _(n):
        chunk = pl.ds(pl.multiple_of(n * step, 16), step)
        total = terms[0](chunk).astype(F32)
        for term in terms[1:]:
            total = total + term(chunk).astype(F32)
        store(chunk, total)


class Links:
    def __init__(self, planes, group, send_sems, recv_sems):
        r, f = lax.axis_index("rep"), lax.axis_index("fsdp")
        self.xb, self.yb, self.c, self.z = r % 2, (f // 2) % 2, f % 2, f // 4
        self.x = (r + 1 - 2 * self.xb, f)
        self.y = (r, f + 2 - 4 * self.yb)
        self.core = (r, f + 1 - 2 * self.c)
        self.diagonal = (r, f + 3 - 4 * self.yb - 2 * self.c)
        self.others = {1: self.core, 2: self.y, 3: self.diagonal, 4: self.x}
        self.others.update({4 + n: (self.x[0], self.others[n][1]) for n in (1, 2, 3)})
        self.along = [None] + [(r, (f + 4 * k) % group) for k in range(1, planes)]
        self.planes, self.send_sems, self.recv_sems, self.copies = planes, send_sems, recv_sems, []

    def barrier(self, devices):
        semaphore = pltpu.get_barrier_semaphore()
        for device in devices:
            pl.semaphore_signal(
                semaphore, inc=1, device_id=device, device_id_type=pl.DeviceIdType.MESH
            )
        pl.semaphore_wait(semaphore, len(devices))

    def make(self, src, dst, device):
        n = len(self.copies)
        copy = pltpu.make_async_remote_copy(
            src_ref=src,
            dst_ref=dst,
            send_sem=self.send_sems.at[n],
            recv_sem=self.recv_sems.at[n],
            device_id=device,
            device_id_type=pl.DeviceIdType.MESH,
        )
        self.copies.append(copy)
        return copy

    def send(self, src, dst, device):
        copy = self.make(src, dst, device)
        copy.start()
        return copy

    def finish(self):
        for copy in self.copies:
            copy.wait_send()


def comm_params(number):
    return pltpu.CompilerParams(
        collective_id=number, has_side_effects=True, vmem_limit_bytes=56 * 2**20
    )


def dma_pairs(count):
    return [pltpu.SemaphoreType.DMA((count,)), pltpu.SemaphoreType.DMA((count,))]


def whole_vmem():
    return pl.BlockSpec(memory_space=pltpu.VMEM)


def anywhere():
    return pl.BlockSpec(memory_space=pl.ANY)


def share_of(half, share):
    return int(half * share) // 128 * 128


def both_sides(values, store, pair):
    low = lax.broadcasted_iota(jnp.int32, values.shape, 1) < HEAD
    swapped = pltpu.roll(values, HEAD, 1)
    store(0, 2 * pair, jnp.where(low, values, 0.0).astype(BF))
    store(1, 2 * pair, jnp.where(low, 0.0, swapped).astype(BF))
    store(0, 2 * pair + 1, jnp.where(low, swapped, 0.0).astype(BF))
    store(1, 2 * pair + 1, jnp.where(low, 0.0, values).astype(BF))


def fill_bias(bias, start):
    length = bias.shape[0]

    def body(chunk):
        shape = (chunk.size, length)
        i = lax.broadcasted_iota(jnp.int32, shape, 0) + chunk.start
        j = lax.broadcasted_iota(jnp.int32, shape, 1)
        in_i = (i >= start) & (i < start + PIECE)
        in_j = (j >= start) & (j < start + PIECE)
        bias[chunk] = jnp.where((j <= i) | (in_i & in_j), 0.0, NEG_FILL)

    row_loop(length, 64, body)


def softmax_rows(query, key, bias):
    scores = dot_nt(query, key) + bias
    exponent = jnp.exp(scores - jnp.max(scores, axis=1, keepdims=True))
    return exponent * (1.0 / jnp.sum(exponent, axis=1, keepdims=True))


PAIRS = HEADS // 2
GROUP = HEADS // KV_HEADS
LANES = 2 * HEAD


class FrontGather:
    def __init__(self, at, own, full, base, part, own_sem):
        self.at, self.own, self.full, self.base = at, own, full, base
        self.ds, self.half = own.shape
        self.first, self.second = (0, part), (part, self.half - part)
        self.every = (0, self.half)
        self.own_copy = pltpu.make_async_copy(own, self.region(0, 0, 0, self.every), own_sem)
        self.x_first, self.x_second, self.y_first, self.y_second, self.far = [], [], [], [], []

    def region(self, k, dx, dy, span):
        at = self.at
        row = (((at.z + at.planes - k) % at.planes) * 4 + (at.yb + dy) % 2 * 2 + at.c) * self.ds
        col = self.base + (at.xb + dx) % 2 * self.half + span[0]
        return self.full.at[
            pl.ds(pl.multiple_of(row, 16), self.ds), pl.ds(pl.multiple_of(col, 128), span[1])
        ]

    def pass_on(self, k, dx, dy, span, device):
        here = self.region(k, dx, dy, span)
        return self.at.send(here, here, device)

    def start(self):
        at = self.at
        self.own_copy.start()
        here = self.region(0, 0, 0, self.every)
        self.arrive = [None] + [at.send(self.own, here, at.along[k]) for k in range(1, at.planes)]

    def start_plane(self):
        here = self.region(0, 0, 0, self.every)
        self.to_core = [self.at.send(self.own, here, self.at.core)]
        self.spread(0)

    def spread(self, k):
        at = self.at
        for device, span, copies in (
            (at.x, self.first, self.x_first),
            (at.y, self.second, self.y_second),
            (at.x, self.second, self.x_second),
            (at.y, self.first, self.y_first),
        ):
            here = self.region(k, 0, 0, span)
            src = self.own.at[:, pl.ds(span[0], span[1])] if k == 0 else here
            copies.append(at.send(src, here, device))
        if k > 0:
            self.to_core.append(self.pass_on(k, 0, 0, self.every, at.core))

    def advance(self, k):
        self.arrive[k].wait_recv()
        self.spread(k)

    def onward(self, k):
        at = self.at
        self.x_first[k].wait_recv()
        self.far.append((k, self.first, self.pass_on(k, 1, 0, self.first, at.y)))
        self.y_second[k].wait_recv()
        self.far.append((k, self.second, self.pass_on(k, 0, 1, self.second, at.x)))
        self.x_second[k].wait_recv()
        self.to_core.append(self.pass_on(k, 1, 0, self.every, at.core))
        self.y_first[k].wait_recv()
        self.to_core.append(self.pass_on(k, 0, 1, self.every, at.core))

    def finish_far(self):
        for k, span, copy in self.far:
            copy.wait_recv()
            self.to_core.append(self.pass_on(k, 1, 1, span, self.at.core))

    def finish(self):
        for copy in self.to_core:
            copy.wait_recv()
        self.own_copy.wait()

    @staticmethod
    def copies(planes):
        return planes - 1 + planes * 11


def forward(
    starts, tokens, cotangent, own_mix, own_out, shares, w_gate, w_up, w_down, planes, group
):
    length, width = tokens.shape
    ds = own_mix.shape[0]
    hid, hs = w_gate.shape[2], w_down.shape[0]
    wide = 3 * hid
    kvd = KV_HEADS * HEAD
    mix = width + 2 * kvd
    base = 2 * own_mix.shape[1]
    columns = base + width
    row_half = length // 2
    low_rows, high_rows = pl.ds(0, row_half), pl.ds(row_half, row_half)
    tables = turn_tables(length)

    def kernel(
        starts_ref,
        x_ref,
        cot_ref,
        own_mix_ref,
        own_out_ref,
        share_ref,
        gate_hbm,
        up_hbm,
        down_hbm,
        tab_ref,
        front_out,
        wall_a,
        wall_b,
        grads_out,
        shares_out,
        gain_ref,
        q_ref,
        kk_ref,
        vv_ref,
        att_ref,
        res_ref,
        n1_ref,
        n2_ref,
        front,
        bias,
        packed,
        raw_in,
        raw_down,
        send_sems,
        recv_sems,
        local_sems,
        load_sems,
    ):
        at = Links(planes, group, send_sems, recv_sems)
        at.barrier(list(at.others.values()) + at.along[1:])
        walls = (wall_a, wall_b)
        shard = at.yb * 2 + at.c

        order = [(s, e) for e in range(EPD) for s in range(4)]

        def load(n):
            s, e = order[n]
            index = (at.xb * 4 + s) * EPD + e
            copies = [
                pltpu.make_async_copy(src, dst, load_sems.at[n % 2, i])
                for i, (src, dst) in enumerate(
                    (
                        (gate_hbm.at[:, index], raw_in.at[n % 2, 0]),
                        (up_hbm.at[:, index], raw_in.at[n % 2, 1]),
                        (down_hbm.at[:, index], raw_down.at[n % 2]),
                    )
                )
            ]
            for copy in copies:
                copy.start()
            return copies

        loads = {n: load(n) for n in range(2)}

        def pack(e):
            for n in range(4 * e, 4 * e + 4):
                s = order[n][0]
                for copy in loads[n]:
                    copy.wait()

                def cast(chunk, n=n, s=s):
                    packed[s, e, chunk, :hid] = raw_in[n % 2, 0, chunk].astype(BF)
                    packed[s, e, chunk, hid : 2 * hid] = raw_in[n % 2, 1, chunk].astype(BF)

                row_loop(ds, 16, cast)
                for i in range(width // hid):
                    packed[s, e, i * hs : (i + 1) * hs, 2 * hid :] = raw_down[
                        n % 2, :, i * hid : (i + 1) * hid
                    ].astype(BF)
                if n + 2 < len(order):
                    loads[n + 2] = load(n + 2)
            copy = pltpu.make_async_copy(
                packed.at[shard, e], walls[e].at[at.z, shard], local_sems.at[e]
            )
            copy.start()
            locals_.append(copy)

        locals_ = []

        def exchange(e):
            copies = []
            for dy, dc, device in ((1, 0, at.y), (1, 1, at.diagonal), (0, 1, at.core)):
                target = (at.yb + dy) % 2 * 2 + (at.c + dc) % 2
                copies.append(
                    at.send(packed.at[target, e], walls[e].at[at.z, shard], device)
                )
            return copies

        ring = {}

        def ring_first(e, copies):
            sent = [
                at.send(packed.at[shard, e], walls[e].at[at.z, shard], at.along[1])
            ]
            for copy, (dy, dc) in zip(copies, ((1, 0), (1, 1), (0, 1))):
                copy.wait_recv()
                piece = walls[e].at[at.z, (at.yb + dy) % 2 * 2 + (at.c + dc) % 2]
                sent.append(at.send(piece, piece, at.along[1]))
            ring[e] = (1, sent)

        def ring_next(e):
            step, sent = ring[e]
            for copy in sent:
                copy.wait_recv()
            if step < planes - 1:
                piece = walls[e].at[(at.z + planes - step) % planes]
                ring[e] = (step + 1, [at.send(piece, piece, at.along[1])])
            else:
                ring[e] = (planes, [])

        mixing = FrontGather(
            at, own_mix_ref, front, 0, share_of(base // 2, 0.25), local_sems.at[2]
        )
        closing = FrontGather(
            at, own_out_ref, front, base, share_of(width // 2, 0.25), local_sems.at[5]
        )

        def share_slot(j):
            return shares_out.at[j // 2, :, pl.ds(j % 2 * length, length)]

        mixing.start()
        mixing.start_plane()
        closing.start()
        pack(0)
        first_exchange = exchange(0)
        place = at.xb * 4 + shard
        locals_.append(pltpu.make_async_copy(share_ref.at[place], share_slot(0), local_sems.at[6]))
        locals_[-1].start()
        got_shares = []
        for j, device in at.others.items():
            other = (
                (at.xb + j // 4) % 2 * 4 + (at.yb + j // 2 % 2) % 2 * 2 + (at.c + j % 2) % 2
            )
            got_shares.append(at.send(share_ref.at[other], share_slot(j), device))
        pack(1)
        fill_bias(bias, starts_ref[0])
        for k in range(1, planes):
            mixing.advance(k)
            mixing.onward(k - 1)
        ring_first(0, first_exchange)
        mixing.onward(planes - 1)
        mixing.finish_far()
        closing.start_plane()
        for k in range(1, planes):
            closing.advance(k)
        mixing.finish()
        def gather_start(src, out):
            def slot(j, rows=pl.ds(0, length)):
                return out.at[j, rows]

            got = {
                "x_low": at.send(src.at[low_rows], slot(4, low_rows), at.x),
                "y_high": at.send(src.at[high_rows], slot(2, high_rows), at.y),
                "x_high": at.send(src.at[high_rows], slot(4, high_rows), at.x),
                "y_low": at.send(src.at[low_rows], slot(2, low_rows), at.y),
                "core": [at.send(src, slot(1), at.core)],
            }
            return slot, got

        def gather_middle(slot, got):
            got["x_low"].wait_recv()
            got["far_low"] = at.send(slot(4, low_rows), slot(6, low_rows), at.y)
            got["core"].append(at.send(slot(4, low_rows), slot(5, low_rows), at.core))
            got["y_high"].wait_recv()
            got["far_high"] = at.send(slot(2, high_rows), slot(6, high_rows), at.x)
            got["core"].append(at.send(slot(2, high_rows), slot(3, high_rows), at.core))

        def gather_last(slot, got):
            got["x_high"].wait_recv()
            got["core"].append(at.send(slot(4, high_rows), slot(5, high_rows), at.core))
            got["y_low"].wait_recv()
            got["core"].append(at.send(slot(2, low_rows), slot(3, low_rows), at.core))
            got["far_low"].wait_recv()
            got["core"].append(at.send(slot(6, low_rows), slot(7, low_rows), at.core))
            got["far_high"].wait_recv()
            got["core"].append(at.send(slot(6, high_rows), slot(7, high_rows), at.core))

        gain_ref[...] = front[:, mix : mix + 128].astype(F32).T[:8]

        def norm(chunk):
            x = x_ref[chunk].astype(F32)
            inv = lax.rsqrt(jnp.mean(x * x, axis=1, keepdims=True) + EPSILON)
            n1_ref[chunk] = (x * inv * gain_ref[0:1, :]).astype(BF)

        row_loop(length, 64, norm)
        block = 4 * LANES
        for n in range(mix // block):
            raw = dot(n1_ref[...], front[:, n * block : (n + 1) * block])
            for j in range(4):
                col = n * block + j * LANES
                values = raw[:, j * LANES : (j + 1) * LANES]
                if col < width:
                    turned_low = turned(values, tab_ref, 1.0).astype(BF).astype(F32)
                    q_ref[:, col : col + LANES] = (turned_low * (1.0 / math.sqrt(HEAD))).astype(BF)
                else:
                    target, start = (kk_ref, width) if col < width + kvd else (vv_ref, width + kvd)
                    if col < width + kvd:
                        values = turned(values, tab_ref, 1.0)

                    def store(side, head, side_values, target=target):
                        target[side, head] = side_values

                    both_sides(values, store, (col - start) // LANES)
        ring_next(0)
        grads = gather_start(cot_ref, grads_out)
        cot_copy = pltpu.make_async_copy(cot_ref, grads_out.at[0], local_sems.at[4])
        cot_copy.start()


        def attend(pairs):
            @pl.loop(*pairs)
            def _(p):
                cols = pl.ds(pl.multiple_of(p * LANES, LANES), LANES)
                total = None
                for side in range(2):
                    head = (2 * p + side) // GROUP
                    probs = softmax_rows(q_ref[:, cols], kk_ref[side, head], bias[...])
                    term = dot(probs.astype(BF), vv_ref[side, head])
                    total = term if total is None else total + term
                att_ref[:, cols] = total.astype(BF)

        attend((0, PAIRS // 3))
        for k in range(planes):
            closing.onward(k)
        attend((PAIRS // 3, 2 * PAIRS // 3))
        gather_middle(*grads)
        second_exchange = exchange(1)
        attend((2 * PAIRS // 3, PAIRS))
        closing.finish_far()
        closing.finish()
        front_copy = pltpu.make_async_copy(front, front_out, local_sems.at[3])
        front_copy.start()
        ring_next(0)
        for n in range(width // block):
            cols = slice(n * block, (n + 1) * block)
            res_ref[:, cols] = x_ref[:, cols].astype(F32) + dot(
                att_ref[...], front[:, base + n * block : base + (n + 1) * block]
            )

        def norm_two(chunk):
            r = res_ref[chunk]
            inv = lax.rsqrt(jnp.mean(r * r, axis=1, keepdims=True) + EPSILON)
            n2_ref[chunk] = (r * inv * gain_ref[1:2, :]).astype(BF)

        row_loop(length, 64, norm_two)
        gather_last(*grads)
        while ring[0][0] < planes:
            ring_next(0)
        for copy in grads[1]["core"] + second_exchange + got_shares:
            copy.wait_recv()
        for copy in locals_ + [front_copy, cot_copy]:
            copy.wait()
        at.finish()

    shape = jax.ShapeDtypeStruct
    count = 2 * FrontGather.copies(planes) + 2 * 3 + 4 + planes - 2 + 13 + 7
    return pl.pallas_call(
        kernel,
        out_shape=[
            shape((width, columns), BF),
            shape((planes, 4, ds, wide), BF),
            shape((planes, 4, ds, wide), BF),
            shape((PLANE, length, width), BF),
            shape((PLANE // 2, 8, 2 * length), F32),
            shape((8, width), F32),
            shape((length, width), BF),
            shape((2, KV_HEADS, length, LANES), BF),
            shape((2, KV_HEADS, length, LANES), BF),
            shape((length, width), BF),
            shape((length, width), F32),
            shape((length, width), BF),
            shape((length, width), BF),
        ],
        in_specs=[pl.BlockSpec(memory_space=pltpu.SMEM)]
        + [whole_vmem()] * 5
        + [anywhere()] * 3
        + [whole_vmem()],
        out_specs=[anywhere()] * 5 + [whole_vmem()] * 8,
        scratch_shapes=[
            pltpu.VMEM((width, columns), BF),
            pltpu.VMEM((length, length), F32),
            pltpu.VMEM((4, EPD, ds, wide), BF),
            pltpu.VMEM((2, 2, ds, hid), F32),
            pltpu.VMEM((2, hs, width), F32),
        ]
        + dma_pairs(count)
        + [pltpu.SemaphoreType.DMA((7,)), pltpu.SemaphoreType.DMA((2, 3))],
        compiler_params=comm_params(0),
        cost_estimate=pl.CostEstimate(
            flops=150_000_000_000, bytes_accessed=20_000_000, transcendentals=0
        ),
    )(
        starts, tokens, cotangent, own_mix, own_out, shares, w_gate, w_up, w_down, tables
    )


class PlaneSum:
    def __init__(self, at, length, odd, even, from_core, far, near):
        self.at, self.odd, self.even, self.core = at, odd, even, from_core
        self.far, self.near = far, near
        self.length = length
        self.half = self.length // 2
        self.low, self.high = pl.ds(0, self.half), pl.ds(self.half, self.half)
        self.arrive = {
            j: at.make(odd(j), self.part(j, pl.ds(0, length)), at.core) for j in (3, 2, 1, 0)
        }
        low, high = self.low, self.high
        self.far_y = at.make(self.part(3, low), far.at[0], at.y)
        self.far_x = at.make(self.part(3, high), far.at[1], at.x)
        self.x_high = at.make(self.part(2, high), near.at[0, high], at.x)
        self.y_low = at.make(self.part(1, low), near.at[1, low], at.y)
        self.x_low = at.make(self.part(2, low), near.at[0, low], at.x)
        self.y_high = at.make(self.part(1, high), near.at[1, high], at.y)

    def rows(self, j, chunk, base=0):
        return pl.ds(pl.multiple_of(chunk.start + j * self.length + base, 16), chunk.size)

    def part(self, j, rows):
        return self.core.at[pl.ds(j * self.length + rows.start, rows.size)]

    def start(self, j):
        self.arrive[j].start()

    def add_core(self, j):
        self.arrive[j].wait_recv()
        core = self.core

        def store(chunk, total):
            core[self.rows(j, chunk)] = total.astype(BF)

        add_rows(store, [lambda q: self.even(j, q), lambda q: core[self.rows(j, q)]], self.length)

    def add_far(self, j, n, base):
        core, far = self.core, self.far

        def store(chunk, total):
            core[self.rows(j, chunk, base)] = total.astype(BF)

        add_rows(store, [lambda q: core[self.rows(j, q, base)], lambda q: far[n, q]], self.half)

    def send_far(self):
        self.add_core(3)
        self.far_y.start()
        self.far_x.start()

    def send_x(self):
        self.add_core(2)
        self.x_high.start()

    def send_y(self):
        self.add_core(1)
        self.y_low.start()

    def onward_x(self):
        self.far_y.wait_recv()
        self.add_far(2, 0, 0)
        self.x_low.start()

    def onward_y(self):
        self.far_x.wait_recv()
        self.add_far(1, 1, self.half)
        self.y_high.start()

    def end(self, store):
        self.arrive[0].wait_recv()
        for copy in (self.x_high, self.y_low, self.x_low, self.y_high):
            copy.wait_recv()
        core, near = self.core, self.near
        terms = [lambda q: self.even(0, q), lambda q: core[q]]
        terms += [lambda q: near[0, q], lambda q: near[1, q]]
        add_rows(store, terms, self.length)

    copies = 10


class RingSum:
    def __init__(self, at, pack, own, own_sem):
        self.at, self.pack, self.own, self.own_sem = at, pack, own, own_sem
        self.index = [(at.z + at.planes - k) % at.planes for k in range(at.planes)]

    def block(self, k):
        return self.pack.at[self.index[k]]

    def fetch(self, k):
        self.fetched = pltpu.make_async_copy(self.block(k), self.own, self.own_sem)
        self.fetched.start()

    def add(self, source, target):
        self.fetched.wait()

        def store(chunk, total):
            target[chunk] = total.astype(BF)

        add_rows(store, [lambda q: source[q], lambda q: self.own[q]], self.own.shape[0], 16)

    def first(self, slots):
        self.slots, self.step = slots, 1
        sources = [self.block(1)] + slots[:-1]
        self.sent = [
            self.at.make(src, dst, self.at.along[1]) for src, dst in zip(sources, slots)
        ]
        self.fetches = {
            k: pltpu.make_async_copy(self.block(k), self.own, self.own_sem)
            for k in range(2, len(slots) + 1)
        }
        self.sent[0].start()
        self.begin_fetch(2)

    def begin_fetch(self, k):
        if k in self.fetches:
            self.fetched = self.fetches[k]
            self.fetched.start()

    def next(self):
        if self.step < len(self.slots):
            here = self.slots[self.step - 1]
            self.sent[self.step - 1].wait_recv()
            self.add(here, here)
            self.sent[self.step].start()
            self.step += 1
            self.begin_fetch(self.step + 1)

    def rest(self):
        while self.step < len(self.slots):
            self.next()
        self.sent[-1].wait_recv()

    def last(self, before, sent, landing):
        self.add(before, sent)
        self.landing = landing
        self.copy = self.at.send(sent, landing, self.at.along[1])
        self.fetch(0)

    def total(self):
        self.copy.wait_recv()
        self.add(self.landing, self.landing)
        return self.landing


def run_experts(tokens, grads, shares, wall_a, wall_b, planes, group):
    pairs, count, width = grads.shape
    length = count // 2
    piece, wide = wall_a.shape[1:]
    hid = wide // 3
    ds, hs, blocks = width // group, hid // group, width // hid
    half = length // 2
    low, high, full = pl.ds(0, half), pl.ds(half, half), pl.ds(0, length)

    def kernel(
        n2_hbm,
        g_hbm,
        share_ref,
        wall_a_ref,
        wall_b_ref,
        out_hbm,
        pack_a,
        pack_b,
        sum_ref,
        passed,
        xs,
        dxs,
        w_a,
        w_b,
        down_a,
        down_b,
        in_sum,
        down_sum,
        g_tile,
        o_tile,
        pre,
        act,
        far,
        near,
        ring_slots,
        own,
        free,
        send_sems,
        recv_sems,
        local_sems,
    ):
        at = Links(planes, group, send_sems, recv_sems)
        at.barrier([at.x, at.y, at.core] + at.along[1:])
        index = [(at.z + planes - k) % planes for k in range(planes)]

        def local(src, dst, n):
            copy = pltpu.make_async_copy(src, dst, local_sems.at[n])
            copy.start()
            return copy

        def slot(j, rows=full):
            return xs.at[j // 2, pl.ds(j % 2 * length + rows.start, rows.size)]

        pieces = [
            w_b.at[pl.ds(pl.multiple_of(index[k] * piece, 16), piece)] for k in range(planes)
        ]

        local(n2_hbm, slot(0), 0).wait()
        x_low = at.send(slot(0, low), slot(4, low), at.x)
        y_high = at.send(slot(0, high), slot(2, high), at.y)
        x_high = at.send(slot(0, high), slot(4, high), at.x)
        y_low = at.send(slot(0, low), slot(2, low), at.y)
        near_core = at.send(slot(0), slot(1), at.core)
        ring = [at.make(wall_b_ref.at[at.z], pieces[0], at.along[1])]
        ring += [at.make(piece_ref, piece_ref, at.along[1]) for piece_ref in pieces[1:-1]]
        ring[0].start()
        load_b = local(wall_b_ref.at[at.z], pieces[0], 1)
        loads = [
            local(wall_a_ref.at[n], w_a.at[pl.ds(n * piece, piece)], 2 + n) for n in range(planes)
        ]
        state = {"ring": 0}
        far_low = at.make(slot(4, low), slot(6, low), at.y)
        far_high = at.make(slot(2, high), slot(6, high), at.x)
        passed_on = {
            (j, rows.start): at.make(slot(j, rows), slot(j + 1, rows), at.core)
            for j in (4, 2, 6)
            for rows in (low, high)
        }

        def ring_next():
            ring[state["ring"]].wait_recv()
            state["ring"] += 1
            if state["ring"] < planes - 1:
                ring[state["ring"]].start()

        def core_arrival(j):
            passed_on[j, low.start].wait_recv()
            passed_on[j, high.start].wait_recv()

        def spread():
            x_low.wait_recv()
            far_low.start()
            passed_on[4, low.start].start()
            y_high.wait_recv()
            far_high.start()
            passed_on[2, high.start].start()
            x_high.wait_recv()
            passed_on[4, high.start].start()
            y_low.wait_recv()
            passed_on[2, low.start].start()
            core_arrival(4)

        def spread_far():
            far_low.wait_recv()
            passed_on[6, low.start].start()
            far_high.wait_recv()
            passed_on[6, high.start].start()
            core_arrival(6)

        def unpack_down(w, down):
            for s in range(group):
                for b in range(blocks):
                    down[s * hs : (s + 1) * hs, b * hid : (b + 1) * hid] = w[
                        s * ds + b * hs : s * ds + (b + 1) * hs, 2 * hid :
                    ]

        def clear():
            def body(chunk):
                in_sum[chunk] = jnp.zeros((chunk.size, 2 * hid), F32)

            row_loop(width, 64, body)

            def body_down(chunk):
                down_sum[chunk] = jnp.zeros((chunk.size, width), F32)

            row_loop(hid, 64, body_down)

        def out_copy(pair):
            return pltpu.make_async_copy(o_tile, out_hbm.at[pair], local_sems.at[0])

        def tile(e, step, pair, w, down, middle):
            g_load = pltpu.make_async_copy(g_hbm.at[pair], g_tile, local_sems.at[1])
            g_load.start()
            x = xs.at[pair]
            share = share_ref[pair].T[:, e : e + 1]
            part = hid // 2
            for n in range(2):
                cols = slice(n * part, (n + 1) * part)
                up_cols = slice(hid + n * part, hid + (n + 1) * part)
                gate = dot(x[...], w[:, cols])
                up = dot(x[...], w[:, up_cols])
                if n == 0:
                    g_load.wait()
                inner = dot_nt(g_tile[...], down[cols, :]) * share
                sig = jax.nn.sigmoid(gate)
                swish = gate * sig
                act[:, cols] = (share * (swish * up)).astype(BF)
                pre[:, cols] = (inner * up * sig * (1.0 + gate * (1.0 - sig))).astype(BF)
                pre[:, up_cols] = (inner * swish).astype(BF)
            middle()

            @pl.when(step > 0)
            def _():
                out_copy(pair).wait()

            if e > 0:
                before = pltpu.make_async_copy(out_hbm.at[pair], o_tile, local_sems.at[2])
                before.start()
                before.wait()
            for n in range(width // hid):
                cols = slice(n * hid, (n + 1) * hid)
                out = dot(act[...], down[:, cols])
                dx = dot_nt(pre[...], w[cols, : 2 * hid])
                if e > 0:
                    out = out + o_tile[:, cols].astype(F32)
                    dx = dx + dxs[pair, :, cols].astype(F32)
                o_tile[:, cols] = out.astype(BF)
                dxs[pair, :, cols] = dx.astype(BF)
                in_sum[cols, :] += dot_tn(x[:, cols], pre[...])
                down_sum[:, cols] += dot_tn(act[...], g_tile[:, cols])
            out_copy(pair).start()

        def pack(target):
            out_copy(0).wait()
            copies = [None, None]
            for n in range(planes):
                base = n % 2 * piece
                if copies[n % 2] is not None:
                    copies[n % 2].wait()

                def body(chunk, n=n, base=base):
                    rows = pl.ds(pl.multiple_of(chunk.start + base, 16), chunk.size)
                    source = pl.ds(pl.multiple_of(chunk.start + n * piece, 16), chunk.size)
                    o_tile[rows, : 2 * hid] = in_sum[source].astype(BF)

                row_loop(piece, 32, body)
                for s in range(4):
                    for b in range(blocks):
                        row = base + s * ds + b * hs
                        o_tile[row : row + hs, 2 * hid :] = down_sum[
                            (n * 4 + s) * hs : (n * 4 + s + 1) * hs, b * hid : (b + 1) * hid
                        ].astype(BF)
                copies[n % 2] = local(o_tile.at[pl.ds(base, piece)], target.at[n], 3 + n % 2)
            for copy in copies:
                copy.wait()

        clear()
        for copy in loads:
            copy.wait()
        load_b.wait()
        unpack_down(w_a, down_a)
        near_core.wait_recv()

        @pl.loop(0, pairs)
        def _(step):
            @pl.when(step == 1)
            def _():
                spread()
                ring_next()

            @pl.when(step == 2)
            def _():
                core_arrival(2)

            @pl.when(step == 3)
            def _():
                spread_far()
                ring_next()

            tile(0, step, 2 * step % 3 + step // 3 * 3, w_a, down_a, lambda: None)

        pl.semaphore_signal(free, inc=1, device_id=at.core, device_id_type=pl.DeviceIdType.MESH)
        pack(pack_a)
        sums = RingSum(at, pack_a, own, local_sems.at[5])
        sums.first([ring_slots.at[n] for n in range(planes - 3)] + [passed])
        clear()
        while state["ring"] < planes - 1:
            ring_next()
        unpack_down(w_b, down_b)
        pl.semaphore_wait(free, 1)
        plane = PlaneSum(
            at,
            length,
            lambda j: dxs.at[j, pl.ds(length, length)],
            lambda j, q: dxs[j, q],
            w_a,
            far,
            near,
        )

        @pl.loop(0, pairs)
        def _(step):
            def middle():
                @pl.when(step == 1)
                def _():
                    plane.send_far()

                @pl.when(step == 2)
                def _():
                    plane.send_x()
                    sums.next()

                @pl.when(step == 3)
                def _():
                    plane.send_y()
                    plane.onward_y()

            tile(1, step, pairs - 1 - step, w_b, down_b, middle)
            for n in range(pairs):

                @pl.when(step == n)
                def _(n=n):
                    plane.start(pairs - 1 - n)
                    if n == 2:
                        plane.onward_x()

        pack(pack_b)

        def store(chunk, total):
            sum_ref[chunk] = total

        plane.end(store)
        sums.rest()
        at.finish()

    shape = jax.ShapeDtypeStruct
    return pl.pallas_call(
        kernel,
        in_specs=[anywhere()] * 2 + [whole_vmem()] + [anywhere()] * 2,
        out_specs=[anywhere()] * 3 + [whole_vmem()] * 2,
        out_shape=[
            shape((pairs, count, width), BF),
            shape((planes, piece, wide), BF),
            shape((planes, piece, wide), BF),
            shape((length, width), F32),
            shape((piece, wide), BF),
        ],
        scratch_shapes=[
            pltpu.VMEM((pairs, count, width), BF),
            pltpu.VMEM((pairs, count, width), BF),
            pltpu.VMEM((width, wide), BF),
            pltpu.VMEM((width, wide), BF),
            pltpu.VMEM((hid, width), BF),
            pltpu.VMEM((hid, width), BF),
            pltpu.VMEM((width, 2 * hid), F32),
            pltpu.VMEM((hid, width), F32),
            pltpu.VMEM((count, width), BF),
            pltpu.VMEM((count, width), BF),
            pltpu.VMEM((count, 2 * hid), BF),
            pltpu.VMEM((count, hid), BF),
            pltpu.VMEM((2, half, width), BF),
            pltpu.VMEM((2, length, width), BF),
            pltpu.VMEM((planes - 3, piece, wide), BF),
            pltpu.VMEM((piece, wide), BF),
            pltpu.SemaphoreType.REGULAR,
        ]
        + dma_pairs(13 + planes - 1 + PlaneSum.copies + planes - 2)
        + [pltpu.SemaphoreType.DMA((2 + planes,))],
        compiler_params=pltpu.CompilerParams(
            collective_id=2, has_side_effects=True, vmem_limit_bytes=63 * 2**20
        ),
        cost_estimate=pl.CostEstimate(
            flops=100_000_000_000, bytes_accessed=50_000_000, transcendentals=0
        ),
    )(tokens, grads, shares, wall_a, wall_b)


class Exchange:
    def __init__(self, at, total, out, ds):
        self.at, self.total, self.out, self.ds = at, total, out, ds
        self.shard = at.yb * 2 + at.c

    def place(self, dx, dy, dc):
        at = self.at
        return (at.xb + dx) % 2 * 4 + (at.yb + dy) % 2 * 2 + (at.c + dc) % 2

    def rows(self, dy, dc):
        at = self.at
        shard = (at.yb + dy) % 2 * 2 + (at.c + dc) % 2
        return self.total.at[pl.ds(pl.multiple_of(shard * self.ds, 16), self.ds)]

    def start(self, sem):
        at = self.at
        here = self.out.at[self.place(0, 0, 0)]
        self.local = pltpu.make_async_copy(self.rows(0, 0), here, sem)
        self.local.start()
        self.got = [
            (dy, dc, at.send(self.rows(dy, dc), here, device))
            for dy, dc, device in ((1, 0, at.y), (1, 1, at.diagonal), (0, 1, at.core))
        ]
        self.across = [at.send(self.rows(0, 0), here, at.x)]

    def onward(self):
        at = self.at
        for dy, dc, copy in self.got:
            copy.wait_recv()
            piece = self.out.at[self.place(0, dy, dc)]
            self.across.append(at.send(piece, piece, at.x))

    def end(self):
        for copy in self.across:
            copy.wait_recv()
        self.local.wait()

    copies = 7


def backward(
    starts,
    grad_two,
    cotangent,
    tokens,
    residual,
    front,
    gains,
    q,
    kk,
    vv,
    att,
    n1,
    outs,
    pack_a,
    before_a,
    pack_b,
    planes,
    group,
):
    length, width = tokens.shape
    columns = front.shape[1]
    kvd = KV_HEADS * HEAD
    mix = width + 2 * kvd
    block = 4 * LANES
    tables = turn_tables(length)
    piece, wide = pack_a.shape[1:]
    ds = piece // 4
    extra = columns - mix - width
    part = block // 2

    def kernel(
        starts_ref,
        d_ref,
        cot_ref,
        tab_ref,
        gain_ref,
        q_ref,
        kk_ref,
        vv_ref,
        att_ref,
        before_ref,
        x_hbm,
        n1_hbm,
        res_hbm,
        w_hbm,
        outs_ref,
        pack_a_ref,
        pack_b_ref,
        in_ref,
        sum_ref,
        passed_b,
        grad_hbm,
        shards_ref,
        bias,
        gain_sum,
        mixed,
        context,
        grad_mix,
        key_sum,
        value_sum,
        w_ref,
        stage,
        even,
        from_core,
        far,
        near,
        own_a,
        sent_a,
        landing_a,
        own_b,
        slots_b,
        send_sems,
        recv_sems,
        local_sems,
    ):
        at = Links(planes, group, send_sems, recv_sems)
        at.barrier([at.x, at.y, at.core, at.diagonal] + at.along[1:])

        def local(src, dst, n):
            copy = pltpu.make_async_copy(src, dst, local_sems.at[n])
            copy.start()
            return copy

        load_res = local(res_hbm, in_ref, 0)
        load_out_w = local(
            w_hbm.at[:, pl.ds(mix + extra, width)], w_ref.at[:, pl.ds(0, width)], 1
        )
        plane = PlaneSum(
            at,
            length,
            lambda j: outs_ref.at[2 * j + 1],
            lambda j, q: even[j, q],
            from_core,
            far,
            near,
        )
        for j in (3, 2, 1, 0):
            plane.start(j)
        ring_a = RingSum(at, pack_a_ref, own_a, local_sems.at[6])
        ring_b = RingSum(at, pack_b_ref, own_b, local_sems.at[7])
        ring_a.fetch(planes - 1)
        loads = [local(outs_ref.at[2 * j], even.at[j], 2 + j) for j in range(4)]
        ring_a.last(before_ref, sent_a, landing_a)
        ring_b.first([slots_b.at[n] for n in range(planes - 3)] + [passed_b])
        staged = [None, None]
        turn = [0]

        def put(values, column, count):
            for base in range(0, count, part):
                n = turn[0] % 2
                turn[0] += 1
                if staged[n] is not None:
                    staged[n].wait()
                stage[n] = values[:, base : base + part]
                staged[n] = local(
                    stage.at[n], grad_hbm.at[:, pl.ds(column + base, part)], 8 + n
                )

        fill_bias(bias, starts_ref[0])
        gain_sum[...] = jnp.zeros_like(gain_sum)

        load_res.wait()

        def residual_grad(chunk):
            d, r = d_ref[chunk], in_ref[chunk]
            inv = lax.rsqrt(jnp.mean(r * r, axis=1, keepdims=True) + EPSILON)
            scaled = d * gain_ref[1:2, :]
            grad = (
                cot_ref[chunk].astype(F32)
                + inv * scaled
                - r * (inv * inv * inv * jnp.mean(scaled * r, axis=1, keepdims=True))
            )
            sum_ref[chunk] = grad
            mixed[chunk] = grad.astype(BF)
            gain_sum[1:2, :] += jnp.sum(d * r * inv, axis=0, keepdims=True)

        row_loop(length, 32, residual_grad)
        load_out_w.wait()
        for n in range(width // block):
            cols = slice(n * block, (n + 1) * block)
            context[:, cols] = dot_nt(mixed[...], w_ref[cols, :width]).astype(BF)
        load_mix_w = local(w_hbm.at[:, pl.ds(0, mix)], w_ref, 1)
        for n in range(width // block):
            cols = slice(n * block, (n + 1) * block)
            put(dot_tn(att_ref[...], mixed[:, cols]).astype(BF), mix + extra + n * block, block)
        load_n1 = local(n1_hbm, mixed, 0)
        for copy in loads:
            copy.wait()
        plane.send_far()
        plane.send_x()
        plane.send_y()
        key_sum[...] = jnp.zeros_like(key_sum)
        value_sum[...] = jnp.zeros_like(value_sum)

        def attend(lower, upper):
            @pl.loop(lower, upper)
            def _(p):
                cols = pl.ds(pl.multiple_of(p * LANES, LANES), LANES)
                total = None
                for side in range(2):
                    head = (2 * p + side) // GROUP
                    query, grad = q_ref[:, cols], context[:, cols]
                    probs = softmax_rows(query, kk_ref[side, head], bias[...])
                    grad_probs = dot_nt(grad, vv_ref[side, head])
                    value_sum[side, head] += dot_tn(probs.astype(BF), grad)
                    inner = jnp.sum(probs * grad_probs, axis=1, keepdims=True)
                    logit = (probs * (grad_probs - inner)).astype(BF)
                    term = dot(logit, kk_ref[side, head])
                    total = term if total is None else total + term
                    key_sum[side, head] += dot_tn(logit, query)
                back = turned(total, tab_ref, -1.0) * (1.0 / math.sqrt(HEAD))
                grad_mix[:, cols] = back.astype(BF)

        attend(0, PAIRS // 3)
        plane.onward_x()
        plane.onward_y()
        exchange = Exchange(at, ring_a.total(), shards_ref, ds)
        exchange.start(local_sems.at[10])
        attend(PAIRS // 3, 2 * PAIRS // 3)
        ring_b.next()
        exchange.onward()
        attend(2 * PAIRS // 3, PAIRS)
        load_x = local(x_hbm, context, 11)
        load_n1.wait()
        for pair in range(KV_HEADS // 2):
            for sums, base in ((key_sum, width), (value_sum, width + kvd)):

                def join(chunk, pair=pair, sums=sums, base=base):
                    low = lax.broadcasted_iota(jnp.int32, (chunk.size, LANES), 1) < HEAD
                    even = sums[0, 2 * pair, chunk] + pltpu.roll(sums[1, 2 * pair, chunk], HEAD, 1)
                    odd = sums[1, 2 * pair + 1, chunk] + pltpu.roll(
                        sums[0, 2 * pair + 1, chunk], HEAD, 1
                    )
                    values = jnp.where(low, even, odd)
                    if base == width:
                        values = turned(values, tab_ref.at[:, chunk], -1.0)
                    grad_mix[chunk, base + pair * LANES : base + (pair + 1) * LANES] = values.astype(BF)

                row_loop(length, 64, join)
        for n in range(mix // block):
            cols = slice(n * block, (n + 1) * block)
            put(dot_tn(mixed[...], grad_mix[:, cols]).astype(BF), n * block, block)
        load_mix_w.wait()
        for n in range(width // block):
            cols = slice(n * block, (n + 1) * block)
            in_ref[:, cols] = dot_nt(grad_mix[...], w_ref[cols, :mix])

        load_x.wait()

        def input_grad(chunk):
            d, x = in_ref[chunk], context[chunk].astype(F32)
            inv = lax.rsqrt(jnp.mean(x * x, axis=1, keepdims=True) + EPSILON)
            scaled = d * gain_ref[0:1, :]
            gain_sum[0:1, :] += jnp.sum(d * x * inv, axis=0, keepdims=True)
            in_ref[chunk] = (
                sum_ref[chunk]
                + inv * scaled
                - x * (inv * inv * inv * jnp.mean(scaled * x, axis=1, keepdims=True))
            )

        row_loop(length, 32, input_grad)
        gain_rows = jnp.concatenate([gain_sum[...].T, jnp.zeros((width, extra - 8), F32)], axis=1)
        put(gain_rows.astype(BF), mix, extra)

        def store(chunk, total):
            sum_ref[chunk] = total

        plane.end(store)
        ring_b.rest()
        exchange.end()
        for copy in staged:
            copy.wait()
        at.finish()

    shape = jax.ShapeDtypeStruct
    return pl.pallas_call(
        kernel,
        in_specs=[pl.BlockSpec(memory_space=pltpu.SMEM)]
        + [whole_vmem()] * 9
        + [anywhere()] * 7,
        out_specs=[whole_vmem()] * 3 + [anywhere()] * 2,
        out_shape=[
            shape((length, width), F32),
            shape((length, width), F32),
            shape((piece, wide), BF),
            shape((width, columns), BF),
            shape((PLANE, ds, wide), BF),
        ],
        scratch_shapes=[
            pltpu.VMEM((length, length), F32),
            pltpu.VMEM((8, width), F32),
            pltpu.VMEM((length, width), BF),
            pltpu.VMEM((length, width), BF),
            pltpu.VMEM((length, mix), BF),
            pltpu.VMEM((2, KV_HEADS, length, LANES), F32),
            pltpu.VMEM((2, KV_HEADS, length, LANES), F32),
            pltpu.VMEM((width, mix), BF),
            pltpu.VMEM((2, width, part), BF),
            pltpu.VMEM((4, length, width), BF),
            pltpu.VMEM((4 * length, width), BF),
            pltpu.VMEM((2, length // 2, width), BF),
            pltpu.VMEM((2, length, width), BF),
            pltpu.VMEM((piece, wide), BF),
            pltpu.VMEM((piece, wide), BF),
            pltpu.VMEM((piece, wide), BF),
            pltpu.VMEM((piece, wide), BF),
            pltpu.VMEM((planes - 3, piece, wide), BF),
        ]
        + dma_pairs(PlaneSum.copies + 1 + Exchange.copies + planes - 2)
        + [pltpu.SemaphoreType.DMA((12,))],
        compiler_params=pltpu.CompilerParams(
            collective_id=1, has_side_effects=True, vmem_limit_bytes=62 * 2**20
        ),
        cost_estimate=pl.CostEstimate(
            flops=80_000_000_000, bytes_accessed=50_000_000, transcendentals=0
        ),
    )(
        starts,
        grad_two,
        cotangent,
        tables,
        gains,
        q,
        kk,
        vv,
        att,
        before_a,
        tokens,
        n1,
        residual,
        front,
        outs,
        pack_a,
        pack_b,
    )


def scatter_front(grad, pack, before, planes, group):
    rows, columns = grad.shape
    ds, half = rows // (4 * planes), columns // 2
    part = share_of(half, 0.6)
    first, second = pl.ds(0, part), pl.ds(part, half - part)
    block, wide = pack.shape[1:]

    def kernel(
        g_ref,
        pack_ref,
        before_ref,
        out_ref,
        shards_ref,
        from_core,
        kept,
        far_a,
        far_b,
        near_x,
        near_y,
        total_ref,
        from_z,
        own,
        passed,
        landing,
        send_sems,
        recv_sems,
        local_sems,
    ):
        at = Links(planes, group, send_sems, recv_sems)
        at.barrier([at.x, at.y, at.core, at.diagonal] + at.along[1:])
        ring = RingSum(at, pack_ref, own, local_sems.at[0])
        ring.fetch(planes - 1)

        def row(k, dy, core):
            owner = ((at.z + k) % planes) * 4 + (at.yb + dy) % 2 * 2 + core
            return pl.multiple_of(owner * ds, 16)

        def column(dx):
            return pl.ds(pl.multiple_of((at.xb + dx) % 2 * half, 128), half)

        order = list(range(1, planes)) + [0]
        arrive = {}
        for k in order:
            for dy in (1, 0):
                arrive[k, dy] = at.send(
                    g_ref.at[pl.ds(row(k, dy, 1 - at.c), ds)], from_core.at[k, dy], at.core
                )
        ring.last(before_ref, passed, landing)
        step = 16
        x_second, y_first, x_first, y_second, to_x, to_y = {}, {}, {}, {}, {}, {}
        for k in order:
            for dy in (1, 0):
                arrive[k, dy].wait_recv()
                for dx in (1, 0):

                    def store(chunk, total, k=k, dx=dx, dy=dy):
                        kept[k, dx, dy, chunk] = total.astype(BF)

                    add_rows(
                        store,
                        [
                            lambda q, k=k, dx=dx, dy=dy: g_ref[
                                pl.ds(pl.multiple_of(row(k, dy, at.c) + q.start, 16), q.size),
                                column(dx),
                            ],
                            lambda q, k=k, dx=dx, dy=dy: from_core[k, dy, q, column(dx)],
                        ],
                        ds,
                        step,
                    )
                    if (dx, dy) == (1, 1):
                        to_y[k] = at.send(kept.at[k, 1, 1, :, first], far_a.at[k], at.y)
                        to_x[k] = at.send(kept.at[k, 1, 1, :, second], far_b.at[k], at.x)
                    elif (dx, dy) == (0, 1):
                        y_first[k] = at.send(
                            kept.at[k, 0, 1, :, first], near_y.at[k, :, first], at.y
                        )
                    elif (dx, dy) == (1, 0):
                        x_second[k] = at.send(
                            kept.at[k, 1, 0, :, second], near_x.at[k, :, second], at.x
                        )
        for k in order:
            to_y[k].wait_recv()

            def store(chunk, total, k=k):
                kept[k, 1, 0, chunk, first] = total.astype(BF)

            add_rows(
                store,
                [lambda q, k=k: kept[k, 1, 0, q, first], lambda q, k=k: far_a[k, q]],
                ds,
                step,
            )
            x_first[k] = at.send(kept.at[k, 1, 0, :, first], near_x.at[k, :, first], at.x)
            to_x[k].wait_recv()

            def store(chunk, total, k=k):
                kept[k, 0, 1, chunk, second] = total.astype(BF)

            add_rows(
                store,
                [lambda q, k=k: kept[k, 0, 1, q, second], lambda q, k=k: far_b[k, q]],
                ds,
                step,
            )
            y_second[k] = at.send(kept.at[k, 0, 1, :, second], near_y.at[k, :, second], at.y)
        exchange = Exchange(at, ring.total(), shards_ref, ds)
        exchange.start(local_sems.at[1])
        arrive_z = {}
        for k in order:
            for copies in (x_second, y_first, x_first, y_second):
                copies[k].wait_recv()

            def store(chunk, total, k=k):
                total_ref[k, chunk] = total.astype(BF)

            add_rows(
                store,
                [
                    lambda q, k=k: kept[k, 0, 0, q],
                    lambda q, k=k: near_x[k, q],
                    lambda q, k=k: near_y[k, q],
                ],
                ds,
                step,
            )
            if k > 0:
                arrive_z[k] = at.send(total_ref.at[k], from_z.at[k], at.along[k])
        exchange.onward()
        for k in range(1, planes):
            arrive_z[k].wait_recv()

        def store(chunk, total):
            out_ref[chunk] = total.astype(BF)

        add_rows(
            store,
            [lambda q: total_ref[0, q]]
            + [lambda q, k=k: from_z[k, q] for k in range(1, planes)],
            ds,
            step,
        )
        exchange.end()
        at.finish()

    return pl.pallas_call(
        kernel,
        out_shape=[
            jax.ShapeDtypeStruct((ds, half), BF),
            jax.ShapeDtypeStruct((PLANE, ds, wide), BF),
        ],
        in_specs=[whole_vmem(), anywhere(), whole_vmem()],
        out_specs=[whole_vmem(), anywhere()],
        scratch_shapes=[
            pltpu.VMEM((planes, 2, ds, columns), BF),
            pltpu.VMEM((planes, 2, 2, ds, half), BF),
            pltpu.VMEM((planes, ds, part), BF),
            pltpu.VMEM((planes, ds, half - part), BF),
            pltpu.VMEM((planes, ds, half), BF),
            pltpu.VMEM((planes, ds, half), BF),
            pltpu.VMEM((planes, ds, half), BF),
            pltpu.VMEM((planes, ds, half), BF),
            pltpu.VMEM((block, wide), BF),
            pltpu.VMEM((block, wide), BF),
            pltpu.VMEM((block, wide), BF),
        ]
        + dma_pairs(planes * 8 + planes - 1 + 1 + Exchange.copies)
        + [pltpu.SemaphoreType.DMA((2,))],
        compiler_params=comm_params(3),
        cost_estimate=pl.CostEstimate(
            flops=50_000_000_000, bytes_accessed=20_000_000, transcendentals=0
        ),
    )(grad, pack, before)


def unpack(packs, residual, term, hs):
    ds, wide = packs[0].shape[1:]
    hid = wide // 3
    blocks = ds // hs

    def kernel(*refs):
        ins, (res_ref, term_ref) = refs[:EPD], refs[EPD : EPD + 2]
        gate_out, up_out, down_out, sum_ref, raw_in, raw_down, sems = refs[EPD + 2 :]
        copies = {}
        for n, (p, e) in enumerate((p, e) for p in range(PLANE) for e in range(EPD)):
            slot = n % 4
            if n >= 4:
                for copy in copies[n - 4]:
                    copy.wait()

            def cast(chunk, p=p, e=e, slot=slot):
                raw_in[slot, 0, chunk] = ins[e][p, chunk, :hid].astype(F32)
                raw_in[slot, 1, chunk] = ins[e][p, chunk, hid : 2 * hid].astype(F32)

            row_loop(ds, 16, cast)
            for b in range(blocks):
                raw_down[slot, :, b * hid : (b + 1) * hid] = ins[e][
                    p, b * hs : (b + 1) * hs, 2 * hid :
                ].astype(F32)
            index = p * EPD + e
            copies[n] = [
                pltpu.make_async_copy(src, dst, sems.at[slot, i])
                for i, (src, dst) in enumerate(
                    (
                        (raw_in.at[slot, 0], gate_out.at[:, index]),
                        (raw_in.at[slot, 1], up_out.at[:, index]),
                        (raw_down.at[slot], down_out.at[:, index]),
                    )
                )
            ]
            for copy in copies[n]:
                copy.start()

        def add(chunk):
            sum_ref[chunk] = res_ref[chunk] + term_ref[chunk]

        row_loop(residual.shape[0], 32, add)
        for n in range(EXP - 4, EXP):
            for copy in copies[n]:
                copy.wait()

    shape = jax.ShapeDtypeStruct
    return pl.pallas_call(
        kernel,
        in_specs=[whole_vmem()] * (EPD + 2),
        out_specs=[anywhere()] * 3 + [whole_vmem()],
        out_shape=[
            shape((ds, EXP, hid), F32),
            shape((ds, EXP, hid), F32),
            shape((hs, EXP, blocks * hid), F32),
            shape(residual.shape, F32),
        ],
        scratch_shapes=[
            pltpu.VMEM((4, 2, ds, hid), F32),
            pltpu.VMEM((4, hs, blocks * hid), F32),
            pltpu.SemaphoreType.DMA((4, 3)),
        ],
        compiler_params=pltpu.CompilerParams(vmem_limit_bytes=32 * 2**20),
    )(*packs, residual, term)


def shards(
    reps,
    group,
    tokens,
    cotangent,
    routes,
    gates,
    starts,
    norm1_gain,
    w_query,
    w_key,
    w_value,
    w_out,
    norm2_gain,
    w_gate,
    w_up,
    w_down,
):
    planes = group // 4
    r, f = lax.axis_index("rep"), lax.axis_index("fsdp")
    xb, yb, c, z = r % 2, (f // 2) % 2, f % 2, f // 4
    mine = xb * 4 + yb * 2 + c

    def perm(to):
        return [
            (a * group + b, to(a, b)[0] * group + to(a, b)[1])
            for a in range(reps)
            for b in range(group)
        ]

    def pp(value, to):
        return lax.ppermute(value, AXES, perm(to))

    def go(value, dx, dy, dc):
        return pp(value, lambda a, b: (a ^ dx, b ^ (dy * 2 + dc)))

    def along(value, k):
        return pp(value, lambda a, b: (a, (b + 4 * k) % group))

    def all_reps(value):
        step = 2
        while step < reps:
            value = value + pp(value, lambda a, b, s=step: (a ^ s, b))
            step *= 2
        return value

    length, width = tokens.shape
    ds = w_query.shape[0]
    hs = w_down.shape[0]
    hid = w_gate.shape[2]
    kvd = w_key.shape[1]
    half_rows = length // 2

    mix = width + 2 * kvd
    gain_end = mix + 256
    gains = jnp.stack([norm1_gain.astype(BF), norm2_gain.astype(BF)], axis=1)
    own_mix = jnp.concatenate(
        [
            w_query.astype(BF),
            w_key.astype(BF),
            w_value.astype(BF),
            gains,
            jnp.zeros((ds, 254), BF),
        ],
        axis=1,
    )

    def rep_half(own):
        half = own.shape[1] // 2
        return lax.dynamic_slice(own, (0, xb * half), (ds, half))

    experts = jnp.arange(EXP, dtype=jnp.int32)[:, None, None]
    share = jnp.sum(jnp.where(routes[None] == experts, gates[None], 0.0), axis=2)
    pairs = PLANE // 2
    share = jnp.pad(share.reshape(PLANE, EPD, length), ((0, 0), (0, 8 - EPD), (0, 0)))

    front, wall_a, wall_b, grads_all, shares, gains_all, q, kk, vv, att, residual, n1, n2 = forward(
        starts,
        tokens,
        cotangent,
        rep_half(own_mix),
        rep_half(w_out.astype(BF)),
        share,
        w_gate,
        w_up,
        w_down,
        planes,
        group,
    )
    out_sum, pack_a, pack_b, grad_normed_two, before_a = run_experts(
        n2,
        grads_all.reshape(pairs, 2 * length, width),
        shares,
        wall_a.reshape(planes, 4 * ds, 3 * hid),
        wall_b.reshape(planes, 4 * ds, 3 * hid),
        planes,
        group,
    )
    input_grad, out_term, before_b, front_grad, shards_a = backward(
        starts,
        grad_normed_two,
        cotangent,
        tokens,
        residual,
        front,
        gains_all,
        q,
        kk,
        vv,
        att,
        n1,
        out_sum.reshape(PLANE, length, width),
        pack_a,
        before_a,
        pack_b,
        planes,
        group,
    )
    front_total, shards_b = scatter_front(front_grad, pack_b, before_b, planes, group)
    total = all_reps(front_total)
    gate_shard, up_shard, down_shard, output = unpack(
        [all_reps(shards_a), all_reps(shards_b)], residual, out_term, hs
    )
    other = go(total, 1, 0, 0)
    front_shard = jnp.where(
        xb == 0,
        jnp.concatenate([total, other], axis=1),
        jnp.concatenate([other, total], axis=1),
    ).astype(F32)
    return (
        output,
        input_grad,
        front_shard[:, mix],
        front_shard[:, :width],
        front_shard[:, width : width + kvd],
        front_shard[:, width + kvd : mix],
        front_shard[:, gain_end:],
        front_shard[:, mix + 1],
        gate_shard,
        up_shard,
        down_shard,
    )


def solution(mesh):
    reps, group = mesh.shape["rep"], mesh.shape["fsdp"]
    both, one = P(AXES, None), P("fsdp")
    flat, deep = P("fsdp", None), P("fsdp", None, None)

    def whole(*args):
        return shards(reps, group, *args)

    return jax.shard_map(
        whole,
        mesh=mesh,
        in_specs=(both, both, both, both, P(AXES), one, flat, flat, flat, flat, one, deep, deep, deep),
        out_specs=(both, both, one, flat, flat, flat, flat, one, deep, deep, deep),
        check_vma=False,
    )
```

```python
import math

import jax
import jax.numpy as jnp
from jax import lax
from jax.experimental import pallas as pl
from jax.experimental.pallas import tpu as pltpu
from jax.sharding import PartitionSpec as P

HEADS = 24
KV_HEADS = 8
HEAD = 64
EXP = 16
PIECE = 256
AXES = ("rep", "fsdp")
EPSILON = 1e-05
NEG_FILL = -1e30
BF = jnp.bfloat16
F32 = jnp.float32
PLANE = 8
EPD = EXP // PLANE


def turn_tables(length):
    positions = jnp.arange(length, dtype=F32)[:, None]
    lanes = jnp.arange(2 * HEAD)
    rates = jnp.exp((lanes % (HEAD // 2)).astype(F32) * (-2.0 * math.log(10000.0) / HEAD))
    angles = positions * rates[None, :]
    low = (lanes % HEAD < HEAD // 2)[None, :]
    sines = jnp.sin(angles)
    return jnp.stack([jnp.cos(angles), jnp.where(low, -sines, 0.0), jnp.where(low, 0.0, sines)])


def turned(values, tables, sign):
    ahead = pltpu.roll(values, 2 * HEAD - HEAD // 2, 1)
    back = pltpu.roll(values, HEAD // 2, 1)
    return values * tables[0] + sign * (ahead * tables[1] + back * tables[2])


def row_loop(rows, step, body):
    @pl.loop(0, rows // step)
    def _(n):
        body(pl.ds(pl.multiple_of(n * step, step), step))


def dot(a, b):
    return jnp.dot(a, b, preferred_element_type=F32)


def dot_nt(a, b):
    return lax.dot_general(a, b, (((1,), (1,)), ((), ())), preferred_element_type=F32)


def dot_tn(a, b):
    return lax.dot_general(a, b, (((0,), (0,)), ((), ())), preferred_element_type=F32)


def add_rows(store, terms, rows, step=32):
    step = min(step, rows)

    @pl.loop(0, rows // step)
    def _(n):
        chunk = pl.ds(pl.multiple_of(n * step, 16), step)
        total = terms[0](chunk).astype(F32)
        for term in terms[1:]:
            total = total + term(chunk).astype(F32)
        store(chunk, total)


class Links:
    def __init__(self, planes, group, send_sems, recv_sems):
        r, f = lax.axis_index("rep"), lax.axis_index("fsdp")
        self.xb, self.yb, self.c, self.z = r % 2, (f // 2) % 2, f % 2, f // 4
        self.x = (r + 1 - 2 * self.xb, f)
        self.y = (r, f + 2 - 4 * self.yb)
        self.core = (r, f + 1 - 2 * self.c)
        self.diagonal = (r, f + 3 - 4 * self.yb - 2 * self.c)
        self.others = {1: self.core, 2: self.y, 3: self.diagonal, 4: self.x}
        self.others.update({4 + n: (self.x[0], self.others[n][1]) for n in (1, 2, 3)})
        self.along = [None] + [(r, (f + 4 * k) % group) for k in range(1, planes)]
        self.planes, self.send_sems, self.recv_sems, self.copies = planes, send_sems, recv_sems, []

    def barrier(self, devices):
        semaphore = pltpu.get_barrier_semaphore()
        for device in devices:
            pl.semaphore_signal(
                semaphore, inc=1, device_id=device, device_id_type=pl.DeviceIdType.MESH
            )
        pl.semaphore_wait(semaphore, len(devices))

    def make(self, src, dst, device):
        n = len(self.copies)
        copy = pltpu.make_async_remote_copy(
            src_ref=src,
            dst_ref=dst,
            send_sem=self.send_sems.at[n],
            recv_sem=self.recv_sems.at[n],
            device_id=device,
            device_id_type=pl.DeviceIdType.MESH,
        )
        self.copies.append(copy)
        return copy

    def send(self, src, dst, device):
        copy = self.make(src, dst, device)
        copy.start()
        return copy

    def finish(self):
        for copy in self.copies:
            copy.wait_send()


def comm_params(number):
    return pltpu.CompilerParams(
        collective_id=number, has_side_effects=True, vmem_limit_bytes=56 * 2**20
    )


def dma_pairs(count):
    return [pltpu.SemaphoreType.DMA((count,)), pltpu.SemaphoreType.DMA((count,))]


def whole_vmem():
    return pl.BlockSpec(memory_space=pltpu.VMEM)


def anywhere():
    return pl.BlockSpec(memory_space=pl.ANY)


def share_of(half, share):
    return int(half * share) // 128 * 128


def both_sides(values, store, pair):
    low = lax.broadcasted_iota(jnp.int32, values.shape, 1) < HEAD
    swapped = pltpu.roll(values, HEAD, 1)
    store(0, 2 * pair, jnp.where(low, values, 0.0).astype(BF))
    store(1, 2 * pair, jnp.where(low, 0.0, swapped).astype(BF))
    store(0, 2 * pair + 1, jnp.where(low, swapped, 0.0).astype(BF))
    store(1, 2 * pair + 1, jnp.where(low, 0.0, values).astype(BF))


def fill_bias(bias, start):
    length = bias.shape[0]

    def body(chunk):
        shape = (chunk.size, length)
        i = lax.broadcasted_iota(jnp.int32, shape, 0) + chunk.start
        j = lax.broadcasted_iota(jnp.int32, shape, 1)
        in_i = (i >= start) & (i < start + PIECE)
        in_j = (j >= start) & (j < start + PIECE)
        bias[chunk] = jnp.where((j <= i) | (in_i & in_j), 0.0, NEG_FILL)

    row_loop(length, 64, body)


def softmax_rows(query, key, bias):
    scores = dot_nt(query, key) + bias
    exponent = jnp.exp(scores - jnp.max(scores, axis=1, keepdims=True))
    return exponent * (1.0 / jnp.sum(exponent, axis=1, keepdims=True))


PAIRS = HEADS // 2
GROUP = HEADS // KV_HEADS
LANES = 2 * HEAD


class FrontGather:
    def __init__(self, at, own, full, base, part, own_sem):
        self.at, self.own, self.full, self.base = at, own, full, base
        self.ds, self.half = own.shape
        self.first, self.second = (0, part), (part, self.half - part)
        self.every = (0, self.half)
        self.own_copy = pltpu.make_async_copy(own, self.region(0, 0, 0, self.every), own_sem)
        self.x_first, self.x_second, self.y_first, self.y_second, self.far = [], [], [], [], []

    def region(self, k, dx, dy, span):
        at = self.at
        row = (((at.z + at.planes - k) % at.planes) * 4 + (at.yb + dy) % 2 * 2 + at.c) * self.ds
        col = self.base + (at.xb + dx) % 2 * self.half + span[0]
        return self.full.at[
            pl.ds(pl.multiple_of(row, 16), self.ds), pl.ds(pl.multiple_of(col, 128), span[1])
        ]

    def pass_on(self, k, dx, dy, span, device):
        here = self.region(k, dx, dy, span)
        return self.at.send(here, here, device)

    def start(self):
        at = self.at
        self.own_copy.start()
        here = self.region(0, 0, 0, self.every)
        self.arrive = [None] + [at.send(self.own, here, at.along[k]) for k in range(1, at.planes)]

    def start_plane(self):
        here = self.region(0, 0, 0, self.every)
        self.to_core = [self.at.send(self.own, here, self.at.core)]
        self.spread(0)

    def spread(self, k):
        at = self.at
        for device, span, copies in (
            (at.x, self.first, self.x_first),
            (at.y, self.second, self.y_second),
            (at.x, self.second, self.x_second),
            (at.y, self.first, self.y_first),
        ):
            here = self.region(k, 0, 0, span)
            src = self.own.at[:, pl.ds(span[0], span[1])] if k == 0 else here
            copies.append(at.send(src, here, device))
        if k > 0:
            self.to_core.append(self.pass_on(k, 0, 0, self.every, at.core))

    def advance(self, k):
        self.arrive[k].wait_recv()
        self.spread(k)

    def onward(self, k):
        at = self.at
        self.x_first[k].wait_recv()
        self.far.append((k, self.first, self.pass_on(k, 1, 0, self.first, at.y)))
        self.y_second[k].wait_recv()
        self.far.append((k, self.second, self.pass_on(k, 0, 1, self.second, at.x)))
        self.x_second[k].wait_recv()
        self.to_core.append(self.pass_on(k, 1, 0, self.every, at.core))
        self.y_first[k].wait_recv()
        self.to_core.append(self.pass_on(k, 0, 1, self.every, at.core))

    def finish_far(self):
        for k, span, copy in self.far:
            copy.wait_recv()
            self.to_core.append(self.pass_on(k, 1, 1, span, self.at.core))

    def finish(self):
        for copy in self.to_core:
            copy.wait_recv()
        self.own_copy.wait()

    @staticmethod
    def copies(planes):
        return planes - 1 + planes * 11


def forward(
    starts, tokens, cotangent, own_mix, own_out, shares, w_gate, w_up, w_down, planes, group
):
    length, width = tokens.shape
    ds = own_mix.shape[0]
    hid, hs = w_gate.shape[2], w_down.shape[0]
    wide = 3 * hid
    kvd = KV_HEADS * HEAD
    mix = width + 2 * kvd
    base = 2 * own_mix.shape[1]
    columns = base + width
    row_half = length // 2
    low_rows, high_rows = pl.ds(0, row_half), pl.ds(row_half, row_half)
    tables = turn_tables(length)

    def kernel(
        starts_ref,
        x_ref,
        cot_ref,
        own_mix_ref,
        own_out_ref,
        share_ref,
        gate_hbm,
        up_hbm,
        down_hbm,
        tab_ref,
        front_out,
        wall_a,
        wall_b,
        grads_out,
        shares_out,
        gain_ref,
        q_out,
        kk_out,
        vv_out,
        att_out,
        res_out,
        n1_out,
        n2_out,
        q_ref,
        kk_ref,
        vv_ref,
        att_ref,
        res_ref,
        n1_ref,
        n2_ref,
        front,
        bias,
        packed,
        raw_in,
        raw_down,
        send_sems,
        recv_sems,
        local_sems,
        load_sems,
    ):
        at = Links(planes, group, send_sems, recv_sems)
        at.barrier(list(at.others.values()) + at.along[1:])
        walls = (wall_a, wall_b)
        shard = at.yb * 2 + at.c

        order = [(s, e) for e in range(EPD) for s in range(4)]

        def load(n):
            s, e = order[n]
            index = (at.xb * 4 + s) * EPD + e
            copies = [
                pltpu.make_async_copy(src, dst, load_sems.at[n % 2, i])
                for i, (src, dst) in enumerate(
                    (
                        (gate_hbm.at[:, index], raw_in.at[n % 2, 0]),
                        (up_hbm.at[:, index], raw_in.at[n % 2, 1]),
                        (down_hbm.at[:, index], raw_down.at[n % 2]),
                    )
                )
            ]
            for copy in copies:
                copy.start()
            return copies

        loads = {n: load(n) for n in range(2)}

        def pack(e):
            for n in range(4 * e, 4 * e + 4):
                s = order[n][0]
                for copy in loads[n]:
                    copy.wait()

                def cast(chunk, n=n, s=s):
                    packed[s, e, chunk, :hid] = raw_in[n % 2, 0, chunk].astype(BF)
                    packed[s, e, chunk, hid : 2 * hid] = raw_in[n % 2, 1, chunk].astype(BF)

                row_loop(ds, 16, cast)
                for i in range(width // hid):
                    packed[s, e, i * hs : (i + 1) * hs, 2 * hid :] = raw_down[
                        n % 2, :, i * hid : (i + 1) * hid
                    ].astype(BF)
                if n + 2 < len(order):
                    loads[n + 2] = load(n + 2)
            copy = pltpu.make_async_copy(
                packed.at[shard, e], walls[e].at[at.z, shard], local_sems.at[e]
            )
            copy.start()
            locals_.append(copy)

        locals_ = []

        def put(*pairs):
            for src, dst in pairs:
                n = len(stored)
                stored.append(pltpu.make_async_copy(src, dst, local_sems.at[7 + n]))
                stored[n].start()

        stored = []

        def exchange(e):
            copies = []
            for dy, dc, device in ((1, 0, at.y), (1, 1, at.diagonal), (0, 1, at.core)):
                target = (at.yb + dy) % 2 * 2 + (at.c + dc) % 2
                copies.append(
                    at.send(packed.at[target, e], walls[e].at[at.z, shard], device)
                )
            return copies

        ring = {}

        def ring_first(e, copies):
            sent = [
                at.send(packed.at[shard, e], walls[e].at[at.z, shard], at.along[1])
            ]
            for copy, (dy, dc) in zip(copies, ((1, 0), (1, 1), (0, 1))):
                copy.wait_recv()
                piece = walls[e].at[at.z, (at.yb + dy) % 2 * 2 + (at.c + dc) % 2]
                sent.append(at.send(piece, piece, at.along[1]))
            ring[e] = (1, sent)

        def ring_next(e):
            step, sent = ring[e]
            for copy in sent:
                copy.wait_recv()
            if step < planes - 1:
                piece = walls[e].at[(at.z + planes - step) % planes]
                ring[e] = (step + 1, [at.send(piece, piece, at.along[1])])
            else:
                ring[e] = (planes, [])

        mixing = FrontGather(
            at, own_mix_ref, front, 0, share_of(base // 2, 0.25), local_sems.at[2]
        )
        closing = FrontGather(
            at, own_out_ref, front, base, share_of(width // 2, 0.25), local_sems.at[5]
        )

        def share_slot(j):
            return shares_out.at[j // 2, :, pl.ds(j % 2 * length, length)]

        mixing.start()
        mixing.start_plane()
        closing.start()
        pack(0)
        first_exchange = exchange(0)
        place = at.xb * 4 + shard
        locals_.append(pltpu.make_async_copy(share_ref.at[place], share_slot(0), local_sems.at[6]))
        locals_[-1].start()
        got_shares = []
        for j, device in at.others.items():
            other = (
                (at.xb + j // 4) % 2 * 4 + (at.yb + j // 2 % 2) % 2 * 2 + (at.c + j % 2) % 2
            )
            got_shares.append(at.send(share_ref.at[other], share_slot(j), device))
        pack(1)
        fill_bias(bias, starts_ref[0])
        for k in range(1, planes):
            mixing.advance(k)
            mixing.onward(k - 1)
        ring_first(0, first_exchange)
        mixing.onward(planes - 1)
        mixing.finish_far()
        closing.start_plane()
        for k in range(1, planes):
            closing.advance(k)
        mixing.finish()
        def gather_start(src, out):
            def slot(j, rows=pl.ds(0, length)):
                return out.at[j, rows]

            got = {
                "x_low": at.send(src.at[low_rows], slot(4, low_rows), at.x),
                "y_high": at.send(src.at[high_rows], slot(2, high_rows), at.y),
                "x_high": at.send(src.at[high_rows], slot(4, high_rows), at.x),
                "y_low": at.send(src.at[low_rows], slot(2, low_rows), at.y),
                "core": [at.send(src, slot(1), at.core)],
            }
            return slot, got

        def gather_middle(slot, got):
            got["x_low"].wait_recv()
            got["far_low"] = at.send(slot(4, low_rows), slot(6, low_rows), at.y)
            got["core"].append(at.send(slot(4, low_rows), slot(5, low_rows), at.core))
            got["y_high"].wait_recv()
            got["far_high"] = at.send(slot(2, high_rows), slot(6, high_rows), at.x)
            got["core"].append(at.send(slot(2, high_rows), slot(3, high_rows), at.core))

        def gather_last(slot, got):
            got["x_high"].wait_recv()
            got["core"].append(at.send(slot(4, high_rows), slot(5, high_rows), at.core))
            got["y_low"].wait_recv()
            got["core"].append(at.send(slot(2, low_rows), slot(3, low_rows), at.core))
            got["far_low"].wait_recv()
            got["core"].append(at.send(slot(6, low_rows), slot(7, low_rows), at.core))
            got["far_high"].wait_recv()
            got["core"].append(at.send(slot(6, high_rows), slot(7, high_rows), at.core))

        gain_ref[...] = front[:, mix : mix + 128].astype(F32).T[:8]

        def norm(chunk):
            x = x_ref[chunk].astype(F32)
            inv = lax.rsqrt(jnp.mean(x * x, axis=1, keepdims=True) + EPSILON)
            n1_ref[chunk] = (x * inv * gain_ref[0:1, :]).astype(BF)

        row_loop(length, 64, norm)
        block = 4 * LANES
        for n in range(mix // block):
            raw = dot(n1_ref[...], front[:, n * block : (n + 1) * block])
            for j in range(4):
                col = n * block + j * LANES
                values = raw[:, j * LANES : (j + 1) * LANES]
                if col < width:
                    turned_low = turned(values, tab_ref, 1.0).astype(BF).astype(F32)
                    q_ref[:, col : col + LANES] = (turned_low * (1.0 / math.sqrt(HEAD))).astype(BF)
                else:
                    target, start = (kk_ref, width) if col < width + kvd else (vv_ref, width + kvd)
                    if col < width + kvd:
                        values = turned(values, tab_ref, 1.0)

                    def store(side, head, side_values, target=target):
                        target[side, head] = side_values

                    both_sides(values, store, (col - start) // LANES)
        ring_next(0)
        put((q_ref, q_out), (kk_ref, kk_out), (vv_ref, vv_out), (n1_ref, n1_out))
        grads = gather_start(cot_ref, grads_out)
        cot_copy = pltpu.make_async_copy(cot_ref, grads_out.at[0], local_sems.at[4])
        cot_copy.start()


        def attend(pairs):
            @pl.loop(*pairs)
            def _(p):
                cols = pl.ds(pl.multiple_of(p * LANES, LANES), LANES)
                total = None
                for side in range(2):
                    head = (2 * p + side) // GROUP
                    probs = softmax_rows(q_ref[:, cols], kk_ref[side, head], bias[...])
                    term = dot(probs.astype(BF), vv_ref[side, head])
                    total = term if total is None else total + term
                att_ref[:, cols] = total.astype(BF)

        attend((0, PAIRS // 3))
        for k in range(planes):
            closing.onward(k)
        attend((PAIRS // 3, 2 * PAIRS // 3))
        gather_middle(*grads)
        second_exchange = exchange(1)
        attend((2 * PAIRS // 3, PAIRS))
        put((att_ref, att_out))
        closing.finish_far()
        closing.finish()
        front_copy = pltpu.make_async_copy(front, front_out, local_sems.at[3])
        front_copy.start()
        ring_next(0)
        for n in range(width // block):
            cols = slice(n * block, (n + 1) * block)
            res_ref[:, cols] = x_ref[:, cols].astype(F32) + dot(
                att_ref[...], front[:, base + n * block : base + (n + 1) * block]
            )

        def norm_two(chunk):
            r = res_ref[chunk]
            inv = lax.rsqrt(jnp.mean(r * r, axis=1, keepdims=True) + EPSILON)
            n2_ref[chunk] = (r * inv * gain_ref[1:2, :]).astype(BF)

        row_loop(length, 64, norm_two)
        put((n2_ref, n2_out), (res_ref, res_out))
        gather_last(*grads)
        while ring[0][0] < planes:
            ring_next(0)
        for copy in grads[1]["core"] + second_exchange + got_shares:
            copy.wait_recv()
        for copy in locals_ + stored + [front_copy, cot_copy]:
            copy.wait()
        at.finish()

    shape = jax.ShapeDtypeStruct
    count = 2 * FrontGather.copies(planes) + 2 * 3 + 4 + planes - 2 + 13 + 7
    return pl.pallas_call(
        kernel,
        out_shape=[
            shape((width, columns), BF),
            shape((planes, 4, ds, wide), BF),
            shape((planes, 4, ds, wide), BF),
            shape((PLANE, length, width), BF),
            shape((PLANE // 2, 8, 2 * length), F32),
            shape((8, width), F32),
            shape((length, width), BF),
            shape((2, KV_HEADS, length, LANES), BF),
            shape((2, KV_HEADS, length, LANES), BF),
            shape((length, width), BF),
            shape((length, width), F32),
            shape((length, width), BF),
            shape((length, width), BF),
        ],
        in_specs=[pl.BlockSpec(memory_space=pltpu.SMEM)]
        + [whole_vmem()] * 5
        + [anywhere()] * 3
        + [whole_vmem()],
        out_specs=[anywhere()] * 5 + [whole_vmem()] + [anywhere()] * 7,
        scratch_shapes=[
            pltpu.VMEM((length, width), BF),
            pltpu.VMEM((2, KV_HEADS, length, LANES), BF),
            pltpu.VMEM((2, KV_HEADS, length, LANES), BF),
            pltpu.VMEM((length, width), BF),
            pltpu.VMEM((length, width), F32),
            pltpu.VMEM((length, width), BF),
            pltpu.VMEM((length, width), BF),
            pltpu.VMEM((width, columns), BF),
            pltpu.VMEM((length, length), F32),
            pltpu.VMEM((4, EPD, ds, wide), BF),
            pltpu.VMEM((2, 2, ds, hid), F32),
            pltpu.VMEM((2, hs, width), F32),
        ]
        + dma_pairs(count)
        + [pltpu.SemaphoreType.DMA((14,)), pltpu.SemaphoreType.DMA((2, 3))],
        compiler_params=comm_params(0),
        cost_estimate=pl.CostEstimate(
            flops=150_000_000_000, bytes_accessed=20_000_000, transcendentals=0
        ),
    )(
        starts, tokens, cotangent, own_mix, own_out, shares, w_gate, w_up, w_down, tables
    )


class PlaneSum:
    def __init__(self, at, length, odd, even, from_core, far, near):
        self.at, self.odd, self.even, self.core = at, odd, even, from_core
        self.far, self.near = far, near
        self.length = length
        self.half = self.length // 2
        self.low, self.high = pl.ds(0, self.half), pl.ds(self.half, self.half)
        self.arrive = {
            j: at.make(odd(j), self.part(j, pl.ds(0, length)), at.core) for j in (3, 2, 1, 0)
        }
        low, high = self.low, self.high
        self.far_y = at.make(self.part(3, low), far.at[0], at.y)
        self.far_x = at.make(self.part(3, high), far.at[1], at.x)
        self.x_high = at.make(self.part(2, high), near.at[0, high], at.x)
        self.y_low = at.make(self.part(1, low), near.at[1, low], at.y)
        self.x_low = at.make(self.part(2, low), near.at[0, low], at.x)
        self.y_high = at.make(self.part(1, high), near.at[1, high], at.y)

    def rows(self, j, chunk, base=0):
        return pl.ds(pl.multiple_of(chunk.start + j * self.length + base, 16), chunk.size)

    def part(self, j, rows):
        return self.core.at[pl.ds(j * self.length + rows.start, rows.size)]

    def start(self, j):
        self.arrive[j].start()

    def add_core(self, j):
        self.arrive[j].wait_recv()
        core = self.core

        def store(chunk, total):
            core[self.rows(j, chunk)] = total.astype(BF)

        add_rows(store, [lambda q: self.even(j, q), lambda q: core[self.rows(j, q)]], self.length)

    def add_far(self, j, n, base):
        core, far = self.core, self.far

        def store(chunk, total):
            core[self.rows(j, chunk, base)] = total.astype(BF)

        add_rows(store, [lambda q: core[self.rows(j, q, base)], lambda q: far[n, q]], self.half)

    def send_far(self):
        self.add_core(3)
        self.far_y.start()
        self.far_x.start()

    def send_x(self):
        self.add_core(2)
        self.x_high.start()

    def send_y(self):
        self.add_core(1)
        self.y_low.start()

    def onward_x(self):
        self.far_y.wait_recv()
        self.add_far(2, 0, 0)
        self.x_low.start()

    def onward_y(self):
        self.far_x.wait_recv()
        self.add_far(1, 1, self.half)
        self.y_high.start()

    def end(self, store):
        self.arrive[0].wait_recv()
        for copy in (self.x_high, self.y_low, self.x_low, self.y_high):
            copy.wait_recv()
        core, near = self.core, self.near
        terms = [lambda q: self.even(0, q), lambda q: core[q]]
        terms += [lambda q: near[0, q], lambda q: near[1, q]]
        add_rows(store, terms, self.length)

    copies = 10


class RingSum:
    def __init__(self, at, pack, own, own_sem):
        self.at, self.pack, self.own, self.own_sem = at, pack, own, own_sem
        self.index = [(at.z + at.planes - k) % at.planes for k in range(at.planes)]

    def block(self, k):
        return self.pack.at[self.index[k]]

    def fetch(self, k):
        self.fetched = pltpu.make_async_copy(self.block(k), self.own, self.own_sem)
        self.fetched.start()

    def add(self, source, target):
        self.fetched.wait()

        def store(chunk, total):
            target[chunk] = total.astype(BF)

        add_rows(store, [lambda q: source[q], lambda q: self.own[q]], self.own.shape[0], 16)

    def first(self, slots):
        self.slots, self.step = slots, 1
        sources = [self.block(1)] + slots[:-1]
        self.sent = [
            self.at.make(src, dst, self.at.along[1]) for src, dst in zip(sources, slots)
        ]
        self.fetches = {
            k: pltpu.make_async_copy(self.block(k), self.own, self.own_sem)
            for k in range(2, len(slots) + 1)
        }
        self.sent[0].start()
        self.begin_fetch(2)

    def begin_fetch(self, k):
        if k in self.fetches:
            self.fetched = self.fetches[k]
            self.fetched.start()

    def next(self):
        if self.step < len(self.slots):
            here = self.slots[self.step - 1]
            self.sent[self.step - 1].wait_recv()
            self.add(here, here)
            self.sent[self.step].start()
            self.step += 1
            self.begin_fetch(self.step + 1)

    def rest(self):
        while self.step < len(self.slots):
            self.next()
        self.sent[-1].wait_recv()

    def last(self, before, sent, landing):
        self.add(before, sent)
        self.landing = landing
        self.copy = self.at.send(sent, landing, self.at.along[1])
        self.fetch(0)

    def total(self):
        self.copy.wait_recv()
        self.add(self.landing, self.landing)
        return self.landing


def run_experts(tokens, grads, shares, wall_a, wall_b, planes, group):
    pairs, count, width = grads.shape
    length = count // 2
    piece, wide = wall_a.shape[1:]
    hid = wide // 3
    ds, hs, blocks = width // group, hid // group, width // hid
    half = length // 2
    low, high, full = pl.ds(0, half), pl.ds(half, half), pl.ds(0, length)

    def kernel(
        n2_hbm,
        g_hbm,
        share_ref,
        wall_a_ref,
        wall_b_ref,
        out_hbm,
        pack_a,
        pack_b,
        sum_ref,
        passed,
        xs,
        dxs,
        w_a,
        w_b,
        down_a,
        down_b,
        in_sum,
        down_sum,
        g_tile,
        o_tile,
        pre,
        act,
        far,
        near,
        ring_slots,
        own,
        free,
        send_sems,
        recv_sems,
        local_sems,
    ):
        at = Links(planes, group, send_sems, recv_sems)
        at.barrier([at.x, at.y, at.core] + at.along[1:])
        index = [(at.z + planes - k) % planes for k in range(planes)]

        def local(src, dst, n):
            copy = pltpu.make_async_copy(src, dst, local_sems.at[n])
            copy.start()
            return copy

        def slot(j, rows=full):
            return xs.at[j // 2, pl.ds(j % 2 * length + rows.start, rows.size)]

        pieces = [
            w_b.at[pl.ds(pl.multiple_of(index[k] * piece, 16), piece)] for k in range(planes)
        ]

        local(n2_hbm, slot(0), 0).wait()
        x_low = at.send(slot(0, low), slot(4, low), at.x)
        y_high = at.send(slot(0, high), slot(2, high), at.y)
        x_high = at.send(slot(0, high), slot(4, high), at.x)
        y_low = at.send(slot(0, low), slot(2, low), at.y)
        near_core = at.send(slot(0), slot(1), at.core)
        ring = [at.make(wall_b_ref.at[at.z], pieces[0], at.along[1])]
        ring += [at.make(piece_ref, piece_ref, at.along[1]) for piece_ref in pieces[1:-1]]
        ring[0].start()
        load_b = local(wall_b_ref.at[at.z], pieces[0], 1)
        loads = [
            local(wall_a_ref.at[n], w_a.at[pl.ds(n * piece, piece)], 2 + n) for n in range(planes)
        ]
        state = {"ring": 0}
        far_low = at.make(slot(4, low), slot(6, low), at.y)
        far_high = at.make(slot(2, high), slot(6, high), at.x)
        passed_on = {
            (j, rows.start): at.make(slot(j, rows), slot(j + 1, rows), at.core)
            for j in (4, 2, 6)
            for rows in (low, high)
        }

        def ring_next():
            ring[state["ring"]].wait_recv()
            state["ring"] += 1
            if state["ring"] < planes - 1:
                ring[state["ring"]].start()

        def core_arrival(j):
            passed_on[j, low.start].wait_recv()
            passed_on[j, high.start].wait_recv()

        def spread():
            x_low.wait_recv()
            far_low.start()
            passed_on[4, low.start].start()
            y_high.wait_recv()
            far_high.start()
            passed_on[2, high.start].start()
            ring_next()
            x_high.wait_recv()
            passed_on[4, high.start].start()
            y_low.wait_recv()
            passed_on[2, low.start].start()
            core_arrival(4)

        def spread_far():
            far_low.wait_recv()
            passed_on[6, low.start].start()
            far_high.wait_recv()
            passed_on[6, high.start].start()
            core_arrival(6)

        def unpack_down(w, down):
            for s in range(group):
                for b in range(blocks):
                    down[s * hs : (s + 1) * hs, b * hid : (b + 1) * hid] = w[
                        s * ds + b * hs : s * ds + (b + 1) * hs, 2 * hid :
                    ]

        def clear():
            def body(chunk):
                in_sum[chunk] = jnp.zeros((chunk.size, 2 * hid), F32)

            row_loop(width, 64, body)

            def body_down(chunk):
                down_sum[chunk] = jnp.zeros((chunk.size, width), F32)

            row_loop(hid, 64, body_down)

        def out_copy(pair):
            return pltpu.make_async_copy(o_tile, out_hbm.at[pair], local_sems.at[0])

        def tile(e, step, pair, w, down, middle):
            g_load = pltpu.make_async_copy(g_hbm.at[pair], g_tile, local_sems.at[1])
            g_load.start()
            x = xs.at[pair]
            share = share_ref[pair].T[:, e : e + 1]
            part = hid // 2
            for n in range(2):
                cols = slice(n * part, (n + 1) * part)
                up_cols = slice(hid + n * part, hid + (n + 1) * part)
                gate = dot(x[...], w[:, cols])
                up = dot(x[...], w[:, up_cols])
                if n == 0:
                    g_load.wait()
                inner = dot_nt(g_tile[...], down[cols, :]) * share
                sig = jax.nn.sigmoid(gate)
                swish = gate * sig
                act[:, cols] = (share * (swish * up)).astype(BF)
                pre[:, cols] = (inner * up * sig * (1.0 + gate * (1.0 - sig))).astype(BF)
                pre[:, up_cols] = (inner * swish).astype(BF)
            middle()

            @pl.when(step > 0)
            def _():
                out_copy(pair).wait()

            if e > 0:
                before = pltpu.make_async_copy(out_hbm.at[pair], o_tile, local_sems.at[2])
                before.start()
                before.wait()
            for n in range(width // hid):
                cols = slice(n * hid, (n + 1) * hid)
                out = dot(act[...], down[:, cols])
                dx = dot_nt(pre[...], w[cols, : 2 * hid])
                if e > 0:
                    out = out + o_tile[:, cols].astype(F32)
                    dx = dx + dxs[pair, :, cols].astype(F32)
                o_tile[:, cols] = out.astype(BF)
                dxs[pair, :, cols] = dx.astype(BF)
                in_sum[cols, :] += dot_tn(x[:, cols], pre[...])
                down_sum[:, cols] += dot_tn(act[...], g_tile[:, cols])
            out_copy(pair).start()

        def pack(target):
            out_copy(0).wait()
            copies = [None, None]
            for n in range(planes):
                base = n % 2 * piece
                if copies[n % 2] is not None:
                    copies[n % 2].wait()

                def body(chunk, n=n, base=base):
                    rows = pl.ds(pl.multiple_of(chunk.start + base, 16), chunk.size)
                    source = pl.ds(pl.multiple_of(chunk.start + n * piece, 16), chunk.size)
                    o_tile[rows, : 2 * hid] = in_sum[source].astype(BF)

                row_loop(piece, 32, body)
                for s in range(4):
                    for b in range(blocks):
                        row = base + s * ds + b * hs
                        o_tile[row : row + hs, 2 * hid :] = down_sum[
                            (n * 4 + s) * hs : (n * 4 + s + 1) * hs, b * hid : (b + 1) * hid
                        ].astype(BF)
                copies[n % 2] = local(o_tile.at[pl.ds(base, piece)], target.at[n], 3 + n % 2)
            for copy in copies:
                copy.wait()

        clear()
        for copy in loads:
            copy.wait()
        load_b.wait()
        unpack_down(w_a, down_a)
        near_core.wait_recv()

        @pl.loop(0, pairs)
        def _(step):
            @pl.when(step == 1)
            def _():
                spread()

            @pl.when(step == 2)
            def _():
                core_arrival(2)

            @pl.when(step == 3)
            def _():
                spread_far()

            def middle():
                @pl.when(step == 2)
                def _():
                    ring_next()

            tile(0, step, 2 * step % 3 + step // 3 * 3, w_a, down_a, middle)

        pl.semaphore_signal(free, inc=1, device_id=at.core, device_id_type=pl.DeviceIdType.MESH)
        pack(pack_a)
        sums = RingSum(at, pack_a, own, local_sems.at[5])
        sums.first([ring_slots.at[n] for n in range(planes - 3)] + [passed])
        clear()
        while state["ring"] < planes - 1:
            ring_next()
        unpack_down(w_b, down_b)
        pl.semaphore_wait(free, 1)
        plane = PlaneSum(
            at,
            length,
            lambda j: dxs.at[j, pl.ds(length, length)],
            lambda j, q: dxs[j, q],
            w_a,
            far,
            near,
        )

        @pl.loop(0, pairs)
        def _(step):
            def middle():
                @pl.when(step == 1)
                def _():
                    plane.send_far()

                @pl.when(step == 2)
                def _():
                    plane.send_x()
                    sums.next()

                @pl.when(step == 3)
                def _():
                    plane.send_y()
                    plane.onward_y()

            tile(1, step, pairs - 1 - step, w_b, down_b, middle)
            for n in range(pairs):

                @pl.when(step == n)
                def _(n=n):
                    plane.start(pairs - 1 - n)
                    if n == 2:
                        plane.onward_x()

        pack(pack_b)

        def store(chunk, total):
            sum_ref[chunk] = total

        plane.end(store)
        sums.rest()
        at.finish()

    shape = jax.ShapeDtypeStruct
    return pl.pallas_call(
        kernel,
        in_specs=[anywhere()] * 2 + [whole_vmem()] + [anywhere()] * 2,
        out_specs=[anywhere()] * 3 + [whole_vmem()] * 2,
        out_shape=[
            shape((pairs, count, width), BF),
            shape((planes, piece, wide), BF),
            shape((planes, piece, wide), BF),
            shape((length, width), F32),
            shape((piece, wide), BF),
        ],
        scratch_shapes=[
            pltpu.VMEM((pairs, count, width), BF),
            pltpu.VMEM((pairs, count, width), BF),
            pltpu.VMEM((width, wide), BF),
            pltpu.VMEM((width, wide), BF),
            pltpu.VMEM((hid, width), BF),
            pltpu.VMEM((hid, width), BF),
            pltpu.VMEM((width, 2 * hid), F32),
            pltpu.VMEM((hid, width), F32),
            pltpu.VMEM((count, width), BF),
            pltpu.VMEM((count, width), BF),
            pltpu.VMEM((count, 2 * hid), BF),
            pltpu.VMEM((count, hid), BF),
            pltpu.VMEM((2, half, width), BF),
            pltpu.VMEM((2, length, width), BF),
            pltpu.VMEM((planes - 3, piece, wide), BF),
            pltpu.VMEM((piece, wide), BF),
            pltpu.SemaphoreType.REGULAR,
        ]
        + dma_pairs(13 + planes - 1 + PlaneSum.copies + planes - 2)
        + [pltpu.SemaphoreType.DMA((2 + planes,))],
        compiler_params=pltpu.CompilerParams(
            collective_id=2, has_side_effects=True, vmem_limit_bytes=63 * 2**20
        ),
        cost_estimate=pl.CostEstimate(
            flops=100_000_000_000, bytes_accessed=50_000_000, transcendentals=0
        ),
    )(tokens, grads, shares, wall_a, wall_b)


class Exchange:
    def __init__(self, at, total, out, ds):
        self.at, self.total, self.out, self.ds = at, total, out, ds
        self.shard = at.yb * 2 + at.c

    def place(self, dx, dy, dc):
        at = self.at
        return (at.xb + dx) % 2 * 4 + (at.yb + dy) % 2 * 2 + (at.c + dc) % 2

    def rows(self, dy, dc):
        at = self.at
        shard = (at.yb + dy) % 2 * 2 + (at.c + dc) % 2
        return self.total.at[pl.ds(pl.multiple_of(shard * self.ds, 16), self.ds)]

    def start(self, sem):
        at = self.at
        here = self.out.at[self.place(0, 0, 0)]
        self.local = pltpu.make_async_copy(self.rows(0, 0), here, sem)
        self.local.start()
        self.got = [
            (dy, dc, at.send(self.rows(dy, dc), here, device))
            for dy, dc, device in ((1, 0, at.y), (1, 1, at.diagonal), (0, 1, at.core))
        ]
        self.across = [at.send(self.rows(0, 0), here, at.x)]

    def onward(self):
        at = self.at
        for dy, dc, copy in self.got:
            copy.wait_recv()
            piece = self.out.at[self.place(0, dy, dc)]
            self.across.append(at.send(piece, piece, at.x))

    def end(self):
        for copy in self.across:
            copy.wait_recv()
        self.local.wait()

    copies = 7


def backward(
    starts,
    grad_two,
    cotangent,
    tokens,
    residual,
    front,
    gains,
    q,
    kk,
    vv,
    att,
    n1,
    outs,
    pack_a,
    before_a,
    pack_b,
    planes,
    group,
):
    length, width = tokens.shape
    columns = front.shape[1]
    kvd = KV_HEADS * HEAD
    mix = width + 2 * kvd
    block = 4 * LANES
    tables = turn_tables(length)
    piece, wide = pack_a.shape[1:]
    ds = piece // 4
    extra = columns - mix - width
    part = block // 2

    def kernel(
        starts_ref,
        d_ref,
        cot_ref,
        tab_ref,
        gain_ref,
        before_ref,
        q_hbm,
        kk_hbm,
        vv_hbm,
        att_hbm,
        x_hbm,
        n1_hbm,
        res_hbm,
        w_hbm,
        outs_ref,
        pack_a_ref,
        pack_b_ref,
        in_ref,
        sum_ref,
        passed_b,
        grad_hbm,
        shards_ref,
        q_ref,
        kk_ref,
        vv_ref,
        att_ref,
        bias,
        gain_sum,
        mixed,
        context,
        grad_mix,
        key_sum,
        value_sum,
        w_ref,
        stage,
        even,
        from_core,
        far,
        near,
        own_a,
        sent_a,
        landing_a,
        own_b,
        slots_b,
        send_sems,
        recv_sems,
        local_sems,
    ):
        at = Links(planes, group, send_sems, recv_sems)
        at.barrier([at.x, at.y, at.core, at.diagonal] + at.along[1:])

        def local(src, dst, n):
            copy = pltpu.make_async_copy(src, dst, local_sems.at[n])
            copy.start()
            return copy

        load_res = local(res_hbm, in_ref, 0)
        load_att = local(att_hbm, att_ref, 12)
        load_heads = [
            local(src, dst, 13 + n)
            for n, (src, dst) in enumerate(((q_hbm, q_ref), (kk_hbm, kk_ref), (vv_hbm, vv_ref)))
        ]
        load_out_w = local(
            w_hbm.at[:, pl.ds(mix + extra, width)], w_ref.at[:, pl.ds(0, width)], 1
        )
        plane = PlaneSum(
            at,
            length,
            lambda j: outs_ref.at[2 * j + 1],
            lambda j, q: even[j, q],
            from_core,
            far,
            near,
        )
        for j in (3, 2, 1, 0):
            plane.start(j)
        ring_a = RingSum(at, pack_a_ref, own_a, local_sems.at[6])
        ring_b = RingSum(at, pack_b_ref, own_b, local_sems.at[7])
        ring_a.fetch(planes - 1)
        loads = [local(outs_ref.at[2 * j], even.at[j], 2 + j) for j in range(4)]
        ring_a.last(before_ref, sent_a, landing_a)
        ring_b.first([slots_b.at[n] for n in range(planes - 3)] + [passed_b])
        staged = [None, None]
        turn = [0]

        def put(values, column, count):
            for base in range(0, count, part):
                n = turn[0] % 2
                turn[0] += 1
                if staged[n] is not None:
                    staged[n].wait()
                stage[n] = values[:, base : base + part]
                staged[n] = local(
                    stage.at[n], grad_hbm.at[:, pl.ds(column + base, part)], 8 + n
                )

        fill_bias(bias, starts_ref[0])
        gain_sum[...] = jnp.zeros_like(gain_sum)

        load_res.wait()

        def residual_grad(chunk):
            d, r = d_ref[chunk], in_ref[chunk]
            inv = lax.rsqrt(jnp.mean(r * r, axis=1, keepdims=True) + EPSILON)
            scaled = d * gain_ref[1:2, :]
            grad = (
                cot_ref[chunk].astype(F32)
                + inv * scaled
                - r * (inv * inv * inv * jnp.mean(scaled * r, axis=1, keepdims=True))
            )
            sum_ref[chunk] = grad
            mixed[chunk] = grad.astype(BF)
            gain_sum[1:2, :] += jnp.sum(d * r * inv, axis=0, keepdims=True)

        row_loop(length, 32, residual_grad)
        load_out_w.wait()
        for n in range(width // block):
            cols = slice(n * block, (n + 1) * block)
            context[:, cols] = dot_nt(mixed[...], w_ref[cols, :width]).astype(BF)
        load_mix_w = local(w_hbm.at[:, pl.ds(0, mix)], w_ref, 1)
        load_att.wait()
        for n in range(width // block):
            cols = slice(n * block, (n + 1) * block)
            put(dot_tn(att_ref[...], mixed[:, cols]).astype(BF), mix + extra + n * block, block)
        load_n1 = local(n1_hbm, mixed, 0)
        for copy in loads:
            copy.wait()
        plane.send_far()
        plane.send_x()
        plane.send_y()
        key_sum[...] = jnp.zeros_like(key_sum)
        value_sum[...] = jnp.zeros_like(value_sum)

        def attend(lower, upper):
            @pl.loop(lower, upper)
            def _(p):
                cols = pl.ds(pl.multiple_of(p * LANES, LANES), LANES)
                total = None
                for side in range(2):
                    head = (2 * p + side) // GROUP
                    query, grad = q_ref[:, cols], context[:, cols]
                    probs = softmax_rows(query, kk_ref[side, head], bias[...])
                    grad_probs = dot_nt(grad, vv_ref[side, head])
                    value_sum[side, head] += dot_tn(probs.astype(BF), grad)
                    inner = jnp.sum(probs * grad_probs, axis=1, keepdims=True)
                    logit = (probs * (grad_probs - inner)).astype(BF)
                    term = dot(logit, kk_ref[side, head])
                    total = term if total is None else total + term
                    key_sum[side, head] += dot_tn(logit, query)
                back = turned(total, tab_ref, -1.0) * (1.0 / math.sqrt(HEAD))
                grad_mix[:, cols] = back.astype(BF)

        for copy in load_heads:
            copy.wait()
        attend(0, PAIRS // 3)
        plane.onward_x()
        plane.onward_y()
        exchange = Exchange(at, ring_a.total(), shards_ref, ds)
        exchange.start(local_sems.at[10])
        attend(PAIRS // 3, 2 * PAIRS // 3)
        ring_b.next()
        exchange.onward()
        attend(2 * PAIRS // 3, PAIRS)
        load_x = local(x_hbm, context, 11)
        load_n1.wait()
        for pair in range(KV_HEADS // 2):
            for sums, base in ((key_sum, width), (value_sum, width + kvd)):

                def join(chunk, pair=pair, sums=sums, base=base):
                    low = lax.broadcasted_iota(jnp.int32, (chunk.size, LANES), 1) < HEAD
                    even = sums[0, 2 * pair, chunk] + pltpu.roll(sums[1, 2 * pair, chunk], HEAD, 1)
                    odd = sums[1, 2 * pair + 1, chunk] + pltpu.roll(
                        sums[0, 2 * pair + 1, chunk], HEAD, 1
                    )
                    values = jnp.where(low, even, odd)
                    if base == width:
                        values = turned(values, tab_ref.at[:, chunk], -1.0)
                    grad_mix[chunk, base + pair * LANES : base + (pair + 1) * LANES] = values.astype(BF)

                row_loop(length, 64, join)
        for n in range(mix // block):
            cols = slice(n * block, (n + 1) * block)
            put(dot_tn(mixed[...], grad_mix[:, cols]).astype(BF), n * block, block)
        load_mix_w.wait()
        for n in range(width // block):
            cols = slice(n * block, (n + 1) * block)
            in_ref[:, cols] = dot_nt(grad_mix[...], w_ref[cols, :mix])

        load_x.wait()

        def input_grad(chunk):
            d, x = in_ref[chunk], context[chunk].astype(F32)
            inv = lax.rsqrt(jnp.mean(x * x, axis=1, keepdims=True) + EPSILON)
            scaled = d * gain_ref[0:1, :]
            gain_sum[0:1, :] += jnp.sum(d * x * inv, axis=0, keepdims=True)
            in_ref[chunk] = (
                sum_ref[chunk]
                + inv * scaled
                - x * (inv * inv * inv * jnp.mean(scaled * x, axis=1, keepdims=True))
            )

        row_loop(length, 32, input_grad)
        gain_rows = jnp.concatenate([gain_sum[...].T, jnp.zeros((width, extra - 8), F32)], axis=1)
        put(gain_rows.astype(BF), mix, extra)

        def store(chunk, total):
            sum_ref[chunk] = total

        plane.end(store)
        ring_b.rest()
        exchange.end()
        for copy in staged:
            copy.wait()
        at.finish()

    shape = jax.ShapeDtypeStruct
    return pl.pallas_call(
        kernel,
        in_specs=[pl.BlockSpec(memory_space=pltpu.SMEM)]
        + [whole_vmem()] * 5
        + [anywhere()] * 11,
        out_specs=[whole_vmem()] * 3 + [anywhere()] * 2,
        out_shape=[
            shape((length, width), F32),
            shape((length, width), F32),
            shape((piece, wide), BF),
            shape((width, columns), BF),
            shape((PLANE, ds, wide), BF),
        ],
        scratch_shapes=[
            pltpu.VMEM((length, width), BF),
            pltpu.VMEM((2, KV_HEADS, length, LANES), BF),
            pltpu.VMEM((2, KV_HEADS, length, LANES), BF),
            pltpu.VMEM((length, width), BF),
            pltpu.VMEM((length, length), F32),
            pltpu.VMEM((8, width), F32),
            pltpu.VMEM((length, width), BF),
            pltpu.VMEM((length, width), BF),
            pltpu.VMEM((length, mix), BF),
            pltpu.VMEM((2, KV_HEADS, length, LANES), F32),
            pltpu.VMEM((2, KV_HEADS, length, LANES), F32),
            pltpu.VMEM((width, mix), BF),
            pltpu.VMEM((2, width, part), BF),
            pltpu.VMEM((4, length, width), BF),
            pltpu.VMEM((4 * length, width), BF),
            pltpu.VMEM((2, length // 2, width), BF),
            pltpu.VMEM((2, length, width), BF),
            pltpu.VMEM((piece, wide), BF),
            pltpu.VMEM((piece, wide), BF),
            pltpu.VMEM((piece, wide), BF),
            pltpu.VMEM((piece, wide), BF),
            pltpu.VMEM((planes - 3, piece, wide), BF),
        ]
        + dma_pairs(PlaneSum.copies + 1 + Exchange.copies + planes - 2)
        + [pltpu.SemaphoreType.DMA((16,))],
        compiler_params=pltpu.CompilerParams(
            collective_id=1, has_side_effects=True, vmem_limit_bytes=62 * 2**20
        ),
        cost_estimate=pl.CostEstimate(
            flops=80_000_000_000, bytes_accessed=50_000_000, transcendentals=0
        ),
    )(
        starts,
        grad_two,
        cotangent,
        tables,
        gains,
        before_a,
        q,
        kk,
        vv,
        att,
        tokens,
        n1,
        residual,
        front,
        outs,
        pack_a,
        pack_b,
    )


def scatter_front(grad, pack, before, planes, group):
    rows, columns = grad.shape
    ds, half = rows // (4 * planes), columns // 2
    part = share_of(half, 0.66)
    first, second = pl.ds(0, part), pl.ds(part, half - part)
    block, wide = pack.shape[1:]

    def kernel(
        g_ref,
        pack_ref,
        before_ref,
        out_ref,
        shards_ref,
        from_core,
        kept,
        far_a,
        far_b,
        near_x,
        near_y,
        total_ref,
        from_z,
        own,
        passed,
        landing,
        rows_own,
        send_sems,
        recv_sems,
        local_sems,
    ):
        at = Links(planes, group, send_sems, recv_sems)
        at.barrier([at.x, at.y, at.core, at.diagonal] + at.along[1:])
        ring = RingSum(at, pack_ref, own, local_sems.at[0])
        ring.fetch(planes - 1)

        def row(k, dy, core):
            owner = ((at.z + k) % planes) * 4 + (at.yb + dy) % 2 * 2 + core
            return pl.multiple_of(owner * ds, 16)

        def column(dx):
            return pl.ds(pl.multiple_of((at.xb + dx) % 2 * half, 128), half)

        order = list(range(1, planes)) + [0]
        arrive, loads = {}, {}
        for k in order:
            for dy in (1, 0):
                loads[k, dy] = pltpu.make_async_copy(
                    g_ref.at[pl.ds(row(k, dy, at.c), ds)],
                    rows_own.at[k, dy],
                    local_sems.at[2 + 2 * k + dy],
                )
                loads[k, dy].start()
                arrive[k, dy] = at.send(
                    g_ref.at[pl.ds(row(k, dy, 1 - at.c), ds)], from_core.at[k, dy], at.core
                )
        ring.last(before_ref, passed, landing)
        step = 16
        x_second, y_first, x_first, y_second, to_x, to_y = {}, {}, {}, {}, {}, {}
        for k in order:
            for dy in (1, 0):
                loads[k, dy].wait()
                arrive[k, dy].wait_recv()
                for dx in (1, 0):

                    def store(chunk, total, k=k, dx=dx, dy=dy):
                        kept[k, dx, dy, chunk] = total.astype(BF)

                    add_rows(
                        store,
                        [
                            lambda q, k=k, dx=dx, dy=dy: rows_own[k, dy, q, column(dx)],
                            lambda q, k=k, dx=dx, dy=dy: from_core[k, dy, q, column(dx)],
                        ],
                        ds,
                        step,
                    )
                    if (dx, dy) == (1, 1):
                        to_y[k] = at.send(kept.at[k, 1, 1, :, first], far_a.at[k], at.y)
                        to_x[k] = at.send(kept.at[k, 1, 1, :, second], far_b.at[k], at.x)
                    elif (dx, dy) == (0, 1):
                        y_first[k] = at.send(
                            kept.at[k, 0, 1, :, first], near_y.at[k, :, first], at.y
                        )
                    elif (dx, dy) == (1, 0):
                        x_second[k] = at.send(
                            kept.at[k, 1, 0, :, second], near_x.at[k, :, second], at.x
                        )
        for k in order:
            to_y[k].wait_recv()

            def store(chunk, total, k=k):
                kept[k, 1, 0, chunk, first] = total.astype(BF)

            add_rows(
                store,
                [lambda q, k=k: kept[k, 1, 0, q, first], lambda q, k=k: far_a[k, q]],
                ds,
                step,
            )
            x_first[k] = at.send(kept.at[k, 1, 0, :, first], near_x.at[k, :, first], at.x)
            to_x[k].wait_recv()

            def store(chunk, total, k=k):
                kept[k, 0, 1, chunk, second] = total.astype(BF)

            add_rows(
                store,
                [lambda q, k=k: kept[k, 0, 1, q, second], lambda q, k=k: far_b[k, q]],
                ds,
                step,
            )
            y_second[k] = at.send(kept.at[k, 0, 1, :, second], near_y.at[k, :, second], at.y)
        exchange = Exchange(at, ring.total(), shards_ref, ds)
        exchange.start(local_sems.at[1])
        arrive_z = {}
        for k in order:
            for copies in (x_second, y_first, x_first, y_second):
                copies[k].wait_recv()

            def store(chunk, total, k=k):
                total_ref[k, chunk] = total.astype(BF)

            add_rows(
                store,
                [
                    lambda q, k=k: kept[k, 0, 0, q],
                    lambda q, k=k: near_x[k, q],
                    lambda q, k=k: near_y[k, q],
                ],
                ds,
                step,
            )
            if k > 0:
                arrive_z[k] = at.send(total_ref.at[k], from_z.at[k], at.along[k])
        exchange.onward()
        for k in range(1, planes):
            arrive_z[k].wait_recv()

        def store(chunk, total):
            out_ref[chunk] = total.astype(BF)

        add_rows(
            store,
            [lambda q: total_ref[0, q]]
            + [lambda q, k=k: from_z[k, q] for k in range(1, planes)],
            ds,
            step,
        )
        exchange.end()
        at.finish()

    return pl.pallas_call(
        kernel,
        out_shape=[
            jax.ShapeDtypeStruct((ds, half), BF),
            jax.ShapeDtypeStruct((PLANE, ds, wide), BF),
        ],
        in_specs=[anywhere(), anywhere(), whole_vmem()],
        out_specs=[whole_vmem(), anywhere()],
        scratch_shapes=[
            pltpu.VMEM((planes, 2, ds, columns), BF),
            pltpu.VMEM((planes, 2, 2, ds, half), BF),
            pltpu.VMEM((planes, ds, part), BF),
            pltpu.VMEM((planes, ds, half - part), BF),
            pltpu.VMEM((planes, ds, half), BF),
            pltpu.VMEM((planes, ds, half), BF),
            pltpu.VMEM((planes, ds, half), BF),
            pltpu.VMEM((planes, ds, half), BF),
            pltpu.VMEM((block, wide), BF),
            pltpu.VMEM((block, wide), BF),
            pltpu.VMEM((block, wide), BF),
            pltpu.VMEM((planes, 2, ds, columns), BF),
        ]
        + dma_pairs(planes * 8 + planes - 1 + 1 + Exchange.copies)
        + [pltpu.SemaphoreType.DMA((2 + 2 * planes,))],
        compiler_params=comm_params(3),
        cost_estimate=pl.CostEstimate(
            flops=50_000_000_000, bytes_accessed=20_000_000, transcendentals=0
        ),
    )(grad, pack, before)


def unpack(packs, residual, term, hs):
    ds, wide = packs[0].shape[1:]
    hid = wide // 3
    blocks = ds // hs

    def kernel(*refs):
        sources = refs[: EPD + 2]
        gate_out, up_out, down_out, sum_ref, raw_in, raw_down = refs[EPD + 2 : EPD + 8]
        held, (sems, load_sems) = refs[EPD + 8 : -2], refs[-2:]
        ins, (res_ref, term_ref) = held[:EPD], held[EPD:]
        loads = [
            pltpu.make_async_copy(src, dst, load_sems.at[n])
            for n, (src, dst) in enumerate(zip(sources, held))
        ]
        for copy in loads:
            copy.start()
        copies = {}
        for n, (e, p) in enumerate((e, p) for e in range(EPD) for p in range(PLANE)):
            slot = n % 4
            if p == 0:
                loads[e].wait()
            if n >= 4:
                for copy in copies[n - 4]:
                    copy.wait()

            def cast(chunk, p=p, e=e, slot=slot):
                raw_in[slot, 0, chunk] = ins[e][p, chunk, :hid].astype(F32)
                raw_in[slot, 1, chunk] = ins[e][p, chunk, hid : 2 * hid].astype(F32)

            row_loop(ds, 16, cast)
            for b in range(blocks):
                raw_down[slot, :, b * hid : (b + 1) * hid] = ins[e][
                    p, b * hs : (b + 1) * hs, 2 * hid :
                ].astype(F32)
            index = p * EPD + e
            copies[n] = [
                pltpu.make_async_copy(src, dst, sems.at[slot, i])
                for i, (src, dst) in enumerate(
                    (
                        (raw_in.at[slot, 0], gate_out.at[:, index]),
                        (raw_in.at[slot, 1], up_out.at[:, index]),
                        (raw_down.at[slot], down_out.at[:, index]),
                    )
                )
            ]
            for copy in copies[n]:
                copy.start()

        def add(chunk):
            sum_ref[chunk] = res_ref[chunk] + term_ref[chunk]

        for copy in loads[EPD:]:
            copy.wait()
        row_loop(residual.shape[0], 32, add)
        for n in range(EXP - 4, EXP):
            for copy in copies[n]:
                copy.wait()

    shape = jax.ShapeDtypeStruct
    return pl.pallas_call(
        kernel,
        in_specs=[anywhere()] * (EPD + 2),
        out_specs=[anywhere()] * 3 + [whole_vmem()],
        out_shape=[
            shape((ds, EXP, hid), F32),
            shape((ds, EXP, hid), F32),
            shape((hs, EXP, blocks * hid), F32),
            shape(residual.shape, F32),
        ],
        scratch_shapes=[
            pltpu.VMEM((4, 2, ds, hid), F32),
            pltpu.VMEM((4, hs, blocks * hid), F32),
        ]
        + [pltpu.VMEM(packs[0].shape, BF)] * EPD
        + [pltpu.VMEM(residual.shape, F32)] * 2
        + [pltpu.SemaphoreType.DMA((4, 3)), pltpu.SemaphoreType.DMA((EPD + 2,))],
        compiler_params=pltpu.CompilerParams(vmem_limit_bytes=60 * 2**20),
    )(*packs, residual, term)


def shards(
    reps,
    group,
    tokens,
    cotangent,
    routes,
    gates,
    starts,
    norm1_gain,
    w_query,
    w_key,
    w_value,
    w_out,
    norm2_gain,
    w_gate,
    w_up,
    w_down,
):
    planes = group // 4
    r, f = lax.axis_index("rep"), lax.axis_index("fsdp")
    xb, yb, c, z = r % 2, (f // 2) % 2, f % 2, f // 4
    mine = xb * 4 + yb * 2 + c

    def perm(to):
        return [
            (a * group + b, to(a, b)[0] * group + to(a, b)[1])
            for a in range(reps)
            for b in range(group)
        ]

    def pp(value, to):
        return lax.ppermute(value, AXES, perm(to))

    def go(value, dx, dy, dc):
        return pp(value, lambda a, b: (a ^ dx, b ^ (dy * 2 + dc)))

    def along(value, k):
        return pp(value, lambda a, b: (a, (b + 4 * k) % group))

    def all_reps(value):
        step = 2
        while step < reps:
            value = value + pp(value, lambda a, b, s=step: (a ^ s, b))
            step *= 2
        return value

    length, width = tokens.shape
    ds = w_query.shape[0]
    hs = w_down.shape[0]
    hid = w_gate.shape[2]
    kvd = w_key.shape[1]
    half_rows = length // 2

    mix = width + 2 * kvd
    gain_end = mix + 256
    gains = jnp.stack([norm1_gain.astype(BF), norm2_gain.astype(BF)], axis=1)
    own_mix = jnp.concatenate(
        [
            w_query.astype(BF),
            w_key.astype(BF),
            w_value.astype(BF),
            gains,
            jnp.zeros((ds, 254), BF),
        ],
        axis=1,
    )

    def rep_half(own):
        half = own.shape[1] // 2
        return lax.dynamic_slice(own, (0, xb * half), (ds, half))

    experts = jnp.arange(EXP, dtype=jnp.int32)[:, None, None]
    share = jnp.sum(jnp.where(routes[None] == experts, gates[None], 0.0), axis=2)
    pairs = PLANE // 2
    share = jnp.pad(share.reshape(PLANE, EPD, length), ((0, 0), (0, 8 - EPD), (0, 0)))

    front, wall_a, wall_b, grads_all, shares, gains_all, q, kk, vv, att, residual, n1, n2 = forward(
        starts,
        tokens,
        cotangent,
        rep_half(own_mix),
        rep_half(w_out.astype(BF)),
        share,
        w_gate,
        w_up,
        w_down,
        planes,
        group,
    )
    out_sum, pack_a, pack_b, grad_normed_two, before_a = run_experts(
        n2,
        grads_all.reshape(pairs, 2 * length, width),
        shares,
        wall_a.reshape(planes, 4 * ds, 3 * hid),
        wall_b.reshape(planes, 4 * ds, 3 * hid),
        planes,
        group,
    )
    input_grad, out_term, before_b, front_grad, shards_a = backward(
        starts,
        grad_normed_two,
        cotangent,
        tokens,
        residual,
        front,
        gains_all,
        q,
        kk,
        vv,
        att,
        n1,
        out_sum.reshape(PLANE, length, width),
        pack_a,
        before_a,
        pack_b,
        planes,
        group,
    )
    front_total, shards_b = scatter_front(front_grad, pack_b, before_b, planes, group)
    total = all_reps(front_total)
    gate_shard, up_shard, down_shard, output = unpack(
        [all_reps(shards_a), all_reps(shards_b)], residual, out_term, hs
    )
    other = go(total, 1, 0, 0)
    front_shard = jnp.where(
        xb == 0,
        jnp.concatenate([total, other], axis=1),
        jnp.concatenate([other, total], axis=1),
    ).astype(F32)
    return (
        output,
        input_grad,
        front_shard[:, mix],
        front_shard[:, :width],
        front_shard[:, width : width + kvd],
        front_shard[:, width + kvd : mix],
        front_shard[:, gain_end:],
        front_shard[:, mix + 1],
        gate_shard,
        up_shard,
        down_shard,
    )


def solution(mesh):
    reps, group = mesh.shape["rep"], mesh.shape["fsdp"]
    both, one = P(AXES, None), P("fsdp")
    flat, deep = P("fsdp", None), P("fsdp", None, None)

    def whole(*args):
        return shards(reps, group, *args)

    return jax.shard_map(
        whole,
        mesh=mesh,
        in_specs=(both, both, both, both, P(AXES), one, flat, flat, flat, flat, one, deep, deep, deep),
        out_specs=(both, both, one, flat, flat, flat, flat, one, deep, deep, deep),
        check_vma=False,
    )
```

```python
import math

import jax
import jax.numpy as jnp
import numpy as np
from jax import lax
from jax.experimental import pallas as pl
from jax.experimental.pallas import tpu as pltpu
from jax.sharding import PartitionSpec as P

HEADS = 24
KV_HEADS = 8
HEAD = 64
EXP = 16
PIECE = 256
AXES = ("rep", "fsdp")
EPSILON = 1e-05
NEG_FILL = -1e30
BF = jnp.bfloat16
F32 = jnp.float32
PLANE = 8
EPD = EXP // PLANE


def turn_tables(length):
    positions = np.arange(length, dtype=np.float32)[:, None]
    lanes = np.arange(2 * HEAD)
    powers = (lanes % (HEAD // 2)).astype(np.float32)
    rates = np.exp(powers * np.float32(-2.0 * math.log(10000.0) / HEAD))
    angles = positions * rates[None, :]
    low = (lanes % HEAD < HEAD // 2)[None, :]
    sines = np.sin(angles)
    tables = [np.cos(angles), np.where(low, -sines, 0.0), np.where(low, 0.0, sines)]
    return jnp.asarray(np.stack(tables).astype(np.float32))


def turned(values, tables, sign):
    ahead = pltpu.roll(values, 2 * HEAD - HEAD // 2, 1)
    back = pltpu.roll(values, HEAD // 2, 1)
    return values * tables[0] + sign * (ahead * tables[1] + back * tables[2])


def row_loop(rows, step, body):
    @pl.loop(0, rows // step)
    def _(n):
        body(pl.ds(pl.multiple_of(n * step, step), step))


def dot(a, b):
    return jnp.dot(a, b, preferred_element_type=F32)


def dot_nt(a, b):
    return lax.dot_general(a, b, (((1,), (1,)), ((), ())), preferred_element_type=F32)


def dot_tn(a, b):
    return lax.dot_general(a, b, (((0,), (0,)), ((), ())), preferred_element_type=F32)


def add_rows(store, terms, rows, step=32):
    step = min(step, rows)

    @pl.loop(0, rows // step)
    def _(n):
        chunk = pl.ds(pl.multiple_of(n * step, 16), step)
        total = terms[0](chunk).astype(F32)
        for term in terms[1:]:
            total = total + term(chunk).astype(F32)
        store(chunk, total)


class Links:
    def __init__(self, planes, group, send_sems, recv_sems):
        r, f = lax.axis_index("rep"), lax.axis_index("fsdp")
        self.xb, self.yb, self.c, self.z = r % 2, (f // 2) % 2, f % 2, f // 4
        self.x = (r + 1 - 2 * self.xb, f)
        self.y = (r, f + 2 - 4 * self.yb)
        self.core = (r, f + 1 - 2 * self.c)
        self.diagonal = (r, f + 3 - 4 * self.yb - 2 * self.c)
        self.others = {1: self.core, 2: self.y, 3: self.diagonal, 4: self.x}
        self.others.update({4 + n: (self.x[0], self.others[n][1]) for n in (1, 2, 3)})
        self.along = [None] + [(r, (f + 4 * k) % group) for k in range(1, planes)]
        self.planes, self.send_sems, self.recv_sems, self.copies = planes, send_sems, recv_sems, []

    def barrier(self, devices):
        semaphore = pltpu.get_barrier_semaphore()
        for device in devices:
            pl.semaphore_signal(
                semaphore, inc=1, device_id=device, device_id_type=pl.DeviceIdType.MESH
            )
        pl.semaphore_wait(semaphore, len(devices))

    def make(self, src, dst, device):
        n = len(self.copies)
        copy = pltpu.make_async_remote_copy(
            src_ref=src,
            dst_ref=dst,
            send_sem=self.send_sems.at[n],
            recv_sem=self.recv_sems.at[n],
            device_id=device,
            device_id_type=pl.DeviceIdType.MESH,
        )
        self.copies.append(copy)
        return copy

    def send(self, src, dst, device):
        copy = self.make(src, dst, device)
        copy.start()
        return copy

    def finish(self):
        for copy in self.copies:
            copy.wait_send()


def comm_params(number):
    return pltpu.CompilerParams(
        collective_id=number, has_side_effects=True, vmem_limit_bytes=56 * 2**20
    )


def dma_pairs(count):
    return [pltpu.SemaphoreType.DMA((count,)), pltpu.SemaphoreType.DMA((count,))]


def whole_vmem():
    return pl.BlockSpec(memory_space=pltpu.VMEM)


def anywhere():
    return pl.BlockSpec(memory_space=pl.ANY)


def share_of(half, share):
    return int(half * share) // 128 * 128


def both_sides(values, store, pair):
    low = lax.broadcasted_iota(jnp.int32, values.shape, 1) < HEAD
    swapped = pltpu.roll(values, HEAD, 1)
    store(0, 2 * pair, jnp.where(low, values, 0.0).astype(BF))
    store(1, 2 * pair, jnp.where(low, 0.0, swapped).astype(BF))
    store(0, 2 * pair + 1, jnp.where(low, swapped, 0.0).astype(BF))
    store(1, 2 * pair + 1, jnp.where(low, 0.0, values).astype(BF))


def fill_bias(bias, start):
    length = bias.shape[0]

    def body(chunk):
        shape = (chunk.size, length)
        i = lax.broadcasted_iota(jnp.int32, shape, 0) + chunk.start
        j = lax.broadcasted_iota(jnp.int32, shape, 1)
        in_i = (i >= start) & (i < start + PIECE)
        in_j = (j >= start) & (j < start + PIECE)
        bias[chunk] = jnp.where((j <= i) | (in_i & in_j), 0.0, NEG_FILL)

    row_loop(length, 64, body)


def softmax_rows(query, key, bias):
    scores = dot_nt(query, key) + bias
    exponent = jnp.exp(scores - jnp.max(scores, axis=1, keepdims=True))
    return exponent * (1.0 / jnp.sum(exponent, axis=1, keepdims=True))


PAIRS = HEADS // 2
GROUP = HEADS // KV_HEADS
LANES = 2 * HEAD


class FrontGather:
    def __init__(self, at, own, full, base, part, own_sem):
        self.at, self.own, self.full, self.base = at, own, full, base
        self.ds, self.half = own.shape
        self.first, self.second = (0, part), (part, self.half - part)
        self.every = (0, self.half)
        self.own_copy = pltpu.make_async_copy(own, self.region(0, 0, 0, self.every), own_sem)
        self.x_first, self.x_second, self.y_first, self.y_second, self.far = [], [], [], [], []

    def region(self, k, dx, dy, span):
        at = self.at
        row = (((at.z + at.planes - k) % at.planes) * 4 + (at.yb + dy) % 2 * 2 + at.c) * self.ds
        col = self.base + (at.xb + dx) % 2 * self.half + span[0]
        return self.full.at[
            pl.ds(pl.multiple_of(row, 16), self.ds), pl.ds(pl.multiple_of(col, 128), span[1])
        ]

    def pass_on(self, k, dx, dy, span, device):
        here = self.region(k, dx, dy, span)
        return self.at.send(here, here, device)

    def start(self):
        at = self.at
        self.own_copy.start()
        here = self.region(0, 0, 0, self.every)
        self.arrive = [None] + [at.send(self.own, here, at.along[k]) for k in range(1, at.planes)]

    def start_plane(self):
        here = self.region(0, 0, 0, self.every)
        self.to_core = [self.at.send(self.own, here, self.at.core)]
        self.spread(0)

    def spread(self, k):
        at = self.at
        for device, span, copies in (
            (at.x, self.first, self.x_first),
            (at.y, self.second, self.y_second),
            (at.x, self.second, self.x_second),
            (at.y, self.first, self.y_first),
        ):
            here = self.region(k, 0, 0, span)
            src = self.own.at[:, pl.ds(span[0], span[1])] if k == 0 else here
            copies.append(at.send(src, here, device))
        if k > 0:
            self.to_core.append(self.pass_on(k, 0, 0, self.every, at.core))

    def advance(self, k):
        self.arrive[k].wait_recv()
        self.spread(k)

    def onward(self, k):
        at = self.at
        self.x_first[k].wait_recv()
        self.far.append((k, self.first, self.pass_on(k, 1, 0, self.first, at.y)))
        self.y_second[k].wait_recv()
        self.far.append((k, self.second, self.pass_on(k, 0, 1, self.second, at.x)))
        self.x_second[k].wait_recv()
        self.to_core.append(self.pass_on(k, 1, 0, self.every, at.core))
        self.y_first[k].wait_recv()
        self.to_core.append(self.pass_on(k, 0, 1, self.every, at.core))

    def finish_far(self):
        for k, span, copy in self.far:
            copy.wait_recv()
            self.to_core.append(self.pass_on(k, 1, 1, span, self.at.core))

    def finish(self):
        for copy in self.to_core:
            copy.wait_recv()
        self.own_copy.wait()

    @staticmethod
    def copies(planes):
        return planes - 1 + planes * 11


def forward(
    starts, tokens, cotangent, own_mix, own_out, shares, w_gate, w_up, w_down, planes, group
):
    length, width = tokens.shape
    ds = own_mix.shape[0]
    hid, hs = w_gate.shape[2], w_down.shape[0]
    wide = 3 * hid
    kvd = KV_HEADS * HEAD
    mix = width + 2 * kvd
    base = 2 * own_mix.shape[1]
    columns = base + width
    row_half = length // 2
    low_rows, high_rows = pl.ds(0, row_half), pl.ds(row_half, row_half)
    tables = turn_tables(length)

    def kernel(
        starts_ref,
        x_ref,
        cot_ref,
        own_mix_ref,
        own_out_ref,
        share_ref,
        gate_hbm,
        up_hbm,
        down_hbm,
        tab_ref,
        front_out,
        wall_a,
        wall_b,
        grads_out,
        shares_out,
        gain_ref,
        q_out,
        kk_out,
        vv_out,
        att_out,
        res_out,
        n1_out,
        n2_out,
        q_ref,
        kk_ref,
        vv_ref,
        att_ref,
        res_ref,
        n1_ref,
        n2_ref,
        front,
        bias,
        packed,
        raw_in,
        raw_down,
        send_sems,
        recv_sems,
        local_sems,
        load_sems,
    ):
        at = Links(planes, group, send_sems, recv_sems)
        at.barrier(list(at.others.values()) + at.along[1:])
        walls = (wall_a, wall_b)
        shard = at.yb * 2 + at.c

        order = [(s, e) for e in range(EPD) for s in range(4)]

        def load(n):
            s, e = order[n]
            index = (at.xb * 4 + s) * EPD + e
            copies = [
                pltpu.make_async_copy(src, dst, load_sems.at[n % 2, i])
                for i, (src, dst) in enumerate(
                    (
                        (gate_hbm.at[:, index], raw_in.at[n % 2, 0]),
                        (up_hbm.at[:, index], raw_in.at[n % 2, 1]),
                        (down_hbm.at[:, index], raw_down.at[n % 2]),
                    )
                )
            ]
            for copy in copies:
                copy.start()
            return copies

        loads = {n: load(n) for n in range(2)}

        def pack(e):
            for n in range(4 * e, 4 * e + 4):
                s = order[n][0]
                for copy in loads[n]:
                    copy.wait()

                def cast(chunk, n=n, s=s):
                    packed[s, e, chunk, :hid] = raw_in[n % 2, 0, chunk].astype(BF)
                    packed[s, e, chunk, hid : 2 * hid] = raw_in[n % 2, 1, chunk].astype(BF)

                row_loop(ds, 16, cast)
                for i in range(width // hid):
                    packed[s, e, i * hs : (i + 1) * hs, 2 * hid :] = raw_down[
                        n % 2, :, i * hid : (i + 1) * hid
                    ].astype(BF)
                if n + 2 < len(order):
                    loads[n + 2] = load(n + 2)
            copy = pltpu.make_async_copy(
                packed.at[shard, e], walls[e].at[at.z, shard], local_sems.at[e]
            )
            copy.start()
            locals_.append(copy)

        locals_ = []

        def put(*pairs):
            for src, dst in pairs:
                n = len(stored)
                stored.append(pltpu.make_async_copy(src, dst, local_sems.at[7 + n]))
                stored[n].start()

        stored = []

        def exchange(e):
            copies = []
            for dy, dc, device in ((1, 0, at.y), (1, 1, at.diagonal), (0, 1, at.core)):
                target = (at.yb + dy) % 2 * 2 + (at.c + dc) % 2
                copies.append(
                    at.send(packed.at[target, e], walls[e].at[at.z, shard], device)
                )
            return copies

        ring = {}

        def ring_first(e, copies):
            sent = [
                at.send(packed.at[shard, e], walls[e].at[at.z, shard], at.along[1])
            ]
            for copy, (dy, dc) in zip(copies, ((1, 0), (1, 1), (0, 1))):
                copy.wait_recv()
                piece = walls[e].at[at.z, (at.yb + dy) % 2 * 2 + (at.c + dc) % 2]
                sent.append(at.send(piece, piece, at.along[1]))
            ring[e] = (1, sent)

        def ring_next(e):
            step, sent = ring[e]
            for copy in sent:
                copy.wait_recv()
            if step < planes - 1:
                piece = walls[e].at[(at.z + planes - step) % planes]
                ring[e] = (step + 1, [at.send(piece, piece, at.along[1])])
            else:
                ring[e] = (planes, [])

        mixing = FrontGather(
            at, own_mix_ref, front, 0, share_of(base // 2, 0.25), local_sems.at[2]
        )
        closing = FrontGather(
            at, own_out_ref, front, base, share_of(width // 2, 0.25), local_sems.at[5]
        )

        def share_slot(j):
            return shares_out.at[j // 2, :, pl.ds(j % 2 * length, length)]

        mixing.start()
        mixing.start_plane()
        closing.start()
        pack(0)
        first_exchange = exchange(0)
        place = at.xb * 4 + shard
        locals_.append(pltpu.make_async_copy(share_ref.at[place], share_slot(0), local_sems.at[6]))
        locals_[-1].start()
        got_shares = []
        for j, device in at.others.items():
            other = (
                (at.xb + j // 4) % 2 * 4 + (at.yb + j // 2 % 2) % 2 * 2 + (at.c + j % 2) % 2
            )
            got_shares.append(at.send(share_ref.at[other], share_slot(j), device))
        pack(1)
        fill_bias(bias, starts_ref[0])
        for k in range(1, planes):
            mixing.advance(k)
            mixing.onward(k - 1)
        ring_first(0, first_exchange)
        mixing.onward(planes - 1)
        mixing.finish_far()
        closing.start_plane()
        for k in range(1, planes):
            closing.advance(k)
        mixing.finish()
        def gather_start(src, out):
            def slot(j, rows=pl.ds(0, length)):
                return out.at[j, rows]

            got = {
                "x_low": at.send(src.at[low_rows], slot(4, low_rows), at.x),
                "y_high": at.send(src.at[high_rows], slot(2, high_rows), at.y),
                "x_high": at.send(src.at[high_rows], slot(4, high_rows), at.x),
                "y_low": at.send(src.at[low_rows], slot(2, low_rows), at.y),
                "core": [at.send(src, slot(1), at.core)],
            }
            return slot, got

        def gather_middle(slot, got):
            got["x_low"].wait_recv()
            got["far_low"] = at.send(slot(4, low_rows), slot(6, low_rows), at.y)
            got["core"].append(at.send(slot(4, low_rows), slot(5, low_rows), at.core))
            got["y_high"].wait_recv()
            got["far_high"] = at.send(slot(2, high_rows), slot(6, high_rows), at.x)
            got["core"].append(at.send(slot(2, high_rows), slot(3, high_rows), at.core))

        def gather_last(slot, got):
            got["x_high"].wait_recv()
            got["core"].append(at.send(slot(4, high_rows), slot(5, high_rows), at.core))
            got["y_low"].wait_recv()
            got["core"].append(at.send(slot(2, low_rows), slot(3, low_rows), at.core))
            got["far_low"].wait_recv()
            got["core"].append(at.send(slot(6, low_rows), slot(7, low_rows), at.core))
            got["far_high"].wait_recv()
            got["core"].append(at.send(slot(6, high_rows), slot(7, high_rows), at.core))

        gain_ref[...] = front[:, mix : mix + 128].astype(F32).T[:8]

        def norm(chunk):
            x = x_ref[chunk].astype(F32)
            inv = lax.rsqrt(jnp.mean(x * x, axis=1, keepdims=True) + EPSILON)
            n1_ref[chunk] = (x * inv * gain_ref[0:1, :]).astype(BF)

        row_loop(length, 64, norm)
        block = 4 * LANES
        for n in range(mix // block):
            raw = dot(n1_ref[...], front[:, n * block : (n + 1) * block])
            for j in range(4):
                col = n * block + j * LANES
                values = raw[:, j * LANES : (j + 1) * LANES]
                if col < width:
                    turned_low = turned(values, tab_ref, 1.0).astype(BF).astype(F32)
                    q_ref[:, col : col + LANES] = (turned_low * (1.0 / math.sqrt(HEAD))).astype(BF)
                else:
                    target, start = (kk_ref, width) if col < width + kvd else (vv_ref, width + kvd)
                    if col < width + kvd:
                        values = turned(values, tab_ref, 1.0)

                    def store(side, head, side_values, target=target):
                        target[side, head] = side_values

                    both_sides(values, store, (col - start) // LANES)
        ring_next(0)
        put((q_ref, q_out), (kk_ref, kk_out), (vv_ref, vv_out), (n1_ref, n1_out))
        grads = gather_start(cot_ref, grads_out)
        cot_copy = pltpu.make_async_copy(cot_ref, grads_out.at[0], local_sems.at[4])
        cot_copy.start()


        def attend(pairs):
            @pl.loop(*pairs)
            def _(p):
                cols = pl.ds(pl.multiple_of(p * LANES, LANES), LANES)
                total = None
                for side in range(2):
                    head = (2 * p + side) // GROUP
                    probs = softmax_rows(q_ref[:, cols], kk_ref[side, head], bias[...])
                    term = dot(probs.astype(BF), vv_ref[side, head])
                    total = term if total is None else total + term
                att_ref[:, cols] = total.astype(BF)

        attend((0, PAIRS // 3))
        for k in range(planes):
            closing.onward(k)
        attend((PAIRS // 3, 2 * PAIRS // 3))
        gather_middle(*grads)
        second_exchange = exchange(1)
        attend((2 * PAIRS // 3, PAIRS))
        put((att_ref, att_out))
        closing.finish_far()
        closing.finish()
        front_copy = pltpu.make_async_copy(front, front_out, local_sems.at[3])
        front_copy.start()
        ring_next(0)
        for n in range(width // block):
            cols = slice(n * block, (n + 1) * block)
            res_ref[:, cols] = x_ref[:, cols].astype(F32) + dot(
                att_ref[...], front[:, base + n * block : base + (n + 1) * block]
            )

        def norm_two(chunk):
            r = res_ref[chunk]
            inv = lax.rsqrt(jnp.mean(r * r, axis=1, keepdims=True) + EPSILON)
            n2_ref[chunk] = (r * inv * gain_ref[1:2, :]).astype(BF)

        row_loop(length, 64, norm_two)
        put((n2_ref, n2_out), (res_ref, res_out))
        gather_last(*grads)
        while ring[0][0] < planes:
            ring_next(0)
        for copy in grads[1]["core"] + second_exchange + got_shares:
            copy.wait_recv()
        for copy in locals_ + stored + [front_copy, cot_copy]:
            copy.wait()
        at.finish()

    shape = jax.ShapeDtypeStruct
    count = 2 * FrontGather.copies(planes) + 2 * 3 + 4 + planes - 2 + 13 + 7
    return pl.pallas_call(
        kernel,
        out_shape=[
            shape((width, columns), BF),
            shape((planes, 4, ds, wide), BF),
            shape((planes, 4, ds, wide), BF),
            shape((PLANE, length, width), BF),
            shape((PLANE // 2, 8, 2 * length), F32),
            shape((8, width), F32),
            shape((length, width), BF),
            shape((2, KV_HEADS, length, LANES), BF),
            shape((2, KV_HEADS, length, LANES), BF),
            shape((length, width), BF),
            shape((length, width), F32),
            shape((length, width), BF),
            shape((length, width), BF),
        ],
        in_specs=[pl.BlockSpec(memory_space=pltpu.SMEM)]
        + [whole_vmem()] * 5
        + [anywhere()] * 3
        + [whole_vmem()],
        out_specs=[anywhere()] * 5 + [whole_vmem()] + [anywhere()] * 7,
        scratch_shapes=[
            pltpu.VMEM((length, width), BF),
            pltpu.VMEM((2, KV_HEADS, length, LANES), BF),
            pltpu.VMEM((2, KV_HEADS, length, LANES), BF),
            pltpu.VMEM((length, width), BF),
            pltpu.VMEM((length, width), F32),
            pltpu.VMEM((length, width), BF),
            pltpu.VMEM((length, width), BF),
            pltpu.VMEM((width, columns), BF),
            pltpu.VMEM((length, length), F32),
            pltpu.VMEM((4, EPD, ds, wide), BF),
            pltpu.VMEM((2, 2, ds, hid), F32),
            pltpu.VMEM((2, hs, width), F32),
        ]
        + dma_pairs(count)
        + [pltpu.SemaphoreType.DMA((14,)), pltpu.SemaphoreType.DMA((2, 3))],
        compiler_params=comm_params(0),
        cost_estimate=pl.CostEstimate(
            flops=150_000_000_000, bytes_accessed=20_000_000, transcendentals=0
        ),
    )(
        starts, tokens, cotangent, own_mix, own_out, shares, w_gate, w_up, w_down, tables
    )


class PlaneSum:
    def __init__(self, at, length, odd, even, from_core, far, near):
        self.at, self.odd, self.even, self.core = at, odd, even, from_core
        self.far, self.near = far, near
        self.length = length
        self.half = self.length // 2
        self.low, self.high = pl.ds(0, self.half), pl.ds(self.half, self.half)
        self.arrive = {
            j: at.make(odd(j), self.part(j, pl.ds(0, length)), at.core) for j in (3, 2, 1, 0)
        }
        low, high = self.low, self.high
        self.far_y = at.make(self.part(3, low), far.at[0], at.y)
        self.far_x = at.make(self.part(3, high), far.at[1], at.x)
        self.x_high = at.make(self.part(2, high), near.at[0, high], at.x)
        self.y_low = at.make(self.part(1, low), near.at[1, low], at.y)
        self.x_low = at.make(self.part(2, low), near.at[0, low], at.x)
        self.y_high = at.make(self.part(1, high), near.at[1, high], at.y)

    def rows(self, j, chunk, base=0):
        return pl.ds(pl.multiple_of(chunk.start + j * self.length + base, 16), chunk.size)

    def part(self, j, rows):
        return self.core.at[pl.ds(j * self.length + rows.start, rows.size)]

    def start(self, j):
        self.arrive[j].start()

    def add_core(self, j):
        self.arrive[j].wait_recv()
        core = self.core

        def store(chunk, total):
            core[self.rows(j, chunk)] = total.astype(BF)

        add_rows(store, [lambda q: self.even(j, q), lambda q: core[self.rows(j, q)]], self.length)

    def add_far(self, j, n, base):
        core, far = self.core, self.far

        def store(chunk, total):
            core[self.rows(j, chunk, base)] = total.astype(BF)

        add_rows(store, [lambda q: core[self.rows(j, q, base)], lambda q: far[n, q]], self.half)

    def send_far(self):
        self.add_core(3)
        self.far_y.start()
        self.far_x.start()

    def send_x(self):
        self.add_core(2)
        self.x_high.start()

    def send_y(self):
        self.add_core(1)
        self.y_low.start()

    def onward_x(self):
        self.far_y.wait_recv()
        self.add_far(2, 0, 0)
        self.x_low.start()

    def onward_y(self):
        self.far_x.wait_recv()
        self.add_far(1, 1, self.half)
        self.y_high.start()

    def end(self, store):
        self.arrive[0].wait_recv()
        for copy in (self.x_high, self.y_low, self.x_low, self.y_high):
            copy.wait_recv()
        core, near = self.core, self.near
        terms = [lambda q: self.even(0, q), lambda q: core[q]]
        terms += [lambda q: near[0, q], lambda q: near[1, q]]
        add_rows(store, terms, self.length)

    copies = 10


class RingSum:
    def __init__(self, at, pack, own, own_sem):
        self.at, self.pack, self.own, self.own_sem = at, pack, own, own_sem
        self.index = [(at.z + at.planes - k) % at.planes for k in range(at.planes)]

    def block(self, k):
        return self.pack.at[self.index[k]]

    def fetch(self, k):
        self.fetched = pltpu.make_async_copy(self.block(k), self.own, self.own_sem)
        self.fetched.start()

    def add(self, source, target):
        self.fetched.wait()

        def store(chunk, total):
            target[chunk] = total.astype(BF)

        add_rows(store, [lambda q: source[q], lambda q: self.own[q]], self.own.shape[0], 16)

    def first(self, slots):
        self.slots, self.step = slots, 1
        sources = [self.block(1)] + slots[:-1]
        self.sent = [
            self.at.make(src, dst, self.at.along[1]) for src, dst in zip(sources, slots)
        ]
        self.fetches = {
            k: pltpu.make_async_copy(self.block(k), self.own, self.own_sem)
            for k in range(2, len(slots) + 1)
        }
        self.sent[0].start()
        self.begin_fetch(2)

    def begin_fetch(self, k):
        if k in self.fetches:
            self.fetched = self.fetches[k]
            self.fetched.start()

    def next(self):
        if self.step < len(self.slots):
            here = self.slots[self.step - 1]
            self.sent[self.step - 1].wait_recv()
            self.add(here, here)
            self.sent[self.step].start()
            self.step += 1
            self.begin_fetch(self.step + 1)

    def rest(self):
        while self.step < len(self.slots):
            self.next()
        self.sent[-1].wait_recv()

    def last(self, before, sent, landing):
        self.add(before, sent)
        self.landing = landing
        self.copy = self.at.send(sent, landing, self.at.along[1])
        self.fetch(0)

    def total(self):
        self.copy.wait_recv()
        self.add(self.landing, self.landing)
        return self.landing


def run_experts(tokens, grads, shares, wall_a, wall_b, planes, group):
    pairs, count, width = grads.shape
    length = count // 2
    piece, wide = wall_a.shape[1:]
    hid = wide // 3
    ds, hs, blocks = width // group, hid // group, width // hid
    half = length // 2
    low, high, full = pl.ds(0, half), pl.ds(half, half), pl.ds(0, length)

    def kernel(
        n2_hbm,
        g_hbm,
        share_ref,
        wall_a_ref,
        wall_b_ref,
        out_hbm,
        pack_a,
        pack_b,
        sum_ref,
        passed,
        xs,
        dxs,
        w_a,
        w_b,
        down_a,
        down_b,
        in_sum,
        down_sum,
        g_tile,
        o_tile,
        pre,
        act,
        far,
        near,
        ring_slots,
        own,
        free,
        send_sems,
        recv_sems,
        local_sems,
    ):
        at = Links(planes, group, send_sems, recv_sems)
        at.barrier([at.x, at.y, at.core] + at.along[1:])
        index = [(at.z + planes - k) % planes for k in range(planes)]

        def local(src, dst, n):
            copy = pltpu.make_async_copy(src, dst, local_sems.at[n])
            copy.start()
            return copy

        def slot(j, rows=full):
            return xs.at[j // 2, pl.ds(j % 2 * length + rows.start, rows.size)]

        pieces = [
            w_b.at[pl.ds(pl.multiple_of(index[k] * piece, 16), piece)] for k in range(planes)
        ]

        local(n2_hbm, slot(0), 0).wait()
        x_low = at.send(slot(0, low), slot(4, low), at.x)
        y_high = at.send(slot(0, high), slot(2, high), at.y)
        x_high = at.send(slot(0, high), slot(4, high), at.x)
        y_low = at.send(slot(0, low), slot(2, low), at.y)
        near_core = at.send(slot(0), slot(1), at.core)
        ring = [at.make(wall_b_ref.at[at.z], pieces[0], at.along[1])]
        ring += [at.make(piece_ref, piece_ref, at.along[1]) for piece_ref in pieces[1:-1]]
        ring[0].start()
        load_b = local(wall_b_ref.at[at.z], pieces[0], 1)
        loads = [
            local(wall_a_ref.at[n], w_a.at[pl.ds(n * piece, piece)], 2 + n) for n in range(planes)
        ]
        state = {"ring": 0}
        far_low = at.make(slot(4, low), slot(6, low), at.y)
        far_high = at.make(slot(2, high), slot(6, high), at.x)
        passed_on = {
            (j, rows.start): at.make(slot(j, rows), slot(j + 1, rows), at.core)
            for j in (4, 2, 6)
            for rows in (low, high)
        }

        def ring_next():
            ring[state["ring"]].wait_recv()
            state["ring"] += 1
            if state["ring"] < planes - 1:
                ring[state["ring"]].start()

        def core_arrival(j):
            passed_on[j, low.start].wait_recv()
            passed_on[j, high.start].wait_recv()

        def spread():
            x_low.wait_recv()
            far_low.start()
            passed_on[4, low.start].start()
            y_high.wait_recv()
            far_high.start()
            passed_on[2, high.start].start()
            ring_next()
            x_high.wait_recv()
            passed_on[4, high.start].start()
            y_low.wait_recv()
            passed_on[2, low.start].start()
            core_arrival(4)

        def spread_far():
            far_low.wait_recv()
            passed_on[6, low.start].start()
            far_high.wait_recv()
            passed_on[6, high.start].start()
            core_arrival(6)

        def unpack_down(w, down):
            for s in range(group):
                for b in range(blocks):
                    down[s * hs : (s + 1) * hs, b * hid : (b + 1) * hid] = w[
                        s * ds + b * hs : s * ds + (b + 1) * hs, 2 * hid :
                    ]

        def clear():
            def body(chunk):
                in_sum[chunk] = jnp.zeros((chunk.size, 2 * hid), F32)

            row_loop(width, 64, body)

            def body_down(chunk):
                down_sum[chunk] = jnp.zeros((chunk.size, width), F32)

            row_loop(hid, 64, body_down)

        def out_copy(pair):
            return pltpu.make_async_copy(o_tile, out_hbm.at[pair], local_sems.at[0])

        def tile(e, step, pair, w, down, middle):
            g_load = pltpu.make_async_copy(g_hbm.at[pair], g_tile, local_sems.at[1])
            g_load.start()
            x = xs.at[pair]
            share = share_ref[pair].T[:, e : e + 1]
            part = hid // 2
            for n in range(2):
                cols = slice(n * part, (n + 1) * part)
                up_cols = slice(hid + n * part, hid + (n + 1) * part)
                gate = dot(x[...], w[:, cols])
                up = dot(x[...], w[:, up_cols])
                if n == 0:
                    g_load.wait()
                inner = dot_nt(g_tile[...], down[cols, :]) * share
                sig = jax.nn.sigmoid(gate)
                swish = gate * sig
                act[:, cols] = (share * (swish * up)).astype(BF)
                pre[:, cols] = (inner * up * sig * (1.0 + gate * (1.0 - sig))).astype(BF)
                pre[:, up_cols] = (inner * swish).astype(BF)
            middle()

            @pl.when(step > 0)
            def _():
                out_copy(pair).wait()

            if e > 0:
                before = pltpu.make_async_copy(out_hbm.at[pair], o_tile, local_sems.at[2])
                before.start()
                before.wait()
            for n in range(width // hid):
                cols = slice(n * hid, (n + 1) * hid)
                out = dot(act[...], down[:, cols])
                dx = dot_nt(pre[...], w[cols, : 2 * hid])
                if e > 0:
                    out = out + o_tile[:, cols].astype(F32)
                    dx = dx + dxs[pair, :, cols].astype(F32)
                o_tile[:, cols] = out.astype(BF)
                dxs[pair, :, cols] = dx.astype(BF)
                in_sum[cols, :] += dot_tn(x[:, cols], pre[...])
                down_sum[:, cols] += dot_tn(act[...], g_tile[:, cols])
            out_copy(pair).start()

        def pack(target):
            out_copy(0).wait()
            copies = [None, None]
            for n in range(planes):
                base = n % 2 * piece
                if copies[n % 2] is not None:
                    copies[n % 2].wait()

                def body(chunk, n=n, base=base):
                    rows = pl.ds(pl.multiple_of(chunk.start + base, 16), chunk.size)
                    source = pl.ds(pl.multiple_of(chunk.start + n * piece, 16), chunk.size)
                    o_tile[rows, : 2 * hid] = in_sum[source].astype(BF)

                row_loop(piece, 32, body)
                for s in range(4):
                    for b in range(blocks):
                        row = base + s * ds + b * hs
                        o_tile[row : row + hs, 2 * hid :] = down_sum[
                            (n * 4 + s) * hs : (n * 4 + s + 1) * hs, b * hid : (b + 1) * hid
                        ].astype(BF)
                copies[n % 2] = local(o_tile.at[pl.ds(base, piece)], target.at[n], 3 + n % 2)
            for copy in copies:
                copy.wait()

        clear()
        for copy in loads:
            copy.wait()
        load_b.wait()
        unpack_down(w_a, down_a)
        near_core.wait_recv()

        @pl.loop(0, pairs)
        def _(step):
            @pl.when(step == 1)
            def _():
                spread()

            @pl.when(step == 2)
            def _():
                core_arrival(2)

            @pl.when(step == 3)
            def _():
                spread_far()

            def middle():
                @pl.when(step == 2)
                def _():
                    ring_next()

            tile(0, step, 2 * step % 3 + step // 3 * 3, w_a, down_a, middle)

        pl.semaphore_signal(free, inc=1, device_id=at.core, device_id_type=pl.DeviceIdType.MESH)
        pack(pack_a)
        sums = RingSum(at, pack_a, own, local_sems.at[5])
        sums.first([ring_slots.at[n] for n in range(planes - 3)] + [passed])
        clear()
        while state["ring"] < planes - 1:
            ring_next()
        unpack_down(w_b, down_b)
        pl.semaphore_wait(free, 1)
        plane = PlaneSum(
            at,
            length,
            lambda j: dxs.at[j, pl.ds(length, length)],
            lambda j, q: dxs[j, q],
            w_a,
            far,
            near,
        )

        @pl.loop(0, pairs)
        def _(step):
            def middle():
                @pl.when(step == 1)
                def _():
                    plane.send_far()

                @pl.when(step == 2)
                def _():
                    plane.send_x()
                    sums.next()

                @pl.when(step == 3)
                def _():
                    plane.send_y()
                    plane.onward_y()

            tile(1, step, pairs - 1 - step, w_b, down_b, middle)
            for n in range(pairs):

                @pl.when(step == n)
                def _(n=n):
                    plane.start(pairs - 1 - n)
                    if n == 2:
                        plane.onward_x()

        pack(pack_b)

        def store(chunk, total):
            sum_ref[chunk] = total

        plane.end(store)
        sums.rest()
        at.finish()

    shape = jax.ShapeDtypeStruct
    return pl.pallas_call(
        kernel,
        in_specs=[anywhere()] * 2 + [whole_vmem()] + [anywhere()] * 2,
        out_specs=[anywhere()] * 3 + [whole_vmem()] * 2,
        out_shape=[
            shape((pairs, count, width), BF),
            shape((planes, piece, wide), BF),
            shape((planes, piece, wide), BF),
            shape((length, width), F32),
            shape((piece, wide), BF),
        ],
        scratch_shapes=[
            pltpu.VMEM((pairs, count, width), BF),
            pltpu.VMEM((pairs, count, width), BF),
            pltpu.VMEM((width, wide), BF),
            pltpu.VMEM((width, wide), BF),
            pltpu.VMEM((hid, width), BF),
            pltpu.VMEM((hid, width), BF),
            pltpu.VMEM((width, 2 * hid), F32),
            pltpu.VMEM((hid, width), F32),
            pltpu.VMEM((count, width), BF),
            pltpu.VMEM((count, width), BF),
            pltpu.VMEM((count, 2 * hid), BF),
            pltpu.VMEM((count, hid), BF),
            pltpu.VMEM((2, half, width), BF),
            pltpu.VMEM((2, length, width), BF),
            pltpu.VMEM((planes - 3, piece, wide), BF),
            pltpu.VMEM((piece, wide), BF),
            pltpu.SemaphoreType.REGULAR,
        ]
        + dma_pairs(13 + planes - 1 + PlaneSum.copies + planes - 2)
        + [pltpu.SemaphoreType.DMA((2 + planes,))],
        compiler_params=pltpu.CompilerParams(
            collective_id=2, has_side_effects=True, vmem_limit_bytes=63 * 2**20
        ),
        cost_estimate=pl.CostEstimate(
            flops=100_000_000_000, bytes_accessed=50_000_000, transcendentals=0
        ),
    )(tokens, grads, shares, wall_a, wall_b)


class Exchange:
    def __init__(self, at, total, out, ds):
        self.at, self.total, self.out, self.ds = at, total, out, ds
        self.shard = at.yb * 2 + at.c

    def place(self, dx, dy, dc):
        at = self.at
        return (at.xb + dx) % 2 * 4 + (at.yb + dy) % 2 * 2 + (at.c + dc) % 2

    def rows(self, dy, dc):
        at = self.at
        shard = (at.yb + dy) % 2 * 2 + (at.c + dc) % 2
        return self.total.at[pl.ds(pl.multiple_of(shard * self.ds, 16), self.ds)]

    def start(self, sem):
        at = self.at
        here = self.out.at[self.place(0, 0, 0)]
        self.local = pltpu.make_async_copy(self.rows(0, 0), here, sem)
        self.local.start()
        self.got = [
            (dy, dc, at.send(self.rows(dy, dc), here, device))
            for dy, dc, device in ((1, 0, at.y), (1, 1, at.diagonal), (0, 1, at.core))
        ]
        self.across = [at.send(self.rows(0, 0), here, at.x)]

    def onward(self):
        at = self.at
        for dy, dc, copy in self.got:
            copy.wait_recv()
            piece = self.out.at[self.place(0, dy, dc)]
            self.across.append(at.send(piece, piece, at.x))

    def end(self):
        for copy in self.across:
            copy.wait_recv()
        self.local.wait()

    copies = 7


def backward(
    starts,
    grad_two,
    cotangent,
    tokens,
    residual,
    front,
    gains,
    q,
    kk,
    vv,
    att,
    n1,
    outs,
    pack_a,
    before_a,
    pack_b,
    planes,
    group,
):
    length, width = tokens.shape
    columns = front.shape[1]
    kvd = KV_HEADS * HEAD
    mix = width + 2 * kvd
    block = 4 * LANES
    tables = turn_tables(length)
    piece, wide = pack_a.shape[1:]
    ds = piece // 4
    extra = columns - mix - width
    part = block // 2

    def kernel(
        starts_ref,
        d_ref,
        cot_ref,
        tab_ref,
        gain_ref,
        before_ref,
        q_hbm,
        kk_hbm,
        vv_hbm,
        att_hbm,
        x_hbm,
        n1_hbm,
        res_hbm,
        w_hbm,
        outs_ref,
        pack_a_ref,
        pack_b_ref,
        in_ref,
        sum_ref,
        passed_b,
        grad_hbm,
        shards_ref,
        q_ref,
        kk_ref,
        vv_ref,
        att_ref,
        bias,
        gain_sum,
        mixed,
        context,
        grad_mix,
        key_sum,
        value_sum,
        w_ref,
        stage,
        even,
        from_core,
        far,
        near,
        own_a,
        sent_a,
        landing_a,
        own_b,
        slots_b,
        send_sems,
        recv_sems,
        local_sems,
    ):
        at = Links(planes, group, send_sems, recv_sems)
        at.barrier([at.x, at.y, at.core, at.diagonal] + at.along[1:])

        def local(src, dst, n):
            copy = pltpu.make_async_copy(src, dst, local_sems.at[n])
            copy.start()
            return copy

        load_res = local(res_hbm, in_ref, 0)
        load_att = local(att_hbm, att_ref, 12)
        load_heads = [
            local(src, dst, 13 + n)
            for n, (src, dst) in enumerate(((q_hbm, q_ref), (kk_hbm, kk_ref), (vv_hbm, vv_ref)))
        ]
        load_out_w = local(
            w_hbm.at[:, pl.ds(mix + extra, width)], w_ref.at[:, pl.ds(0, width)], 1
        )
        plane = PlaneSum(
            at,
            length,
            lambda j: outs_ref.at[2 * j + 1],
            lambda j, q: even[j, q],
            from_core,
            far,
            near,
        )
        for j in (3, 2, 1, 0):
            plane.start(j)
        ring_a = RingSum(at, pack_a_ref, own_a, local_sems.at[6])
        ring_b = RingSum(at, pack_b_ref, own_b, local_sems.at[7])
        ring_a.fetch(planes - 1)
        loads = [local(outs_ref.at[2 * j], even.at[j], 2 + j) for j in range(4)]
        ring_a.last(before_ref, sent_a, landing_a)
        ring_b.first([slots_b.at[n] for n in range(planes - 3)] + [passed_b])
        staged = [None, None]
        turn = [0]

        def put(values, column, count):
            for base in range(0, count, part):
                n = turn[0] % 2
                turn[0] += 1
                if staged[n] is not None:
                    staged[n].wait()
                stage[n] = values[:, base : base + part]
                staged[n] = local(
                    stage.at[n], grad_hbm.at[:, pl.ds(column + base, part)], 8 + n
                )

        fill_bias(bias, starts_ref[0])
        gain_sum[...] = jnp.zeros_like(gain_sum)

        load_res.wait()

        def residual_grad(chunk):
            d, r = d_ref[chunk], in_ref[chunk]
            inv = lax.rsqrt(jnp.mean(r * r, axis=1, keepdims=True) + EPSILON)
            scaled = d * gain_ref[1:2, :]
            grad = (
                cot_ref[chunk].astype(F32)
                + inv * scaled
                - r * (inv * inv * inv * jnp.mean(scaled * r, axis=1, keepdims=True))
            )
            sum_ref[chunk] = grad
            mixed[chunk] = grad.astype(BF)
            gain_sum[1:2, :] += jnp.sum(d * r * inv, axis=0, keepdims=True)

        row_loop(length, 32, residual_grad)
        load_out_w.wait()
        for n in range(width // block):
            cols = slice(n * block, (n + 1) * block)
            context[:, cols] = dot_nt(mixed[...], w_ref[cols, :width]).astype(BF)
        load_mix_w = local(w_hbm.at[:, pl.ds(0, mix)], w_ref, 1)
        load_att.wait()
        for n in range(width // block):
            cols = slice(n * block, (n + 1) * block)
            put(dot_tn(att_ref[...], mixed[:, cols]).astype(BF), mix + extra + n * block, block)
        load_n1 = local(n1_hbm, mixed, 0)
        for copy in loads:
            copy.wait()
        plane.send_far()
        plane.send_x()
        plane.send_y()
        key_sum[...] = jnp.zeros_like(key_sum)
        value_sum[...] = jnp.zeros_like(value_sum)

        def attend(lower, upper):
            @pl.loop(lower, upper)
            def _(p):
                cols = pl.ds(pl.multiple_of(p * LANES, LANES), LANES)
                total = None
                for side in range(2):
                    head = (2 * p + side) // GROUP
                    query, grad = q_ref[:, cols], context[:, cols]
                    probs = softmax_rows(query, kk_ref[side, head], bias[...])
                    grad_probs = dot_nt(grad, vv_ref[side, head])
                    value_sum[side, head] += dot_tn(probs.astype(BF), grad)
                    inner = jnp.sum(probs * grad_probs, axis=1, keepdims=True)
                    logit = (probs * (grad_probs - inner)).astype(BF)
                    term = dot(logit, kk_ref[side, head])
                    total = term if total is None else total + term
                    key_sum[side, head] += dot_tn(logit, query)
                back = turned(total, tab_ref, -1.0) * (1.0 / math.sqrt(HEAD))
                grad_mix[:, cols] = back.astype(BF)

        for copy in load_heads:
            copy.wait()
        attend(0, PAIRS // 3)
        plane.onward_x()
        plane.onward_y()
        exchange = Exchange(at, ring_a.total(), shards_ref, ds)
        exchange.start(local_sems.at[10])
        attend(PAIRS // 3, 2 * PAIRS // 3)
        ring_b.next()
        exchange.onward()
        attend(2 * PAIRS // 3, PAIRS)
        load_x = local(x_hbm, context, 11)
        load_n1.wait()
        for pair in range(KV_HEADS // 2):
            for sums, base in ((key_sum, width), (value_sum, width + kvd)):

                def join(chunk, pair=pair, sums=sums, base=base):
                    low = lax.broadcasted_iota(jnp.int32, (chunk.size, LANES), 1) < HEAD
                    even = sums[0, 2 * pair, chunk] + pltpu.roll(sums[1, 2 * pair, chunk], HEAD, 1)
                    odd = sums[1, 2 * pair + 1, chunk] + pltpu.roll(
                        sums[0, 2 * pair + 1, chunk], HEAD, 1
                    )
                    values = jnp.where(low, even, odd)
                    if base == width:
                        values = turned(values, tab_ref.at[:, chunk], -1.0)
                    grad_mix[chunk, base + pair * LANES : base + (pair + 1) * LANES] = values.astype(BF)

                row_loop(length, 64, join)
        for n in range(mix // block):
            cols = slice(n * block, (n + 1) * block)
            put(dot_tn(mixed[...], grad_mix[:, cols]).astype(BF), n * block, block)
        load_mix_w.wait()
        for n in range(width // block):
            cols = slice(n * block, (n + 1) * block)
            in_ref[:, cols] = dot_nt(grad_mix[...], w_ref[cols, :mix])

        load_x.wait()

        def input_grad(chunk):
            d, x = in_ref[chunk], context[chunk].astype(F32)
            inv = lax.rsqrt(jnp.mean(x * x, axis=1, keepdims=True) + EPSILON)
            scaled = d * gain_ref[0:1, :]
            gain_sum[0:1, :] += jnp.sum(d * x * inv, axis=0, keepdims=True)
            in_ref[chunk] = (
                sum_ref[chunk]
                + inv * scaled
                - x * (inv * inv * inv * jnp.mean(scaled * x, axis=1, keepdims=True))
            )

        row_loop(length, 32, input_grad)
        gain_rows = jnp.concatenate([gain_sum[...].T, jnp.zeros((width, extra - 8), F32)], axis=1)
        put(gain_rows.astype(BF), mix, extra)

        def store(chunk, total):
            sum_ref[chunk] = total

        plane.end(store)
        ring_b.rest()
        exchange.end()
        for copy in staged:
            copy.wait()
        at.finish()

    shape = jax.ShapeDtypeStruct
    return pl.pallas_call(
        kernel,
        in_specs=[pl.BlockSpec(memory_space=pltpu.SMEM)]
        + [whole_vmem()] * 5
        + [anywhere()] * 11,
        out_specs=[whole_vmem()] * 3 + [anywhere()] * 2,
        out_shape=[
            shape((length, width), F32),
            shape((length, width), F32),
            shape((piece, wide), BF),
            shape((width, columns), BF),
            shape((PLANE, ds, wide), BF),
        ],
        scratch_shapes=[
            pltpu.VMEM((length, width), BF),
            pltpu.VMEM((2, KV_HEADS, length, LANES), BF),
            pltpu.VMEM((2, KV_HEADS, length, LANES), BF),
            pltpu.VMEM((length, width), BF),
            pltpu.VMEM((length, length), F32),
            pltpu.VMEM((8, width), F32),
            pltpu.VMEM((length, width), BF),
            pltpu.VMEM((length, width), BF),
            pltpu.VMEM((length, mix), BF),
            pltpu.VMEM((2, KV_HEADS, length, LANES), F32),
            pltpu.VMEM((2, KV_HEADS, length, LANES), F32),
            pltpu.VMEM((width, mix), BF),
            pltpu.VMEM((2, width, part), BF),
            pltpu.VMEM((4, length, width), BF),
            pltpu.VMEM((4 * length, width), BF),
            pltpu.VMEM((2, length // 2, width), BF),
            pltpu.VMEM((2, length, width), BF),
            pltpu.VMEM((piece, wide), BF),
            pltpu.VMEM((piece, wide), BF),
            pltpu.VMEM((piece, wide), BF),
            pltpu.VMEM((piece, wide), BF),
            pltpu.VMEM((planes - 3, piece, wide), BF),
        ]
        + dma_pairs(PlaneSum.copies + 1 + Exchange.copies + planes - 2)
        + [pltpu.SemaphoreType.DMA((16,))],
        compiler_params=pltpu.CompilerParams(
            collective_id=1, has_side_effects=True, vmem_limit_bytes=62 * 2**20
        ),
        cost_estimate=pl.CostEstimate(
            flops=80_000_000_000, bytes_accessed=50_000_000, transcendentals=0
        ),
    )(
        starts,
        grad_two,
        cotangent,
        tables,
        gains,
        before_a,
        q,
        kk,
        vv,
        att,
        tokens,
        n1,
        residual,
        front,
        outs,
        pack_a,
        pack_b,
    )


def scatter_front(grad, pack, before, planes, group):
    rows, columns = grad.shape
    ds, half = rows // (4 * planes), columns // 2
    part = share_of(half, 0.66)
    first, second = pl.ds(0, part), pl.ds(part, half - part)
    block, wide = pack.shape[1:]

    def kernel(
        g_ref,
        pack_ref,
        before_ref,
        out_ref,
        shards_ref,
        from_core,
        kept,
        far_a,
        far_b,
        near_x,
        near_y,
        total_ref,
        from_z,
        own,
        passed,
        landing,
        rows_own,
        send_sems,
        recv_sems,
        local_sems,
    ):
        at = Links(planes, group, send_sems, recv_sems)
        at.barrier([at.x, at.y, at.core, at.diagonal] + at.along[1:])
        ring = RingSum(at, pack_ref, own, local_sems.at[0])
        ring.fetch(planes - 1)

        def row(k, dy, core):
            owner = ((at.z + k) % planes) * 4 + (at.yb + dy) % 2 * 2 + core
            return pl.multiple_of(owner * ds, 16)

        def column(dx):
            return pl.ds(pl.multiple_of((at.xb + dx) % 2 * half, 128), half)

        order = list(range(1, planes)) + [0]
        arrive, loads = {}, {}
        for k in order:
            for dy in (1, 0):
                loads[k, dy] = pltpu.make_async_copy(
                    g_ref.at[pl.ds(row(k, dy, at.c), ds)],
                    rows_own.at[k, dy],
                    local_sems.at[2 + 2 * k + dy],
                )
                loads[k, dy].start()
                arrive[k, dy] = at.send(
                    g_ref.at[pl.ds(row(k, dy, 1 - at.c), ds)], from_core.at[k, dy], at.core
                )
        ring.last(before_ref, passed, landing)
        step = 16
        x_second, y_first, x_first, y_second, to_x, to_y = {}, {}, {}, {}, {}, {}
        for k in order:
            for dy in (1, 0):
                loads[k, dy].wait()
                arrive[k, dy].wait_recv()
                for dx in (1, 0):

                    def store(chunk, total, k=k, dx=dx, dy=dy):
                        kept[k, dx, dy, chunk] = total.astype(BF)

                    add_rows(
                        store,
                        [
                            lambda q, k=k, dx=dx, dy=dy: rows_own[k, dy, q, column(dx)],
                            lambda q, k=k, dx=dx, dy=dy: from_core[k, dy, q, column(dx)],
                        ],
                        ds,
                        step,
                    )
                    if (dx, dy) == (1, 1):
                        to_y[k] = at.send(kept.at[k, 1, 1, :, first], far_a.at[k], at.y)
                        to_x[k] = at.send(kept.at[k, 1, 1, :, second], far_b.at[k], at.x)
                    elif (dx, dy) == (0, 1):
                        y_first[k] = at.send(
                            kept.at[k, 0, 1, :, first], near_y.at[k, :, first], at.y
                        )
                    elif (dx, dy) == (1, 0):
                        x_second[k] = at.send(
                            kept.at[k, 1, 0, :, second], near_x.at[k, :, second], at.x
                        )
        for k in order:
            to_y[k].wait_recv()

            def store(chunk, total, k=k):
                kept[k, 1, 0, chunk, first] = total.astype(BF)

            add_rows(
                store,
                [lambda q, k=k: kept[k, 1, 0, q, first], lambda q, k=k: far_a[k, q]],
                ds,
                step,
            )
            x_first[k] = at.send(kept.at[k, 1, 0, :, first], near_x.at[k, :, first], at.x)
            to_x[k].wait_recv()

            def store(chunk, total, k=k):
                kept[k, 0, 1, chunk, second] = total.astype(BF)

            add_rows(
                store,
                [lambda q, k=k: kept[k, 0, 1, q, second], lambda q, k=k: far_b[k, q]],
                ds,
                step,
            )
            y_second[k] = at.send(kept.at[k, 0, 1, :, second], near_y.at[k, :, second], at.y)
        arrive_z = {}
        for k in order:
            for copies in (x_second, y_first, x_first, y_second):
                copies[k].wait_recv()

            def store(chunk, total, k=k):
                total_ref[k, chunk] = total.astype(BF)

            add_rows(
                store,
                [
                    lambda q, k=k: kept[k, 0, 0, q],
                    lambda q, k=k: near_x[k, q],
                    lambda q, k=k: near_y[k, q],
                ],
                ds,
                step,
            )
            if k > 0:
                arrive_z[k] = at.send(total_ref.at[k], from_z.at[k], at.along[k])
            if k == order[1]:
                exchange = Exchange(at, ring.total(), shards_ref, ds)
                exchange.start(local_sems.at[1])
        exchange.onward()
        for k in range(1, planes):
            arrive_z[k].wait_recv()

        def store(chunk, total):
            out_ref[chunk] = total.astype(BF)

        add_rows(
            store,
            [lambda q: total_ref[0, q]]
            + [lambda q, k=k: from_z[k, q] for k in range(1, planes)],
            ds,
            step,
        )
        exchange.end()
        at.finish()

    return pl.pallas_call(
        kernel,
        out_shape=[
            jax.ShapeDtypeStruct((ds, half), BF),
            jax.ShapeDtypeStruct((PLANE, ds, wide), BF),
        ],
        in_specs=[anywhere(), anywhere(), whole_vmem()],
        out_specs=[whole_vmem(), anywhere()],
        scratch_shapes=[
            pltpu.VMEM((planes, 2, ds, columns), BF),
            pltpu.VMEM((planes, 2, 2, ds, half), BF),
            pltpu.VMEM((planes, ds, part), BF),
            pltpu.VMEM((planes, ds, half - part), BF),
            pltpu.VMEM((planes, ds, half), BF),
            pltpu.VMEM((planes, ds, half), BF),
            pltpu.VMEM((planes, ds, half), BF),
            pltpu.VMEM((planes, ds, half), BF),
            pltpu.VMEM((block, wide), BF),
            pltpu.VMEM((block, wide), BF),
            pltpu.VMEM((block, wide), BF),
            pltpu.VMEM((planes, 2, ds, columns), BF),
        ]
        + dma_pairs(planes * 8 + planes - 1 + 1 + Exchange.copies)
        + [pltpu.SemaphoreType.DMA((2 + 2 * planes,))],
        compiler_params=comm_params(3),
        cost_estimate=pl.CostEstimate(
            flops=50_000_000_000, bytes_accessed=20_000_000, transcendentals=0
        ),
    )(grad, pack, before)


def unpack(packs, residual, term, hs):
    ds, wide = packs[0].shape[1:]
    hid = wide // 3
    blocks = ds // hs

    def kernel(*refs):
        sources = refs[: EPD + 2]
        gate_out, up_out, down_out, sum_ref, raw_in, raw_down = refs[EPD + 2 : EPD + 8]
        held, (sems, load_sems) = refs[EPD + 8 : -2], refs[-2:]
        ins, (res_ref, term_ref) = held[:EPD], held[EPD:]
        loads = [
            pltpu.make_async_copy(src, dst, load_sems.at[n])
            for n, (src, dst) in enumerate(zip(sources, held))
        ]
        for copy in loads:
            copy.start()
        copies = {}
        for n, (e, p) in enumerate((e, p) for e in range(EPD) for p in range(PLANE)):
            slot = n % 4
            if p == 0:
                loads[e].wait()
            if n >= 4:
                for copy in copies[n - 4]:
                    copy.wait()

            def cast(chunk, p=p, e=e, slot=slot):
                raw_in[slot, 0, chunk] = ins[e][p, chunk, :hid].astype(F32)
                raw_in[slot, 1, chunk] = ins[e][p, chunk, hid : 2 * hid].astype(F32)

            row_loop(ds, 16, cast)
            for b in range(blocks):
                raw_down[slot, :, b * hid : (b + 1) * hid] = ins[e][
                    p, b * hs : (b + 1) * hs, 2 * hid :
                ].astype(F32)
            index = p * EPD + e
            copies[n] = [
                pltpu.make_async_copy(src, dst, sems.at[slot, i])
                for i, (src, dst) in enumerate(
                    (
                        (raw_in.at[slot, 0], gate_out.at[:, index]),
                        (raw_in.at[slot, 1], up_out.at[:, index]),
                        (raw_down.at[slot], down_out.at[:, index]),
                    )
                )
            ]
            for copy in copies[n]:
                copy.start()

        def add(chunk):
            sum_ref[chunk] = res_ref[chunk] + term_ref[chunk]

        for copy in loads[EPD:]:
            copy.wait()
        row_loop(residual.shape[0], 32, add)
        for n in range(EXP - 4, EXP):
            for copy in copies[n]:
                copy.wait()

    shape = jax.ShapeDtypeStruct
    return pl.pallas_call(
        kernel,
        in_specs=[anywhere()] * (EPD + 2),
        out_specs=[anywhere()] * 3 + [whole_vmem()],
        out_shape=[
            shape((ds, EXP, hid), F32),
            shape((ds, EXP, hid), F32),
            shape((hs, EXP, blocks * hid), F32),
            shape(residual.shape, F32),
        ],
        scratch_shapes=[
            pltpu.VMEM((4, 2, ds, hid), F32),
            pltpu.VMEM((4, hs, blocks * hid), F32),
        ]
        + [pltpu.VMEM(packs[0].shape, BF)] * EPD
        + [pltpu.VMEM(residual.shape, F32)] * 2
        + [pltpu.SemaphoreType.DMA((4, 3)), pltpu.SemaphoreType.DMA((EPD + 2,))],
        compiler_params=pltpu.CompilerParams(vmem_limit_bytes=60 * 2**20),
    )(*packs, residual, term)


def shards(
    reps,
    group,
    tokens,
    cotangent,
    routes,
    gates,
    starts,
    norm1_gain,
    w_query,
    w_key,
    w_value,
    w_out,
    norm2_gain,
    w_gate,
    w_up,
    w_down,
):
    planes = group // 4
    r, f = lax.axis_index("rep"), lax.axis_index("fsdp")
    xb, yb, c, z = r % 2, (f // 2) % 2, f % 2, f // 4
    mine = xb * 4 + yb * 2 + c

    def perm(to):
        return [
            (a * group + b, to(a, b)[0] * group + to(a, b)[1])
            for a in range(reps)
            for b in range(group)
        ]

    def pp(value, to):
        return lax.ppermute(value, AXES, perm(to))

    def go(value, dx, dy, dc):
        return pp(value, lambda a, b: (a ^ dx, b ^ (dy * 2 + dc)))

    def along(value, k):
        return pp(value, lambda a, b: (a, (b + 4 * k) % group))

    def all_reps(value):
        step = 2
        while step < reps:
            value = value + pp(value, lambda a, b, s=step: (a ^ s, b))
            step *= 2
        return value

    length, width = tokens.shape
    ds = w_query.shape[0]
    hs = w_down.shape[0]
    hid = w_gate.shape[2]
    kvd = w_key.shape[1]
    half_rows = length // 2

    mix = width + 2 * kvd
    gain_end = mix + 256
    gains = jnp.stack([norm1_gain.astype(BF), norm2_gain.astype(BF)], axis=1)
    own_mix = jnp.concatenate(
        [
            w_query.astype(BF),
            w_key.astype(BF),
            w_value.astype(BF),
            gains,
            jnp.zeros((ds, 254), BF),
        ],
        axis=1,
    )

    def rep_half(own):
        half = own.shape[1] // 2
        return lax.dynamic_slice(own, (0, xb * half), (ds, half))

    experts = jnp.arange(EXP, dtype=jnp.int32)[:, None, None]
    share = jnp.sum(jnp.where(routes[None] == experts, gates[None], 0.0), axis=2)
    pairs = PLANE // 2
    share = jnp.pad(share.reshape(PLANE, EPD, length), ((0, 0), (0, 8 - EPD), (0, 0)))

    front, wall_a, wall_b, grads_all, shares, gains_all, q, kk, vv, att, residual, n1, n2 = forward(
        starts,
        tokens,
        cotangent,
        rep_half(own_mix),
        rep_half(w_out.astype(BF)),
        share,
        w_gate,
        w_up,
        w_down,
        planes,
        group,
    )
    out_sum, pack_a, pack_b, grad_normed_two, before_a = run_experts(
        n2,
        grads_all.reshape(pairs, 2 * length, width),
        shares,
        wall_a.reshape(planes, 4 * ds, 3 * hid),
        wall_b.reshape(planes, 4 * ds, 3 * hid),
        planes,
        group,
    )
    input_grad, out_term, before_b, front_grad, shards_a = backward(
        starts,
        grad_normed_two,
        cotangent,
        tokens,
        residual,
        front,
        gains_all,
        q,
        kk,
        vv,
        att,
        n1,
        out_sum.reshape(PLANE, length, width),
        pack_a,
        before_a,
        pack_b,
        planes,
        group,
    )
    front_total, shards_b = scatter_front(front_grad, pack_b, before_b, planes, group)
    total = all_reps(front_total)
    gate_shard, up_shard, down_shard, output = unpack(
        [all_reps(shards_a), all_reps(shards_b)], residual, out_term, hs
    )
    other = go(total, 1, 0, 0)
    front_shard = jnp.where(
        xb == 0,
        jnp.concatenate([total, other], axis=1),
        jnp.concatenate([other, total], axis=1),
    ).astype(F32)
    return (
        output,
        input_grad,
        front_shard[:, mix],
        front_shard[:, :width],
        front_shard[:, width : width + kvd],
        front_shard[:, width + kvd : mix],
        front_shard[:, gain_end:],
        front_shard[:, mix + 1],
        gate_shard,
        up_shard,
        down_shard,
    )


def solution(mesh):
    reps, group = mesh.shape["rep"], mesh.shape["fsdp"]
    both, one = P(AXES, None), P("fsdp")
    flat, deep = P("fsdp", None), P("fsdp", None, None)

    def whole(*args):
        return shards(reps, group, *args)

    return jax.shard_map(
        whole,
        mesh=mesh,
        in_specs=(both, both, both, both, P(AXES), one, flat, flat, flat, flat, one, deep, deep, deep),
        out_specs=(both, both, one, flat, flat, flat, flat, one, deep, deep, deep),
        check_vma=False,
    )
```

```python
import math

import jax
import jax.numpy as jnp
import numpy as np
from jax import lax
from jax.experimental import pallas as pl
from jax.experimental.pallas import tpu as pltpu
from jax.sharding import PartitionSpec as P

HEADS = 24
KV_HEADS = 8
HEAD = 64
EXP = 16
PIECE = 256
AXES = ("rep", "fsdp")
EPSILON = 1e-05
NEG_FILL = -1e30
BF = jnp.bfloat16
F32 = jnp.float32
PLANE = 8
EPD = EXP // PLANE


def turn_tables(length):
    positions = np.arange(length, dtype=np.float32)[:, None]
    lanes = np.arange(2 * HEAD)
    powers = (lanes % (HEAD // 2)).astype(np.float32)
    rates = np.exp(powers * np.float32(-2.0 * math.log(10000.0) / HEAD))
    angles = positions * rates[None, :]
    low = (lanes % HEAD < HEAD // 2)[None, :]
    sines = np.sin(angles)
    tables = [np.cos(angles), np.where(low, -sines, 0.0), np.where(low, 0.0, sines)]
    return jnp.asarray(np.stack(tables).astype(np.float32))


def turned(values, tables, sign):
    ahead = pltpu.roll(values, 2 * HEAD - HEAD // 2, 1)
    back = pltpu.roll(values, HEAD // 2, 1)
    return values * tables[0] + sign * (ahead * tables[1] + back * tables[2])


def row_loop(rows, step, body):
    @pl.loop(0, rows // step)
    def _(n):
        body(pl.ds(pl.multiple_of(n * step, step), step))


def dot(a, b):
    return jnp.dot(a, b, preferred_element_type=F32)


def dot_nt(a, b):
    return lax.dot_general(a, b, (((1,), (1,)), ((), ())), preferred_element_type=F32)


def dot_tn(a, b):
    return lax.dot_general(a, b, (((0,), (0,)), ((), ())), preferred_element_type=F32)


def add_rows(store, terms, rows, step=32):
    step = min(step, rows)

    @pl.loop(0, rows // step)
    def _(n):
        chunk = pl.ds(pl.multiple_of(n * step, 16), step)
        total = terms[0](chunk).astype(F32)
        for term in terms[1:]:
            total = total + term(chunk).astype(F32)
        store(chunk, total)


class Links:
    def __init__(self, planes, group, send_sems, recv_sems):
        r, f = lax.axis_index("rep"), lax.axis_index("fsdp")
        self.xb, self.yb, self.c, self.z = r % 2, (f // 2) % 2, f % 2, f // 4
        self.x = (r + 1 - 2 * self.xb, f)
        self.y = (r, f + 2 - 4 * self.yb)
        self.core = (r, f + 1 - 2 * self.c)
        self.diagonal = (r, f + 3 - 4 * self.yb - 2 * self.c)
        self.others = {1: self.core, 2: self.y, 3: self.diagonal, 4: self.x}
        self.others.update({4 + n: (self.x[0], self.others[n][1]) for n in (1, 2, 3)})
        self.along = [None] + [(r, (f + 4 * k) % group) for k in range(1, planes)]
        self.planes, self.send_sems, self.recv_sems, self.copies = planes, send_sems, recv_sems, []

    def barrier(self, devices):
        semaphore = pltpu.get_barrier_semaphore()
        for device in devices:
            pl.semaphore_signal(
                semaphore, inc=1, device_id=device, device_id_type=pl.DeviceIdType.MESH
            )
        pl.semaphore_wait(semaphore, len(devices))

    def make(self, src, dst, device):
        n = len(self.copies)
        copy = pltpu.make_async_remote_copy(
            src_ref=src,
            dst_ref=dst,
            send_sem=self.send_sems.at[n],
            recv_sem=self.recv_sems.at[n],
            device_id=device,
            device_id_type=pl.DeviceIdType.MESH,
        )
        self.copies.append(copy)
        return copy

    def send(self, src, dst, device):
        copy = self.make(src, dst, device)
        copy.start()
        return copy

    def finish(self):
        for copy in self.copies:
            copy.wait_send()


def comm_params(number):
    return pltpu.CompilerParams(
        collective_id=number, has_side_effects=True, vmem_limit_bytes=56 * 2**20
    )


def dma_pairs(count):
    return [pltpu.SemaphoreType.DMA((count,)), pltpu.SemaphoreType.DMA((count,))]


def whole_vmem():
    return pl.BlockSpec(memory_space=pltpu.VMEM)


def anywhere():
    return pl.BlockSpec(memory_space=pl.ANY)


def share_of(half, share):
    return int(half * share) // 128 * 128


def both_sides(values, store, pair):
    low = lax.broadcasted_iota(jnp.int32, values.shape, 1) < HEAD
    swapped = pltpu.roll(values, HEAD, 1)
    store(0, 2 * pair, jnp.where(low, values, 0.0).astype(BF))
    store(1, 2 * pair, jnp.where(low, 0.0, swapped).astype(BF))
    store(0, 2 * pair + 1, jnp.where(low, swapped, 0.0).astype(BF))
    store(1, 2 * pair + 1, jnp.where(low, 0.0, values).astype(BF))


def fill_bias(bias, start):
    length = bias.shape[0]

    def body(chunk):
        shape = (chunk.size, length)
        i = lax.broadcasted_iota(jnp.int32, shape, 0) + chunk.start
        j = lax.broadcasted_iota(jnp.int32, shape, 1)
        in_i = (i >= start) & (i < start + PIECE)
        in_j = (j >= start) & (j < start + PIECE)
        bias[chunk] = jnp.where((j <= i) | (in_i & in_j), 0.0, NEG_FILL)

    row_loop(length, 64, body)


def softmax_rows(query, key, bias):
    scores = dot_nt(query, key) + bias
    exponent = jnp.exp(scores - jnp.max(scores, axis=1, keepdims=True))
    return exponent * (1.0 / jnp.sum(exponent, axis=1, keepdims=True))


PAIRS = HEADS // 2
GROUP = HEADS // KV_HEADS
LANES = 2 * HEAD


class FrontGather:
    def __init__(self, at, own, full, base, part, own_sem):
        self.at, self.own, self.full, self.base = at, own, full, base
        self.ds, self.half = own.shape
        self.first, self.second = (0, part), (part, self.half - part)
        self.every = (0, self.half)
        self.own_copy = pltpu.make_async_copy(own, self.region(0, 0, 0, self.every), own_sem)
        self.x_first, self.x_second, self.y_first, self.y_second, self.far = [], [], [], [], []

    def region(self, k, dx, dy, span):
        at = self.at
        row = (((at.z + at.planes - k) % at.planes) * 4 + (at.yb + dy) % 2 * 2 + at.c) * self.ds
        col = self.base + (at.xb + dx) % 2 * self.half + span[0]
        return self.full.at[
            pl.ds(pl.multiple_of(row, 16), self.ds), pl.ds(pl.multiple_of(col, 128), span[1])
        ]

    def pass_on(self, k, dx, dy, span, device):
        here = self.region(k, dx, dy, span)
        return self.at.send(here, here, device)

    def start(self):
        at = self.at
        self.own_copy.start()
        here = self.region(0, 0, 0, self.every)
        self.arrive = [None] + [at.send(self.own, here, at.along[k]) for k in range(1, at.planes)]

    def start_plane(self):
        here = self.region(0, 0, 0, self.every)
        self.to_core = [self.at.send(self.own, here, self.at.core)]
        self.spread(0)

    def spread(self, k):
        at = self.at
        for device, span, copies in (
            (at.x, self.first, self.x_first),
            (at.y, self.second, self.y_second),
            (at.x, self.second, self.x_second),
            (at.y, self.first, self.y_first),
        ):
            here = self.region(k, 0, 0, span)
            src = self.own.at[:, pl.ds(span[0], span[1])] if k == 0 else here
            copies.append(at.send(src, here, device))
        if k > 0:
            self.to_core.append(self.pass_on(k, 0, 0, self.every, at.core))

    def advance(self, k):
        self.arrive[k].wait_recv()
        self.spread(k)

    def onward(self, k):
        at = self.at
        self.x_first[k].wait_recv()
        self.far.append((k, self.first, self.pass_on(k, 1, 0, self.first, at.y)))
        self.y_second[k].wait_recv()
        self.far.append((k, self.second, self.pass_on(k, 0, 1, self.second, at.x)))
        self.x_second[k].wait_recv()
        self.to_core.append(self.pass_on(k, 1, 0, self.every, at.core))
        self.y_first[k].wait_recv()
        self.to_core.append(self.pass_on(k, 0, 1, self.every, at.core))

    def finish_far(self):
        for k, span, copy in self.far:
            copy.wait_recv()
            self.to_core.append(self.pass_on(k, 1, 1, span, self.at.core))

    def finish(self):
        for copy in self.to_core:
            copy.wait_recv()
        self.own_copy.wait()

    @staticmethod
    def copies(planes):
        return planes - 1 + planes * 11


def forward(
    starts, tokens, cotangent, own_mix, own_out, shares, w_gate, w_up, w_down, planes, group
):
    length, width = tokens.shape
    ds = own_mix.shape[0]
    hid, hs = w_gate.shape[2], w_down.shape[0]
    wide = 3 * hid
    kvd = KV_HEADS * HEAD
    mix = width + 2 * kvd
    base = 2 * own_mix.shape[1]
    columns = base + width
    row_half = length // 2
    low_rows, high_rows = pl.ds(0, row_half), pl.ds(row_half, row_half)
    tables = turn_tables(length)

    def kernel(
        starts_ref,
        x_ref,
        cot_ref,
        own_mix_ref,
        own_out_ref,
        share_ref,
        gate_hbm,
        up_hbm,
        down_hbm,
        tab_ref,
        front_out,
        wall_a,
        wall_b,
        grads_out,
        shares_out,
        gain_ref,
        q_out,
        kk_out,
        vv_out,
        att_out,
        res_out,
        n1_out,
        n2_out,
        q_ref,
        kk_ref,
        vv_ref,
        att_ref,
        res_ref,
        n1_ref,
        n2_ref,
        front,
        bias,
        packed,
        raw_in,
        raw_down,
        send_sems,
        recv_sems,
        local_sems,
        load_sems,
    ):
        at = Links(planes, group, send_sems, recv_sems)
        at.barrier(list(at.others.values()) + at.along[1:])
        walls = (wall_a, wall_b)
        shard = at.yb * 2 + at.c

        order = [(s, e) for e in range(EPD) for s in range(4)]

        def load(n):
            s, e = order[n]
            index = (at.xb * 4 + s) * EPD + e
            copies = [
                pltpu.make_async_copy(src, dst, load_sems.at[n % 2, i])
                for i, (src, dst) in enumerate(
                    (
                        (gate_hbm.at[:, index], raw_in.at[n % 2, 0]),
                        (up_hbm.at[:, index], raw_in.at[n % 2, 1]),
                        (down_hbm.at[:, index], raw_down.at[n % 2]),
                    )
                )
            ]
            for copy in copies:
                copy.start()
            return copies

        loads = {n: load(n) for n in range(2)}

        def pack(e):
            for n in range(4 * e, 4 * e + 4):
                s = order[n][0]
                for copy in loads[n]:
                    copy.wait()

                def cast(chunk, n=n, s=s):
                    packed[s, e, chunk, :hid] = raw_in[n % 2, 0, chunk].astype(BF)
                    packed[s, e, chunk, hid : 2 * hid] = raw_in[n % 2, 1, chunk].astype(BF)

                row_loop(ds, 16, cast)
                for i in range(width // hid):
                    packed[s, e, i * hs : (i + 1) * hs, 2 * hid :] = raw_down[
                        n % 2, :, i * hid : (i + 1) * hid
                    ].astype(BF)
                if n + 2 < len(order):
                    loads[n + 2] = load(n + 2)
            copy = pltpu.make_async_copy(
                packed.at[shard, e], walls[e].at[at.z, shard], local_sems.at[e]
            )
            copy.start()
            locals_.append(copy)

        locals_ = []

        def put(*pairs):
            for src, dst in pairs:
                n = len(stored)
                stored.append(pltpu.make_async_copy(src, dst, local_sems.at[7 + n]))
                stored[n].start()

        stored = []

        def exchange(e):
            copies = []
            for dy, dc, device in ((1, 0, at.y), (1, 1, at.diagonal), (0, 1, at.core)):
                target = (at.yb + dy) % 2 * 2 + (at.c + dc) % 2
                copies.append(
                    at.send(packed.at[target, e], walls[e].at[at.z, shard], device)
                )
            return copies

        ring = {}

        def ring_first(e, copies):
            sent = [
                at.send(packed.at[shard, e], walls[e].at[at.z, shard], at.along[1])
            ]
            for copy, (dy, dc) in zip(copies, ((1, 0), (1, 1), (0, 1))):
                copy.wait_recv()
                piece = walls[e].at[at.z, (at.yb + dy) % 2 * 2 + (at.c + dc) % 2]
                sent.append(at.send(piece, piece, at.along[1]))
            ring[e] = (1, sent)

        def ring_next(e):
            step, sent = ring[e]
            for copy in sent:
                copy.wait_recv()
            if step < planes - 1:
                piece = walls[e].at[(at.z + planes - step) % planes]
                ring[e] = (step + 1, [at.send(piece, piece, at.along[1])])
            else:
                ring[e] = (planes, [])

        mixing = FrontGather(
            at, own_mix_ref, front, 0, share_of(base // 2, 0.25), local_sems.at[2]
        )
        closing = FrontGather(
            at, own_out_ref, front, base, share_of(width // 2, 0.25), local_sems.at[5]
        )

        def share_slot(j):
            return shares_out.at[j // 2, :, pl.ds(j % 2 * length, length)]

        mixing.start()
        mixing.start_plane()
        closing.start()
        pack(0)
        first_exchange = exchange(0)
        place = at.xb * 4 + shard
        locals_.append(pltpu.make_async_copy(share_ref.at[place], share_slot(0), local_sems.at[6]))
        locals_[-1].start()
        got_shares = []
        for j, device in at.others.items():
            other = (
                (at.xb + j // 4) % 2 * 4 + (at.yb + j // 2 % 2) % 2 * 2 + (at.c + j % 2) % 2
            )
            got_shares.append(at.send(share_ref.at[other], share_slot(j), device))
        pack(1)
        fill_bias(bias, starts_ref[0])
        for k in range(1, planes):
            mixing.advance(k)
            mixing.onward(k - 1)
        ring_first(0, first_exchange)
        mixing.onward(planes - 1)
        mixing.finish_far()
        closing.start_plane()
        for k in range(1, planes):
            closing.advance(k)
        mixing.finish()
        def gather_start(src, out):
            def slot(j, rows=pl.ds(0, length)):
                return out.at[j, rows]

            got = {
                "x_low": at.send(src.at[low_rows], slot(4, low_rows), at.x),
                "y_high": at.send(src.at[high_rows], slot(2, high_rows), at.y),
                "x_high": at.send(src.at[high_rows], slot(4, high_rows), at.x),
                "y_low": at.send(src.at[low_rows], slot(2, low_rows), at.y),
                "core": [at.send(src, slot(1), at.core)],
            }
            return slot, got

        def gather_middle(slot, got):
            got["x_low"].wait_recv()
            got["far_low"] = at.send(slot(4, low_rows), slot(6, low_rows), at.y)
            got["core"].append(at.send(slot(4, low_rows), slot(5, low_rows), at.core))
            got["y_high"].wait_recv()
            got["far_high"] = at.send(slot(2, high_rows), slot(6, high_rows), at.x)
            got["core"].append(at.send(slot(2, high_rows), slot(3, high_rows), at.core))

        def gather_last(slot, got):
            got["x_high"].wait_recv()
            got["core"].append(at.send(slot(4, high_rows), slot(5, high_rows), at.core))
            got["y_low"].wait_recv()
            got["core"].append(at.send(slot(2, low_rows), slot(3, low_rows), at.core))
            got["far_low"].wait_recv()
            got["core"].append(at.send(slot(6, low_rows), slot(7, low_rows), at.core))
            got["far_high"].wait_recv()
            got["core"].append(at.send(slot(6, high_rows), slot(7, high_rows), at.core))

        gain_ref[...] = front[:, mix : mix + 128].astype(F32).T[:8]

        def norm(chunk):
            x = x_ref[chunk].astype(F32)
            inv = lax.rsqrt(jnp.mean(x * x, axis=1, keepdims=True) + EPSILON)
            n1_ref[chunk] = (x * inv * gain_ref[0:1, :]).astype(BF)

        row_loop(length, 64, norm)
        block = 4 * LANES
        for n in range(mix // block):
            raw = dot(n1_ref[...], front[:, n * block : (n + 1) * block])
            for j in range(4):
                col = n * block + j * LANES
                values = raw[:, j * LANES : (j + 1) * LANES]
                if col < width:
                    turned_low = turned(values, tab_ref, 1.0).astype(BF).astype(F32)
                    q_ref[:, col : col + LANES] = (turned_low * (1.0 / math.sqrt(HEAD))).astype(BF)
                else:
                    target, start = (kk_ref, width) if col < width + kvd else (vv_ref, width + kvd)
                    if col < width + kvd:
                        values = turned(values, tab_ref, 1.0)

                    def store(side, head, side_values, target=target):
                        target[side, head] = side_values

                    both_sides(values, store, (col - start) // LANES)
        ring_next(0)
        put((q_ref, q_out), (kk_ref, kk_out), (vv_ref, vv_out), (n1_ref, n1_out))
        grads = gather_start(cot_ref, grads_out)
        cot_copy = pltpu.make_async_copy(cot_ref, grads_out.at[0], local_sems.at[4])
        cot_copy.start()


        def attend(pairs):
            @pl.loop(*pairs)
            def _(p):
                cols = pl.ds(pl.multiple_of(p * LANES, LANES), LANES)
                total = None
                for side in range(2):
                    head = (2 * p + side) // GROUP
                    probs = softmax_rows(q_ref[:, cols], kk_ref[side, head], bias[...])
                    term = dot(probs.astype(BF), vv_ref[side, head])
                    total = term if total is None else total + term
                att_ref[:, cols] = total.astype(BF)

        attend((0, PAIRS // 3))
        for k in range(planes):
            closing.onward(k)
        attend((PAIRS // 3, 2 * PAIRS // 3))
        gather_middle(*grads)
        second_exchange = exchange(1)
        attend((2 * PAIRS // 3, PAIRS))
        put((att_ref, att_out))
        closing.finish_far()
        closing.finish()
        front_copy = pltpu.make_async_copy(front, front_out, local_sems.at[3])
        front_copy.start()
        ring_next(0)
        for n in range(width // block):
            cols = slice(n * block, (n + 1) * block)
            res_ref[:, cols] = x_ref[:, cols].astype(F32) + dot(
                att_ref[...], front[:, base + n * block : base + (n + 1) * block]
            )

        def norm_two(chunk):
            r = res_ref[chunk]
            inv = lax.rsqrt(jnp.mean(r * r, axis=1, keepdims=True) + EPSILON)
            n2_ref[chunk] = (r * inv * gain_ref[1:2, :]).astype(BF)

        row_loop(length, 64, norm_two)
        put((n2_ref, n2_out), (res_ref, res_out))
        gather_last(*grads)
        while ring[0][0] < planes:
            ring_next(0)
        for copy in grads[1]["core"] + second_exchange + got_shares:
            copy.wait_recv()
        for copy in locals_ + stored + [front_copy, cot_copy]:
            copy.wait()
        at.finish()

    shape = jax.ShapeDtypeStruct
    count = 2 * FrontGather.copies(planes) + 2 * 3 + 4 + planes - 2 + 13 + 7
    return pl.pallas_call(
        kernel,
        out_shape=[
            shape((width, columns), BF),
            shape((planes, 4, ds, wide), BF),
            shape((planes, 4, ds, wide), BF),
            shape((PLANE, length, width), BF),
            shape((PLANE // 2, 8, 2 * length), F32),
            shape((8, width), F32),
            shape((length, width), BF),
            shape((2, KV_HEADS, length, LANES), BF),
            shape((2, KV_HEADS, length, LANES), BF),
            shape((length, width), BF),
            shape((length, width), F32),
            shape((length, width), BF),
            shape((length, width), BF),
        ],
        in_specs=[pl.BlockSpec(memory_space=pltpu.SMEM)]
        + [whole_vmem()] * 5
        + [anywhere()] * 3
        + [whole_vmem()],
        out_specs=[anywhere()] * 5 + [whole_vmem()] + [anywhere()] * 7,
        scratch_shapes=[
            pltpu.VMEM((length, width), BF),
            pltpu.VMEM((2, KV_HEADS, length, LANES), BF),
            pltpu.VMEM((2, KV_HEADS, length, LANES), BF),
            pltpu.VMEM((length, width), BF),
            pltpu.VMEM((length, width), F32),
            pltpu.VMEM((length, width), BF),
            pltpu.VMEM((length, width), BF),
            pltpu.VMEM((width, columns), BF),
            pltpu.VMEM((length, length), F32),
            pltpu.VMEM((4, EPD, ds, wide), BF),
            pltpu.VMEM((2, 2, ds, hid), F32),
            pltpu.VMEM((2, hs, width), F32),
        ]
        + dma_pairs(count)
        + [pltpu.SemaphoreType.DMA((14,)), pltpu.SemaphoreType.DMA((2, 3))],
        compiler_params=comm_params(0),
        cost_estimate=pl.CostEstimate(
            flops=150_000_000_000, bytes_accessed=20_000_000, transcendentals=0
        ),
    )(
        starts, tokens, cotangent, own_mix, own_out, shares, w_gate, w_up, w_down, tables
    )


class PlaneSum:
    def __init__(self, at, length, odd, even, from_core, far, near):
        self.at, self.odd, self.even, self.core = at, odd, even, from_core
        self.far, self.near = far, near
        self.length = length
        self.half = self.length // 2
        self.low, self.high = pl.ds(0, self.half), pl.ds(self.half, self.half)
        self.arrive = {
            j: at.make(odd(j), self.part(j, pl.ds(0, length)), at.core) for j in (3, 2, 1, 0)
        }
        low, high = self.low, self.high
        self.far_y = at.make(self.part(3, low), far.at[0], at.y)
        self.far_x = at.make(self.part(3, high), far.at[1], at.x)
        self.x_high = at.make(self.part(2, high), near.at[0, high], at.x)
        self.y_low = at.make(self.part(1, low), near.at[1, low], at.y)
        self.x_low = at.make(self.part(2, low), near.at[0, low], at.x)
        self.y_high = at.make(self.part(1, high), near.at[1, high], at.y)

    def rows(self, j, chunk, base=0):
        return pl.ds(pl.multiple_of(chunk.start + j * self.length + base, 16), chunk.size)

    def part(self, j, rows):
        return self.core.at[pl.ds(j * self.length + rows.start, rows.size)]

    def start(self, j):
        self.arrive[j].start()

    def add_core(self, j):
        self.arrive[j].wait_recv()
        core = self.core

        def store(chunk, total):
            core[self.rows(j, chunk)] = total.astype(BF)

        add_rows(store, [lambda q: self.even(j, q), lambda q: core[self.rows(j, q)]], self.length)

    def add_far(self, j, n, base):
        core, far = self.core, self.far

        def store(chunk, total):
            core[self.rows(j, chunk, base)] = total.astype(BF)

        add_rows(store, [lambda q: core[self.rows(j, q, base)], lambda q: far[n, q]], self.half)

    def send_far(self):
        self.add_core(3)
        self.far_y.start()
        self.far_x.start()

    def send_x(self):
        self.add_core(2)
        self.x_high.start()

    def send_y(self):
        self.add_core(1)
        self.y_low.start()

    def onward_x(self):
        self.far_y.wait_recv()
        self.add_far(2, 0, 0)
        self.x_low.start()

    def onward_y(self):
        self.far_x.wait_recv()
        self.add_far(1, 1, self.half)
        self.y_high.start()

    def end(self, store):
        self.arrive[0].wait_recv()
        for copy in (self.x_high, self.y_low, self.x_low, self.y_high):
            copy.wait_recv()
        core, near = self.core, self.near
        terms = [lambda q: self.even(0, q), lambda q: core[q]]
        terms += [lambda q: near[0, q], lambda q: near[1, q]]
        add_rows(store, terms, self.length)

    copies = 10


class RingSum:
    def __init__(self, at, pack, own, own_sem):
        self.at, self.pack, self.own, self.own_sem = at, pack, own, own_sem
        self.index = [(at.z + at.planes - k) % at.planes for k in range(at.planes)]

    def block(self, k):
        return self.pack.at[self.index[k]]

    def fetch(self, k):
        self.fetched = pltpu.make_async_copy(self.block(k), self.own, self.own_sem)
        self.fetched.start()

    def add(self, source, target):
        self.fetched.wait()

        def store(chunk, total):
            target[chunk] = total.astype(BF)

        add_rows(store, [lambda q: source[q], lambda q: self.own[q]], self.own.shape[0], 16)

    def first(self, slots):
        self.slots, self.step = slots, 1
        sources = [self.block(1)] + slots[:-1]
        self.sent = [
            self.at.make(src, dst, self.at.along[1]) for src, dst in zip(sources, slots)
        ]
        self.fetches = {
            k: pltpu.make_async_copy(self.block(k), self.own, self.own_sem)
            for k in range(2, len(slots) + 1)
        }
        self.sent[0].start()
        self.begin_fetch(2)

    def begin_fetch(self, k):
        if k in self.fetches:
            self.fetched = self.fetches[k]
            self.fetched.start()

    def next(self):
        if self.step < len(self.slots):
            here = self.slots[self.step - 1]
            self.sent[self.step - 1].wait_recv()
            self.add(here, here)
            self.sent[self.step].start()
            self.step += 1
            self.begin_fetch(self.step + 1)

    def rest(self):
        while self.step < len(self.slots):
            self.next()
        self.sent[-1].wait_recv()

    def last(self, before, sent, landing):
        self.add(before, sent)
        self.landing = landing
        self.copy = self.at.send(sent, landing, self.at.along[1])
        self.fetch(0)

    def total(self):
        self.copy.wait_recv()
        self.add(self.landing, self.landing)
        return self.landing


def run_experts(tokens, grads, shares, wall_a, wall_b, planes, group):
    pairs, count, width = grads.shape
    length = count // 2
    piece, wide = wall_a.shape[1:]
    hid = wide // 3
    ds, hs, blocks = width // group, hid // group, width // hid
    half = length // 2
    low, high, full = pl.ds(0, half), pl.ds(half, half), pl.ds(0, length)

    def kernel(
        n2_hbm,
        g_hbm,
        share_ref,
        wall_a_ref,
        wall_b_ref,
        out_hbm,
        pack_a,
        pack_b,
        sum_ref,
        passed,
        xs,
        dxs,
        w_a,
        w_b,
        down_a,
        down_b,
        in_sum,
        down_sum,
        g_tile,
        o_tile,
        pre,
        act,
        far,
        near,
        ring_slots,
        own,
        free,
        send_sems,
        recv_sems,
        local_sems,
    ):
        at = Links(planes, group, send_sems, recv_sems)
        at.barrier([at.x, at.y, at.core] + at.along[1:])
        index = [(at.z + planes - k) % planes for k in range(planes)]

        def local(src, dst, n):
            copy = pltpu.make_async_copy(src, dst, local_sems.at[n])
            copy.start()
            return copy

        def slot(j, rows=full):
            return xs.at[j // 2, pl.ds(j % 2 * length + rows.start, rows.size)]

        pieces = [
            w_b.at[pl.ds(pl.multiple_of(index[k] * piece, 16), piece)] for k in range(planes)
        ]

        local(n2_hbm, slot(0), 0).wait()
        x_low = at.send(slot(0, low), slot(4, low), at.x)
        y_high = at.send(slot(0, high), slot(2, high), at.y)
        x_high = at.send(slot(0, high), slot(4, high), at.x)
        y_low = at.send(slot(0, low), slot(2, low), at.y)
        near_core = at.send(slot(0), slot(1), at.core)
        ring = [at.make(wall_b_ref.at[at.z], pieces[0], at.along[1])]
        ring += [at.make(piece_ref, piece_ref, at.along[1]) for piece_ref in pieces[1:-1]]
        ring[0].start()
        load_b = local(wall_b_ref.at[at.z], pieces[0], 1)
        loads = [
            local(wall_a_ref.at[n], w_a.at[pl.ds(n * piece, piece)], 2 + n) for n in range(planes)
        ]
        state = {"ring": 0}
        far_low = at.make(slot(4, low), slot(6, low), at.y)
        far_high = at.make(slot(2, high), slot(6, high), at.x)
        passed_on = {
            (j, rows.start): at.make(slot(j, rows), slot(j + 1, rows), at.core)
            for j in (4, 2, 6)
            for rows in (low, high)
        }

        def ring_next():
            ring[state["ring"]].wait_recv()
            state["ring"] += 1
            if state["ring"] < planes - 1:
                ring[state["ring"]].start()

        def core_arrival(j):
            passed_on[j, low.start].wait_recv()
            passed_on[j, high.start].wait_recv()

        def spread():
            x_low.wait_recv()
            far_low.start()
            passed_on[4, low.start].start()
            y_high.wait_recv()
            far_high.start()
            passed_on[2, high.start].start()
            ring_next()
            x_high.wait_recv()
            passed_on[4, high.start].start()
            y_low.wait_recv()
            passed_on[2, low.start].start()
            core_arrival(4)

        def spread_far():
            far_low.wait_recv()
            passed_on[6, low.start].start()
            far_high.wait_recv()
            passed_on[6, high.start].start()
            core_arrival(6)

        def unpack_down(w, down):
            for s in range(group):
                for b in range(blocks):
                    down[s * hs : (s + 1) * hs, b * hid : (b + 1) * hid] = w[
                        s * ds + b * hs : s * ds + (b + 1) * hs, 2 * hid :
                    ]

        def clear():
            def body(chunk):
                in_sum[chunk] = jnp.zeros((chunk.size, 2 * hid), F32)

            row_loop(width, 64, body)

            def body_down(chunk):
                down_sum[chunk] = jnp.zeros((chunk.size, width), F32)

            row_loop(hid, 64, body_down)

        def out_copy(pair):
            return pltpu.make_async_copy(o_tile, out_hbm.at[pair], local_sems.at[0])

        def out_free(step, pair):
            @pl.when(step > 0)
            def _():
                out_copy(pair).wait()

        def tile(e, step, pair, w, down, middle):
            g_load = pltpu.make_async_copy(g_hbm.at[pair], g_tile, local_sems.at[1])
            g_load.start()
            x = xs.at[pair]
            share = share_ref[pair].T[:, e : e + 1]
            part = hid // 2
            for n in range(2):
                cols = slice(n * part, (n + 1) * part)
                up_cols = slice(hid + n * part, hid + (n + 1) * part)
                gate = dot(x[...], w[:, cols])
                up = dot(x[...], w[:, up_cols])
                if n == 0:
                    g_load.wait()
                    if e > 0:
                        out_free(step, pair)
                        before = pltpu.make_async_copy(out_hbm.at[pair], o_tile, local_sems.at[2])
                        before.start()
                inner = dot_nt(g_tile[...], down[cols, :]) * share
                sig = jax.nn.sigmoid(gate)
                swish = gate * sig
                act[:, cols] = (share * (swish * up)).astype(BF)
                pre[:, cols] = (inner * up * sig * (1.0 + gate * (1.0 - sig))).astype(BF)
                pre[:, up_cols] = (inner * swish).astype(BF)
            middle()
            if e > 0:
                before.wait()
            else:
                out_free(step, pair)
            for n in range(width // hid):
                cols = slice(n * hid, (n + 1) * hid)
                out = dot(act[...], down[:, cols])
                dx = dot_nt(pre[...], w[cols, : 2 * hid])
                if e > 0:
                    out = out + o_tile[:, cols].astype(F32)
                    dx = dx + dxs[pair, :, cols].astype(F32)
                o_tile[:, cols] = out.astype(BF)
                dxs[pair, :, cols] = dx.astype(BF)
                in_sum[cols, :] += dot_tn(x[:, cols], pre[...])
                down_sum[:, cols] += dot_tn(act[...], g_tile[:, cols])
            out_copy(pair).start()

        def pack(target):
            out_copy(0).wait()
            copies = [None, None]
            for n in range(planes):
                base = n % 2 * piece
                if copies[n % 2] is not None:
                    copies[n % 2].wait()

                def body(chunk, n=n, base=base):
                    rows = pl.ds(pl.multiple_of(chunk.start + base, 16), chunk.size)
                    source = pl.ds(pl.multiple_of(chunk.start + n * piece, 16), chunk.size)
                    o_tile[rows, : 2 * hid] = in_sum[source].astype(BF)

                row_loop(piece, 32, body)
                for s in range(4):
                    for b in range(blocks):
                        row = base + s * ds + b * hs
                        o_tile[row : row + hs, 2 * hid :] = down_sum[
                            (n * 4 + s) * hs : (n * 4 + s + 1) * hs, b * hid : (b + 1) * hid
                        ].astype(BF)
                copies[n % 2] = local(o_tile.at[pl.ds(base, piece)], target.at[n], 3 + n % 2)
            for copy in copies:
                copy.wait()

        clear()
        for copy in loads:
            copy.wait()
        load_b.wait()
        unpack_down(w_a, down_a)
        near_core.wait_recv()

        @pl.loop(0, pairs)
        def _(step):
            @pl.when(step == 1)
            def _():
                spread()

            @pl.when(step == 2)
            def _():
                core_arrival(2)

            @pl.when(step == 3)
            def _():
                spread_far()

            def middle():
                @pl.when(step == 2)
                def _():
                    ring_next()

            tile(0, step, 2 * step % 3 + step // 3 * 3, w_a, down_a, middle)

        pl.semaphore_signal(free, inc=1, device_id=at.core, device_id_type=pl.DeviceIdType.MESH)
        pack(pack_a)
        sums = RingSum(at, pack_a, own, local_sems.at[5])
        sums.first([ring_slots.at[n] for n in range(planes - 3)] + [passed])
        clear()
        while state["ring"] < planes - 1:
            ring_next()
        unpack_down(w_b, down_b)
        pl.semaphore_wait(free, 1)
        plane = PlaneSum(
            at,
            length,
            lambda j: dxs.at[j, pl.ds(length, length)],
            lambda j, q: dxs[j, q],
            w_a,
            far,
            near,
        )

        @pl.loop(0, pairs)
        def _(step):
            def middle():
                @pl.when(step == 1)
                def _():
                    plane.send_far()

                @pl.when(step == 2)
                def _():
                    plane.send_x()
                    sums.next()

                @pl.when(step == 3)
                def _():
                    plane.send_y()
                    plane.onward_y()

            tile(1, step, pairs - 1 - step, w_b, down_b, middle)
            for n in range(pairs):

                @pl.when(step == n)
                def _(n=n):
                    plane.start(pairs - 1 - n)
                    if n == 2:
                        plane.onward_x()

        pack(pack_b)

        def store(chunk, total):
            sum_ref[chunk] = total

        plane.end(store)
        sums.rest()
        at.finish()

    shape = jax.ShapeDtypeStruct
    return pl.pallas_call(
        kernel,
        in_specs=[anywhere()] * 2 + [whole_vmem()] + [anywhere()] * 2,
        out_specs=[anywhere()] * 3 + [whole_vmem()] * 2,
        out_shape=[
            shape((pairs, count, width), BF),
            shape((planes, piece, wide), BF),
            shape((planes, piece, wide), BF),
            shape((length, width), F32),
            shape((piece, wide), BF),
        ],
        scratch_shapes=[
            pltpu.VMEM((pairs, count, width), BF),
            pltpu.VMEM((pairs, count, width), BF),
            pltpu.VMEM((width, wide), BF),
            pltpu.VMEM((width, wide), BF),
            pltpu.VMEM((hid, width), BF),
            pltpu.VMEM((hid, width), BF),
            pltpu.VMEM((width, 2 * hid), F32),
            pltpu.VMEM((hid, width), F32),
            pltpu.VMEM((count, width), BF),
            pltpu.VMEM((count, width), BF),
            pltpu.VMEM((count, 2 * hid), BF),
            pltpu.VMEM((count, hid), BF),
            pltpu.VMEM((2, half, width), BF),
            pltpu.VMEM((2, length, width), BF),
            pltpu.VMEM((planes - 3, piece, wide), BF),
            pltpu.VMEM((piece, wide), BF),
            pltpu.SemaphoreType.REGULAR,
        ]
        + dma_pairs(13 + planes - 1 + PlaneSum.copies + planes - 2)
        + [pltpu.SemaphoreType.DMA((2 + planes,))],
        compiler_params=pltpu.CompilerParams(
            collective_id=2, has_side_effects=True, vmem_limit_bytes=63 * 2**20
        ),
        cost_estimate=pl.CostEstimate(
            flops=100_000_000_000, bytes_accessed=50_000_000, transcendentals=0
        ),
    )(tokens, grads, shares, wall_a, wall_b)


class Exchange:
    def __init__(self, at, total, out, ds):
        self.at, self.total, self.out, self.ds = at, total, out, ds
        self.shard = at.yb * 2 + at.c

    def place(self, dx, dy, dc):
        at = self.at
        return (at.xb + dx) % 2 * 4 + (at.yb + dy) % 2 * 2 + (at.c + dc) % 2

    def rows(self, dy, dc):
        at = self.at
        shard = (at.yb + dy) % 2 * 2 + (at.c + dc) % 2
        return self.total.at[pl.ds(pl.multiple_of(shard * self.ds, 16), self.ds)]

    def start(self, sem):
        at = self.at
        here = self.out.at[self.place(0, 0, 0)]
        self.local = pltpu.make_async_copy(self.rows(0, 0), here, sem)
        self.local.start()
        self.got = [
            (dy, dc, at.send(self.rows(dy, dc), here, device))
            for dy, dc, device in ((1, 0, at.y), (1, 1, at.diagonal), (0, 1, at.core))
        ]
        self.across = [at.send(self.rows(0, 0), here, at.x)]

    def onward(self):
        at = self.at
        for dy, dc, copy in self.got:
            copy.wait_recv()
            piece = self.out.at[self.place(0, dy, dc)]
            self.across.append(at.send(piece, piece, at.x))

    def end(self):
        for copy in self.across:
            copy.wait_recv()
        self.local.wait()

    copies = 7


def backward(
    starts,
    grad_two,
    cotangent,
    tokens,
    residual,
    front,
    gains,
    q,
    kk,
    vv,
    att,
    n1,
    outs,
    pack_a,
    before_a,
    pack_b,
    planes,
    group,
):
    length, width = tokens.shape
    columns = front.shape[1]
    kvd = KV_HEADS * HEAD
    mix = width + 2 * kvd
    block = 4 * LANES
    tables = turn_tables(length)
    piece, wide = pack_a.shape[1:]
    ds = piece // 4
    extra = columns - mix - width
    part = block // 2

    def kernel(
        starts_ref,
        d_ref,
        cot_ref,
        tab_ref,
        gain_ref,
        before_ref,
        q_hbm,
        kk_hbm,
        vv_hbm,
        att_hbm,
        x_hbm,
        n1_hbm,
        res_hbm,
        w_hbm,
        outs_ref,
        pack_a_ref,
        pack_b_ref,
        in_ref,
        sum_ref,
        passed_b,
        grad_hbm,
        shards_ref,
        q_ref,
        kk_ref,
        vv_ref,
        att_ref,
        bias,
        gain_sum,
        mixed,
        context,
        grad_mix,
        key_sum,
        value_sum,
        w_ref,
        stage,
        even,
        from_core,
        far,
        near,
        own_a,
        sent_a,
        landing_a,
        own_b,
        slots_b,
        send_sems,
        recv_sems,
        local_sems,
    ):
        at = Links(planes, group, send_sems, recv_sems)
        at.barrier([at.x, at.y, at.core, at.diagonal] + at.along[1:])

        def local(src, dst, n):
            copy = pltpu.make_async_copy(src, dst, local_sems.at[n])
            copy.start()
            return copy

        load_res = local(res_hbm, in_ref, 0)
        load_att = local(att_hbm, att_ref, 12)
        load_heads = [
            local(src, dst, 13 + n)
            for n, (src, dst) in enumerate(((q_hbm, q_ref), (kk_hbm, kk_ref), (vv_hbm, vv_ref)))
        ]
        load_out_w = local(
            w_hbm.at[:, pl.ds(mix + extra, width)], w_ref.at[:, pl.ds(0, width)], 1
        )
        plane = PlaneSum(
            at,
            length,
            lambda j: outs_ref.at[2 * j + 1],
            lambda j, q: even[j, q],
            from_core,
            far,
            near,
        )
        for j in (3, 2, 1, 0):
            plane.start(j)
        ring_a = RingSum(at, pack_a_ref, own_a, local_sems.at[6])
        ring_b = RingSum(at, pack_b_ref, own_b, local_sems.at[7])
        ring_a.fetch(planes - 1)
        loads = [local(outs_ref.at[2 * j], even.at[j], 2 + j) for j in range(4)]
        ring_a.last(before_ref, sent_a, landing_a)
        ring_b.first([slots_b.at[n] for n in range(planes - 3)] + [passed_b])
        staged = [None, None]
        turn = [0]

        def put(values, column, count):
            for base in range(0, count, part):
                n = turn[0] % 2
                turn[0] += 1
                if staged[n] is not None:
                    staged[n].wait()
                stage[n] = values[:, base : base + part]
                staged[n] = local(
                    stage.at[n], grad_hbm.at[:, pl.ds(column + base, part)], 8 + n
                )

        fill_bias(bias, starts_ref[0])
        gain_sum[...] = jnp.zeros_like(gain_sum)

        load_res.wait()

        def residual_grad(chunk):
            d, r = d_ref[chunk], in_ref[chunk]
            inv = lax.rsqrt(jnp.mean(r * r, axis=1, keepdims=True) + EPSILON)
            scaled = d * gain_ref[1:2, :]
            grad = (
                cot_ref[chunk].astype(F32)
                + inv * scaled
                - r * (inv * inv * inv * jnp.mean(scaled * r, axis=1, keepdims=True))
            )
            sum_ref[chunk] = grad
            mixed[chunk] = grad.astype(BF)
            gain_sum[1:2, :] += jnp.sum(d * r * inv, axis=0, keepdims=True)

        row_loop(length, 32, residual_grad)
        load_out_w.wait()
        for n in range(width // block):
            cols = slice(n * block, (n + 1) * block)
            context[:, cols] = dot_nt(mixed[...], w_ref[cols, :width]).astype(BF)
        load_mix_w = local(w_hbm.at[:, pl.ds(0, mix)], w_ref, 1)
        load_att.wait()
        for n in range(width // block):
            cols = slice(n * block, (n + 1) * block)
            put(dot_tn(att_ref[...], mixed[:, cols]).astype(BF), mix + extra + n * block, block)
        load_n1 = local(n1_hbm, mixed, 0)
        for copy in loads:
            copy.wait()
        plane.send_far()
        plane.send_x()
        plane.send_y()
        key_sum[...] = jnp.zeros_like(key_sum)
        value_sum[...] = jnp.zeros_like(value_sum)

        def attend(lower, upper):
            @pl.loop(lower, upper)
            def _(p):
                cols = pl.ds(pl.multiple_of(p * LANES, LANES), LANES)
                total = None
                for side in range(2):
                    head = (2 * p + side) // GROUP
                    query, grad = q_ref[:, cols], context[:, cols]
                    probs = softmax_rows(query, kk_ref[side, head], bias[...])
                    grad_probs = dot_nt(grad, vv_ref[side, head])
                    value_sum[side, head] += dot_tn(probs.astype(BF), grad)
                    inner = jnp.sum(probs * grad_probs, axis=1, keepdims=True)
                    logit = (probs * (grad_probs - inner)).astype(BF)
                    term = dot(logit, kk_ref[side, head])
                    total = term if total is None else total + term
                    key_sum[side, head] += dot_tn(logit, query)
                back = turned(total, tab_ref, -1.0) * (1.0 / math.sqrt(HEAD))
                grad_mix[:, cols] = back.astype(BF)

        for copy in load_heads:
            copy.wait()
        attend(0, PAIRS // 3)
        plane.onward_x()
        plane.onward_y()
        exchange = Exchange(at, ring_a.total(), shards_ref, ds)
        exchange.start(local_sems.at[10])
        attend(PAIRS // 3, 2 * PAIRS // 3)
        ring_b.next()
        exchange.onward()
        attend(2 * PAIRS // 3, PAIRS)
        load_x = local(x_hbm, context, 11)
        load_n1.wait()
        for pair in range(KV_HEADS // 2):
            for sums, base in ((key_sum, width), (value_sum, width + kvd)):

                def join(chunk, pair=pair, sums=sums, base=base):
                    low = lax.broadcasted_iota(jnp.int32, (chunk.size, LANES), 1) < HEAD
                    even = sums[0, 2 * pair, chunk] + pltpu.roll(sums[1, 2 * pair, chunk], HEAD, 1)
                    odd = sums[1, 2 * pair + 1, chunk] + pltpu.roll(
                        sums[0, 2 * pair + 1, chunk], HEAD, 1
                    )
                    values = jnp.where(low, even, odd)
                    if base == width:
                        values = turned(values, tab_ref.at[:, chunk], -1.0)
                    grad_mix[chunk, base + pair * LANES : base + (pair + 1) * LANES] = values.astype(BF)

                row_loop(length, 64, join)
        for n in range(mix // block):
            cols = slice(n * block, (n + 1) * block)
            put(dot_tn(mixed[...], grad_mix[:, cols]).astype(BF), n * block, block)
        load_mix_w.wait()
        for n in range(width // block):
            cols = slice(n * block, (n + 1) * block)
            in_ref[:, cols] = dot_nt(grad_mix[...], w_ref[cols, :mix])

        load_x.wait()

        def input_grad(chunk):
            d, x = in_ref[chunk], context[chunk].astype(F32)
            inv = lax.rsqrt(jnp.mean(x * x, axis=1, keepdims=True) + EPSILON)
            scaled = d * gain_ref[0:1, :]
            gain_sum[0:1, :] += jnp.sum(d * x * inv, axis=0, keepdims=True)
            in_ref[chunk] = (
                sum_ref[chunk]
                + inv * scaled
                - x * (inv * inv * inv * jnp.mean(scaled * x, axis=1, keepdims=True))
            )

        row_loop(length, 32, input_grad)
        gain_rows = jnp.concatenate([gain_sum[...].T, jnp.zeros((width, extra - 8), F32)], axis=1)
        put(gain_rows.astype(BF), mix, extra)

        def store(chunk, total):
            sum_ref[chunk] = total

        plane.end(store)
        ring_b.rest()
        exchange.end()
        for copy in staged:
            copy.wait()
        at.finish()

    shape = jax.ShapeDtypeStruct
    return pl.pallas_call(
        kernel,
        in_specs=[pl.BlockSpec(memory_space=pltpu.SMEM)]
        + [whole_vmem()] * 5
        + [anywhere()] * 11,
        out_specs=[whole_vmem()] * 3 + [anywhere()] * 2,
        out_shape=[
            shape((length, width), F32),
            shape((length, width), F32),
            shape((piece, wide), BF),
            shape((width, columns), BF),
            shape((PLANE, ds, wide), BF),
        ],
        scratch_shapes=[
            pltpu.VMEM((length, width), BF),
            pltpu.VMEM((2, KV_HEADS, length, LANES), BF),
            pltpu.VMEM((2, KV_HEADS, length, LANES), BF),
            pltpu.VMEM((length, width), BF),
            pltpu.VMEM((length, length), F32),
            pltpu.VMEM((8, width), F32),
            pltpu.VMEM((length, width), BF),
            pltpu.VMEM((length, width), BF),
            pltpu.VMEM((length, mix), BF),
            pltpu.VMEM((2, KV_HEADS, length, LANES), F32),
            pltpu.VMEM((2, KV_HEADS, length, LANES), F32),
            pltpu.VMEM((width, mix), BF),
            pltpu.VMEM((2, width, part), BF),
            pltpu.VMEM((4, length, width), BF),
            pltpu.VMEM((4 * length, width), BF),
            pltpu.VMEM((2, length // 2, width), BF),
            pltpu.VMEM((2, length, width), BF),
            pltpu.VMEM((piece, wide), BF),
            pltpu.VMEM((piece, wide), BF),
            pltpu.VMEM((piece, wide), BF),
            pltpu.VMEM((piece, wide), BF),
            pltpu.VMEM((planes - 3, piece, wide), BF),
        ]
        + dma_pairs(PlaneSum.copies + 1 + Exchange.copies + planes - 2)
        + [pltpu.SemaphoreType.DMA((16,))],
        compiler_params=pltpu.CompilerParams(
            collective_id=1, has_side_effects=True, vmem_limit_bytes=62 * 2**20
        ),
        cost_estimate=pl.CostEstimate(
            flops=80_000_000_000, bytes_accessed=50_000_000, transcendentals=0
        ),
    )(
        starts,
        grad_two,
        cotangent,
        tables,
        gains,
        before_a,
        q,
        kk,
        vv,
        att,
        tokens,
        n1,
        residual,
        front,
        outs,
        pack_a,
        pack_b,
    )


def scatter_front(grad, pack, before, planes, group):
    rows, columns = grad.shape
    ds, half = rows // (4 * planes), columns // 2
    part = share_of(half, 0.66)
    first, second = pl.ds(0, part), pl.ds(part, half - part)
    block, wide = pack.shape[1:]

    def kernel(
        g_ref,
        pack_ref,
        before_ref,
        out_ref,
        shards_ref,
        from_core,
        kept,
        far_a,
        far_b,
        near_x,
        near_y,
        total_ref,
        from_z,
        own,
        passed,
        landing,
        rows_own,
        send_sems,
        recv_sems,
        local_sems,
    ):
        at = Links(planes, group, send_sems, recv_sems)
        at.barrier([at.x, at.y, at.core, at.diagonal] + at.along[1:])
        ring = RingSum(at, pack_ref, own, local_sems.at[0])
        ring.fetch(planes - 1)

        def row(k, dy, core):
            owner = ((at.z + k) % planes) * 4 + (at.yb + dy) % 2 * 2 + core
            return pl.multiple_of(owner * ds, 16)

        def column(dx):
            return pl.ds(pl.multiple_of((at.xb + dx) % 2 * half, 128), half)

        order = list(range(1, planes)) + [0]
        arrive, loads = {}, {}
        for k in order:
            for dy in (1, 0):
                loads[k, dy] = pltpu.make_async_copy(
                    g_ref.at[pl.ds(row(k, dy, at.c), ds)],
                    rows_own.at[k, dy],
                    local_sems.at[2 + 2 * k + dy],
                )
                loads[k, dy].start()
                arrive[k, dy] = at.send(
                    g_ref.at[pl.ds(row(k, dy, 1 - at.c), ds)], from_core.at[k, dy], at.core
                )
        ring.last(before_ref, passed, landing)
        step = 16
        x_second, y_first, x_first, y_second, to_x, to_y = {}, {}, {}, {}, {}, {}
        for k in order:
            for dy in (1, 0):
                loads[k, dy].wait()
                arrive[k, dy].wait_recv()
                for dx in (1, 0):

                    def store(chunk, total, k=k, dx=dx, dy=dy):
                        kept[k, dx, dy, chunk] = total.astype(BF)

                    add_rows(
                        store,
                        [
                            lambda q, k=k, dx=dx, dy=dy: rows_own[k, dy, q, column(dx)],
                            lambda q, k=k, dx=dx, dy=dy: from_core[k, dy, q, column(dx)],
                        ],
                        ds,
                        step,
                    )
                    if (dx, dy) == (1, 1):
                        to_y[k] = at.send(kept.at[k, 1, 1, :, first], far_a.at[k], at.y)
                        to_x[k] = at.send(kept.at[k, 1, 1, :, second], far_b.at[k], at.x)
                    elif (dx, dy) == (0, 1):
                        y_first[k] = at.send(
                            kept.at[k, 0, 1, :, first], near_y.at[k, :, first], at.y
                        )
                    elif (dx, dy) == (1, 0):
                        x_second[k] = at.send(
                            kept.at[k, 1, 0, :, second], near_x.at[k, :, second], at.x
                        )
        for k in order:
            to_y[k].wait_recv()

            def store(chunk, total, k=k):
                kept[k, 1, 0, chunk, first] = total.astype(BF)

            add_rows(
                store,
                [lambda q, k=k: kept[k, 1, 0, q, first], lambda q, k=k: far_a[k, q]],
                ds,
                step,
            )
            x_first[k] = at.send(kept.at[k, 1, 0, :, first], near_x.at[k, :, first], at.x)
            to_x[k].wait_recv()

            def store(chunk, total, k=k):
                kept[k, 0, 1, chunk, second] = total.astype(BF)

            add_rows(
                store,
                [lambda q, k=k: kept[k, 0, 1, q, second], lambda q, k=k: far_b[k, q]],
                ds,
                step,
            )
            y_second[k] = at.send(kept.at[k, 0, 1, :, second], near_y.at[k, :, second], at.y)
        arrive_z = {}
        for k in order:
            for copies in (x_second, y_first, x_first, y_second):
                copies[k].wait_recv()

            def store(chunk, total, k=k):
                total_ref[k, chunk] = total.astype(BF)

            add_rows(
                store,
                [
                    lambda q, k=k: kept[k, 0, 0, q],
                    lambda q, k=k: near_x[k, q],
                    lambda q, k=k: near_y[k, q],
                ],
                ds,
                step,
            )
            if k > 0:
                arrive_z[k] = at.send(total_ref.at[k], from_z.at[k], at.along[k])
            if k == order[1]:
                exchange = Exchange(at, ring.total(), shards_ref, ds)
                exchange.start(local_sems.at[1])
        exchange.onward()
        for k in range(1, planes):
            arrive_z[k].wait_recv()

        def store(chunk, total):
            out_ref[chunk] = total.astype(BF)

        add_rows(
            store,
            [lambda q: total_ref[0, q]]
            + [lambda q, k=k: from_z[k, q] for k in range(1, planes)],
            ds,
            step,
        )
        exchange.end()
        at.finish()

    return pl.pallas_call(
        kernel,
        out_shape=[
            jax.ShapeDtypeStruct((ds, half), BF),
            jax.ShapeDtypeStruct((PLANE, ds, wide), BF),
        ],
        in_specs=[anywhere(), anywhere(), whole_vmem()],
        out_specs=[whole_vmem(), anywhere()],
        scratch_shapes=[
            pltpu.VMEM((planes, 2, ds, columns), BF),
            pltpu.VMEM((planes, 2, 2, ds, half), BF),
            pltpu.VMEM((planes, ds, part), BF),
            pltpu.VMEM((planes, ds, half - part), BF),
            pltpu.VMEM((planes, ds, half), BF),
            pltpu.VMEM((planes, ds, half), BF),
            pltpu.VMEM((planes, ds, half), BF),
            pltpu.VMEM((planes, ds, half), BF),
            pltpu.VMEM((block, wide), BF),
            pltpu.VMEM((block, wide), BF),
            pltpu.VMEM((block, wide), BF),
            pltpu.VMEM((planes, 2, ds, columns), BF),
        ]
        + dma_pairs(planes * 8 + planes - 1 + 1 + Exchange.copies)
        + [pltpu.SemaphoreType.DMA((2 + 2 * planes,))],
        compiler_params=comm_params(3),
        cost_estimate=pl.CostEstimate(
            flops=50_000_000_000, bytes_accessed=20_000_000, transcendentals=0
        ),
    )(grad, pack, before)


def unpack(packs, residual, term, hs):
    ds, wide = packs[0].shape[1:]
    hid = wide // 3
    blocks = ds // hs

    def kernel(*refs):
        sources = refs[: EPD + 2]
        gate_out, up_out, down_out, sum_ref, raw_in, raw_down = refs[EPD + 2 : EPD + 8]
        held, (sems, load_sems) = refs[EPD + 8 : -2], refs[-2:]
        ins, (res_ref, term_ref) = held[:EPD], held[EPD:]
        loads = [
            pltpu.make_async_copy(src, dst, load_sems.at[n])
            for n, (src, dst) in enumerate(zip(sources, held))
        ]
        for copy in loads:
            copy.start()
        copies = {}
        for n, (e, p) in enumerate((e, p) for e in range(EPD) for p in range(PLANE)):
            slot = n % 4
            if p == 0:
                loads[e].wait()
            if n >= 4:
                for copy in copies[n - 4]:
                    copy.wait()

            def cast(chunk, p=p, e=e, slot=slot):
                raw_in[slot, 0, chunk] = ins[e][p, chunk, :hid].astype(F32)
                raw_in[slot, 1, chunk] = ins[e][p, chunk, hid : 2 * hid].astype(F32)

            row_loop(ds, 16, cast)
            for b in range(blocks):
                raw_down[slot, :, b * hid : (b + 1) * hid] = ins[e][
                    p, b * hs : (b + 1) * hs, 2 * hid :
                ].astype(F32)
            index = p * EPD + e
            copies[n] = [
                pltpu.make_async_copy(src, dst, sems.at[slot, i])
                for i, (src, dst) in enumerate(
                    (
                        (raw_in.at[slot, 0], gate_out.at[:, index]),
                        (raw_in.at[slot, 1], up_out.at[:, index]),
                        (raw_down.at[slot], down_out.at[:, index]),
                    )
                )
            ]
            for copy in copies[n]:
                copy.start()

        def add(chunk):
            sum_ref[chunk] = res_ref[chunk] + term_ref[chunk]

        for copy in loads[EPD:]:
            copy.wait()
        row_loop(residual.shape[0], 32, add)
        for n in range(EXP - 4, EXP):
            for copy in copies[n]:
                copy.wait()

    shape = jax.ShapeDtypeStruct
    return pl.pallas_call(
        kernel,
        in_specs=[anywhere()] * (EPD + 2),
        out_specs=[anywhere()] * 3 + [whole_vmem()],
        out_shape=[
            shape((ds, EXP, hid), F32),
            shape((ds, EXP, hid), F32),
            shape((hs, EXP, blocks * hid), F32),
            shape(residual.shape, F32),
        ],
        scratch_shapes=[
            pltpu.VMEM((4, 2, ds, hid), F32),
            pltpu.VMEM((4, hs, blocks * hid), F32),
        ]
        + [pltpu.VMEM(packs[0].shape, BF)] * EPD
        + [pltpu.VMEM(residual.shape, F32)] * 2
        + [pltpu.SemaphoreType.DMA((4, 3)), pltpu.SemaphoreType.DMA((EPD + 2,))],
        compiler_params=pltpu.CompilerParams(vmem_limit_bytes=60 * 2**20),
    )(*packs, residual, term)


def shards(
    reps,
    group,
    tokens,
    cotangent,
    routes,
    gates,
    starts,
    norm1_gain,
    w_query,
    w_key,
    w_value,
    w_out,
    norm2_gain,
    w_gate,
    w_up,
    w_down,
):
    planes = group // 4
    r, f = lax.axis_index("rep"), lax.axis_index("fsdp")
    xb, yb, c, z = r % 2, (f // 2) % 2, f % 2, f // 4
    mine = xb * 4 + yb * 2 + c

    def perm(to):
        return [
            (a * group + b, to(a, b)[0] * group + to(a, b)[1])
            for a in range(reps)
            for b in range(group)
        ]

    def pp(value, to):
        return lax.ppermute(value, AXES, perm(to))

    def go(value, dx, dy, dc):
        return pp(value, lambda a, b: (a ^ dx, b ^ (dy * 2 + dc)))

    def along(value, k):
        return pp(value, lambda a, b: (a, (b + 4 * k) % group))

    def all_reps(value):
        step = 2
        while step < reps:
            value = value + pp(value, lambda a, b, s=step: (a ^ s, b))
            step *= 2
        return value

    length, width = tokens.shape
    ds = w_query.shape[0]
    hs = w_down.shape[0]
    hid = w_gate.shape[2]
    kvd = w_key.shape[1]
    half_rows = length // 2

    mix = width + 2 * kvd
    gain_end = mix + 256
    gains = jnp.stack([norm1_gain.astype(BF), norm2_gain.astype(BF)], axis=1)
    own_mix = jnp.concatenate(
        [
            w_query.astype(BF),
            w_key.astype(BF),
            w_value.astype(BF),
            gains,
            jnp.zeros((ds, 254), BF),
        ],
        axis=1,
    )

    def rep_half(own):
        half = own.shape[1] // 2
        return lax.dynamic_slice(own, (0, xb * half), (ds, half))

    experts = jnp.arange(EXP, dtype=jnp.int32)[:, None, None]
    share = jnp.sum(jnp.where(routes[None] == experts, gates[None], 0.0), axis=2)
    pairs = PLANE // 2
    share = jnp.pad(share.reshape(PLANE, EPD, length), ((0, 0), (0, 8 - EPD), (0, 0)))

    front, wall_a, wall_b, grads_all, shares, gains_all, q, kk, vv, att, residual, n1, n2 = forward(
        starts,
        tokens,
        cotangent,
        rep_half(own_mix),
        rep_half(w_out.astype(BF)),
        share,
        w_gate,
        w_up,
        w_down,
        planes,
        group,
    )
    out_sum, pack_a, pack_b, grad_normed_two, before_a = run_experts(
        n2,
        grads_all.reshape(pairs, 2 * length, width),
        shares,
        wall_a.reshape(planes, 4 * ds, 3 * hid),
        wall_b.reshape(planes, 4 * ds, 3 * hid),
        planes,
        group,
    )
    input_grad, out_term, before_b, front_grad, shards_a = backward(
        starts,
        grad_normed_two,
        cotangent,
        tokens,
        residual,
        front,
        gains_all,
        q,
        kk,
        vv,
        att,
        n1,
        out_sum.reshape(PLANE, length, width),
        pack_a,
        before_a,
        pack_b,
        planes,
        group,
    )
    front_total, shards_b = scatter_front(front_grad, pack_b, before_b, planes, group)
    total = all_reps(front_total)
    gate_shard, up_shard, down_shard, output = unpack(
        [all_reps(shards_a), all_reps(shards_b)], residual, out_term, hs
    )
    other = go(total, 1, 0, 0)
    front_shard = jnp.where(
        xb == 0,
        jnp.concatenate([total, other], axis=1),
        jnp.concatenate([other, total], axis=1),
    ).astype(F32)
    return (
        output,
        input_grad,
        front_shard[:, mix],
        front_shard[:, :width],
        front_shard[:, width : width + kvd],
        front_shard[:, width + kvd : mix],
        front_shard[:, gain_end:],
        front_shard[:, mix + 1],
        gate_shard,
        up_shard,
        down_shard,
    )


def solution(mesh):
    reps, group = mesh.shape["rep"], mesh.shape["fsdp"]
    both, one = P(AXES, None), P("fsdp")
    flat, deep = P("fsdp", None), P("fsdp", None, None)

    def whole(*args):
        return shards(reps, group, *args)

    return jax.shard_map(
        whole,
        mesh=mesh,
        in_specs=(both, both, both, both, P(AXES), one, flat, flat, flat, flat, one, deep, deep, deep),
        out_specs=(both, both, one, flat, flat, flat, flat, one, deep, deep, deep),
        check_vma=False,
    )
```
